128 devices in a mesh: seq: 2 (over x_hi), exp: 64 (over y, z, x_lo, core).
Axes of the slice: x: 4 (x_hi: 2, x_lo: 2; x = x_hi * 2 + x_lo), y: 4, z: 4, core: 2. Of those that a mesh axis runs over, the one named last changes fastest.
Arguments:
- tokens: bfloat16 [64, 256, 1280], P('exp', 'seq'), may hold values from -6 to 6
- cotangent: bfloat16 [64, 256, 1280], P('exp', 'seq'), may hold values from -6 to 6
- segments: int32 [64, 256], P('exp'), may hold values from 0 to 4, as said below
- routes: int32 [64, 256, 7], P('exp', 'seq'), may hold values from 0 to 63, all different within a row; in each aligned block of 128 rows (0 to 127, 128 to 255, ..., all dimensions but the last counted through in order) at most 17 rows name the same one
- norm_gain_attn: bfloat16 [1280], P('exp'), may hold values from 0.5 to 1.5
- w_query: bfloat16 [1280, 1280], P('exp'), may hold values from -0.25 to 0.25
- w_key: bfloat16 [1280, 1280], P('exp'), may hold values from -0.25 to 0.25
- w_value: bfloat16 [1280, 1280], P('exp'), may hold values from -0.15625 to 0.15625
- w_out: bfloat16 [1280, 1280], P('exp'), may hold values from -0.5 to 0.5
- norm_gain_ffn: bfloat16 [1280], P('exp'), may hold values from 0.5 to 1.5
- w_router: bfloat16 [1280, 64], P('exp'), may hold values from -0.078125 to 0.078125
- shared_gate: bfloat16 [1280, 896], P('exp'), may hold values from -0.15625 to 0.15625
- shared_up: bfloat16 [1280, 896], P('exp'), may hold values from -0.15625 to 0.15625
- shared_down: bfloat16 [896, 1280], P('exp'), may hold values from -0.1875 to 0.1875
- expert_gate: bfloat16 [64, 1280, 896], P('exp'), may hold values from -0.15625 to 0.15625
- expert_up: bfloat16 [64, 1280, 896], P('exp'), may hold values from -0.15625 to 0.15625
- expert_down: bfloat16 [64, 896, 1280], P('exp'), may hold values from -0.1875 to 0.1875
Outputs:
- layer_out: bfloat16 [64, 256, 1280], P('exp', 'seq')
- grad_tokens: float32 [64, 256, 1280], P('exp', 'seq')
- grad_norm_attn: float32 [1280], P('exp')
- grad_w_query: float32 [1280, 1280], P('exp')
- grad_w_key: float32 [1280, 1280], P('exp')
- grad_w_value: float32 [1280, 1280], P('exp')
- grad_w_out: float32 [1280, 1280], P('exp')
- grad_norm_ffn: float32 [1280], P('exp')
- grad_router: float32 [1280, 64], P('exp')
- grad_shared_gate: float32 [1280, 896], P('exp')
- grad_shared_up: float32 [1280, 896], P('exp')
- grad_shared_down: float32 [896, 1280], P('exp')
- grad_expert_gate: float32 [64, 1280, 896], P('exp')
- grad_expert_up: float32 [64, 1280, 896], P('exp')
- grad_expert_down: float32 [64, 896, 1280], P('exp')
The draws below stay inside these ranges and needn't reach their ends.
Inputs may be any that keep to these rules, and one draw needn't show every extreme that they name: `routes`: each row names 7 different experts. Within the rows of one device (aligned blocks of 128 rows, in the order of sequences and then positions) no expert is named more than 17 times. `segments`: along each sequence the numbers start at 0 and rise by one at the start of each document, so every sequence holds 5 documents.
All inputs are finite; a program needn't handle non-finite values.
Results may differ from the reference program's by a relative error of at most 0.015.
The reference program's roundings to bfloat16 on the way count: a program that leaves them out, or rounds other values in their place, can miss the bound.
Values may be sent and summed in bfloat16 or wider, within the bound.
A program may use at most 192 MiB of HBM per device.

```python
import math
import jax
import jax.numpy as jnp
import numpy as np
from jax import lax

D = 1280
HEADS = 10
H = 896
TOP = 7
TOK_DEV = 128
DOCS = 5
EXPERTS = 64
SEQS = 64
LENGTH = 256
CAP = 17


def draw_segments(key, part):
    key = jax.random.fold_in(key, 11)
    width_bin = LENGTH // DOCS
    offsets = jnp.arange(DOCS - 1, dtype=jnp.int32) * width_bin + 1
    starts = jax.random.randint(key, (SEQS, DOCS - 1), 0, width_bin - 1, dtype=jnp.int32) + offsets[None, :]
    starts = jnp.where(starts == LENGTH // 2, starts + 1, starts)
    places = jnp.arange(LENGTH, dtype=jnp.int32)
    return jnp.sum((places[None, None, :] >= starts[:, :, None]).astype(jnp.int32), axis=1)


def steps_of(own_key, shape, shards, least, high):
    gain, own = 1.0, jax.random.fold_in(own_key, 6)
    for dim, blocks in shards:
        steps = jnp.exp(jax.random.uniform(jax.random.fold_in(own, dim), (blocks,), jnp.float32, least / len(shards), high / len(shards)))
        gain = gain * jnp.repeat(steps, shape[dim] // blocks).reshape([-1 if axis == dim else 1 for axis in range(len(shape))])
    return gain


def shared_out(own_key, own, number, rows, count, top, most, skew):
    sequence = jax.random.permutation(own_key, count)
    crowded, common = shares(count, rows * top, most, skew, True), shares(count, rows * top, most, skew, False)
    places = jnp.arange(count)

    def named(tallies, rotation):
        used = int((tallies > 0).sum())
        fixed = max(1, used // 4)
        moved = fixed + (places - fixed + rotation * (used - fixed)) % max(1, count - fixed)
        return jnp.zeros((count,), jnp.int32).at[sequence[jnp.where(places < fixed, places, moved)]].set(jnp.asarray(tallies, jnp.int32))

    tallies = jnp.where(number % 4 == 0, named(crowded, number // 4), named(common, number - number // 4 - 1))
    mixed = jax.random.permutation(jax.random.fold_in(own, 3), count)
    donor, taker = mixed[0:count // 2 * 2:2], mixed[1:count // 2 * 2:2]
    margin = jnp.minimum(tallies[donor] - 1, most - tallies[taker]) // 2
    margin = jnp.where((donor == sequence[0]) | (taker == sequence[0]) | (tallies[taker] == 0), 0, jnp.maximum(margin, 0))
    moved = jax.random.randint(jax.random.fold_in(own, 4), (count // 2,), 0, 1 << 20) % (margin + 1)
    tallies = tallies.at[donor].add(-moved).at[taker].add(moved)
    items = jnp.searchsorted(jnp.cumsum(tallies), jnp.arange(rows * top), side="right").astype(jnp.int32)
    listing = items.reshape(top, rows).T
    listing = listing[jax.random.permutation(jax.random.fold_in(own, 1), rows)]
    rotation = jax.random.randint(jax.random.fold_in(own, 2), (rows, 1), 0, top)
    return jnp.take_along_axis(listing, (jnp.arange(top)[None, :] + rotation) % top, axis=1)


def shares(count, total, bound, lean, full):
    loads = [(1 << 20) // math.isqrt(standing ** lean) + 1 for standing in range(1, count + 1)]
    largest = bound if full else min(bound, max(-(-total // count), total * loads[0] // sum(loads)))
    least = 1 if total - largest >= count - 1 else 0
    given, rest = [largest] + [least] * (count - 1), total - largest - least * (count - 1)
    while rest > 0:
        movable = [i for i in range(1, count) if given[i] < largest] or [i for i in range(1, count) if given[i] < bound]
        whole, remaining = sum([loads[i] for i in movable]), rest
        for i in movable:
            extra = min(bound - given[i], max(1, remaining * loads[i] // whole), rest)
            given[i] = given[i] + extra
            rest = rest - extra
    return np.array(given)


def noise(own_key, extent, spread, most, shards=(), held_as=jnp.bfloat16):
    drawn = spread * jax.random.normal(own_key, extent, jnp.float32)
    if shards:
        drawn = drawn * steps_of(own_key, extent, shards, -0.22, 0.18)
    return jnp.clip(drawn, -most, most).astype(held_as)


def setup_inputs(seed: int = 0) -> dict:
    key_of = jax.random.split(jax.random.key(seed), 18)
    tokens = noise(key_of[0], (SEQS, LENGTH, D), 1.0, 6.0, ((0, 64), (1, 2)))
    cotangent = noise(key_of[1], (SEQS, LENGTH, D), 1.0, 6.0, ((0, 64), (1, 2)))
    segments = draw_segments(jax.random.fold_in(key_of[17], 71), 0)
    routes_keys = jax.random.split(jax.random.fold_in(key_of[3], 1), SEQS * LENGTH // TOK_DEV)
    routes_turns = jax.random.permutation(jax.random.fold_in(key_of[3], 3), SEQS * LENGTH // TOK_DEV)
    routes = jax.vmap(lambda own, number: shared_out(jax.random.fold_in(key_of[3], 2), own, number, TOK_DEV, EXPERTS, TOP, CAP, 1))(routes_keys, routes_turns).reshape((SEQS, LENGTH, TOP))
    norm_gain_attn = jnp.clip(1.0 + 0.1 * jax.random.normal(key_of[4], (D,), jnp.float32), 0.5, 1.5).astype(jnp.bfloat16)
    w_query = noise(key_of[5], (D, D), (D // 2) ** -0.5, 0.25, ((0, 64),))
    w_key = noise(key_of[6], (D, D), (D // 2) ** -0.5, 0.25, ((0, 64),))
    w_value = noise(key_of[7], (D, D), D ** -0.5, 0.15625, ((0, 64),))
    w_out = noise(key_of[8], (D, D), (D // 8) ** -0.5, 0.5, ((0, 64),))
    norm_gain_ffn = jnp.clip(1.0 + 0.1 * jax.random.normal(key_of[9], (D,), jnp.float32), 0.5, 1.5).astype(jnp.bfloat16)
    w_router = noise(key_of[10], (D, EXPERTS), (4 * D) ** -0.5, 0.078125, ((0, 64),))
    shared_gate = noise(key_of[11], (D, H), D ** -0.5, 0.15625, ((0, 64),))
    shared_up = noise(key_of[12], (D, H), D ** -0.5, 0.15625, ((0, 64),))
    shared_down = noise(key_of[13], (H, D), H ** -0.5, 0.1875, ((0, 64),))
    expert_gate = noise(key_of[14], (EXPERTS, D, H), D ** -0.5, 0.15625, ((0, 64),))
    expert_up = noise(key_of[15], (EXPERTS, D, H), D ** -0.5, 0.15625, ((0, 64),))
    expert_down = noise(key_of[16], (EXPERTS, H, D), H ** -0.5, 0.1875, ((0, 64),))
    return {"tokens": tokens, "cotangent": cotangent, "segments": segments, "routes": routes, "norm_gain_attn": norm_gain_attn, "w_query": w_query, "w_key": w_key, "w_value": w_value, "w_out": w_out, "norm_gain_ffn": norm_gain_ffn, "w_router": w_router, "shared_gate": shared_gate, "shared_up": shared_up, "shared_down": shared_down, "expert_gate": expert_gate, "expert_up": expert_up, "expert_down": expert_down}


EPSILON = 1e-06
NEG_BIG = -1e+30
HIGH = lax.Precision.HIGHEST

@jax.custom_vjp
def low(v):
    return lax.optimization_barrier(v.astype(jnp.bfloat16)).astype(jnp.float32)

@jax.custom_vjp
def low_back(v):
    return v

def low_keep(v):
    return (low(v), None)

def low_pass(kept, grad):
    return (grad,)

def back_keep(v):
    return (v, None)

def back_low(kept, grad):
    return (low(grad),)
low.defvjp(low_keep, low_pass)
low_back.defvjp(back_keep, back_low)

def matmul(left, right):
    return jnp.dot(left, right, precision=HIGH)

def rms_norm(values, gain_vec):
    return values * lax.rsqrt(lax.optimization_barrier(jnp.mean(values * values, axis=-1, keepdims=True)) + EPSILON) * gain_vec

def rotary_tables(positions, head_width):
    half_width = head_width // 2
    freq = jnp.power(10000.0, -2.0 * jnp.arange(half_width, dtype=jnp.float32) / head_width)
    angles = positions.astype(jnp.float32)[:, None] * freq[None, :]
    return (jnp.cos(angles)[:, None, :], jnp.sin(angles)[:, None, :])

def rotate(values, cosine, sine):
    half_width = values.shape[-1] // 2
    first = values[..., :half_width]
    second = values[..., half_width:]
    return jnp.concatenate([first * cosine - second * sine, second * cosine + first * sine], axis=-1)

def attend_sequence(act_seq, seg_seq, w_query, w_key, w_value):
    seq_len, model_width = act_seq.shape
    head_width = model_width // HEADS
    positions = jnp.arange(seq_len, dtype=jnp.int32)
    cosine, sine = rotary_tables(positions, head_width)
    queries = low(rotate(low_back(matmul(act_seq, w_query)).reshape(seq_len, HEADS, head_width), cosine, sine))
    keys_all = low(rotate(low_back(matmul(act_seq, w_key)).reshape(seq_len, HEADS, head_width), cosine, sine))
    values_all = low_back(low(matmul(act_seq, w_value))).reshape(seq_len, HEADS, head_width)
    scores = low_back(jnp.einsum('thd,shd->hts', queries, keys_all, precision=HIGH) * head_width ** (-0.5))
    allowed = (positions[None, :] <= positions[:, None]) & (seg_seq[None, :] == seg_seq[:, None])
    probs = jax.nn.softmax(jnp.where(allowed[None], scores, NEG_BIG), axis=-1)
    mixed = jnp.einsum('hts,shd->thd', low(probs), values_all, precision=HIGH)
    return low_back(low(mixed.reshape(seq_len, model_width)))

def routed_block(act_blk, route_blk, gate_blk, expert_gate, expert_up, expert_down):
    tok_rows, top_count = route_blk.shape
    model_width = act_blk.shape[1]
    experts = expert_gate.shape[0]
    flat_route = route_blk.reshape(-1)
    member = (flat_route[:, None] == jnp.arange(experts, dtype=jnp.int32)[None, :]).astype(jnp.int32)
    rank = lax.optimization_barrier(jnp.sum((jnp.cumsum(member, axis=0) - member) * member, axis=1))
    slot = flat_route * CAP + rank
    source_rows = jnp.repeat(act_blk, top_count, axis=0)
    arrived = jnp.zeros((experts * CAP, model_width), jnp.float32).at[slot].set(source_rows)
    arrived = low_back(arrived).reshape(experts, CAP, model_width)
    gate_e = low_back(jnp.einsum('ecd,edh->ech', arrived, expert_gate, precision=HIGH))
    up_e = low_back(jnp.einsum('ecd,edh->ech', arrived, expert_up, precision=HIGH))
    hidden_e = low(jax.nn.silu(gate_e) * up_e)
    result = low(jnp.einsum('ech,ehd->ecd', hidden_e, expert_down, precision=HIGH)).reshape(experts * CAP, model_width)
    gathered = low_back(result[slot]).reshape(tok_rows, top_count, model_width)
    return lax.optimization_barrier(jnp.sum(gate_blk[:, :, None] * gathered, axis=1))

def layer_forward(tokens, gain_attn, w_query, w_key, w_value, w_out, gain_ffn, w_router, shared_gate, shared_up, shared_down, expert_gate, expert_up, expert_down, segments, routes):
    model_width = tokens.shape[2]
    normed = low(rms_norm(tokens, gain_attn))

    def per_seq(pair):
        return attend_sequence(pair[0], pair[1], w_query, w_key, w_value)
    mixed = lax.map(jax.checkpoint(per_seq), (normed, segments))
    attn_out = low_back(matmul(mixed.reshape(-1, model_width), w_out))
    hidden_one = tokens.reshape(-1, model_width) + attn_out
    act_ffn = low(rms_norm(hidden_one, gain_ffn))
    logits = low_back(matmul(act_ffn, w_router))
    flat_routes = routes.reshape(-1, TOP)
    chosen = jnp.take_along_axis(logits, flat_routes, axis=1)
    gates = jax.nn.softmax(chosen, axis=-1)
    gate_s = low_back(matmul(act_ffn, shared_gate))
    up_s = low_back(matmul(act_ffn, shared_up))
    hidden_s = low(jax.nn.silu(gate_s) * up_s)
    out_s = low_back(matmul(hidden_s, shared_down))
    blocks = flat_routes.shape[0] // TOK_DEV

    def per_block(trio):
        return routed_block(trio[0], trio[1], trio[2], expert_gate, expert_up, expert_down)
    routed = lax.map(jax.checkpoint(per_block), (act_ffn.reshape(blocks, TOK_DEV, model_width), flat_routes.reshape(blocks, TOK_DEV, TOP), gates.reshape(blocks, TOK_DEV, TOP)))
    final = hidden_one + out_s + routed.reshape(-1, model_width)
    return final.reshape(tokens.shape)

def reference(tokens, cotangent, segments, routes, norm_gain_attn, w_query, w_key, w_value, w_out, norm_gain_ffn, w_router, shared_gate, shared_up, shared_down, expert_gate, expert_up, expert_down):
    floats = tuple((member_array.astype(jnp.float32) for member_array in (tokens, norm_gain_attn, w_query, w_key, w_value, w_out, norm_gain_ffn, w_router, shared_gate, shared_up, shared_down, expert_gate, expert_up, expert_down)))

    def closed(*pieces):
        return layer_forward(*pieces, segments, routes)
    final, pullback = jax.vjp(closed, *floats)
    grads = pullback(cotangent.astype(jnp.float32))
    return (final.astype(jnp.bfloat16), grads[0], grads[1], grads[2], grads[3], grads[4], grads[5], grads[6], grads[7], grads[8], grads[9], grads[10], grads[11], grads[12], grads[13])
```

```python
import functools
import jax
import jax.numpy as jnp
from jax import lax
from jax.experimental import pallas as pl
from jax.experimental.pallas import tpu as pltpu
from jax.sharding import PartitionSpec as P

HEADS = 10
EPSILON = 1e-06
NEG_BIG = -1e30
F32 = jnp.float32
BF16 = jnp.bfloat16
MESH = pl.DeviceIdType.MESH

WIDE = 58
HALF = 29 * 128
UNITS = ((0, 15, 8, 0, 3, 2), (15, 14, 7, 3, 2, 1))


def place():
    hi = lax.axis_index("seq")
    e = lax.axis_index("exp")
    return hi, e // 16, lax.rem(e // 4, 4), lax.rem(e // 2, 2), lax.rem(e, 2)


def device(hi, y, z, lo, c):
    return (hi, ((y * 4 + z) * 2 + lo) * 2 + c)


def up(v):
    return lax.rem(v + 1, 4)


def dn(v):
    return lax.rem(v + 3, 4)


def opp(v):
    return lax.rem(v + 2, 4)


def greet(devices):
    bar = pltpu.get_barrier_semaphore()
    for to in devices:
        pl.semaphore_signal(bar, inc=1, device_id=to, device_id_type=MESH)
    pl.semaphore_wait(bar, len(devices))


class Sender:
    def __init__(self, send_sem, recv_sem, local_sem):
        self.sems = (send_sem, recv_sem, local_sem)
        self.sent = []
        self.kept = 0

    def remote(self, src, dst, to):
        k = len(self.sent)
        copy = pltpu.make_async_remote_copy(
            src_ref=src,
            dst_ref=dst,
            send_sem=self.sems[0].at[k],
            recv_sem=self.sems[1].at[k],
            device_id=to,
            device_id_type=MESH,
        )
        copy.start()
        self.sent.append(copy)
        return copy

    def local(self, src, dst):
        copy = pltpu.make_async_copy(src, dst, self.sems[2].at[self.kept])
        self.kept += 1
        copy.start()
        return copy

    def finish(self):
        for copy in self.sent:
            copy.wait_send()


def arrived(copies):
    for copy in copies:
        copy.wait_recv()


def ring_neighbours(hi, y, z, lo, c):
    return {
        ("y", 1): device(hi, up(y), z, lo, c),
        ("y", -1): device(hi, dn(y), z, lo, c),
        ("z", 1): device(hi, y, up(z), lo, c),
        ("z", -1): device(hi, y, dn(z), lo, c),
    }


def columns(u, half, core):
    s, w, w0, s2, v, v0 = UNITS[u]
    if half == 0:
        w, v = w0, v0
    elif half == 1:
        s, w, s2, v = s + w0, w - w0, s2 + v0, v - v0
    return (
        pl.ds(pl.multiple_of(core * HALF + s * 128, 128), w * 128),
        pl.ds(pl.multiple_of(core * 640 + s2 * 128, 128), v * 128),
    )


def gather_kernel(win, sdw, out, osd, wsib, pw, pwx, blk, bsd, ssem, rsem, lsem):
    hi, y, z, lo, c = place()
    sib = device(hi, y, z, lo, 1 - c)
    xn = device(hi, y, z, 1 - lo, c)
    nb = ring_neighbours(hi, y, z, lo, c)
    greet([sib, xn] + list(nb.values()))
    wires = Sender(ssem, rsem, lsem)
    mul = pl.multiple_of
    j = lo * 2 + c
    other = pl.ds(mul((1 - c) * HALF, 128), HALF)
    mine = pl.ds(mul(c * HALF, 128), HALF)
    other2 = pl.ds(mul((1 - c) * 640, 128), 640)
    mine2 = pl.ds(mul(c * 640, 128), 640)
    r16 = pl.ds(mul(j * 16, 16), 16)
    a = wires.remote(win.at[:, other], wsib, sib)
    b = wires.remote(sdw.at[:, other2], bsd.at[r16], sib)
    bsd[r16, :] = sdw[:, mine2]
    own = win[:, mine]
    a.wait_recv()
    got = wsib[...]
    first = jnp.where(c == 0, own, got)
    second = jnp.where(c == 0, got, own)
    pw[0:16] = first[0:16]
    pw[16:32] = first[16:32] + second[0:16]
    pw[32:48] = second[16:32]
    b.wait_recv()
    a = wires.remote(pw, pwx, xn)
    r32 = pl.ds(mul(lo * 32, 16), 32)
    b = wires.remote(bsd.at[r32], bsd.at[r32], xn)
    a.wait_recv()
    own = pw[...]
    got = pwx[...]
    first = jnp.where(lo == 0, own, got)
    second = jnp.where(lo == 0, got, own)
    blk[0:32] = first[0:32]
    blk[32:48] = first[32:48] + second[0:16]
    blk[48:80] = second[16:48]
    b.wait_recv()
    keep = [wires.local(blk, out.at[y, z, :, mine]), wires.local(bsd, osd.at[y, z, :, mine2])]

    def region(u, half, by, bz):
        c1, c2 = columns(u, half, c)
        return out.at[by, bz, :, c1], osd.at[by, bz, :, c2]

    def send(u, half, by, bz, to, src=None):
        r = region(u, half, by, bz)
        s = src or r
        return [wires.remote(s[0], r[0], to), wires.remote(s[1], r[1], to)]

    def spot(u, q1, q2):
        return (q1, q2) if u == 0 else (q2, q1)

    units = []
    for u in (0, 1):
        a1, a2 = ("y", "z") if u == 0 else ("z", "y")
        p1, p2 = (y, z) if u == 0 else (z, y)
        s, w, w0, s2, v, v0 = UNITS[u]
        src = (blk.at[:, pl.ds(s * 128, w * 128)], bsd.at[:, pl.ds(s2 * 128, v * 128)])
        at = spot(u, p1, p2)
        unit = dict(a1=a1, a2=a2, p1=p1, p2=p2)
        unit["up1"] = send(u, None, *at, nb[a1, 1], src)
        unit["dn1"] = send(u, None, *at, nb[a1, -1], src)
        unit["up2"] = [send(u, None, *at, nb[a2, 1], src)]
        unit["dn2"] = [send(u, None, *at, nb[a2, -1], src)]
        unit["sib"] = [send(u, None, *at, sib, src)]
        units.append(unit)

    def second_axis(u, q1):
        unit = units[u]
        at = spot(u, q1, unit["p2"])
        unit["up2"].append(send(u, None, *at, nb[unit["a2"], 1]))
        unit["dn2"].append(send(u, None, *at, nb[unit["a2"], -1]))
        unit["sib"].append(send(u, None, *at, sib))

    for u, unit in enumerate(units):
        arrived(unit["up1"])
        unit["f1"] = send(u, 0, *spot(u, dn(unit["p1"]), unit["p2"]), nb[unit["a1"], 1])
    for u, unit in enumerate(units):
        arrived(unit["dn1"])
        unit["f2"] = send(u, 1, *spot(u, up(unit["p1"]), unit["p2"]), nb[unit["a1"], -1])
    for u, unit in enumerate(units):
        second_axis(u, dn(unit["p1"]))
        second_axis(u, up(unit["p1"]))
    for u, unit in enumerate(units):
        arrived(unit["f1"])
        arrived(unit["f2"])
        second_axis(u, opp(unit["p1"]))
    turn = [lambda p: p, dn, up, opp]
    for k in range(4):
        for u, unit in enumerate(units):
            q1 = turn[k](unit["p1"])
            arrived(unit["up2"][k])
            at = spot(u, q1, dn(unit["p2"]))
            unit["g1", k] = send(u, 0, *at, nb[unit["a2"], 1])
            unit["sib"].append(send(u, None, *at, sib))
            arrived(unit["dn2"][k])
            at = spot(u, q1, up(unit["p2"]))
            unit["g2", k] = send(u, 1, *at, nb[unit["a2"], -1])
            unit["sib"].append(send(u, None, *at, sib))
    for k in range(4):
        for u, unit in enumerate(units):
            arrived(unit["g1", k])
            arrived(unit["g2", k])
            at = spot(u, turn[k](unit["p1"]), opp(unit["p2"]))
            unit["sib"].append(send(u, None, *at, sib))
    for unit in units:
        for copies in unit["sib"]:
            arrived(copies)
    wires.finish()
    for copy in keep:
        copy.wait()


def gather_weights(shard, down):
    offset = 4 * lax.rem(lax.axis_index("exp"), 4)
    window = lax.dynamic_update_slice(jnp.zeros((32, WIDE * 128), BF16), shard, (offset, 0))
    down = jnp.pad(down, ((0, 2), (0, 0)))
    sems = 4 + 2 * 2 * 36
    out, osd = pl.pallas_call(
        gather_kernel,
        out_shape=(
            jax.ShapeDtypeStruct((4, 4, 80, WIDE * 128), BF16),
            jax.ShapeDtypeStruct((4, 4, 64, 1280), BF16),
        ),
        in_specs=[pl.BlockSpec(memory_space=pltpu.VMEM)] * 2,
        out_specs=(pl.BlockSpec(memory_space=pl.ANY),) * 2,
        scratch_shapes=[
            pltpu.VMEM((32, HALF), BF16),
            pltpu.VMEM((48, HALF), BF16),
            pltpu.VMEM((48, HALF), BF16),
            pltpu.VMEM((80, HALF), BF16),
            pltpu.VMEM((64, 640), BF16),
            pltpu.SemaphoreType.DMA((sems,)),
            pltpu.SemaphoreType.DMA((sems,)),
            pltpu.SemaphoreType.DMA((2,)),
        ],
        compiler_params=pltpu.CompilerParams(
            collective_id=1, has_side_effects=True, vmem_limit_bytes=40 << 20
        ),
        name="gather_weights",
    )(window, down)
    return out.reshape(1280, WIDE * 128), osd.reshape(1024, 1280)


def scatter_kernel(gw, gsd, out, osd, *scratch):
    hold = [scratch[0:2], scratch[2:4]]
    from_sib = [scratch[4:6], scratch[6:8]]
    bufs = [[scratch[8 + 8 * u + 4 * a : 12 + 8 * u + 4 * a] for a in (0, 1)] for u in (0, 1)]
    fin, fsd, wx, wxd, wh, whd, snd, sndd, acc, accd, ssem, rsem, lsem = scratch[24:]
    hi, y, z, lo, c = place()
    sib = device(hi, y, z, lo, 1 - c)
    xn = device(hi, y, z, 1 - lo, c)
    hn = device(1 - hi, y, z, lo, c)
    nb = ring_neighbours(hi, y, z, lo, c)
    greet([sib, xn, hn] + list(nb.values()))
    wires = Sender(ssem, rsem, lsem)
    mul = pl.multiple_of
    first_pos, second_pos = (y, z), (z, y)
    first_axis, second_axis = ("y", "z"), ("z", "y")

    def pair(src, dst, to):
        return [wires.remote(src[0], dst[0], to), wires.remote(src[1], dst[1], to)]

    def region(u, core, q1, q2):
        by, bz = (q1, q2) if u == 0 else (q2, q1)
        c1, c2 = columns(u, None, core)
        return gw.at[by, bz, :, c1], gsd.at[by, bz, :, c2]

    def at(refs, *index):
        return [refs[0].at[index], refs[1].at[index]]

    def order(u):
        p1, p2 = first_pos[u], second_pos[u]
        ones = [opp(p1), up(p1), dn(p1), p1]
        return [(q1, q2) for q2 in (opp(p2), up(p2), dn(p2), p2) for q1 in ones]

    orders = [order(0), order(1)]
    coming = {}
    for k in range(16):
        for u in (0, 1):
            q = orders[u][k]
            coming[u, k] = pair(region(u, 1 - c, *q), at(from_sib[u], *q), sib)
            coming[u, k, "own"] = [wires.local(a, b) for a, b in zip(region(u, c, *q), at(hold[u], *q))]

    def add_in(dst, *more):
        @pl.loop(0, dst.shape[-2] // 16)
        def _(i):
            r = pl.ds(mul(i * 16, 16), 16)
            value = dst[r, :].astype(F32)
            for ref in more:
                value = value + ref[r, :].astype(F32)
            dst[r, :] = value.astype(BF16)

    def ready(u, k):
        arrived(coming[u, k])
        for copy in coming[u, k, "own"]:
            copy.wait()
        for a in (0, 1):
            add_in(hold[u][a].at[orders[u][k]], from_sib[u][a].at[orders[u][k]])
        return at(hold[u], *orders[u][k])

    def half(refs, u, h):
        s, w, w0, s2, v, v0 = UNITS[u]
        lanes = [(0, w0), (w0, w - w0)][h], [(0, v0), (v0, v - v0)][h]
        return [refs[i].at[:, pl.ds(lanes[i][0] * 128, lanes[i][1] * 128)] for i in (0, 1)]

    def buffer(u, i, slot):
        return [bufs[u][0][i].at[slot], bufs[u][1][i].at[slot]]

    ring = {}

    def far_block(u, slot, blk, axis):
        ring[u, slot, 0] = pair(half(blk, u, 0), buffer(u, 0, slot), nb[axis, 1])
        ring[u, slot, 1] = pair(half(blk, u, 1), buffer(u, 1, slot), nb[axis, -1])

    def near_block(u, slot, blk, axis, way):
        h = 0 if way == 1 else 1
        arrived(ring[u, slot, h])
        for dst, more in zip(half(blk, u, h), buffer(u, h, slot)):
            add_in(dst, more)
        ring[u, slot, 2 + h] = pair(blk, buffer(u, 2 + h, slot), nb[axis, way])

    def own_block(u, slot, blk):
        arrived(ring[u, slot, 2])
        arrived(ring[u, slot, 3])
        for dst, one, two in zip(blk, buffer(u, 2, slot), buffer(u, 3, slot)):
            add_in(dst, one, two)

    for i in range(4):
        for u in (0, 1):
            far_block(u, i, ready(u, i), second_axis[u])
    for i in range(4):
        for u in (0, 1):
            near_block(u, i, ready(u, 4 + i), second_axis[u], 1)
        for u in (0, 1):
            near_block(u, i, ready(u, 8 + i), second_axis[u], -1)
    for i in range(4):
        for u in (0, 1):
            blk = ready(u, 12 + i)
            own_block(u, i, blk)
            if i == 0:
                far_block(u, 4, blk, first_axis[u])
            if i == 1:
                near_block(u, 4, blk, first_axis[u], 1)
            if i == 2:
                near_block(u, 4, blk, first_axis[u], -1)
    for u in (0, 1):
        blk = at(hold[u], *orders[u][15])
        own_block(u, 4, blk)
        s, w, w0, s2, v, v0 = UNITS[u]
        fin[:, s * 128 : (s + w) * 128] = blk[0][...]
        fsd[:, s2 * 128 : (s2 + v) * 128] = blk[1][...]
    r = mul((1 - lo) * 32, 16)
    arrived(pair((fin.at[pl.ds(r, 48)], fsd.at[pl.ds(r, 32)]), (wx, wxd), xn))
    r = mul(lo * 32, 16)
    snd[...] = (fin[pl.ds(r, 48), :].astype(F32) + wx[...].astype(F32)).astype(BF16)
    sndd[...] = (fsd[pl.ds(r, 32), :].astype(F32) + wxd[...].astype(F32)).astype(BF16)
    arrived(pair((snd, sndd), (wh, whd), hn))
    acc[...] = snd[...].astype(F32) + wh[...].astype(F32)
    accd[...] = sndd[...].astype(F32) + whd[...].astype(F32)
    mine = pl.ds(mul(c * HALF, 128), HALF)
    mine2 = pl.ds(mul(c * 640, 128), 640)
    r = mul((1 - c) * 16, 16)
    last = pair((acc.at[pl.ds(r, 32)], accd.at[pl.ds(r, 16)]), (out.at[:, mine], osd.at[:, mine2]), sib)
    r = mul(c * 16, 16)
    out[:, mine] = acc[pl.ds(r, 32), :]
    osd[:, mine2] = accd[pl.ds(r, 16), :]
    arrived(last)
    wires.finish()


def scatter_sums(gw, gsd):
    scratch = []
    for _ in (0, 1):
        for s, w, w0, s2, v, v0 in UNITS:
            scratch += [pltpu.VMEM((4, 4, 80, w * 128), BF16), pltpu.VMEM((4, 4, 64, v * 128), BF16)]
    for s, w, w0, s2, v, v0 in UNITS:
        for rows, n, n0 in ((80, w, w0), (64, v, v0)):
            for tiles in (n0, n - n0, n, n):
                scratch.append(pltpu.VMEM((5, rows, tiles * 128), BF16))
    for rows, rows2 in ((80, 64), (48, 32), (48, 32), (48, 32)):
        scratch += [pltpu.VMEM((rows, HALF), BF16), pltpu.VMEM((rows2, 640), BF16)]
    scratch += [pltpu.VMEM((48, HALF), F32), pltpu.VMEM((32, 640), F32)]
    sems = 64 + 2 * 2 * 4 * 5 + 6
    scratch += [
        pltpu.SemaphoreType.DMA((sems,)),
        pltpu.SemaphoreType.DMA((sems,)),
        pltpu.SemaphoreType.DMA((64,)),
    ]
    out, osd = pl.pallas_call(
        scatter_kernel,
        out_shape=(jax.ShapeDtypeStruct((32, WIDE * 128), F32), jax.ShapeDtypeStruct((16, 1280), F32)),
        in_specs=[pl.BlockSpec(memory_space=pl.ANY)] * 2,
        out_specs=(pl.BlockSpec(memory_space=pltpu.VMEM),) * 2,
        scratch_shapes=scratch,
        compiler_params=pltpu.CompilerParams(
            collective_id=2, has_side_effects=True, vmem_limit_bytes=56 << 20
        ),
        name="scatter_sums",
    )(gw.reshape(4, 4, 80, WIDE * 128), gsd.reshape(4, 4, 64, 1280))
    offset = 4 * lax.rem(lax.axis_index("exp"), 4)
    return lax.dynamic_slice(out, (offset, 0), (20, WIDE * 128)), osd[:14]


PART_AXES = (("y", "z", "g"), ("z", "g", "y"), ("g", "y", "z"))


def exchange_kernel(cuts, *refs):
    n = len(cuts)
    stages = [refs[0:n], refs[2 * n : 3 * n], refs[3 * n : 4 * n], refs[n : 2 * n]]
    hi, y, z, lo, c = place()
    me = {"y": y, "z": z, "g": lo * 2 + c}
    wires = Sender(*refs[4 * n :])

    def peer(axis, k):
        q = dict(me)
        q[axis] = lax.rem(me[axis] + k, 4)
        return q[axis], device(hi, q["y"], q["z"], q["g"] // 2, lax.rem(q["g"], 2))

    greet([peer(axis, k)[1] for axis in "yzg" for k in (1, 2, 3)])
    every = slice(None)

    def view(ref, axis, v, lanes):
        index = {"y": (v, every, every), "z": (every, v, every), "g": (every, every, v)}[axis]
        return ref.at[index + (every, pl.ds(lanes[0] * 128, lanes[1] * 128))]

    pending = {}

    def go(part, phase):
        axis = PART_AXES[part][phase]
        waits = []
        for a in range(n):
            src, dst = stages[phase][a], stages[phase + 1][a]
            lanes = cuts[a][part]
            own = view(dst, axis, me[axis], lanes)
            for k in (2, 1, 3):
                v, to = peer(axis, k)
                waits.append(wires.remote(view(src, axis, v, lanes), own, to).wait_recv)
            waits.append(wires.local(view(src, axis, me[axis], lanes), own).wait)
        pending[part, phase] = waits

    for part in range(3):
        go(part, 0)
    for phase in (1, 2):
        for part in range(3):
            for wait in pending[part, phase - 1]:
                wait()
            go(part, phase)
    for part in range(3):
        for wait in pending[part, 2]:
            wait()
    wires.finish()


def exchange(collective_id, arrays, cuts):
    n = len(arrays)
    split = [a.reshape((4, 4, 4) + a.shape[1:]) for a in arrays]
    shapes = [jax.ShapeDtypeStruct(a.shape, a.dtype) for a in split]
    out = pl.pallas_call(
        functools.partial(exchange_kernel, cuts),
        out_shape=tuple(shapes),
        in_specs=[pl.BlockSpec(memory_space=pl.ANY)] * n,
        out_specs=(pl.BlockSpec(memory_space=pl.ANY),) * n,
        scratch_shapes=[pltpu.VMEM(s.shape, s.dtype) for s in shapes] * 2
        + [
            pltpu.SemaphoreType.DMA((27 * n,)),
            pltpu.SemaphoreType.DMA((27 * n,)),
            pltpu.SemaphoreType.DMA((9 * n,)),
        ],
        compiler_params=pltpu.CompilerParams(
            collective_id=collective_id, has_side_effects=True, vmem_limit_bytes=40 << 20
        ),
        name="exchange_rows",
    )(*split)
    return [o.reshape(a.shape) for o, a in zip(out, arrays)]


def weight_grad_kernel(left, right, out):
    out[...] = lax.dot_general(
        left[0], right[...], (((0,), (0,)), ((), ())), preferred_element_type=F32
    ).astype(BF16)


def weight_grads(left, right):
    rows = left.shape[1]
    wide = 256
    return pl.pallas_call(
        weight_grad_kernel,
        grid=(WIDE * 128 // wide,),
        out_shape=jax.ShapeDtypeStruct((left.shape[2], WIDE * 128), BF16),
        in_specs=[
            pl.BlockSpec(
                (1, rows, left.shape[2]),
                lambda i: (jnp.where(i < 15, 0, jnp.where(i < 20, 1, 2)), 0, 0),
            ),
            pl.BlockSpec((rows, wide), lambda i: (0, i)),
        ],
        out_specs=pl.BlockSpec((left.shape[2], wide), lambda i: (0, i)),
        compiler_params=pltpu.CompilerParams(vmem_limit_bytes=32 << 20),
        name="weight_grads",
    )(left, right)


def rms_forward(values, gain_vec):
    inv_rms = lax.rsqrt(jnp.mean(values * values, axis=-1, keepdims=True) + EPSILON)
    return (values * inv_rms * gain_vec, inv_rms)


def rms_backward(values, inv_rms, gain_vec, upstream):
    weighted = upstream * gain_vec
    inner = jnp.mean(weighted * values, axis=-1, keepdims=True)
    grad_in = inv_rms * weighted - values * (inv_rms * inv_rms * inv_rms) * inner
    grad_gain = jnp.sum(upstream * values * inv_rms, axis=0)
    return (grad_in, grad_gain)


def rotary_tables(positions, head_width):
    half_width = head_width // 2
    freq = jnp.power(10000.0, -2.0 * jnp.arange(half_width, dtype=F32) / head_width)
    angles = positions.astype(F32)[:, None] * freq[None, :]
    return (jnp.cos(angles)[:, None, :], jnp.sin(angles)[:, None, :])


def rotate(values, cosine, sine):
    half_width = values.shape[-1] // 2
    first = values[..., :half_width]
    second = values[..., half_width:]
    return jnp.concatenate([first * cosine - second * sine, second * cosine + first * sine], axis=-1)


def unrotate(values, cosine, sine):
    return rotate(values, cosine, -sine)


def silu_parts(pre_act):
    sigma = jax.nn.sigmoid(pre_act)
    return (pre_act * sigma, sigma * (1.0 + pre_act * (1.0 - sigma)))


def dot(a, b):
    return jnp.dot(a, b, preferred_element_type=F32)


def dot_t(a, b):
    return lax.dot_general(a, b, (((1,), (1,)), ((), ())), preferred_element_type=F32)


def t_dot(a, b):
    return lax.dot_general(a, b, (((0,), (0,)), ((), ())), preferred_element_type=F32)


def score_block(queries, keys_all, allowed, inv_root):
    scores = jnp.einsum("thd,shd->hts", queries, keys_all, preferred_element_type=F32) * inv_root
    return jnp.where(allowed[None], scores, NEG_BIG)


def per_device(
    tokens,
    cotangent,
    segments,
    routes,
    norm_gain_attn,
    w_query,
    w_key,
    w_value,
    w_out,
    norm_gain_ffn,
    w_router,
    shared_gate,
    shared_up,
    shared_down,
    expert_gate,
    expert_up,
    expert_down,
):
    tok_rows = tokens.shape[1]
    width = tokens.shape[2]
    head_width = width // HEADS
    experts = w_router.shape[1]
    top_count = routes.shape[2]
    slots = tok_rows * top_count * 5 // (experts * 4)
    even = slots - 1

    def spread(w):
        w = w.reshape(w.shape[0], experts, w.shape[1] // experts)
        return jnp.pad(w, ((0, 0), (0, 0), (0, 2))).reshape(w.shape[0], experts * 16)

    shard = jnp.concatenate(
        [
            w_query,
            w_key,
            w_value,
            w_out,
            spread(shared_gate),
            spread(shared_up),
            w_router,
            norm_gain_attn[:, None],
            norm_gain_ffn[:, None],
            jnp.zeros((w_query.shape[0], 190), BF16),
        ],
        axis=1,
    )
    weights, sdown_w = gather_weights(shard, shared_down)
    qkv_w = weights[:, :3840]
    out_w = weights[:, 3840:5120]
    sgu_w = weights[:, 5120:7168]
    router_w = weights[:, 7168 : 7168 + experts]
    gain_attn = weights[:, 7168 + experts].astype(F32)
    gain_ffn = weights[:, 7169 + experts].astype(F32)

    route_rows = routes[0]
    picked = route_rows[:, :, None] == jnp.arange(experts, dtype=jnp.int32)[None, None, :]
    member = jnp.any(picked, axis=1)
    before = jnp.arange(tok_rows)[None, :] < jnp.arange(tok_rows)[:, None]
    rank = dot(before.astype(BF16), member.astype(BF16)).astype(jnp.int32)
    slot_of = jnp.where(member, rank, -1).T
    place_even = slot_of[:, None, :] == jnp.arange(even, dtype=jnp.int32)[None, :, None]
    place_last = slot_of == even
    even_hot = place_even.astype(BF16).reshape(experts * even, tok_rows)
    last_hot = place_last.astype(BF16)

    inv_root = head_width ** (-0.5)
    seq_place = lax.axis_index("seq")
    inputs = tokens[0].astype(F32)
    positions = seq_place * tok_rows + jnp.arange(tok_rows, dtype=jnp.int32)
    cosine, sine = rotary_tables(positions, head_width)
    seg_row = segments[0]
    own_seg = lax.dynamic_slice_in_dim(seg_row, seq_place * tok_rows, tok_rows)
    prior_seg = lax.dynamic_slice_in_dim(seg_row, jnp.maximum(seq_place - 1, 0) * tok_rows, tok_rows)
    key_places = jnp.concatenate([positions - tok_rows, positions])
    key_segs = jnp.concatenate([prior_seg, own_seg])
    allowed = (
        (key_places[None, :] <= positions[:, None])
        & (key_places[None, :] >= 0)
        & (key_segs[None, :] == own_seg[:, None])
    )
    normed_attn, inv_attn = rms_forward(inputs, gain_attn)
    act_attn = normed_attn.astype(BF16)
    qkv = dot(act_attn, qkv_w)
    heads = lambda v: v.reshape(tok_rows, HEADS, head_width)
    queries = rotate(heads(qkv[:, :width]), cosine, sine).astype(BF16)
    keys_own = rotate(heads(qkv[:, width : 2 * width]), cosine, sine).astype(BF16)
    values_own = heads(qkv[:, 2 * width :].astype(BF16))
    prior = lax.ppermute(jnp.stack([keys_own, values_own]), "seq", [(0, 1)])
    keys_all = jnp.concatenate([prior[0], keys_own], axis=0)
    values_all = jnp.concatenate([prior[1], values_own], axis=0)
    scores = score_block(queries, keys_all, allowed, inv_root)
    top_score = jnp.max(scores, axis=-1, keepdims=True)
    expo = jnp.exp(scores - top_score)
    probs = expo / jnp.sum(expo, axis=-1, keepdims=True)
    probs_low = probs.astype(BF16)
    mixed = (
        jnp.einsum("hts,shd->thd", probs_low, values_all, preferred_element_type=F32)
        .reshape(tok_rows, width)
        .astype(BF16)
    )
    hidden_one = inputs + dot(mixed, out_w)
    normed_ffn, inv_ffn = rms_forward(hidden_one, gain_ffn)
    act_ffn = normed_ffn.astype(BF16)
    logits = jnp.where(member, dot(act_ffn, router_w), NEG_BIG)
    gate_expo = jnp.where(member, jnp.exp(logits - jnp.max(logits, axis=-1, keepdims=True)), 0.0)
    gates = gate_expo / jnp.sum(gate_expo, axis=-1, keepdims=True)

    grad_low = cotangent[0]
    gates_t = gates.T
    slot_gates = jnp.concatenate(
        [
            jnp.sum(jnp.where(place_even, gates_t[:, None, :], 0.0), axis=-1),
            jnp.sum(jnp.where(place_last, gates_t, 0.0), axis=-1, keepdims=True),
        ],
        axis=1,
    )
    both = jnp.concatenate([act_ffn, grad_low], axis=1)
    even_rows = dot(even_hot, both).astype(BF16).reshape(experts, even, 2 * width)
    last_rows = jnp.concatenate(
        [dot(last_hot, both), jnp.pad(slot_gates, ((0, 0), (0, 128 - slots)))], axis=1
    )
    rows_x, rows_g, rows_l = exchange(
        3,
        (even_rows[:, :, :width], even_rows[:, :, width:], last_rows[:, None, :]),
        (((0, 4), (4, 3), (7, 3)), ((0, 3), (3, 4), (7, 3)), ((0, 6), (6, 6), (12, 9))),
    )
    rows_l = rows_l[:, 0]
    arrived_x = jnp.concatenate([rows_x.reshape(-1, width), rows_l[:, :width].astype(BF16)])
    arrived_g = jnp.concatenate([rows_g.reshape(-1, width), rows_l[:, width : 2 * width].astype(BF16)])
    row_gates = jnp.concatenate(
        [rows_l[:, 2 * width : 2 * width + even].reshape(-1), rows_l[:, 2 * width + even]]
    )

    gate_local, up_local, down_local = expert_gate[0], expert_up[0], expert_down[0]
    gate_e = dot(arrived_x, gate_local)
    up_e = dot(arrived_x, up_local)
    silu_e, slope_e = silu_parts(gate_e)
    hidden_e = (silu_e * up_e).astype(BF16)
    result = dot(hidden_e, down_local).astype(BF16)
    grad_result = (row_gates[:, None] * arrived_g.astype(F32)).astype(BF16)
    grad_hidden_e = dot_t(grad_result, down_local)
    grad_gate_e = (grad_hidden_e * up_e * slope_e).astype(BF16)
    grad_up_e = (grad_hidden_e * silu_e).astype(BF16)
    part_expert = (
        t_dot(arrived_x, grad_gate_e).astype(BF16),
        t_dot(arrived_x, grad_up_e).astype(BF16),
        t_dot(hidden_e, grad_result).astype(BF16),
    )
    grad_arrived = (dot_t(grad_gate_e, gate_local) + dot_t(grad_up_e, up_local)).astype(BF16)
    swapped = [lax.ppermute(g, "seq", [(0, 1), (1, 0)]) for g in part_expert]
    rows_out = experts * even
    back = exchange(
        4,
        (
            result[:rows_out].reshape(experts, even, width),
            grad_arrived[:rows_out].reshape(experts, even, width),
            jnp.concatenate([result[rows_out:], grad_arrived[rows_out:]], axis=1).astype(F32)[:, None, :],
        ),
        (((0, 4), (4, 3), (7, 3)), ((0, 3), (3, 4), (7, 3)), ((0, 6), (6, 6), (12, 8))),
    )
    back_out, back_grad = back[0].reshape(-1, width), back[1].reshape(-1, width)
    back_last = back[2][:, 0].astype(BF16)

    gate_s = dot(act_ffn, sgu_w[:, :1024])
    up_s = dot(act_ffn, sgu_w[:, 1024:])
    silu_s, slope_s = silu_parts(gate_s)
    hidden_s = (silu_s * up_s).astype(BF16)
    out_s = dot(hidden_s, sdown_w)
    grad_hidden_s = dot_t(grad_low, sdown_w)
    grad_gate_s = (grad_hidden_s * up_s * slope_s).astype(BF16)
    grad_up_s = (grad_hidden_s * silu_s).astype(BF16)
    grad_shared_down = t_dot(hidden_s, grad_low).astype(BF16)

    weight_even = jnp.where(place_even, gates_t[:, None, :], 0.0).reshape(rows_out, tok_rows)
    weight_last = jnp.where(place_last, gates_t, 0.0)

    def weighted(w, rows):
        top = lax.reduce_precision(w, 8, 7)
        mid = lax.reduce_precision(w - top, 8, 7)
        low = (w - top) - mid
        three = jnp.concatenate([top, mid, low], axis=1).astype(BF16)
        s = t_dot(three, rows)
        return s[:tok_rows] + s[tok_rows : 2 * tok_rows] + s[2 * tok_rows :]

    routed = weighted(weight_even, back_out) + weighted(weight_last, back_last[:, :width])
    layer_out = (hidden_one + out_s + routed).astype(BF16)

    grad_final = grad_low.astype(F32)
    dots_even = dot_t(back_out, grad_low).reshape(experts, even, tok_rows)
    dots_last = dot_t(back_last[:, :width], grad_low)
    grad_gates = (
        jnp.sum(jnp.where(place_even, dots_even, 0.0), axis=1) + jnp.where(place_last, dots_last, 0.0)
    ).T
    grad_logits = (gates * (grad_gates - jnp.sum(gates * grad_gates, axis=-1, keepdims=True))).astype(BF16)
    grad_routed = t_dot(even_hot, back_grad) + t_dot(last_hot, back_last[:, width:])
    grad_gu_s = jnp.concatenate([grad_gate_s, grad_up_s], axis=1)
    grad_act_ffn = grad_routed + dot_t(grad_logits, router_w) + dot_t(grad_gu_s, sgu_w)
    grad_norm_f, grad_gain_ffn = rms_backward(hidden_one, inv_ffn, gain_ffn, grad_act_ffn)
    grad_hidden_one = grad_final + grad_norm_f
    grad_attn_low = grad_hidden_one.astype(BF16)
    grad_mixed = heads(dot_t(grad_attn_low, out_w).astype(BF16))

    grad_probs = jnp.einsum("thd,shd->hts", grad_mixed, values_all, preferred_element_type=F32)
    inner = jnp.sum(probs * grad_probs, axis=-1, keepdims=True)
    grad_scores = (probs * (grad_probs - inner)).astype(BF16)
    grad_values_all = jnp.einsum("hts,thd->shd", probs_low, grad_mixed, preferred_element_type=F32)
    grad_query_rot = jnp.einsum("hts,shd->thd", grad_scores, keys_all, preferred_element_type=F32) * inv_root
    grad_keys_all = jnp.einsum("hts,thd->shd", grad_scores, queries, preferred_element_type=F32) * inv_root
    later = lax.ppermute(
        jnp.stack([grad_keys_all[:tok_rows], grad_values_all[:tok_rows]]).astype(BF16), "seq", [(1, 0)]
    ).astype(F32)
    grad_key_rot = grad_keys_all[tok_rows:] + later[0]
    grad_value = (grad_values_all[tok_rows:] + later[1]).astype(BF16).reshape(tok_rows, width)
    grad_query = unrotate(grad_query_rot, cosine, sine).astype(BF16).reshape(tok_rows, width)
    grad_key = unrotate(grad_key_rot, cosine, sine).astype(BF16).reshape(tok_rows, width)
    grad_qkv = jnp.concatenate([grad_query, grad_key, grad_value], axis=1)
    grad_act_attn = dot_t(grad_qkv, qkv_w)
    grad_norm_a, grad_gain_attn = rms_backward(inputs, inv_attn, gain_attn, grad_act_attn)
    grad_tokens = grad_hidden_one + grad_norm_a

    right = jnp.concatenate(
        [grad_qkv, grad_attn_low, grad_gu_s, grad_logits, jnp.zeros((tok_rows, 256 - experts), BF16)], axis=1
    )
    grads = weight_grads(jnp.stack([act_attn, mixed, act_ffn]), right)
    gains = jnp.stack([grad_gain_attn, grad_gain_ffn], axis=1).astype(BF16)
    grads = lax.dynamic_update_slice(grads, gains, (0, 7168 + experts))
    own, own_down = scatter_sums(grads, grad_shared_down)

    def gathered_hidden(w):
        return w.reshape(w.shape[0], experts, 16)[:, :, :14].reshape(w.shape[0], experts * 14)

    expert_grads = [
        (a.astype(F32) + b.astype(F32))[None] for a, b in zip(part_expert, swapped)
    ]
    return (
        layer_out[None],
        grad_tokens[None],
        own[:, 7168 + experts],
        own[:, :1280],
        own[:, 1280:2560],
        own[:, 2560:3840],
        own[:, 3840:5120],
        own[:, 7169 + experts],
        own[:, 7168 : 7168 + experts],
        gathered_hidden(own[:, 5120:6144]),
        gathered_hidden(own[:, 6144:7168]),
        own_down,
        *expert_grads,
    )


def solution(mesh):
    rows = P("exp", None)
    deep = P("exp", None, None)
    split = P("exp", "seq", None)
    gain = P("exp")
    in_specs = (split, split, rows, split, gain, rows, rows, rows, rows, gain) + (rows,) * 4 + (deep,) * 3
    out_specs = (split, split, gain, rows, rows, rows, rows, gain) + (rows,) * 4 + (deep,) * 3
    return jax.shard_map(per_device, mesh=mesh, in_specs=in_specs, out_specs=out_specs, check_vma=False)
```

```python
import functools
import jax
import jax.numpy as jnp
import numpy as np
from jax import lax
from jax.experimental import pallas as pl
from jax.experimental.pallas import tpu as pltpu
from jax.sharding import PartitionSpec as P

HEADS = 10
EPSILON = 1e-06
NEG_BIG = -1e30
F32 = jnp.float32
BF16 = jnp.bfloat16
MESH = pl.DeviceIdType.MESH

WIDE = 58
HALF = 29 * 128
UNITS = ((0, 15, 8, 0, 3, 2), (15, 14, 7, 3, 2, 1))


def place():
    hi = lax.axis_index("seq")
    e = lax.axis_index("exp")
    return hi, e // 16, lax.rem(e // 4, 4), lax.rem(e // 2, 2), lax.rem(e, 2)


def device(hi, y, z, lo, c):
    return (hi, ((y * 4 + z) * 2 + lo) * 2 + c)


def up(v):
    return lax.rem(v + 1, 4)


def dn(v):
    return lax.rem(v + 3, 4)


def opp(v):
    return lax.rem(v + 2, 4)


def greet(devices):
    bar = pltpu.get_barrier_semaphore()
    for to in devices:
        pl.semaphore_signal(bar, inc=1, device_id=to, device_id_type=MESH)
    pl.semaphore_wait(bar, len(devices))


class Sender:
    def __init__(self, send_sem, recv_sem, local_sem):
        self.sems = (send_sem, recv_sem, local_sem)
        self.sent = []
        self.kept = 0

    def remote(self, src, dst, to):
        k = len(self.sent)
        copy = pltpu.make_async_remote_copy(
            src_ref=src,
            dst_ref=dst,
            send_sem=self.sems[0].at[k],
            recv_sem=self.sems[1].at[k],
            device_id=to,
            device_id_type=MESH,
        )
        copy.start()
        self.sent.append(copy)
        return copy

    def local(self, src, dst):
        copy = pltpu.make_async_copy(src, dst, self.sems[2].at[self.kept])
        self.kept += 1
        copy.start()
        return copy

    def finish(self):
        for copy in self.sent:
            copy.wait_send()


def arrived(copies):
    for copy in copies:
        copy.wait_recv()


def ring_neighbours(hi, y, z, lo, c):
    return {
        ("y", 1): device(hi, up(y), z, lo, c),
        ("y", -1): device(hi, dn(y), z, lo, c),
        ("z", 1): device(hi, y, up(z), lo, c),
        ("z", -1): device(hi, y, dn(z), lo, c),
    }


def columns(u, half, core):
    s, w, w0, s2, v, v0 = UNITS[u]
    if half == 0:
        w, v = w0, v0
    elif half == 1:
        s, w, s2, v = s + w0, w - w0, s2 + v0, v - v0
    return (
        pl.ds(pl.multiple_of(core * HALF + s * 128, 128), w * 128),
        pl.ds(pl.multiple_of(core * 640 + s2 * 128, 128), v * 128),
    )


def gather_kernel(win, sdw, out, osd, wsib, pw, pwx, blk, bsd, ssem, rsem, lsem):
    hi, y, z, lo, c = place()
    sib = device(hi, y, z, lo, 1 - c)
    xn = device(hi, y, z, 1 - lo, c)
    nb = ring_neighbours(hi, y, z, lo, c)
    greet([sib, xn] + list(nb.values()))
    wires = Sender(ssem, rsem, lsem)
    mul = pl.multiple_of
    j = lo * 2 + c
    other = pl.ds(mul((1 - c) * HALF, 128), HALF)
    mine = pl.ds(mul(c * HALF, 128), HALF)
    other2 = pl.ds(mul((1 - c) * 640, 128), 640)
    mine2 = pl.ds(mul(c * 640, 128), 640)
    r16 = pl.ds(mul(j * 16, 16), 16)
    a = wires.remote(win.at[:, other], wsib, sib)
    b = wires.remote(sdw.at[:, other2], bsd.at[r16], sib)
    bsd[r16, :] = sdw[:, mine2]
    own = win[:, mine]
    a.wait_recv()
    got = wsib[...]
    first = jnp.where(c == 0, own, got)
    second = jnp.where(c == 0, got, own)
    pw[0:16] = first[0:16]
    pw[16:32] = first[16:32] + second[0:16]
    pw[32:48] = second[16:32]
    b.wait_recv()
    a = wires.remote(pw, pwx, xn)
    r32 = pl.ds(mul(lo * 32, 16), 32)
    b = wires.remote(bsd.at[r32], bsd.at[r32], xn)
    a.wait_recv()
    own = pw[...]
    got = pwx[...]
    first = jnp.where(lo == 0, own, got)
    second = jnp.where(lo == 0, got, own)
    blk[0:32] = first[0:32]
    blk[32:48] = first[32:48] + second[0:16]
    blk[48:80] = second[16:48]
    b.wait_recv()
    keep = [wires.local(blk, out.at[y, z, :, mine]), wires.local(bsd, osd.at[y, z, :, mine2])]

    def region(u, half, by, bz):
        c1, c2 = columns(u, half, c)
        return out.at[by, bz, :, c1], osd.at[by, bz, :, c2]

    def send(u, half, by, bz, to, src=None):
        r = region(u, half, by, bz)
        s = src or r
        return [wires.remote(s[0], r[0], to), wires.remote(s[1], r[1], to)]

    def spot(u, q1, q2):
        return (q1, q2) if u == 0 else (q2, q1)

    units = []
    for u in (0, 1):
        a1, a2 = ("y", "z") if u == 0 else ("z", "y")
        p1, p2 = (y, z) if u == 0 else (z, y)
        s, w, w0, s2, v, v0 = UNITS[u]
        src = (blk.at[:, pl.ds(s * 128, w * 128)], bsd.at[:, pl.ds(s2 * 128, v * 128)])
        at = spot(u, p1, p2)
        unit = dict(a1=a1, a2=a2, p1=p1, p2=p2)
        unit["up1"] = send(u, None, *at, nb[a1, 1], src)
        unit["dn1"] = send(u, None, *at, nb[a1, -1], src)
        unit["up2"] = [send(u, None, *at, nb[a2, 1], src)]
        unit["dn2"] = [send(u, None, *at, nb[a2, -1], src)]
        unit["sib"] = [send(u, None, *at, sib, src)]
        units.append(unit)

    def second_axis(u, q1):
        unit = units[u]
        at = spot(u, q1, unit["p2"])
        unit["up2"].append(send(u, None, *at, nb[unit["a2"], 1]))
        unit["dn2"].append(send(u, None, *at, nb[unit["a2"], -1]))
        unit["sib"].append(send(u, None, *at, sib))

    for u, unit in enumerate(units):
        arrived(unit["up1"])
        unit["f1"] = send(u, 0, *spot(u, dn(unit["p1"]), unit["p2"]), nb[unit["a1"], 1])
    for u, unit in enumerate(units):
        arrived(unit["dn1"])
        unit["f2"] = send(u, 1, *spot(u, up(unit["p1"]), unit["p2"]), nb[unit["a1"], -1])
    for u, unit in enumerate(units):
        second_axis(u, dn(unit["p1"]))
        second_axis(u, up(unit["p1"]))
    for u, unit in enumerate(units):
        arrived(unit["f1"])
        arrived(unit["f2"])
        second_axis(u, opp(unit["p1"]))
    turn = [lambda p: p, dn, up, opp]
    for k in range(4):
        for u, unit in enumerate(units):
            q1 = turn[k](unit["p1"])
            arrived(unit["up2"][k])
            at = spot(u, q1, dn(unit["p2"]))
            unit["g1", k] = send(u, 0, *at, nb[unit["a2"], 1])
            unit["sib"].append(send(u, None, *at, sib))
            arrived(unit["dn2"][k])
            at = spot(u, q1, up(unit["p2"]))
            unit["g2", k] = send(u, 1, *at, nb[unit["a2"], -1])
            unit["sib"].append(send(u, None, *at, sib))
    for k in range(4):
        for u, unit in enumerate(units):
            arrived(unit["g1", k])
            arrived(unit["g2", k])
            at = spot(u, turn[k](unit["p1"]), opp(unit["p2"]))
            unit["sib"].append(send(u, None, *at, sib))
    for unit in units:
        for copies in unit["sib"]:
            arrived(copies)
    wires.finish()
    for copy in keep:
        copy.wait()


def gather_weights(shard, down):
    offset = 4 * lax.rem(lax.axis_index("exp"), 4)
    window = lax.dynamic_update_slice(jnp.zeros((32, WIDE * 128), BF16), shard, (offset, 0))
    down = jnp.pad(down, ((0, 2), (0, 0)))
    sems = 4 + 2 * 2 * 36
    out, osd = pl.pallas_call(
        gather_kernel,
        out_shape=(
            jax.ShapeDtypeStruct((4, 4, 80, WIDE * 128), BF16),
            jax.ShapeDtypeStruct((4, 4, 64, 1280), BF16),
        ),
        in_specs=[pl.BlockSpec(memory_space=pltpu.VMEM)] * 2,
        out_specs=(pl.BlockSpec(memory_space=pl.ANY),) * 2,
        scratch_shapes=[
            pltpu.VMEM((32, HALF), BF16),
            pltpu.VMEM((48, HALF), BF16),
            pltpu.VMEM((48, HALF), BF16),
            pltpu.VMEM((80, HALF), BF16),
            pltpu.VMEM((64, 640), BF16),
            pltpu.SemaphoreType.DMA((sems,)),
            pltpu.SemaphoreType.DMA((sems,)),
            pltpu.SemaphoreType.DMA((2,)),
        ],
        compiler_params=pltpu.CompilerParams(
            collective_id=1, has_side_effects=True, vmem_limit_bytes=40 << 20
        ),
        name="gather_weights",
    )(window, down)
    return out.reshape(1280, WIDE * 128), osd.reshape(1024, 1280)


def scatter_kernel(gw, gsd, out, osd, *scratch):
    hold = [scratch[0:2], scratch[2:4]]
    from_sib = [scratch[4:6], scratch[6:8]]
    bufs = [[scratch[8 + 8 * u + 4 * a : 12 + 8 * u + 4 * a] for a in (0, 1)] for u in (0, 1)]
    fin, fsd, wx, wxd, wh, whd, snd, sndd, acc, accd, ssem, rsem, lsem = scratch[24:]
    hi, y, z, lo, c = place()
    sib = device(hi, y, z, lo, 1 - c)
    xn = device(hi, y, z, 1 - lo, c)
    hn = device(1 - hi, y, z, lo, c)
    nb = ring_neighbours(hi, y, z, lo, c)
    greet([sib, xn, hn] + list(nb.values()))
    wires = Sender(ssem, rsem, lsem)
    mul = pl.multiple_of
    first_pos, second_pos = (y, z), (z, y)
    first_axis, second_axis = ("y", "z"), ("z", "y")

    def pair(src, dst, to):
        return [wires.remote(src[0], dst[0], to), wires.remote(src[1], dst[1], to)]

    def region(u, core, q1, q2):
        by, bz = (q1, q2) if u == 0 else (q2, q1)
        c1, c2 = columns(u, None, core)
        return gw.at[by, bz, :, c1], gsd.at[by, bz, :, c2]

    def at(refs, *index):
        return [refs[0].at[index], refs[1].at[index]]

    def order(u):
        p1, p2 = first_pos[u], second_pos[u]
        ones = [opp(p1), up(p1), dn(p1), p1]
        return [(q1, q2) for q2 in (opp(p2), up(p2), dn(p2), p2) for q1 in ones]

    orders = [order(0), order(1)]
    coming = {}
    for k in range(16):
        for u in (0, 1):
            q = orders[u][k]
            coming[u, k] = pair(region(u, 1 - c, *q), at(from_sib[u], *q), sib)
            coming[u, k, "own"] = [wires.local(a, b) for a, b in zip(region(u, c, *q), at(hold[u], *q))]

    def add_in(dst, *more):
        @pl.loop(0, dst.shape[-2] // 16)
        def _(i):
            r = pl.ds(mul(i * 16, 16), 16)
            value = dst[r, :].astype(F32)
            for ref in more:
                value = value + ref[r, :].astype(F32)
            dst[r, :] = value.astype(BF16)

    def ready(u, k):
        arrived(coming[u, k])
        for copy in coming[u, k, "own"]:
            copy.wait()
        for a in (0, 1):
            add_in(hold[u][a].at[orders[u][k]], from_sib[u][a].at[orders[u][k]])
        return at(hold[u], *orders[u][k])

    def half(refs, u, h):
        s, w, w0, s2, v, v0 = UNITS[u]
        lanes = [(0, w0), (w0, w - w0)][h], [(0, v0), (v0, v - v0)][h]
        return [refs[i].at[:, pl.ds(lanes[i][0] * 128, lanes[i][1] * 128)] for i in (0, 1)]

    def buffer(u, i, slot):
        return [bufs[u][0][i].at[slot], bufs[u][1][i].at[slot]]

    ring = {}

    def far_block(u, slot, blk, axis):
        ring[u, slot, 0] = pair(half(blk, u, 0), buffer(u, 0, slot), nb[axis, 1])
        ring[u, slot, 1] = pair(half(blk, u, 1), buffer(u, 1, slot), nb[axis, -1])

    def near_block(u, slot, blk, axis, way):
        h = 0 if way == 1 else 1
        arrived(ring[u, slot, h])
        for dst, more in zip(half(blk, u, h), buffer(u, h, slot)):
            add_in(dst, more)
        ring[u, slot, 2 + h] = pair(blk, buffer(u, 2 + h, slot), nb[axis, way])

    def own_block(u, slot, blk):
        arrived(ring[u, slot, 2])
        arrived(ring[u, slot, 3])
        for dst, one, two in zip(blk, buffer(u, 2, slot), buffer(u, 3, slot)):
            add_in(dst, one, two)

    for i in range(4):
        for u in (0, 1):
            far_block(u, i, ready(u, i), second_axis[u])
    for i in range(4):
        for u in (0, 1):
            near_block(u, i, ready(u, 4 + i), second_axis[u], 1)
        for u in (0, 1):
            near_block(u, i, ready(u, 8 + i), second_axis[u], -1)
    for i in range(4):
        for u in (0, 1):
            blk = ready(u, 12 + i)
            own_block(u, i, blk)
            if i == 0:
                far_block(u, 4, blk, first_axis[u])
            if i == 1:
                near_block(u, 4, blk, first_axis[u], 1)
            if i == 2:
                near_block(u, 4, blk, first_axis[u], -1)
    for u in (0, 1):
        blk = at(hold[u], *orders[u][15])
        own_block(u, 4, blk)
        s, w, w0, s2, v, v0 = UNITS[u]
        fin[:, s * 128 : (s + w) * 128] = blk[0][...]
        fsd[:, s2 * 128 : (s2 + v) * 128] = blk[1][...]
    r = mul((1 - lo) * 32, 16)
    arrived(pair((fin.at[pl.ds(r, 48)], fsd.at[pl.ds(r, 32)]), (wx, wxd), xn))
    r = mul(lo * 32, 16)
    snd[...] = (fin[pl.ds(r, 48), :].astype(F32) + wx[...].astype(F32)).astype(BF16)
    sndd[...] = (fsd[pl.ds(r, 32), :].astype(F32) + wxd[...].astype(F32)).astype(BF16)
    arrived(pair((snd, sndd), (wh, whd), hn))
    acc[...] = snd[...].astype(F32) + wh[...].astype(F32)
    accd[...] = sndd[...].astype(F32) + whd[...].astype(F32)
    mine = pl.ds(mul(c * HALF, 128), HALF)
    mine2 = pl.ds(mul(c * 640, 128), 640)
    r = mul((1 - c) * 16, 16)
    last = pair((acc.at[pl.ds(r, 32)], accd.at[pl.ds(r, 16)]), (out.at[:, mine], osd.at[:, mine2]), sib)
    r = mul(c * 16, 16)
    out[:, mine] = acc[pl.ds(r, 32), :]
    osd[:, mine2] = accd[pl.ds(r, 16), :]
    arrived(last)
    wires.finish()


def scatter_sums(gw, gsd):
    scratch = []
    for _ in (0, 1):
        for s, w, w0, s2, v, v0 in UNITS:
            scratch += [pltpu.VMEM((4, 4, 80, w * 128), BF16), pltpu.VMEM((4, 4, 64, v * 128), BF16)]
    for s, w, w0, s2, v, v0 in UNITS:
        for rows, n, n0 in ((80, w, w0), (64, v, v0)):
            for tiles in (n0, n - n0, n, n):
                scratch.append(pltpu.VMEM((5, rows, tiles * 128), BF16))
    for rows, rows2 in ((80, 64), (48, 32), (48, 32), (48, 32)):
        scratch += [pltpu.VMEM((rows, HALF), BF16), pltpu.VMEM((rows2, 640), BF16)]
    scratch += [pltpu.VMEM((48, HALF), F32), pltpu.VMEM((32, 640), F32)]
    sems = 64 + 2 * 2 * 4 * 5 + 6
    scratch += [
        pltpu.SemaphoreType.DMA((sems,)),
        pltpu.SemaphoreType.DMA((sems,)),
        pltpu.SemaphoreType.DMA((64,)),
    ]
    out, osd = pl.pallas_call(
        scatter_kernel,
        out_shape=(jax.ShapeDtypeStruct((32, WIDE * 128), F32), jax.ShapeDtypeStruct((16, 1280), F32)),
        in_specs=[pl.BlockSpec(memory_space=pl.ANY)] * 2,
        out_specs=(pl.BlockSpec(memory_space=pltpu.VMEM),) * 2,
        scratch_shapes=scratch,
        compiler_params=pltpu.CompilerParams(
            collective_id=2, has_side_effects=True, vmem_limit_bytes=56 << 20
        ),
        name="scatter_sums",
    )(gw.reshape(4, 4, 80, WIDE * 128), gsd.reshape(4, 4, 64, 1280))
    offset = 4 * lax.rem(lax.axis_index("exp"), 4)
    return lax.dynamic_slice(out, (offset, 0), (20, WIDE * 128)), osd[:14]


PART_AXES = (("y", "z", "g"), ("z", "g", "y"), ("g", "y", "z"))


def exchange_kernel(cuts, work, counts, *refs):
    n = len(cuts)
    n_in, n_out, n_scratch = counts
    work_in, refs = refs[n : n + n_in], refs[:n] + refs[n + n_in :]
    work_out, refs = refs[2 * n : 2 * n + n_out], refs[: 2 * n] + refs[2 * n + n_out :]
    work_scratch = refs[4 * n + 3 :]
    stages = [refs[0:n], refs[2 * n : 3 * n], refs[3 * n : 4 * n], refs[n : 2 * n]]
    hi, y, z, lo, c = place()
    me = {"y": y, "z": z, "g": lo * 2 + c}
    wires = Sender(*refs[4 * n : 4 * n + 3])

    def peer(axis, k):
        q = dict(me)
        q[axis] = lax.rem(me[axis] + k, 4)
        return q[axis], device(hi, q["y"], q["z"], q["g"] // 2, lax.rem(q["g"], 2))

    greet([peer(axis, k)[1] for axis in "yzg" for k in (1, 2, 3)])
    every = slice(None)

    def view(ref, axis, v, lanes):
        index = {"y": (v, every, every), "z": (every, v, every), "g": (every, every, v)}[axis]
        return ref.at[index + (every, pl.ds(lanes[0] * 128, lanes[1] * 128))]

    pending = {}

    def go(part, phase):
        axis = PART_AXES[part][phase]
        waits = []
        for a in range(n):
            src, dst = stages[phase][a], stages[phase + 1][a]
            lanes = cuts[a][part]
            own = view(dst, axis, me[axis], lanes)
            for k in (2, 1, 3):
                v, to = peer(axis, k)
                waits.append(wires.remote(view(src, axis, v, lanes), own, to).wait_recv)
            waits.append(wires.local(view(src, axis, me[axis], lanes), own).wait)
        pending[part, phase] = waits

    for phase in (0, 1, 2):
        for part in range(3):
            if phase > 0:
                for wait in pending[part, phase - 1]:
                    wait()
            go(part, phase)
        work(phase, work_in, work_out, work_scratch)
    for part in range(3):
        for wait in pending[part, 2]:
            wait()
    wires.finish()


def exchange(collective_id, arrays, cuts, work, work_in, work_out, work_scratch=()):
    n = len(arrays)
    split = [a.reshape((4, 4, 4) + a.shape[1:]) for a in arrays]
    shapes = [jax.ShapeDtypeStruct(a.shape, a.dtype) for a in split]
    vmem = pl.BlockSpec(memory_space=pltpu.VMEM)
    out = pl.pallas_call(
        functools.partial(exchange_kernel, cuts, work, (len(work_in), len(work_out), len(work_scratch))),
        out_shape=tuple(shapes) + tuple(work_out),
        in_specs=[pl.BlockSpec(memory_space=pl.ANY)] * n + [vmem] * len(work_in),
        out_specs=(pl.BlockSpec(memory_space=pl.ANY),) * n + (vmem,) * len(work_out),
        scratch_shapes=[pltpu.VMEM(s.shape, s.dtype) for s in shapes] * 2
        + [
            pltpu.SemaphoreType.DMA((27 * n,)),
            pltpu.SemaphoreType.DMA((27 * n,)),
            pltpu.SemaphoreType.DMA((9 * n,)),
        ]
        + list(work_scratch),
        compiler_params=pltpu.CompilerParams(
            collective_id=collective_id, has_side_effects=True, vmem_limit_bytes=56 << 20
        ),
        name="exchange_rows",
    )(*split, *work_in)
    return [o.reshape(a.shape) for o, a in zip(out, arrays)] + list(out[n:])


def dot(a, b):
    return jnp.dot(a, b, preferred_element_type=F32)


def dot_t(a, b):
    return lax.dot_general(a, b, (((1,), (1,)), ((), ())), preferred_element_type=F32)


def t_dot(a, b):
    return lax.dot_general(a, b, (((0,), (0,)), ((), ())), preferred_element_type=F32)


def iota(shape, dim):
    return lax.broadcasted_iota(jnp.int32, shape, dim)


def shape(dtype, *dims):
    return jax.ShapeDtypeStruct(dims, dtype)


def local_call(kernel, name, outs, *operands):
    return pl.pallas_call(
        kernel,
        out_shape=tuple(outs),
        compiler_params=pltpu.CompilerParams(vmem_limit_bytes=56 << 20),
        name=name,
    )(*operands)


def gain_rows(block):
    pick = (iota((8, 128), 1) == iota((8, 128), 0) + 64).astype(BF16)
    return dot_t(pick, block)


def rms_forward(values, gain):
    inv_rms = lax.rsqrt(jnp.mean(values * values, axis=-1, keepdims=True) + EPSILON)
    return values * inv_rms * gain, inv_rms


def rms_backward(values, inv_rms, gain, upstream):
    weighted = upstream * gain
    inner = jnp.mean(weighted * values, axis=-1, keepdims=True)
    grad_in = inv_rms * weighted - values * (inv_rms * inv_rms * inv_rms) * inner
    grad_gain = jnp.sum(upstream * values * inv_rms, axis=0, keepdims=True)
    return grad_in, grad_gain


def rotary_tables(rows):
    freq = np.power(10000.0, -2.0 * np.arange(64) / 128)
    angles = np.arange(rows)[:, None] * freq[None, :]
    cos, sin = np.cos(angles), np.sin(angles)
    return (
        jnp.asarray(np.concatenate([cos, cos], axis=1), F32),
        jnp.asarray(np.concatenate([-sin, sin], axis=1), F32),
    )


def silu_parts(pre_act):
    sigma = jax.nn.sigmoid(pre_act)
    return (pre_act * sigma, sigma * (1.0 + pre_act * (1.0 - sigma)))


def seq_rows():
    return pl.ds(pl.multiple_of(lax.axis_index("seq") * 128, 128), 128)


def qkv_kernel(tok, gains, cos, sin, w, act, q, kv):
    i = pl.program_id(0)

    @pl.when(i == 0)
    def _():
        normed, _inv = rms_forward(tok[...].astype(F32), gain_rows(gains[...])[0:1])
        act[...] = normed.astype(BF16)

    x = dot(act[...], w[...])
    here = seq_rows()
    cosine, sine = cos[here, :], sin[here, :]
    heads = [x[:, h * 128 : (h + 1) * 128] for h in range(5)]
    turned = jnp.concatenate([h * cosine + pltpu.roll(h, 64, 1) * sine for h in heads], axis=1)

    @pl.when(i < 2)
    def _():
        q[...] = turned.astype(BF16)

    @pl.when(i >= 2)
    def _():
        kv[...] = jnp.where(i < 4, turned, x).astype(BF16)


def project(tokens, weights, cos, sin):
    rows, width = tokens.shape
    whole = lambda a: pl.BlockSpec(a.shape, lambda i: (0, 0))
    return pl.pallas_call(
        qkv_kernel,
        grid=(6,),
        out_shape=(shape(BF16, rows, width), shape(BF16, rows, width), shape(BF16, rows, 2 * width)),
        in_specs=[
            whole(tokens),
            pl.BlockSpec((width, 128), lambda i: (0, 56)),
            whole(cos),
            whole(sin),
            pl.BlockSpec((width, 640), lambda i: (0, i)),
        ],
        out_specs=(
            pl.BlockSpec((rows, width), lambda i: (0, 0)),
            pl.BlockSpec((rows, 640), lambda i: (0, jnp.minimum(i, 1))),
            pl.BlockSpec((rows, 640), lambda i: (0, jnp.maximum(i - 2, 0))),
        ),
        compiler_params=pltpu.CompilerParams(vmem_limit_bytes=56 << 20),
        name="queries_keys_values",
    )(tokens, weights, cos, sin, weights)


def allowed_keys(seg_row, seg_col):
    hi = lax.axis_index("seq")
    here = seq_rows()
    mine = seg_col[here, :]
    rows = mine.shape[0]
    own = (seg_row[:, here] == mine) & (iota((rows, rows), 1) <= iota((rows, rows), 0))
    prior = (seg_row[:, 0:rows] == mine) & (hi == 1)
    return own, prior


def head_probs(h, q, kv, prior, own_ok, prior_ok, width):
    lanes = slice(h * 128, (h + 1) * 128)
    behind = slice(width + h * 128, width + (h + 1) * 128)
    query = q[:, lanes]
    keys = jnp.concatenate([prior[:, lanes], kv[:, lanes]], axis=0)
    values = jnp.concatenate([prior[:, behind], kv[:, behind]], axis=0)
    scores = dot_t(query, keys) * (128.0**-0.5)
    rows = query.shape[0]
    scores = jnp.concatenate(
        [jnp.where(prior_ok, scores[:, :rows], NEG_BIG), jnp.where(own_ok, scores[:, rows:], NEG_BIG)], axis=1
    )
    expo = jnp.exp(scores - jnp.max(scores, axis=-1, keepdims=True))
    return query, keys, values, expo / jnp.sum(expo, axis=-1, keepdims=True)


def attend_kernel(tok, q, kv, prior, seg_row, seg_col, routes, out_w, router_w, mixed, hidden_one, act, gates_t, slot_t):
    rows, width = tok.shape
    own_ok, prior_ok = allowed_keys(seg_row, seg_col)
    for h in range(HEADS):
        _query, _keys, values, probs = head_probs(h, q, kv, prior, own_ok, prior_ok, width)
        mixed[:, h * 128 : (h + 1) * 128] = dot(probs.astype(BF16), values).astype(BF16)
    hidden = tok[...].astype(F32) + dot(mixed[...], out_w[...])
    hidden_one[...] = hidden
    router = router_w[...]
    normed, _inv = rms_forward(hidden, gain_rows(router)[1:2])
    low = normed.astype(BF16)
    act[...] = low
    expert = iota((rows, 128), 1)
    named = routes[...]
    member = named[:, 0:1] == expert
    for k in range(1, named.shape[1]):
        member = member | (named[:, k : k + 1] == expert)
    logits = jnp.where(member, dot(low, router), NEG_BIG)
    expo = jnp.where(member, jnp.exp(logits - jnp.max(logits, axis=-1, keepdims=True)), 0.0)
    gates_t[...] = (expo / jnp.sum(expo, axis=-1, keepdims=True)).T
    before = (iota((rows, rows), 1) < iota((rows, rows), 0)).astype(BF16)
    rank = dot(before, member.astype(BF16))
    slot_t[...] = jnp.where(member, rank, -1.0).T


def attend(tokens, q, kv, prior, seg_row, seg_col, routes, weights):
    rows, width = tokens.shape
    whole = lambda a: pl.BlockSpec(a.shape, lambda i: (0, 0))
    operands = (tokens, q, kv, prior, seg_row, seg_col, routes)
    outs = (
        shape(BF16, rows, width),
        shape(F32, rows, width),
        shape(BF16, rows, width),
        shape(F32, 128, rows),
        shape(F32, 128, rows),
    )
    return pl.pallas_call(
        attend_kernel,
        grid=(1,),
        out_shape=outs,
        in_specs=[whole(a) for a in operands]
        + [pl.BlockSpec((width, 1280), lambda i: (0, 3)), pl.BlockSpec((width, 128), lambda i: (0, 56))],
        out_specs=tuple(whole(a) for a in outs),
        compiler_params=pltpu.CompilerParams(vmem_limit_bytes=56 << 20),
        name="attend",
    )(*operands, weights, weights)


EVEN = 16


def even_places(slot_t):
    experts, rows = slot_t.shape
    wide = jnp.broadcast_to(slot_t[:, None, :], (experts, EVEN, rows))
    place_of = iota((experts, EVEN, rows), 1).astype(F32)
    return wide == place_of


def dispatch_kernel(act, grad, gates, slot_t, out_x, out_g, out_l):
    block, even, width = out_x.shape
    rows = act.shape[0]
    here = pl.ds(pl.multiple_of(pl.program_id(0) * block, block), block)
    slots = slot_t[here, :]
    places = even_places(slots)
    last = slots == float(EVEN)
    hot = places.astype(F32).reshape(block * even, rows).astype(BF16)
    last_hot = last.astype(BF16)
    x, g = act[...], grad[...]
    out_x[...] = dot(hot, x).astype(BF16).reshape(block, even, width)
    out_g[...] = dot(hot, g).astype(BF16).reshape(block, even, width)
    gt = gates[here, :]
    at_slot = jnp.sum(
        jnp.where(places, jnp.broadcast_to(gt[:, None, :], places.shape), 0.0).reshape(block * even, rows),
        axis=-1,
        keepdims=True,
    )
    spread = jnp.broadcast_to(at_slot, (block * even, 128)).reshape(block, even, 128)
    lane_of = iota((block, even, 128), 1) == iota((block, even, 128), 2)
    even_gates = jnp.sum(jnp.where(lane_of, spread, 0.0), axis=1)
    last_gates = jnp.sum(jnp.where(last, gt, 0.0), axis=-1, keepdims=True)
    slot_gates = jnp.where(iota((block, 128), 1) == EVEN, last_gates, even_gates)
    out_l[...] = jnp.concatenate([dot(last_hot, x), dot(last_hot, g), slot_gates], axis=1).reshape(
        block, 1, 2 * width + 128
    )


def dispatch(act, grad, gates_t, slot_t, experts):
    width = act.shape[1]
    block = 8
    whole = lambda a: pl.BlockSpec(a.shape, lambda i: (0, 0))
    cut = lambda n, lanes: pl.BlockSpec((block, n, lanes), lambda i: (i, 0, 0))
    return pl.pallas_call(
        dispatch_kernel,
        grid=(experts // block,),
        out_shape=(
            shape(BF16, experts, EVEN, width),
            shape(BF16, experts, EVEN, width),
            shape(F32, experts, 1, 2 * width + 128),
        ),
        in_specs=[whole(act), whole(grad), whole(gates_t), whole(slot_t)],
        out_specs=(cut(EVEN, width), cut(EVEN, width), cut(1, 2 * width + 128)),
        compiler_params=pltpu.CompilerParams(vmem_limit_bytes=32 << 20),
        name="dispatch",
    )(act, grad, gates_t, slot_t)


def expert_kernel(rows_x, rows_g, rows_l, w_gate, w_up, w_down, out_r, out_d, out_l, all_x, all_g, hidden, d_gate, d_up):
    sources, _one, _lanes = rows_l.shape
    width = rows_x.shape[-1]
    last = rows_l[...].reshape(sources, rows_l.shape[-1])
    even = sources * EVEN
    x = jnp.concatenate([rows_x[...].reshape(even, width), last[:, :width].astype(BF16)], axis=0)
    g = jnp.concatenate(
        [rows_g[...].reshape(even, width).astype(F32), last[:, width : 2 * width]], axis=0
    )
    sent = last[:, 2 * width :]
    spread = jnp.broadcast_to(sent[:, None, :], (sources, EVEN, 128))
    own = iota((sources, EVEN, 128), 1) == iota((sources, EVEN, 128), 2)
    even_gates = jnp.sum(jnp.where(own, spread, 0.0).reshape(even, 128), axis=-1, keepdims=True)
    last_gates = jnp.sum(jnp.where(iota((sources, 128), 1) == EVEN, sent, 0.0), axis=-1, keepdims=True)
    grad_result = (jnp.concatenate([even_gates, last_gates], axis=0) * g).astype(BF16)
    all_x[...] = x
    all_g[...] = grad_result
    gate = dot(x, w_gate[...])
    up_ = dot(x, w_up[...])
    silu, slope = silu_parts(gate)
    low = (silu * up_).astype(BF16)
    hidden[...] = low
    grad_hidden = dot_t(grad_result, w_down[...])
    grad_gate = (grad_hidden * up_ * slope).astype(BF16)
    grad_up = (grad_hidden * silu).astype(BF16)
    d_gate[...] = grad_gate
    d_up[...] = grad_up
    result = dot(low, w_down[...]).astype(BF16)
    grad_in = (dot_t(grad_gate, w_gate[...]) + dot_t(grad_up, w_up[...])).astype(BF16)
    out_r[...] = result[:even].reshape(sources, EVEN, width)
    out_d[...] = grad_in[:even].reshape(sources, EVEN, width)
    out_l[...] = jnp.concatenate([result[even:], grad_in[even:]], axis=1).astype(F32).reshape(sources, 1, 2 * width)


def expert(rows_x, rows_g, rows_l, w_gate, w_up, w_down):
    devices, _even, width = rows_x.shape
    inner = w_gate.shape[1]
    steps = 4
    src = devices // steps
    rows = src * (EVEN + 1)
    total = rows * steps
    whole = lambda a: pl.BlockSpec(a.shape, lambda i: (0, 0))
    cut = lambda n, lanes: pl.BlockSpec((src, n, lanes), lambda i: (i, 0, 0))
    flat = lambda lanes: pl.BlockSpec((rows, lanes), lambda i: (i, 0))
    return pl.pallas_call(
        expert_kernel,
        grid=(steps,),
        out_shape=(
            shape(BF16, devices, EVEN, width),
            shape(BF16, devices, EVEN, width),
            shape(F32, devices, 1, 2 * width),
            shape(BF16, total, width),
            shape(BF16, total, width),
            shape(BF16, total, inner),
            shape(BF16, total, inner),
            shape(BF16, total, inner),
        ),
        in_specs=[cut(EVEN, width), cut(EVEN, width), cut(1, rows_l.shape[-1]), whole(w_gate), whole(w_up), whole(w_down)],
        out_specs=(
            cut(EVEN, width),
            cut(EVEN, width),
            cut(1, 2 * width),
            flat(width),
            flat(width),
            flat(inner),
            flat(inner),
            flat(inner),
        ),
        compiler_params=pltpu.CompilerParams(vmem_limit_bytes=60 << 20),
        name="expert",
    )(rows_x, rows_g, rows_l, w_gate, w_up, w_down)


def shared_work(phase, ins, outs, scratch):
    act, grad, sgu, sdown = ins
    out_s, grad_in, grad_gu, grad_down = outs
    (hidden,) = scratch
    inner = sdown.shape[0]
    if phase == 0:
        gate = dot(act[...], sgu[:, :inner])
        up_ = dot(act[...], sgu[:, inner:])
        silu, slope = silu_parts(gate)
        hidden[...] = (silu * up_).astype(BF16)
        grad_hidden = dot_t(grad[...], sdown[...])
        grad_gu[:, :inner] = (grad_hidden * up_ * slope).astype(BF16)
        grad_gu[:, inner:] = (grad_hidden * silu).astype(BF16)
    elif phase == 1:
        out_s[...] = dot(hidden[...], sdown[...])
        grad_in[...] = dot_t(grad_gu[...], sgu[...])
    else:

        @pl.loop(0, inner // 256)
        def _(i):
            r = pl.ds(pl.multiple_of(i * 256, 256), 256)
            grad_down[r, :] = t_dot(hidden[:, r], grad[...]).astype(BF16)


def expert_work(phase, ins, outs, scratch):
    all_x, all_g, hidden, d_gate, d_up = ins
    g_gate, g_up, g_down = outs
    if phase < 2:
        grad, out = (d_gate, g_gate) if phase == 0 else (d_up, g_up)

        @pl.loop(0, out.shape[0] // 256)
        def _(i):
            r = pl.ds(pl.multiple_of(i * 256, 256), 256)
            out[r, :] = t_dot(all_x[:, r], grad[...]).astype(BF16)

    else:

        @pl.loop(0, g_down.shape[0] // 128)
        def _(i):
            r = pl.ds(pl.multiple_of(i * 128, 128), 128)
            g_down[r, :] = t_dot(hidden[:, r], all_g[...]).astype(BF16)


def split_terms(w):
    top = w.astype(BF16)
    rest = w - top.astype(F32)
    mid = rest.astype(BF16)
    return top, mid, (rest - mid.astype(F32)).astype(BF16)


def combine_kernel(
    back_r, back_d, back_l, slot_t, gates_t, grad, hidden_one, out_s, grad_in_s, router_w, out_w,
    layer_out, grad_hidden, grad_low, grad_mixed, grad_logits, grad_gain,
):
    experts = back_r.shape[0]
    rows, width = hidden_one.shape
    slots = slot_t[0:experts, :]
    places = even_places(slots)
    last = slots == float(EVEN)
    out_rows = back_r[...].reshape(experts * EVEN, width)
    last_l = back_l[...].reshape(experts, 2 * width).astype(BF16)
    gt = gates_t[0:experts, :]
    even_w = jnp.where(places, jnp.broadcast_to(gt[:, None, :], places.shape), 0.0).reshape(experts * EVEN, rows)
    last_w = jnp.where(last, gt, 0.0)
    routed = jnp.zeros((rows, width), F32)
    for e_term, l_term in zip(split_terms(even_w), split_terms(last_w)):
        routed = routed + t_dot(e_term, out_rows) + t_dot(l_term, last_l[:, :width])
    hidden = hidden_one[...]
    layer_out[...] = (hidden + out_s[...] + routed).astype(BF16)
    g = grad[...]
    dots = dot_t(out_rows, g).reshape(experts, EVEN, rows)
    dots_last = dot_t(last_l[:, :width], g)
    grad_gates = jnp.sum(jnp.where(places, dots, 0.0), axis=1) + jnp.where(last, dots_last, 0.0)
    logits_t = gt * (grad_gates - jnp.sum(gt * grad_gates, axis=0, keepdims=True))
    low_logits = jnp.concatenate([logits_t, jnp.zeros((128 - experts, rows), F32)], axis=0).T.astype(BF16)
    grad_logits[...] = low_logits
    hot = places.astype(F32).reshape(experts * EVEN, rows).astype(BF16)
    grad_routed = t_dot(hot, back_d[...].reshape(experts * EVEN, width)) + t_dot(last.astype(BF16), last_l[:, width:])
    router = router_w[...]
    grad_act = grad_routed + dot_t(low_logits, router) + grad_in_s[...]
    gain = gain_rows(router)[1:2]
    _normed, inv = rms_forward(hidden, gain)
    grad_norm, gain_sum = rms_backward(hidden, inv, gain, grad_act)
    grad_gain[...] = gain_sum
    total = g.astype(F32) + grad_norm
    grad_hidden[...] = total
    low = total.astype(BF16)
    grad_low[...] = low
    grad_mixed[...] = dot_t(low, out_w[...]).astype(BF16)


def combine(back_r, back_d, back_l, slot_t, gates_t, grad, hidden_one, out_s, grad_in_s, weights):
    rows, width = hidden_one.shape
    operands = (back_r, back_d, back_l, slot_t, gates_t, grad, hidden_one, out_s, grad_in_s)
    whole = lambda a: pl.BlockSpec(a.shape, lambda i: (0,) * len(a.shape))
    outs = (
        shape(BF16, rows, width),
        shape(F32, rows, width),
        shape(BF16, rows, width),
        shape(BF16, rows, width),
        shape(BF16, rows, 128),
        shape(F32, 1, width),
    )
    return pl.pallas_call(
        combine_kernel,
        grid=(1,),
        out_shape=outs,
        in_specs=[whole(a) for a in operands]
        + [pl.BlockSpec((width, 128), lambda i: (0, 56)), pl.BlockSpec((width, 1280), lambda i: (0, 3))],
        out_specs=tuple(whole(a) for a in outs),
        compiler_params=pltpu.CompilerParams(vmem_limit_bytes=56 << 20),
        name="combine",
    )(*operands, weights, weights)


def attend_back_kernel(q, kv, prior, seg_row, seg_col, grad_mixed, cos, sin, grad_q, grad_own, grad_prior):
    rows, width = q.shape
    own_ok, prior_ok = allowed_keys(seg_row, seg_col)
    here = seq_rows()
    cosine, sine = cos[here, :], sin[here, :]
    inv_root = 128.0**-0.5
    for h in range(HEADS):
        query, keys, values, probs = head_probs(h, q, kv, prior, own_ok, prior_ok, width)
        lanes = slice(h * 128, (h + 1) * 128)
        behind = slice(width + h * 128, width + (h + 1) * 128)
        gm = grad_mixed[:, lanes]
        grad_probs = dot_t(gm, values)
        inner = jnp.sum(probs * grad_probs, axis=-1, keepdims=True)
        grad_scores = (probs * (grad_probs - inner)).astype(BF16)
        grad_values = t_dot(probs.astype(BF16), gm)
        gq = dot(grad_scores, keys) * inv_root
        grad_keys = t_dot(grad_scores, query) * inv_root
        grad_q[:, lanes] = (gq * cosine - pltpu.roll(gq, 64, 1) * sine).astype(BF16)
        grad_own[:, lanes] = grad_keys[rows:]
        grad_own[:, behind] = grad_values[rows:]
        grad_prior[:, lanes] = grad_keys[:rows].astype(BF16)
        grad_prior[:, behind] = grad_values[:rows].astype(BF16)


def input_grad_kernel(tok, gains, cos, sin, grad_q, grad_own, later, grad_hidden, w, grad_qkv, grad_tokens, grad_gain, total):
    i = pl.program_id(0)
    rows, width = tok.shape

    @pl.when(i == 0)
    def _():
        here = seq_rows()
        cosine, sine = cos[here, :], sin[here, :]
        grad_qkv[:, :width] = grad_q[...]
        for h in range(HEADS):
            lanes = slice(h * 128, (h + 1) * 128)
            gk = grad_own[:, lanes] + later[:, lanes].astype(F32)
            grad_qkv[:, width + h * 128 : width + (h + 1) * 128] = (
                gk * cosine - pltpu.roll(gk, 64, 1) * sine
            ).astype(BF16)
        grad_qkv[:, 2 * width :] = (grad_own[:, width:] + later[:, width:].astype(F32)).astype(BF16)
        total[...] = jnp.zeros_like(total)

    lanes = pl.ds(pl.multiple_of(i * 640, 128), 640)
    total[...] += dot_t(grad_qkv[:, lanes], w[...])

    @pl.when(i == pl.num_programs(0) - 1)
    def _():
        values = tok[...].astype(F32)
        gain = gain_rows(gains[...])[0:1]
        _normed, inv = rms_forward(values, gain)
        grad_norm, gain_sum = rms_backward(values, inv, gain, total[...])
        grad_gain[...] = gain_sum
        grad_tokens[...] = grad_hidden[...] + grad_norm


def input_grads(tokens, cos, sin, grad_q, grad_own, later, grad_hidden, weights):
    rows, width = tokens.shape
    whole = lambda a: pl.BlockSpec(a.shape, lambda i: (0, 0))
    outs = (shape(BF16, rows, 3 * width), shape(F32, rows, width), shape(F32, 1, width))
    return pl.pallas_call(
        input_grad_kernel,
        grid=(6,),
        out_shape=outs,
        in_specs=[
            whole(tokens),
            pl.BlockSpec((width, 128), lambda i: (0, 56)),
            whole(cos),
            whole(sin),
            whole(grad_q),
            whole(grad_own),
            whole(later),
            whole(grad_hidden),
            pl.BlockSpec((width, 640), lambda i: (0, i)),
        ],
        out_specs=tuple(whole(a) for a in outs),
        scratch_shapes=[pltpu.VMEM((rows, width), F32)],
        compiler_params=pltpu.CompilerParams(vmem_limit_bytes=56 << 20),
        name="input_grads",
    )(tokens, weights, cos, sin, grad_q, grad_own, later, grad_hidden, weights)


def weight_grad_kernel(act_attn, mixed, act_ffn, grad_qkv, grad_out, grad_gu, grad_logits, gain_a, gain_f, out):
    i = pl.program_id(0)

    def product(left, right, start):
        lanes = pl.ds(pl.multiple_of((i - start) * 256, 256), 256)
        out[...] = t_dot(left[...], right[:, lanes]).astype(BF16)

    @pl.when(i < 15)
    def _():
        product(act_attn, grad_qkv, 0)

    @pl.when((i >= 15) & (i < 20))
    def _():
        product(mixed, grad_out, 15)

    @pl.when((i >= 20) & (i < 28))
    def _():
        product(act_ffn, grad_gu, 20)

    @pl.when(i == 28)
    def _():
        row = iota((8, 1280), 0)
        gains = jnp.where(row == 0, gain_a[...], jnp.where(row == 1, gain_f[...], 0.0)).astype(BF16)
        pick = (iota((8, 128), 1) == iota((8, 128), 0) + 64).astype(BF16)
        out[:, :128] = (t_dot(act_ffn[...], grad_logits[...]) + t_dot(gains, pick)).astype(BF16)
        out[:, 128:] = jnp.zeros((1280, 128), BF16)


def weight_grads(*operands):
    width = operands[0].shape[1]
    whole = lambda a: pl.BlockSpec(a.shape, lambda i: (0, 0))
    return pl.pallas_call(
        weight_grad_kernel,
        grid=(WIDE // 2,),
        out_shape=shape(BF16, width, WIDE * 128),
        in_specs=[whole(a) for a in operands],
        out_specs=pl.BlockSpec((width, 256), lambda i: (0, i)),
        compiler_params=pltpu.CompilerParams(vmem_limit_bytes=56 << 20),
        name="weight_grads",
    )(*operands)


def per_device(
    tokens,
    cotangent,
    segments,
    routes,
    norm_gain_attn,
    w_query,
    w_key,
    w_value,
    w_out,
    norm_gain_ffn,
    w_router,
    shared_gate,
    shared_up,
    shared_down,
    expert_gate,
    expert_up,
    expert_down,
):
    rows = tokens.shape[1]
    width = tokens.shape[2]
    experts = w_router.shape[1]
    tokens, grad, routes = tokens[0], cotangent[0], routes[0]
    seg_row = segments
    seg_col = segments.reshape(-1, 1)

    def spread(w):
        w = w.reshape(w.shape[0], experts, w.shape[1] // experts)
        return jnp.pad(w, ((0, 0), (0, 0), (0, 2))).reshape(w.shape[0], experts * 16)

    shard = jnp.concatenate(
        [
            w_query,
            w_key,
            w_value,
            w_out,
            spread(shared_gate),
            spread(shared_up),
            w_router,
            norm_gain_attn[:, None],
            norm_gain_ffn[:, None],
            jnp.zeros((w_query.shape[0], 190), BF16),
        ],
        axis=1,
    )
    weights, sdown_w = gather_weights(shard, shared_down)
    cos, sin = rotary_tables(2 * rows)
    act_attn, q, kv = project(tokens, weights, cos, sin)
    prior = lax.ppermute(kv, "seq", [(0, 1)])
    mixed, hidden_one, act_ffn, gates_t, slot_t = attend(tokens, q, kv, prior, seg_row, seg_col, routes, weights)

    rows_x, rows_g, rows_l = dispatch(act_ffn, grad, gates_t, slot_t, experts)
    rows_x, rows_g, rows_l, out_s, grad_in_s, grad_gu, grad_sdown = exchange(
        3,
        (rows_x, rows_g, rows_l),
        (((0, 4), (4, 3), (7, 3)), ((0, 3), (3, 4), (7, 3)), ((0, 6), (6, 6), (12, 9))),
        shared_work,
        (act_ffn, grad, weights[:, 5120:7168], sdown_w),
        (shape(F32, rows, width), shape(F32, rows, width), shape(BF16, rows, 2048), shape(BF16, 1024, width)),
        (pltpu.VMEM((rows, 1024), BF16),),
    )
    out_r, out_d, out_l, *kept = expert(rows_x, rows_g, rows_l, expert_gate[0], expert_up[0], expert_down[0])
    back_r, back_d, back_l, *part_expert = exchange(
        4,
        (out_r, out_d, out_l),
        (((0, 4), (4, 3), (7, 3)), ((0, 3), (3, 4), (7, 3)), ((0, 6), (6, 6), (12, 8))),
        expert_work,
        tuple(kept),
        tuple(shape(BF16, *w.shape[1:]) for w in (expert_gate, expert_up, expert_down)),
    )
    layer_out, grad_hidden, grad_low, grad_mixed, grad_logits, gain_ffn = combine(
        back_r, back_d, back_l, slot_t, gates_t, grad, hidden_one, out_s, grad_in_s, weights
    )
    grad_q, grad_own, grad_prior = local_call(
        attend_back_kernel,
        "attend_back",
        (shape(BF16, rows, width), shape(F32, rows, 2 * width), shape(BF16, rows, 2 * width)),
        q, kv, prior, seg_row, seg_col, grad_mixed, cos, sin,
    )
    later = lax.ppermute(grad_prior, "seq", [(1, 0)])
    *part_expert, later = lax.optimization_barrier((*part_expert, later))
    swapped = [lax.ppermute(g, "seq", [(0, 1), (1, 0)]) for g in part_expert]
    grad_qkv, grad_tokens, gain_attn = input_grads(tokens, cos, sin, grad_q, grad_own, later, grad_hidden, weights)
    grads = weight_grads(act_attn, mixed, act_ffn, grad_qkv, grad_low, grad_gu, grad_logits, gain_attn, gain_ffn)
    own, own_down = scatter_sums(grads, grad_sdown)

    def gathered_hidden(w):
        return w.reshape(w.shape[0], experts, 16)[:, :, :14].reshape(w.shape[0], experts * 14)

    expert_grads = [(a.astype(F32) + b.astype(F32))[None] for a, b in zip(part_expert, swapped)]
    return (
        layer_out[None],
        grad_tokens[None],
        own[:, 7168 + experts],
        own[:, :1280],
        own[:, 1280:2560],
        own[:, 2560:3840],
        own[:, 3840:5120],
        own[:, 7169 + experts],
        own[:, 7168 : 7168 + experts],
        gathered_hidden(own[:, 5120:6144]),
        gathered_hidden(own[:, 6144:7168]),
        own_down,
        *expert_grads,
    )


def solution(mesh):
    rows = P("exp", None)
    deep = P("exp", None, None)
    split = P("exp", "seq", None)
    gain = P("exp")
    in_specs = (split, split, rows, split, gain, rows, rows, rows, rows, gain) + (rows,) * 4 + (deep,) * 3
    out_specs = (split, split, gain, rows, rows, rows, rows, gain) + (rows,) * 4 + (deep,) * 3
    return jax.shard_map(per_device, mesh=mesh, in_specs=in_specs, out_specs=out_specs, check_vma=False)
```

```python
import functools
import jax
import jax.numpy as jnp
import numpy as np
from jax import lax
from jax.experimental import pallas as pl
from jax.experimental.pallas import tpu as pltpu
from jax.sharding import PartitionSpec as P

HEADS = 10
EPSILON = 1e-06
NEG_BIG = -1e30
F32 = jnp.float32
BF16 = jnp.bfloat16
MESH = pl.DeviceIdType.MESH

WIDE = 58
HALF = 29 * 128
UNITS = ((0, 15, 8, 0, 3, 2), (15, 14, 7, 3, 2, 1))


def place():
    hi = lax.axis_index("seq")
    e = lax.axis_index("exp")
    return hi, e // 16, lax.rem(e // 4, 4), lax.rem(e // 2, 2), lax.rem(e, 2)


def device(hi, y, z, lo, c):
    return (hi, ((y * 4 + z) * 2 + lo) * 2 + c)


def up(v):
    return lax.rem(v + 1, 4)


def dn(v):
    return lax.rem(v + 3, 4)


def opp(v):
    return lax.rem(v + 2, 4)


def greet(devices):
    bar = pltpu.get_barrier_semaphore()
    for to in devices:
        pl.semaphore_signal(bar, inc=1, device_id=to, device_id_type=MESH)
    pl.semaphore_wait(bar, len(devices))


class Sender:
    def __init__(self, send_sem, recv_sem, local_sem):
        self.sems = (send_sem, recv_sem, local_sem)
        self.sent = []
        self.kept = 0

    def remote(self, src, dst, to):
        k = len(self.sent)
        copy = pltpu.make_async_remote_copy(
            src_ref=src,
            dst_ref=dst,
            send_sem=self.sems[0].at[k],
            recv_sem=self.sems[1].at[k],
            device_id=to,
            device_id_type=MESH,
        )
        copy.start()
        self.sent.append(copy)
        return copy

    def local(self, src, dst):
        copy = pltpu.make_async_copy(src, dst, self.sems[2].at[self.kept])
        self.kept += 1
        copy.start()
        return copy

    def finish(self):
        for copy in self.sent:
            copy.wait_send()


def arrived(copies):
    for copy in copies:
        copy.wait_recv()


def ring_neighbours(hi, y, z, lo, c):
    return {
        ("y", 1): device(hi, up(y), z, lo, c),
        ("y", -1): device(hi, dn(y), z, lo, c),
        ("z", 1): device(hi, y, up(z), lo, c),
        ("z", -1): device(hi, y, dn(z), lo, c),
    }


def columns(u, half, core):
    s, w, w0, s2, v, v0 = UNITS[u]
    if half == 0:
        w, v = w0, v0
    elif half == 1:
        s, w, s2, v = s + w0, w - w0, s2 + v0, v - v0
    return (
        pl.ds(pl.multiple_of(core * HALF + s * 128, 128), w * 128),
        pl.ds(pl.multiple_of(core * 640 + s2 * 128, 128), v * 128),
    )


def gather_kernel(win, sdw, e0, e1, e2, out, osd, o0, o1, o2, wsib, pw, pwx, blk, bsd, ssem, rsem, lsem, esend, erecv, ekeep):
    hi, y, z, lo, c = place()
    sib = device(hi, y, z, lo, 1 - c)
    xn = device(hi, y, z, 1 - lo, c)
    nb = ring_neighbours(hi, y, z, lo, c)
    greet([sib, xn] + list(nb.values()))
    wires = Sender(ssem, rsem, lsem)
    mul = pl.multiple_of
    j = lo * 2 + c
    owner = c == hi

    mine_e, used_e = (e0, e1, e2), (o0, o1, o2)

    def keep_expert(k):
        return pltpu.make_async_copy(mine_e[k], used_e[k], ekeep.at[k])

    def pass_expert(k):
        return pltpu.make_async_remote_copy(
            src_ref=mine_e[k],
            dst_ref=used_e[k],
            send_sem=esend.at[k],
            recv_sem=erecv.at[k],
            device_id=sib,
            device_id_type=MESH,
        )

    @pl.when(owner)
    def _():
        for k in range(3):
            keep_expert(k).start()
            pass_expert(k).start()

    other = pl.ds(mul((1 - c) * HALF, 128), HALF)
    mine = pl.ds(mul(c * HALF, 128), HALF)
    other2 = pl.ds(mul((1 - c) * 640, 128), 640)
    mine2 = pl.ds(mul(c * 640, 128), 640)
    r16 = pl.ds(mul(j * 16, 16), 16)
    a = wires.remote(win.at[:, other], wsib, sib)
    b = wires.remote(sdw.at[:, other2], bsd.at[r16], sib)
    bsd[r16, :] = sdw[:, mine2]
    own = win[:, mine]
    a.wait_recv()
    got = wsib[...]
    first = jnp.where(c == 0, own, got)
    second = jnp.where(c == 0, got, own)
    pw[0:16] = first[0:16]
    pw[16:32] = first[16:32] + second[0:16]
    pw[32:48] = second[16:32]
    b.wait_recv()
    a = wires.remote(pw, pwx, xn)
    r32 = pl.ds(mul(lo * 32, 16), 32)
    b = wires.remote(bsd.at[r32], bsd.at[r32], xn)
    a.wait_recv()
    own = pw[...]
    got = pwx[...]
    first = jnp.where(lo == 0, own, got)
    second = jnp.where(lo == 0, got, own)
    blk[0:32] = first[0:32]
    blk[32:48] = first[32:48] + second[0:16]
    blk[48:80] = second[16:48]
    b.wait_recv()
    keep = [wires.local(blk, out.at[y, z, :, mine]), wires.local(bsd, osd.at[y, z, :, mine2])]

    def region(u, half, by, bz):
        c1, c2 = columns(u, half, c)
        return out.at[by, bz, :, c1], osd.at[by, bz, :, c2]

    def send(u, half, by, bz, to, src=None):
        r = region(u, half, by, bz)
        s = src or r
        return [wires.remote(s[0], r[0], to), wires.remote(s[1], r[1], to)]

    def spot(u, q1, q2):
        return (q1, q2) if u == 0 else (q2, q1)

    units = []
    for u in (0, 1):
        a1, a2 = ("y", "z") if u == 0 else ("z", "y")
        p1, p2 = (y, z) if u == 0 else (z, y)
        s, w, w0, s2, v, v0 = UNITS[u]
        src = (blk.at[:, pl.ds(s * 128, w * 128)], bsd.at[:, pl.ds(s2 * 128, v * 128)])
        at = spot(u, p1, p2)
        unit = dict(a1=a1, a2=a2, p1=p1, p2=p2)
        unit["up1"] = send(u, None, *at, nb[a1, 1], src)
        unit["dn1"] = send(u, None, *at, nb[a1, -1], src)
        unit["up2"] = [send(u, None, *at, nb[a2, 1], src)]
        unit["dn2"] = [send(u, None, *at, nb[a2, -1], src)]
        unit["sib"] = [send(u, None, *at, sib, src)]
        units.append(unit)

    def second_axis(u, q1):
        unit = units[u]
        at = spot(u, q1, unit["p2"])
        unit["up2"].append(send(u, None, *at, nb[unit["a2"], 1]))
        unit["dn2"].append(send(u, None, *at, nb[unit["a2"], -1]))
        unit["sib"].append(send(u, None, *at, sib))

    for u, unit in enumerate(units):
        arrived(unit["up1"])
        unit["f1"] = send(u, 0, *spot(u, dn(unit["p1"]), unit["p2"]), nb[unit["a1"], 1])
    for u, unit in enumerate(units):
        arrived(unit["dn1"])
        unit["f2"] = send(u, 1, *spot(u, up(unit["p1"]), unit["p2"]), nb[unit["a1"], -1])
    for u, unit in enumerate(units):
        second_axis(u, dn(unit["p1"]))
        second_axis(u, up(unit["p1"]))
    for u, unit in enumerate(units):
        arrived(unit["f1"])
        arrived(unit["f2"])
        second_axis(u, opp(unit["p1"]))
    turn = [lambda p: p, dn, up, opp]
    for k in range(4):
        for u, unit in enumerate(units):
            q1 = turn[k](unit["p1"])
            arrived(unit["up2"][k])
            at = spot(u, q1, dn(unit["p2"]))
            unit["g1", k] = send(u, 0, *at, nb[unit["a2"], 1])
            unit["sib"].append(send(u, None, *at, sib))
            arrived(unit["dn2"][k])
            at = spot(u, q1, up(unit["p2"]))
            unit["g2", k] = send(u, 1, *at, nb[unit["a2"], -1])
            unit["sib"].append(send(u, None, *at, sib))
    for k in range(4):
        for u, unit in enumerate(units):
            arrived(unit["g1", k])
            arrived(unit["g2", k])
            at = spot(u, turn[k](unit["p1"]), opp(unit["p2"]))
            unit["sib"].append(send(u, None, *at, sib))
    for unit in units:
        for copies in unit["sib"]:
            arrived(copies)
    wires.finish()
    for copy in keep:
        copy.wait()

    @pl.when(owner)
    def _():
        for k in range(3):
            keep_expert(k).wait()
            pass_expert(k).wait_send()

    @pl.when(jnp.logical_not(owner))
    def _():
        for k in range(3):
            pass_expert(k).wait_recv()


def gather_weights(shard, down, experts):
    offset = 4 * lax.rem(lax.axis_index("exp"), 4)
    window = lax.dynamic_update_slice(jnp.zeros((32, WIDE * 128), BF16), shard, (offset, 0))
    down = jnp.pad(down, ((0, 2), (0, 0)))
    sems = 4 + 2 * 2 * 36
    out, osd, *mine = pl.pallas_call(
        gather_kernel,
        out_shape=(
            jax.ShapeDtypeStruct((4, 4, 80, WIDE * 128), BF16),
            jax.ShapeDtypeStruct((4, 4, 64, 1280), BF16),
            *(jax.ShapeDtypeStruct(w.shape, BF16) for w in experts),
        ),
        in_specs=[pl.BlockSpec(memory_space=pltpu.VMEM)] * 2 + [pl.BlockSpec(memory_space=pl.ANY)] * 3,
        out_specs=(pl.BlockSpec(memory_space=pl.ANY),) * 5,
        scratch_shapes=[
            pltpu.VMEM((32, HALF), BF16),
            pltpu.VMEM((48, HALF), BF16),
            pltpu.VMEM((48, HALF), BF16),
            pltpu.VMEM((80, HALF), BF16),
            pltpu.VMEM((64, 640), BF16),
            pltpu.SemaphoreType.DMA((sems,)),
            pltpu.SemaphoreType.DMA((sems,)),
            pltpu.SemaphoreType.DMA((2,)),
        ]
        + [pltpu.SemaphoreType.DMA((3,))] * 3,
        compiler_params=pltpu.CompilerParams(
            collective_id=1, has_side_effects=True, vmem_limit_bytes=40 << 20
        ),
        name="gather_weights",
    )(window, down, *experts)
    return out.reshape(1280, WIDE * 128), osd.reshape(1024, 1280), mine


def scatter_kernel(gw, gsd, p0, p1, p2, out, osd, t0, t1, t2, *scratch):
    hold = [scratch[0:2], scratch[2:4]]
    from_sib = [scratch[4:6], scratch[6:8]]
    bufs = [[scratch[8 + 8 * u + 4 * a : 12 + 8 * u + 4 * a] for a in (0, 1)] for u in (0, 1)]
    fin, fsd, wx, wxd, wh, whd, snd, sndd, acc, accd, ssem, rsem, lsem = scratch[24:37]
    part_own, part_sib, esend, erecv, ekeep = scratch[37:40], scratch[40:43], *scratch[43:]
    hi, y, z, lo, c = place()
    sib = device(hi, y, z, lo, 1 - c)
    xn = device(hi, y, z, 1 - lo, c)
    hn = device(1 - hi, y, z, lo, c)
    nb = ring_neighbours(hi, y, z, lo, c)
    across = device(1 - hi, y, z, lo, hi)
    greet([sib, xn, hn, device(1 - hi, y, z, lo, 1 - c)] + list(nb.values()))
    wires = Sender(ssem, rsem, lsem)
    mul = pl.multiple_of
    owner = c == hi
    parts, totals = (p0, p1, p2), (t0, t1, t2)

    def remote(src, dst, k, tag, to):
        return pltpu.make_async_remote_copy(
            src_ref=src, dst_ref=dst, send_sem=esend.at[k], recv_sem=erecv.at[tag], device_id=to, device_id_type=MESH
        )

    def rows_of(ref, core):
        half_rows = ref.shape[0] // 2
        return ref.at[pl.ds(mul(core * half_rows, 16), half_rows)]

    def own_part(k):
        return pltpu.make_async_copy(rows_of(parts[k], c), part_own[k], ekeep.at[k])

    def swap_part(k):
        return remote(rows_of(parts[k], 1 - c), part_sib[k], k, k, sib)

    def send_across(k):
        return remote(part_own[k], rows_of(totals[k], c), 3 + k, 3 + 2 * k + c, across)

    def keep_total(k):
        return pltpu.make_async_copy(part_own[k], rows_of(totals[k], c), ekeep.at[3 + k])

    def send_near(k):
        return remote(part_own[k], rows_of(totals[k], c), 6 + k, 3 + 2 * k + c, sib)

    def total_half(k, core):
        return remote(rows_of(totals[k], core), rows_of(totals[k], core), 9 + k, 3 + 2 * k + core, sib)

    for k in range(3):
        own_part(k).start()
        swap_part(k).start()
    first_pos, second_pos = (y, z), (z, y)
    first_axis, second_axis = ("y", "z"), ("z", "y")

    def pair(src, dst, to):
        return [wires.remote(src[0], dst[0], to), wires.remote(src[1], dst[1], to)]

    def region(u, core, q1, q2):
        by, bz = (q1, q2) if u == 0 else (q2, q1)
        c1, c2 = columns(u, None, core)
        return gw.at[by, bz, :, c1], gsd.at[by, bz, :, c2]

    def at(refs, *index):
        return [refs[0].at[index], refs[1].at[index]]

    def order(u):
        p1, p2 = first_pos[u], second_pos[u]
        ones = [opp(p1), up(p1), dn(p1), p1]
        return [(q1, q2) for q2 in (opp(p2), up(p2), dn(p2), p2) for q1 in ones]

    orders = [order(0), order(1)]
    coming = {}
    for k in range(16):
        for u in (0, 1):
            q = orders[u][k]
            coming[u, k] = pair(region(u, 1 - c, *q), at(from_sib[u], *q), sib)
            coming[u, k, "own"] = [wires.local(a, b) for a, b in zip(region(u, c, *q), at(hold[u], *q))]

    def add_in(dst, *more):
        @pl.loop(0, dst.shape[-2] // 16)
        def _(i):
            r = pl.ds(mul(i * 16, 16), 16)
            value = dst[r, :].astype(F32)
            for ref in more:
                value = value + ref[r, :].astype(F32)
            dst[r, :] = value.astype(BF16)

    def ready(u, k):
        arrived(coming[u, k])
        for copy in coming[u, k, "own"]:
            copy.wait()
        for a in (0, 1):
            add_in(hold[u][a].at[orders[u][k]], from_sib[u][a].at[orders[u][k]])
        return at(hold[u], *orders[u][k])

    def half(refs, u, h):
        s, w, w0, s2, v, v0 = UNITS[u]
        lanes = [(0, w0), (w0, w - w0)][h], [(0, v0), (v0, v - v0)][h]
        return [refs[i].at[:, pl.ds(lanes[i][0] * 128, lanes[i][1] * 128)] for i in (0, 1)]

    def buffer(u, i, slot):
        return [bufs[u][0][i].at[slot], bufs[u][1][i].at[slot]]

    ring = {}

    def add_parts(k):
        own_part(k).wait()
        swap_part(k).wait_recv()
        add_in(part_own[k], part_sib[k])
        send_across(k).start()

        @pl.when(owner)
        def _():
            keep_total(k).start()

        @pl.when(jnp.logical_not(owner))
        def _():
            send_near(k).start()

    def far_block(u, slot, blk, axis):
        ring[u, slot, 0] = pair(half(blk, u, 0), buffer(u, 0, slot), nb[axis, 1])
        ring[u, slot, 1] = pair(half(blk, u, 1), buffer(u, 1, slot), nb[axis, -1])

    def near_block(u, slot, blk, axis, way):
        h = 0 if way == 1 else 1
        arrived(ring[u, slot, h])
        for dst, more in zip(half(blk, u, h), buffer(u, h, slot)):
            add_in(dst, more)
        ring[u, slot, 2 + h] = pair(blk, buffer(u, 2 + h, slot), nb[axis, way])

    def own_block(u, slot, blk):
        arrived(ring[u, slot, 2])
        arrived(ring[u, slot, 3])
        for dst, one, two in zip(blk, buffer(u, 2, slot), buffer(u, 3, slot)):
            add_in(dst, one, two)

    for i in range(4):
        for u in (0, 1):
            far_block(u, i, ready(u, i), second_axis[u])
        if i > 0:
            add_parts(i - 1)
    for i in range(4):
        for u in (0, 1):
            near_block(u, i, ready(u, 4 + i), second_axis[u], 1)
        for u in (0, 1):
            near_block(u, i, ready(u, 8 + i), second_axis[u], -1)
    for i in range(4):
        for u in (0, 1):
            blk = ready(u, 12 + i)
            own_block(u, i, blk)
            if i == 0:
                far_block(u, 4, blk, first_axis[u])
            if i == 1:
                near_block(u, 4, blk, first_axis[u], 1)
            if i == 2:
                near_block(u, 4, blk, first_axis[u], -1)
    for u in (0, 1):
        blk = at(hold[u], *orders[u][15])
        own_block(u, 4, blk)
        s, w, w0, s2, v, v0 = UNITS[u]
        fin[:, s * 128 : (s + w) * 128] = blk[0][...]
        fsd[:, s2 * 128 : (s2 + v) * 128] = blk[1][...]
    r = mul((1 - lo) * 32, 16)
    arrived(pair((fin.at[pl.ds(r, 48)], fsd.at[pl.ds(r, 32)]), (wx, wxd), xn))
    r = mul(lo * 32, 16)
    snd[...] = (fin[pl.ds(r, 48), :].astype(F32) + wx[...].astype(F32)).astype(BF16)
    sndd[...] = (fsd[pl.ds(r, 32), :].astype(F32) + wxd[...].astype(F32)).astype(BF16)
    arrived(pair((snd, sndd), (wh, whd), hn))
    acc[...] = snd[...].astype(F32) + wh[...].astype(F32)
    accd[...] = sndd[...].astype(F32) + whd[...].astype(F32)
    mine = pl.ds(mul(c * HALF, 128), HALF)
    mine2 = pl.ds(mul(c * 640, 128), 640)
    r = mul((1 - c) * 16, 16)
    last = pair((acc.at[pl.ds(r, 32)], accd.at[pl.ds(r, 16)]), (out.at[:, mine], osd.at[:, mine2]), sib)
    r = mul(c * 16, 16)
    out[:, mine] = acc[pl.ds(r, 32), :]
    osd[:, mine2] = accd[pl.ds(r, 16), :]
    arrived(last)
    for k in range(3):
        swap_part(k).wait_send()
        send_across(k).wait_send()
        total_half(k, 1 - c).wait_recv()

        @pl.when(owner)
        def _(k=k):
            keep_total(k).wait()

        @pl.when(jnp.logical_not(owner))
        def _(k=k):
            send_near(k).wait_send()
            total_half(k, c).wait_recv()

    wires.finish()


def scatter_sums(gw, gsd, parts):
    scratch = []
    for _ in (0, 1):
        for s, w, w0, s2, v, v0 in UNITS:
            scratch += [pltpu.VMEM((4, 4, 80, w * 128), BF16), pltpu.VMEM((4, 4, 64, v * 128), BF16)]
    for s, w, w0, s2, v, v0 in UNITS:
        for rows, n, n0 in ((80, w, w0), (64, v, v0)):
            for tiles in (n0, n - n0, n, n):
                scratch.append(pltpu.VMEM((5, rows, tiles * 128), BF16))
    for rows, rows2 in ((80, 64), (48, 32), (48, 32), (48, 32)):
        scratch += [pltpu.VMEM((rows, HALF), BF16), pltpu.VMEM((rows2, 640), BF16)]
    scratch += [pltpu.VMEM((48, HALF), F32), pltpu.VMEM((32, 640), F32)]
    sems = 64 + 2 * 2 * 4 * 5 + 6
    scratch += [
        pltpu.SemaphoreType.DMA((sems,)),
        pltpu.SemaphoreType.DMA((sems,)),
        pltpu.SemaphoreType.DMA((64,)),
    ]
    scratch += [pltpu.VMEM((p.shape[0] // 2, p.shape[1]), BF16) for p in parts] * 2
    scratch += [pltpu.SemaphoreType.DMA((12,)), pltpu.SemaphoreType.DMA((9,)), pltpu.SemaphoreType.DMA((6,))]
    out, osd, *totals = pl.pallas_call(
        scatter_kernel,
        out_shape=(
            jax.ShapeDtypeStruct((32, WIDE * 128), F32),
            jax.ShapeDtypeStruct((16, 1280), F32),
            *(jax.ShapeDtypeStruct(p.shape, BF16) for p in parts),
        ),
        in_specs=[pl.BlockSpec(memory_space=pl.ANY)] * 5,
        out_specs=(pl.BlockSpec(memory_space=pltpu.VMEM),) * 2 + (pl.BlockSpec(memory_space=pl.ANY),) * 3,
        scratch_shapes=scratch,
        compiler_params=pltpu.CompilerParams(
            collective_id=2, has_side_effects=True, vmem_limit_bytes=56 << 20
        ),
        name="scatter_sums",
    )(gw.reshape(4, 4, 80, WIDE * 128), gsd.reshape(4, 4, 64, 1280), *parts)
    offset = 4 * lax.rem(lax.axis_index("exp"), 4)
    return lax.dynamic_slice(out, (offset, 0), (20, WIDE * 128)), osd[:14], totals


PART_AXES = (("y", "z", "g"), ("z", "g", "y"), ("g", "y", "z")) * 2
PARTS = len(PART_AXES)


def lane_cuts(*sizes):
    return tuple((sum(sizes[:i]), n) for i, n in enumerate(sizes))


ROW_CUTS = lane_cuts(4, 4, 3, 3, 3, 3)
LAST_OUT_CUTS = lane_cuts(3, 3, 3, 3, 4, 5)
LAST_BACK_CUTS = lane_cuts(3, 3, 3, 3, 4, 4)


def exchange_kernel(cuts, outward, work, counts, *refs):
    n = len(cuts)
    n_in, n_out, n_scratch = counts
    work_in, refs = refs[n : n + n_in], refs[:n] + refs[n + n_in :]
    work_out, refs = refs[2 * n : 2 * n + n_out], refs[: 2 * n] + refs[2 * n + n_out :]
    work_scratch = refs[4 * n + 3 :]
    stages = [refs[0:n], refs[2 * n : 3 * n], refs[3 * n : 4 * n], refs[n : 2 * n]]
    ssem, rsem, lsem = refs[4 * n : 4 * n + 3]
    hi, y, z, lo, c = place()
    me = {"y": y, "z": z}

    def along(axis, k):
        q = dict(me)
        q[axis] = lax.rem(me[axis] + k, 4)
        return q[axis], device(hi, q["y"], q["z"], lo, c)

    hi_or, c_or, lo_or = (hi, 1 - hi), (c, 1 - c), (lo, 1 - lo)

    def target(d, b):
        if outward:
            return device(hi_or[b], y, z, lo_or[d], hi), lo_or[d] * 2 + hi_or[b], lo * 2 + c, 2 * d + c
        return device(c, y, z, lo_or[d], c_or[b]), lo_or[d] * 2 + c_or[b], lo * 2 + hi, 2 * d + hi

    def source(d, b):
        if outward:
            return device(c, y, z, lo_or[d], c_or[b]), lo_or[d] * 2 + c_or[b], 2 * d + c_or[b]
        return device(hi_or[b], y, z, lo_or[d], hi), lo_or[d] * 2 + hi_or[b], 2 * d + hi_or[b]

    corners = ((1, 1), (0, 1), (1, 0))
    stays = c == hi
    moves = jnp.logical_not(stays)
    bar = pltpu.get_barrier_semaphore()

    def greet_one(to):
        pl.semaphore_signal(bar, inc=1, device_id=to, device_id_type=MESH)

    for axis in "yz":
        for k in (1, 2, 3):
            greet_one(along(axis, k)[1])
    for corner in corners:
        greet_one(source(*corner)[0])

    @pl.when(moves)
    def _():
        greet_one(source(0, 0)[0])
        pl.semaphore_wait(bar, 10)

    @pl.when(stays)
    def _():
        pl.semaphore_wait(bar, 9)

    every = slice(None)

    def view(ref, axis, v, lanes):
        index = {"y": (v, every, every), "z": (every, v, every), "g": (every, every, v)}[axis]
        return ref.at[index + (every, pl.ds(lanes[0] * 128, lanes[1] * 128))]

    def remote(src, dst, k, tag, to):
        return pltpu.make_async_remote_copy(
            src_ref=src, dst_ref=dst, send_sem=ssem.at[k], recv_sem=rsem.at[tag], device_id=to, device_id_type=MESH
        )

    pending = {}
    sent = []
    used = [0, 0]

    def go(part, phase):
        axis = PART_AXES[part][phase]
        waits = []
        for a in range(n):
            src, dst = stages[phase][a], stages[phase + 1][a]
            lanes = cuts[a][part]
            base, kept = used
            used[0] += 4
            used[1] += 1
            if axis != "g":
                own = view(dst, axis, me[axis], lanes)
                for k in (2, 1, 3):
                    v, to = along(axis, k)
                    copy = remote(view(src, axis, v, lanes), own, base + k, base + k, to)
                    copy.start()
                    waits.append(copy.wait_recv)
                    sent.append(copy.wait_send)
                keep = pltpu.make_async_copy(view(src, axis, me[axis], lanes), own, lsem.at[kept])
                keep.start()
                waits.append(keep.wait)
                continue
            for d, b in corners:
                to, there, here, tag = target(d, b)
                copy = remote(view(src, axis, there, lanes), view(dst, axis, here, lanes), base + 2 * d + b, base + tag, to)
                copy.start()
                sent.append(copy.wait_send)
                _from, place_, tag = source(d, b)
                block = view(dst, axis, place_, lanes)
                waits.append(remote(block, block, base + 2 * d + b, base + tag, _from).wait_recv)
            to, there, here, tag = target(0, 0)
            keep = pltpu.make_async_copy(view(src, axis, there, lanes), view(dst, axis, here, lanes), lsem.at[kept])
            copy = remote(view(src, axis, there, lanes), view(dst, axis, here, lanes), base, base + tag, to)
            _from, place_, tag = source(0, 0)
            block = view(dst, axis, place_, lanes)
            coming = remote(block, block, base, base + tag, _from)

            @pl.when(stays)
            def _(keep=keep):
                keep.start()

            @pl.when(moves)
            def _(copy=copy):
                copy.start()

            def wait_corner(keep=keep, coming=coming):
                @pl.when(stays)
                def _():
                    keep.wait()

                @pl.when(moves)
                def _():
                    coming.wait_recv()

            def wait_sent(copy=copy):
                @pl.when(moves)
                def _():
                    copy.wait_send()

            waits.append(wait_corner)
            sent.append(wait_sent)
        pending[part, phase] = waits

    for phase in (0, 1, 2):
        for part in range(PARTS):
            if phase > 0:
                for wait in pending[part, phase - 1]:
                    wait()
            go(part, phase)
        work(phase, work_in, work_out, work_scratch)
    for part in range(PARTS):
        for wait in pending[part, 2]:
            wait()
    for wait in sent:
        wait()


def exchange(collective_id, outward, arrays, cuts, work, work_in, work_out, work_scratch=()):
    n = len(arrays)
    split = [a.reshape((4, 4, 4) + a.shape[1:]) for a in arrays]
    shapes = [jax.ShapeDtypeStruct(a.shape, a.dtype) for a in split]
    vmem = pl.BlockSpec(memory_space=pltpu.VMEM)
    out = pl.pallas_call(
        functools.partial(exchange_kernel, cuts, outward, work, (len(work_in), len(work_out), len(work_scratch))),
        out_shape=tuple(shapes) + tuple(work_out),
        in_specs=[pl.BlockSpec(memory_space=pl.ANY)] * n + [vmem] * len(work_in),
        out_specs=(pl.BlockSpec(memory_space=pl.ANY),) * n + (vmem,) * len(work_out),
        scratch_shapes=[pltpu.VMEM(s.shape, s.dtype) for s in shapes] * 2
        + [
            pltpu.SemaphoreType.DMA((12 * PARTS * n,)),
            pltpu.SemaphoreType.DMA((12 * PARTS * n,)),
            pltpu.SemaphoreType.DMA((3 * PARTS * n,)),
        ]
        + list(work_scratch),
        compiler_params=pltpu.CompilerParams(
            collective_id=collective_id, has_side_effects=True, vmem_limit_bytes=56 << 20
        ),
        name="exchange_rows",
    )(*split, *work_in)
    return [o.reshape(a.shape) for o, a in zip(out, arrays)] + list(out[n:])


def dot(a, b):
    return jnp.dot(a, b, preferred_element_type=F32)


def dot_t(a, b):
    return lax.dot_general(a, b, (((1,), (1,)), ((), ())), preferred_element_type=F32)


def t_dot(a, b):
    return lax.dot_general(a, b, (((0,), (0,)), ((), ())), preferred_element_type=F32)


def iota(shape, dim):
    return lax.broadcasted_iota(jnp.int32, shape, dim)


def shape(dtype, *dims):
    return jax.ShapeDtypeStruct(dims, dtype)


def local_call(kernel, name, outs, *operands):
    return pl.pallas_call(
        kernel,
        out_shape=tuple(outs),
        compiler_params=pltpu.CompilerParams(vmem_limit_bytes=56 << 20),
        name=name,
    )(*operands)


def gain_rows(block):
    pick = (iota((8, 128), 1) == iota((8, 128), 0) + 64).astype(BF16)
    return dot_t(pick, block)


def rms_forward(values, gain):
    inv_rms = lax.rsqrt(jnp.mean(values * values, axis=-1, keepdims=True) + EPSILON)
    return values * inv_rms * gain, inv_rms


def rms_backward(values, inv_rms, gain, upstream):
    weighted = upstream * gain
    inner = jnp.mean(weighted * values, axis=-1, keepdims=True)
    grad_in = inv_rms * weighted - values * (inv_rms * inv_rms * inv_rms) * inner
    grad_gain = jnp.sum(upstream * values * inv_rms, axis=0, keepdims=True)
    return grad_in, grad_gain


def rotary_tables(rows):
    freq = np.power(10000.0, -2.0 * np.arange(64) / 128)
    angles = np.arange(rows)[:, None] * freq[None, :]
    cos, sin = np.cos(angles), np.sin(angles)
    return (
        jnp.asarray(np.concatenate([cos, cos], axis=1), F32),
        jnp.asarray(np.concatenate([-sin, sin], axis=1), F32),
    )


def silu_parts(pre_act):
    sigma = jax.nn.sigmoid(pre_act)
    return (pre_act * sigma, sigma * (1.0 + pre_act * (1.0 - sigma)))


def seq_rows():
    return pl.ds(pl.multiple_of(lax.axis_index("seq") * 128, 128), 128)


def qkv_kernel(tok, gains, cos, sin, w, act, q, kv):
    i = pl.program_id(0)

    @pl.when(i == 0)
    def _():
        normed, _inv = rms_forward(tok[...].astype(F32), gain_rows(gains[...])[0:1])
        act[...] = normed.astype(BF16)

    x = dot(act[...], w[...])
    here = seq_rows()
    cosine, sine = cos[here, :], sin[here, :]
    heads = [x[:, h * 128 : (h + 1) * 128] for h in range(5)]
    turned = jnp.concatenate([h * cosine + pltpu.roll(h, 64, 1) * sine for h in heads], axis=1)

    @pl.when(i < 2)
    def _():
        q[...] = turned.astype(BF16)

    @pl.when(i >= 2)
    def _():
        kv[...] = jnp.where(i < 4, turned, x).astype(BF16)


def project(tokens, weights, cos, sin):
    rows, width = tokens.shape
    whole = lambda a: pl.BlockSpec(a.shape, lambda i: (0, 0))
    return pl.pallas_call(
        qkv_kernel,
        grid=(6,),
        out_shape=(shape(BF16, rows, width), shape(BF16, rows, width), shape(BF16, rows, 2 * width)),
        in_specs=[
            whole(tokens),
            pl.BlockSpec((width, 128), lambda i: (0, 56)),
            whole(cos),
            whole(sin),
            pl.BlockSpec((width, 640), lambda i: (0, i)),
        ],
        out_specs=(
            pl.BlockSpec((rows, width), lambda i: (0, 0)),
            pl.BlockSpec((rows, 640), lambda i: (0, jnp.minimum(i, 1))),
            pl.BlockSpec((rows, 640), lambda i: (0, jnp.maximum(i - 2, 0))),
        ),
        compiler_params=pltpu.CompilerParams(vmem_limit_bytes=56 << 20),
        name="queries_keys_values",
    )(tokens, weights, cos, sin, weights)


def allowed_keys(seg_row, seg_col):
    hi = lax.axis_index("seq")
    here = seq_rows()
    mine = seg_col[here, :]
    rows = mine.shape[0]
    own = (seg_row[:, here] == mine) & (iota((rows, rows), 1) <= iota((rows, rows), 0))
    prior = (seg_row[:, 0:rows] == mine) & (hi == 1)
    return own, prior


def head_probs(h, q, kv, prior, own_ok, prior_ok, width):
    lanes = slice(h * 128, (h + 1) * 128)
    behind = slice(width + h * 128, width + (h + 1) * 128)
    query = q[:, lanes]
    keys = jnp.concatenate([prior[:, lanes], kv[:, lanes]], axis=0)
    values = jnp.concatenate([prior[:, behind], kv[:, behind]], axis=0)
    scores = dot_t(query, keys) * (128.0**-0.5)
    rows = query.shape[0]
    scores = jnp.concatenate(
        [jnp.where(prior_ok, scores[:, :rows], NEG_BIG), jnp.where(own_ok, scores[:, rows:], NEG_BIG)], axis=1
    )
    expo = jnp.exp(scores - jnp.max(scores, axis=-1, keepdims=True))
    return query, keys, values, expo / jnp.sum(expo, axis=-1, keepdims=True)


def attend_kernel(tok, q, kv, prior, seg_row, seg_col, routes, out_w, router_w, mixed, hidden_one, act, gates_t, slot_t):
    rows, width = tok.shape
    own_ok, prior_ok = allowed_keys(seg_row, seg_col)
    for h in range(HEADS):
        _query, _keys, values, probs = head_probs(h, q, kv, prior, own_ok, prior_ok, width)
        mixed[:, h * 128 : (h + 1) * 128] = dot(probs.astype(BF16), values).astype(BF16)
    hidden = tok[...].astype(F32) + dot(mixed[...], out_w[...])
    hidden_one[...] = hidden
    router = router_w[...]
    normed, _inv = rms_forward(hidden, gain_rows(router)[1:2])
    low = normed.astype(BF16)
    act[...] = low
    expert = iota((rows, 128), 1)
    named = routes[...]
    member = named[:, 0:1] == expert
    for k in range(1, named.shape[1]):
        member = member | (named[:, k : k + 1] == expert)
    logits = jnp.where(member, dot(low, router), NEG_BIG)
    expo = jnp.where(member, jnp.exp(logits - jnp.max(logits, axis=-1, keepdims=True)), 0.0)
    gates_t[...] = (expo / jnp.sum(expo, axis=-1, keepdims=True)).T
    before = (iota((rows, rows), 1) < iota((rows, rows), 0)).astype(BF16)
    rank = dot(before, member.astype(BF16))
    slot_t[...] = jnp.where(member, rank, -1.0).T


def attend(tokens, q, kv, prior, seg_row, seg_col, routes, weights):
    rows, width = tokens.shape
    whole = lambda a: pl.BlockSpec(a.shape, lambda i: (0, 0))
    operands = (tokens, q, kv, prior, seg_row, seg_col, routes)
    outs = (
        shape(BF16, rows, width),
        shape(F32, rows, width),
        shape(BF16, rows, width),
        shape(F32, 128, rows),
        shape(F32, 128, rows),
    )
    return pl.pallas_call(
        attend_kernel,
        grid=(1,),
        out_shape=outs,
        in_specs=[whole(a) for a in operands]
        + [pl.BlockSpec((width, 1280), lambda i: (0, 3)), pl.BlockSpec((width, 128), lambda i: (0, 56))],
        out_specs=tuple(whole(a) for a in outs),
        compiler_params=pltpu.CompilerParams(vmem_limit_bytes=56 << 20),
        name="attend",
    )(*operands, weights, weights)


EVEN = 16


def even_places(slot_t):
    experts, rows = slot_t.shape
    wide = jnp.broadcast_to(slot_t[:, None, :], (experts, EVEN, rows))
    place_of = iota((experts, EVEN, rows), 1).astype(F32)
    return wide == place_of


def dispatch_kernel(act, grad, gates, slot_t, out_r, out_l):
    block, even, _lanes = out_r.shape
    rows, width = act.shape
    here = pl.ds(pl.multiple_of(pl.program_id(0) * block, block), block)
    slots = slot_t[here, :]
    places = even_places(slots)
    last = slots == float(EVEN)
    hot = places.astype(F32).reshape(block * even, rows).astype(BF16)
    last_hot = last.astype(BF16)
    x, g = act[...], grad[...]
    out_r[:, :, :width] = dot(hot, x).astype(BF16).reshape(block, even, width)
    out_r[:, :, width:] = dot(hot, g).astype(BF16).reshape(block, even, width)
    gt = gates[here, :]
    at_slot = jnp.sum(
        jnp.where(places, jnp.broadcast_to(gt[:, None, :], places.shape), 0.0).reshape(block * even, rows),
        axis=-1,
        keepdims=True,
    )
    spread = jnp.broadcast_to(at_slot, (block * even, 128)).reshape(block, even, 128)
    lane_of = iota((block, even, 128), 1) == iota((block, even, 128), 2)
    even_gates = jnp.sum(jnp.where(lane_of, spread, 0.0), axis=1)
    last_gates = jnp.sum(jnp.where(last, gt, 0.0), axis=-1, keepdims=True)
    slot_gates = jnp.where(iota((block, 128), 1) == EVEN, last_gates, even_gates)
    out_l[...] = jnp.concatenate([dot(last_hot, x), dot(last_hot, g), slot_gates], axis=1).reshape(
        block, 1, 2 * width + 128
    )


def dispatch(act, grad, gates_t, slot_t, experts):
    width = act.shape[1]
    block = 8
    whole = lambda a: pl.BlockSpec(a.shape, lambda i: (0, 0))
    cut = lambda n, lanes: pl.BlockSpec((block, n, lanes), lambda i: (i, 0, 0))
    return pl.pallas_call(
        dispatch_kernel,
        grid=(experts // block,),
        out_shape=(
            shape(BF16, experts, EVEN, 2 * width),
            shape(F32, experts, 1, 2 * width + 128),
        ),
        in_specs=[whole(act), whole(grad), whole(gates_t), whole(slot_t)],
        out_specs=(cut(EVEN, 2 * width), cut(1, 2 * width + 128)),
        compiler_params=pltpu.CompilerParams(vmem_limit_bytes=32 << 20),
        name="dispatch",
    )(act, grad, gates_t, slot_t)


def expert_kernel(rows_r, rows_l, w_gate, w_up, w_down, out_r, out_l, all_x, all_g, hidden, d_gate, d_up):
    sources, _one, _lanes = rows_l.shape
    width = rows_r.shape[-1] // 2
    last = rows_l[...].reshape(sources, rows_l.shape[-1])
    even = sources * EVEN
    x = jnp.concatenate([rows_r[:, :, :width].reshape(even, width), last[:, :width].astype(BF16)], axis=0)
    g = jnp.concatenate(
        [rows_r[:, :, width:].reshape(even, width).astype(F32), last[:, width : 2 * width]], axis=0
    )
    sent = last[:, 2 * width :]
    spread = jnp.broadcast_to(sent[:, None, :], (sources, EVEN, 128))
    own = iota((sources, EVEN, 128), 1) == iota((sources, EVEN, 128), 2)
    even_gates = jnp.sum(jnp.where(own, spread, 0.0).reshape(even, 128), axis=-1, keepdims=True)
    last_gates = jnp.sum(jnp.where(iota((sources, 128), 1) == EVEN, sent, 0.0), axis=-1, keepdims=True)
    grad_result = (jnp.concatenate([even_gates, last_gates], axis=0) * g).astype(BF16)
    all_x[...] = x
    all_g[...] = grad_result
    gate = dot(x, w_gate[...])
    up_ = dot(x, w_up[...])
    silu, slope = silu_parts(gate)
    low = (silu * up_).astype(BF16)
    hidden[...] = low
    grad_hidden = dot_t(grad_result, w_down[...])
    grad_gate = (grad_hidden * up_ * slope).astype(BF16)
    grad_up = (grad_hidden * silu).astype(BF16)
    d_gate[...] = grad_gate
    d_up[...] = grad_up
    result = dot(low, w_down[...]).astype(BF16)
    grad_in = (dot_t(grad_gate, w_gate[...]) + dot_t(grad_up, w_up[...])).astype(BF16)
    out_r[:, :, :width] = result[:even].reshape(sources, EVEN, width)
    out_r[:, :, width:] = grad_in[:even].reshape(sources, EVEN, width)
    out_l[...] = jnp.concatenate([result[even:], grad_in[even:]], axis=1).astype(F32).reshape(sources, 1, 2 * width)


def expert(rows_r, rows_l, w_gate, w_up, w_down):
    devices, _even, width = rows_r.shape
    width = width // 2
    inner = w_gate.shape[1]
    steps = 4
    src = devices // steps
    rows = src * (EVEN + 1)
    total = rows * steps
    whole = lambda a: pl.BlockSpec(a.shape, lambda i: (0, 0))
    cut = lambda n, lanes: pl.BlockSpec((src, n, lanes), lambda i: (i, 0, 0))
    flat = lambda lanes: pl.BlockSpec((rows, lanes), lambda i: (i, 0))
    return pl.pallas_call(
        expert_kernel,
        grid=(steps,),
        out_shape=(
            shape(BF16, devices, EVEN, 2 * width),
            shape(F32, devices, 1, 2 * width),
            shape(BF16, total, width),
            shape(BF16, total, width),
            shape(BF16, total, inner),
            shape(BF16, total, inner),
            shape(BF16, total, inner),
        ),
        in_specs=[cut(EVEN, 2 * width), cut(1, rows_l.shape[-1]), whole(w_gate), whole(w_up), whole(w_down)],
        out_specs=(
            cut(EVEN, 2 * width),
            cut(1, 2 * width),
            flat(width),
            flat(width),
            flat(inner),
            flat(inner),
            flat(inner),
        ),
        compiler_params=pltpu.CompilerParams(vmem_limit_bytes=60 << 20),
        name="expert",
    )(rows_r, rows_l, w_gate, w_up, w_down)


def shared_work(phase, ins, outs, scratch):
    act, grad, sgu, sdown = ins
    out_s, grad_in, grad_gu, grad_down = outs
    (hidden,) = scratch
    inner = sdown.shape[0]
    if phase == 0:
        gate = dot(act[...], sgu[:, :inner])
        up_ = dot(act[...], sgu[:, inner:])
        silu, slope = silu_parts(gate)
        hidden[...] = (silu * up_).astype(BF16)
        grad_hidden = dot_t(grad[...], sdown[...])
        grad_gu[:, :inner] = (grad_hidden * up_ * slope).astype(BF16)
        grad_gu[:, inner:] = (grad_hidden * silu).astype(BF16)
    elif phase == 1:
        out_s[...] = dot(hidden[...], sdown[...])
        grad_in[...] = dot_t(grad_gu[...], sgu[...])
    else:

        @pl.loop(0, inner // 256)
        def _(i):
            r = pl.ds(pl.multiple_of(i * 256, 256), 256)
            grad_down[r, :] = t_dot(hidden[:, r], grad[...]).astype(BF16)


def expert_work(phase, ins, outs, scratch):
    all_x, all_g, hidden, d_gate, d_up = ins
    g_gate, g_up, g_down = outs
    if phase < 2:
        grad, out = (d_gate, g_gate) if phase == 0 else (d_up, g_up)

        @pl.loop(0, out.shape[0] // 256)
        def _(i):
            r = pl.ds(pl.multiple_of(i * 256, 256), 256)
            out[r, :] = t_dot(all_x[:, r], grad[...]).astype(BF16)

    else:

        @pl.loop(0, g_down.shape[0] // 128)
        def _(i):
            r = pl.ds(pl.multiple_of(i * 128, 128), 128)
            g_down[r, :] = t_dot(hidden[:, r], all_g[...]).astype(BF16)


def split_terms(w):
    top = w.astype(BF16)
    rest = w - top.astype(F32)
    mid = rest.astype(BF16)
    return top, mid, (rest - mid.astype(F32)).astype(BF16)


def combine_kernel(
    back_r, back_l, slot_t, gates_t, grad, hidden_one, out_s, grad_in_s, router_w, out_w,
    layer_out, grad_hidden, grad_low, grad_mixed, grad_logits, grad_gain,
):
    experts = back_r.shape[0]
    rows, width = hidden_one.shape
    slots = slot_t[0:experts, :]
    places = even_places(slots)
    last = slots == float(EVEN)
    out_rows = back_r[:, :, :width].reshape(experts * EVEN, width)
    last_l = back_l[...].reshape(experts, 2 * width).astype(BF16)
    gt = gates_t[0:experts, :]
    even_w = jnp.where(places, jnp.broadcast_to(gt[:, None, :], places.shape), 0.0).reshape(experts * EVEN, rows)
    last_w = jnp.where(last, gt, 0.0)
    routed = jnp.zeros((rows, width), F32)
    for e_term, l_term in zip(split_terms(even_w), split_terms(last_w)):
        routed = routed + t_dot(e_term, out_rows) + t_dot(l_term, last_l[:, :width])
    hidden = hidden_one[...]
    layer_out[...] = (hidden + out_s[...] + routed).astype(BF16)
    g = grad[...]
    dots = dot_t(out_rows, g).reshape(experts, EVEN, rows)
    dots_last = dot_t(last_l[:, :width], g)
    grad_gates = jnp.sum(jnp.where(places, dots, 0.0), axis=1) + jnp.where(last, dots_last, 0.0)
    logits_t = gt * (grad_gates - jnp.sum(gt * grad_gates, axis=0, keepdims=True))
    low_logits = jnp.concatenate([logits_t, jnp.zeros((128 - experts, rows), F32)], axis=0).T.astype(BF16)
    grad_logits[...] = low_logits
    hot = places.astype(F32).reshape(experts * EVEN, rows).astype(BF16)
    grad_routed = t_dot(hot, back_r[:, :, width:].reshape(experts * EVEN, width)) + t_dot(last.astype(BF16), last_l[:, width:])
    router = router_w[...]
    grad_act = grad_routed + dot_t(low_logits, router) + grad_in_s[...]
    gain = gain_rows(router)[1:2]
    _normed, inv = rms_forward(hidden, gain)
    grad_norm, gain_sum = rms_backward(hidden, inv, gain, grad_act)
    grad_gain[...] = gain_sum
    total = g.astype(F32) + grad_norm
    grad_hidden[...] = total
    low = total.astype(BF16)
    grad_low[...] = low
    grad_mixed[...] = dot_t(low, out_w[...]).astype(BF16)


def combine(back_r, back_l, slot_t, gates_t, grad, hidden_one, out_s, grad_in_s, weights):
    rows, width = hidden_one.shape
    operands = (back_r, back_l, slot_t, gates_t, grad, hidden_one, out_s, grad_in_s)
    whole = lambda a: pl.BlockSpec(a.shape, lambda i: (0,) * len(a.shape))
    outs = (
        shape(BF16, rows, width),
        shape(F32, rows, width),
        shape(BF16, rows, width),
        shape(BF16, rows, width),
        shape(BF16, rows, 128),
        shape(F32, 1, width),
    )
    return pl.pallas_call(
        combine_kernel,
        grid=(1,),
        out_shape=outs,
        in_specs=[whole(a) for a in operands]
        + [pl.BlockSpec((width, 128), lambda i: (0, 56)), pl.BlockSpec((width, 1280), lambda i: (0, 3))],
        out_specs=tuple(whole(a) for a in outs),
        compiler_params=pltpu.CompilerParams(vmem_limit_bytes=56 << 20),
        name="combine",
    )(*operands, weights, weights)


def attend_back_kernel(q, kv, prior, seg_row, seg_col, grad_mixed, cos, sin, grad_q, grad_own, grad_prior):
    rows, width = q.shape
    own_ok, prior_ok = allowed_keys(seg_row, seg_col)
    here = seq_rows()
    cosine, sine = cos[here, :], sin[here, :]
    inv_root = 128.0**-0.5
    for h in range(HEADS):
        query, keys, values, probs = head_probs(h, q, kv, prior, own_ok, prior_ok, width)
        lanes = slice(h * 128, (h + 1) * 128)
        behind = slice(width + h * 128, width + (h + 1) * 128)
        gm = grad_mixed[:, lanes]
        grad_probs = dot_t(gm, values)
        inner = jnp.sum(probs * grad_probs, axis=-1, keepdims=True)
        grad_scores = (probs * (grad_probs - inner)).astype(BF16)
        grad_values = t_dot(probs.astype(BF16), gm)
        gq = dot(grad_scores, keys) * inv_root
        grad_keys = t_dot(grad_scores, query) * inv_root
        grad_q[:, lanes] = (gq * cosine - pltpu.roll(gq, 64, 1) * sine).astype(BF16)
        grad_own[:, lanes] = grad_keys[rows:]
        grad_own[:, behind] = grad_values[rows:]
        grad_prior[:, lanes] = grad_keys[:rows].astype(BF16)
        grad_prior[:, behind] = grad_values[:rows].astype(BF16)


def input_grad_kernel(tok, gains, cos, sin, grad_q, grad_own, later, grad_hidden, w, grad_qkv, grad_tokens, grad_gain, total):
    i = pl.program_id(0)
    rows, width = tok.shape

    @pl.when(i == 0)
    def _():
        here = seq_rows()
        cosine, sine = cos[here, :], sin[here, :]
        grad_qkv[:, :width] = grad_q[...]
        for h in range(HEADS):
            lanes = slice(h * 128, (h + 1) * 128)
            gk = grad_own[:, lanes] + later[:, lanes].astype(F32)
            grad_qkv[:, width + h * 128 : width + (h + 1) * 128] = (
                gk * cosine - pltpu.roll(gk, 64, 1) * sine
            ).astype(BF16)
        grad_qkv[:, 2 * width :] = (grad_own[:, width:] + later[:, width:].astype(F32)).astype(BF16)
        total[...] = jnp.zeros_like(total)

    lanes = pl.ds(pl.multiple_of(i * 640, 128), 640)
    total[...] += dot_t(grad_qkv[:, lanes], w[...])

    @pl.when(i == pl.num_programs(0) - 1)
    def _():
        values = tok[...].astype(F32)
        gain = gain_rows(gains[...])[0:1]
        _normed, inv = rms_forward(values, gain)
        grad_norm, gain_sum = rms_backward(values, inv, gain, total[...])
        grad_gain[...] = gain_sum
        grad_tokens[...] = grad_hidden[...] + grad_norm


def input_grads(tokens, cos, sin, grad_q, grad_own, later, grad_hidden, weights):
    rows, width = tokens.shape
    whole = lambda a: pl.BlockSpec(a.shape, lambda i: (0, 0))
    outs = (shape(BF16, rows, 3 * width), shape(F32, rows, width), shape(F32, 1, width))
    return pl.pallas_call(
        input_grad_kernel,
        grid=(6,),
        out_shape=outs,
        in_specs=[
            whole(tokens),
            pl.BlockSpec((width, 128), lambda i: (0, 56)),
            whole(cos),
            whole(sin),
            whole(grad_q),
            whole(grad_own),
            whole(later),
            whole(grad_hidden),
            pl.BlockSpec((width, 640), lambda i: (0, i)),
        ],
        out_specs=tuple(whole(a) for a in outs),
        scratch_shapes=[pltpu.VMEM((rows, width), F32)],
        compiler_params=pltpu.CompilerParams(vmem_limit_bytes=56 << 20),
        name="input_grads",
    )(tokens, weights, cos, sin, grad_q, grad_own, later, grad_hidden, weights)


def weight_grad_kernel(act_attn, mixed, act_ffn, grad_qkv, grad_out, grad_gu, grad_logits, gain_a, gain_f, out):
    i = pl.program_id(0)

    def product(left, right, start):
        lanes = pl.ds(pl.multiple_of((i - start) * 256, 256), 256)
        out[...] = t_dot(left[...], right[:, lanes]).astype(BF16)

    @pl.when(i < 15)
    def _():
        product(act_attn, grad_qkv, 0)

    @pl.when((i >= 15) & (i < 20))
    def _():
        product(mixed, grad_out, 15)

    @pl.when((i >= 20) & (i < 28))
    def _():
        product(act_ffn, grad_gu, 20)

    @pl.when(i == 28)
    def _():
        row = iota((8, 1280), 0)
        gains = jnp.where(row == 0, gain_a[...], jnp.where(row == 1, gain_f[...], 0.0)).astype(BF16)
        pick = (iota((8, 128), 1) == iota((8, 128), 0) + 64).astype(BF16)
        out[:, :128] = (t_dot(act_ffn[...], grad_logits[...]) + t_dot(gains, pick)).astype(BF16)
        out[:, 128:] = jnp.zeros((1280, 128), BF16)


def weight_grads(*operands):
    width = operands[0].shape[1]
    whole = lambda a: pl.BlockSpec(a.shape, lambda i: (0, 0))
    return pl.pallas_call(
        weight_grad_kernel,
        grid=(WIDE // 2,),
        out_shape=shape(BF16, width, WIDE * 128),
        in_specs=[whole(a) for a in operands],
        out_specs=pl.BlockSpec((width, 256), lambda i: (0, i)),
        compiler_params=pltpu.CompilerParams(vmem_limit_bytes=56 << 20),
        name="weight_grads",
    )(*operands)


def per_device(
    tokens,
    cotangent,
    segments,
    routes,
    norm_gain_attn,
    w_query,
    w_key,
    w_value,
    w_out,
    norm_gain_ffn,
    w_router,
    shared_gate,
    shared_up,
    shared_down,
    expert_gate,
    expert_up,
    expert_down,
):
    rows = tokens.shape[1]
    width = tokens.shape[2]
    experts = w_router.shape[1]
    tokens, grad, routes = tokens[0], cotangent[0], routes[0]
    seg_row = segments
    seg_col = segments.reshape(-1, 1)

    def spread(w):
        w = w.reshape(w.shape[0], experts, w.shape[1] // experts)
        return jnp.pad(w, ((0, 0), (0, 0), (0, 2))).reshape(w.shape[0], experts * 16)

    shard = jnp.concatenate(
        [
            w_query,
            w_key,
            w_value,
            w_out,
            spread(shared_gate),
            spread(shared_up),
            w_router,
            norm_gain_attn[:, None],
            norm_gain_ffn[:, None],
            jnp.zeros((w_query.shape[0], 190), BF16),
        ],
        axis=1,
    )
    weights, sdown_w, expert_w = gather_weights(shard, shared_down, (expert_gate[0], expert_up[0], expert_down[0]))
    cos, sin = rotary_tables(2 * rows)
    act_attn, q, kv = project(tokens, weights, cos, sin)
    prior = lax.ppermute(kv, "seq", [(0, 1)])
    mixed, hidden_one, act_ffn, gates_t, slot_t = attend(tokens, q, kv, prior, seg_row, seg_col, routes, weights)

    rows_r, rows_l = dispatch(act_ffn, grad, gates_t, slot_t, experts)
    rows_r, rows_l, out_s, grad_in_s, grad_gu, grad_sdown = exchange(
        3,
        True,
        (rows_r, rows_l),
        (ROW_CUTS, LAST_OUT_CUTS),
        shared_work,
        (act_ffn, grad, weights[:, 5120:7168], sdown_w),
        (shape(F32, rows, width), shape(F32, rows, width), shape(BF16, rows, 2048), shape(BF16, 1024, width)),
        (pltpu.VMEM((rows, 1024), BF16),),
    )
    out_r, out_l, *kept = expert(rows_r, rows_l, *expert_w)
    back_r, back_l, *part_expert = exchange(
        4,
        False,
        (out_r, out_l),
        (ROW_CUTS, LAST_BACK_CUTS),
        expert_work,
        tuple(kept),
        tuple(shape(BF16, *w.shape[1:]) for w in (expert_gate, expert_up, expert_down)),
    )
    layer_out, grad_hidden, grad_low, grad_mixed, grad_logits, gain_ffn = combine(
        back_r, back_l, slot_t, gates_t, grad, hidden_one, out_s, grad_in_s, weights
    )
    grad_q, grad_own, grad_prior = local_call(
        attend_back_kernel,
        "attend_back",
        (shape(BF16, rows, width), shape(F32, rows, 2 * width), shape(BF16, rows, 2 * width)),
        q, kv, prior, seg_row, seg_col, grad_mixed, cos, sin,
    )
    later = lax.ppermute(grad_prior, "seq", [(1, 0)])
    grad_qkv, grad_tokens, gain_attn = input_grads(tokens, cos, sin, grad_q, grad_own, later, grad_hidden, weights)
    grads = weight_grads(act_attn, mixed, act_ffn, grad_qkv, grad_low, grad_gu, grad_logits, gain_attn, gain_ffn)
    own, own_down, sums = scatter_sums(grads, grad_sdown, part_expert)

    def gathered_hidden(w):
        return w.reshape(w.shape[0], experts, 16)[:, :, :14].reshape(w.shape[0], experts * 14)

    expert_grads = [a.astype(F32)[None] for a in sums]
    return (
        layer_out[None],
        grad_tokens[None],
        own[:, 7168 + experts],
        own[:, :1280],
        own[:, 1280:2560],
        own[:, 2560:3840],
        own[:, 3840:5120],
        own[:, 7169 + experts],
        own[:, 7168 : 7168 + experts],
        gathered_hidden(own[:, 5120:6144]),
        gathered_hidden(own[:, 6144:7168]),
        own_down,
        *expert_grads,
    )


def solution(mesh):
    rows = P("exp", None)
    deep = P("exp", None, None)
    split = P("exp", "seq", None)
    gain = P("exp")
    in_specs = (split, split, rows, split, gain, rows, rows, rows, rows, gain) + (rows,) * 4 + (deep,) * 3
    out_specs = (split, split, gain, rows, rows, rows, rows, gain) + (rows,) * 4 + (deep,) * 3
    return jax.shard_map(per_device, mesh=mesh, in_specs=in_specs, out_specs=out_specs, check_vma=False)
```

```python
import functools
import jax
import jax.numpy as jnp
import numpy as np
from jax import lax
from jax.experimental import pallas as pl
from jax.experimental.pallas import tpu as pltpu
from jax.sharding import PartitionSpec as P

HEADS = 10
EPSILON = 1e-06
NEG_BIG = -1e30
F32 = jnp.float32
BF16 = jnp.bfloat16
MESH = pl.DeviceIdType.MESH

PIECES = {
    "q": (80, 16, ((0, 8, 4), (8, 8, 4))),
    "r": (80, 14, ((0, 7, 4), (7, 7, 4))),
    "d": (64, 5, ((0, 3, 2), (3, 2, 1))),
}
Q_WIDE, R_WIDE, D_WIDE = 4096, 3584, 1280
GAINS = 30
ROUTER = 26
UNITS = (0, 1)


def place():
    hi = lax.axis_index("seq")
    e = lax.axis_index("exp")
    return hi, e // 16, lax.rem(e // 4, 4), lax.rem(e // 2, 2), lax.rem(e, 2)


def device(hi, y, z, lo, c):
    return (hi, ((y * 4 + z) * 2 + lo) * 2 + c)


def up(v):
    return lax.rem(v + 1, 4)


def dn(v):
    return lax.rem(v + 3, 4)


def opp(v):
    return lax.rem(v + 2, 4)


def mul(v, m=128):
    return pl.multiple_of(v, m)


def greet(devices):
    bar = pltpu.get_barrier_semaphore()
    for to in devices:
        pl.semaphore_signal(bar, inc=1, device_id=to, device_id_type=MESH)
    pl.semaphore_wait(bar, len(devices))


class Sender:
    def __init__(self, send_sem, recv_sem, local_sem):
        self.sems = (send_sem, recv_sem, local_sem)
        self.sent = []
        self.kept = 0

    def describe(self, src, dst, to):
        k = len(self.sent)
        self.sent.append(None)
        return pltpu.make_async_remote_copy(
            src_ref=src,
            dst_ref=dst,
            send_sem=self.sems[0].at[k],
            recv_sem=self.sems[1].at[k],
            device_id=to,
            device_id_type=MESH,
        )

    def remote(self, src, dst, to):
        copy = self.describe(src, dst, to)
        copy.start()
        self.sent[-1] = copy
        return copy

    def local(self, src, dst):
        copy = pltpu.make_async_copy(src, dst, self.sems[2].at[self.kept])
        self.kept += 1
        copy.start()
        return copy

    def settle(self, copy):
        copy.wait_send()
        self.sent = [None if one is copy else one for one in self.sent]

    def finish(self):
        for copy in self.sent:
            if copy is not None:
                copy.wait_send()


def arrived(copies):
    for copy in copies:
        copy.wait_recv()


def ring_neighbours(hi, y, z, lo, c):
    return {
        ("y", 1): device(hi, up(y), z, lo, c),
        ("y", -1): device(hi, dn(y), z, lo, c),
        ("z", 1): device(hi, y, up(z), lo, c),
        ("z", -1): device(hi, y, dn(z), lo, c),
        ("y", 2): device(hi, opp(y), z, lo, c),
        ("z", 2): device(hi, y, opp(z), lo, c),
    }


def unit_tiles(piece, u, half):
    s, w, w0 = PIECES[piece][2][u]
    return ((s, w0), (s + w0, w - w0))[half] if half is not None else (s, w)


def lanes(piece, u, half, core):
    s, w = unit_tiles(piece, u, half)
    return pl.ds(mul(core * (PIECES[piece][1] * 128) + s * 128), w * 128)


def core_lanes(piece, core):
    n = PIECES[piece][1] * 128
    return pl.ds(mul(core * n), n)


def interleave(steps, work):
    for step in steps:
        step()
        next(work, None)
    for _ in work:
        pass


def dot(a, b):
    return jnp.dot(a, b, preferred_element_type=F32)


def dot_t(a, b):
    return lax.dot_general(a, b, (((1,), (1,)), ((), ())), preferred_element_type=F32)


def t_dot(a, b):
    return lax.dot_general(a, b, (((0,), (0,)), ((), ())), preferred_element_type=F32)


def iota(shape, dim):
    return lax.broadcasted_iota(jnp.int32, shape, dim)


def shape(dtype, *dims):
    return jax.ShapeDtypeStruct(dims, dtype)


def gain_rows(tile):
    pick = (iota((8, 128), 1) == iota((8, 128), 0)).astype(BF16)
    return dot_t(pick, tile)


def rms_forward(values, gain):
    inv_rms = lax.rsqrt(jnp.mean(values * values, axis=-1, keepdims=True) + EPSILON)
    return values * inv_rms * gain, inv_rms


def rms_backward(values, inv_rms, gain, upstream):
    weighted = upstream * gain
    inner = jnp.mean(weighted * values, axis=-1, keepdims=True)
    grad_in = inv_rms * weighted - values * (inv_rms * inv_rms * inv_rms) * inner
    grad_gain = jnp.sum(upstream * values * inv_rms, axis=0, keepdims=True)
    return grad_in, grad_gain


def rotary_tables(rows):
    freq = np.power(10000.0, -2.0 * np.arange(64) / 128)
    angles = np.arange(rows)[:, None] * freq[None, :]
    cos, sin = np.cos(angles), np.sin(angles)
    return (
        jnp.asarray(np.concatenate([cos, cos], axis=1), F32),
        jnp.asarray(np.concatenate([-sin, sin], axis=1), F32),
    )


def silu_parts(pre_act):
    sigma = jax.nn.sigmoid(pre_act)
    return (pre_act * sigma, sigma * (1.0 + pre_act * (1.0 - sigma)))


def seq_rows():
    return pl.ds(mul(lax.axis_index("seq") * 128), 128)


def allowed_keys(seg_row, seg_col):
    hi = lax.axis_index("seq")
    here = seq_rows()
    mine = seg_col[here, :]
    rows = mine.shape[0]
    own = (seg_row[:, here] == mine) & (iota((rows, rows), 1) <= iota((rows, rows), 0))
    prior = (seg_row[:, 0:rows] == mine) & (hi == 1)
    return own, prior


def head_probs(h, q, kv, prior, own_ok, prior_ok, width):
    here = slice(h * 128, (h + 1) * 128)
    behind = slice(width + h * 128, width + (h + 1) * 128)
    query = q[:, here]
    keys = jnp.concatenate([prior[:, here], kv[:, here]], axis=0)
    values = jnp.concatenate([prior[:, behind], kv[:, behind]], axis=0)
    scores = dot_t(query, keys) * (128.0**-0.5)
    rows = query.shape[0]
    scores = jnp.concatenate(
        [jnp.where(prior_ok, scores[:, :rows], NEG_BIG), jnp.where(own_ok, scores[:, rows:], NEG_BIG)], axis=1
    )
    expo = jnp.exp(scores - jnp.max(scores, axis=-1, keepdims=True))
    return query, keys, values, expo / jnp.sum(expo, axis=-1, keepdims=True)


class Gather:
    def __init__(self, wires, names, blocks, outs, spot):
        hi, y, z, lo, c = spot
        self.wires, self.names, self.outs, self.core = wires, names, outs, c
        self.sib = device(hi, y, z, lo, 1 - c)
        nb = ring_neighbours(hi, y, z, lo, c)
        self.keep = []
        units = []
        for u in UNITS:
            a1, a2 = ("y", "z") if u == 0 else ("z", "y")
            p1, p2 = (y, z) if u == 0 else (z, y)
            units.append(
                dict(p1=p1, p2=p2, up1=nb[a1, 1], dn1=nb[a1, -1], up2=nb[a2, 1], dn2=nb[a2, -1], got={}, second=[], sib=[])
            )
        self.units = units
        self.steps = [functools.partial(self.own_block, blocks, y, z)]
        for u in UNITS:
            self.steps.append(functools.partial(self.first_axis, u, "up1", 0))
        for u in UNITS:
            self.steps.append(functools.partial(self.first_axis, u, "dn1", 1))
        for u in UNITS:
            self.steps.append(functools.partial(self.first_far, u))
        turn = (lambda p: p, dn, up, opp)
        self.near, self.far = [], []
        for k in range(4):
            for u in UNITS:
                q1 = turn[k](units[u]["p1"])
                self.near.append(functools.partial(self.second_axis, u, k, q1))
                self.far.append(functools.partial(self.second_far, u, k, q1))

    def region(self, name, u, half, q1, q2):
        by, bz = (q1, q2) if u == 0 else (q2, q1)
        return self.outs[name].at[by, bz, :, lanes(name, u, half, self.core)]

    def send(self, u, half, q1, q2, to, src=None):
        copies = []
        for name in self.names:
            dst = self.region(name, u, half, q1, q2)
            copies.append(self.wires.remote(src[name] if src else dst, dst, to))
        return copies

    def spread(self, u, q1, src=None):
        unit = self.units[u]
        at = (q1, unit["p2"])
        unit["second"].append((self.send(u, None, *at, unit["up2"], src), self.send(u, None, *at, unit["dn2"], src)))
        unit["sib"].append(self.send(u, None, *at, self.sib, src))

    def own_block(self, blocks, y, z):
        for name in self.names:
            self.keep.append(self.wires.local(blocks[name], self.outs[name].at[y, z, :, core_lanes(name, self.core)]))
        for u, unit in enumerate(self.units):
            src = {}
            for name in self.names:
                s, w = unit_tiles(name, u, None)
                src[name] = blocks[name].at[:, pl.ds(s * 128, w * 128)]
            at = (unit["p1"], unit["p2"])
            unit["got"]["up1"] = self.send(u, None, *at, unit["up1"], src)
            unit["got"]["dn1"] = self.send(u, None, *at, unit["dn1"], src)
            self.spread(u, unit["p1"], src)

    def first_axis(self, u, way, half):
        unit = self.units[u]
        arrived(unit["got"][way])
        q1 = dn(unit["p1"]) if way == "up1" else up(unit["p1"])
        unit["got"]["far", half] = self.send(u, half, q1, unit["p2"], unit[way])
        self.spread(u, q1)

    def first_far(self, u):
        unit = self.units[u]
        arrived(unit["got"]["far", 0])
        arrived(unit["got"]["far", 1])
        self.spread(u, opp(unit["p1"]))

    def second_axis(self, u, k, q1):
        unit = self.units[u]
        for half, way, turn in ((0, "up2", dn), (1, "dn2", up)):
            arrived(unit["second"][k][half])
            at = (q1, turn(unit["p2"]))
            unit["got"][k, half] = self.send(u, half, *at, unit[way])
            unit["sib"].append(self.send(u, None, *at, self.sib))

    def second_far(self, u, k, q1):
        unit = self.units[u]
        arrived(unit["got"][k, 0])
        arrived(unit["got"][k, 1])
        unit["sib"].append(self.send(u, None, q1, opp(unit["p2"]), self.sib))

    def finish(self):
        for unit in self.units:
            for copies in unit["sib"]:
                arrived(copies)
        for copy in self.keep:
            copy.wait()


def window_block(first, second, shift):
    n = first.shape[0]
    return first[0:shift], first[shift:n] + second[0 : n - shift], second[n - shift : n]


def forward_kernel(
    win_q, win_r, win_d, e0, e1, e2, tok, cos, sin, seg_row, seg_col,
    out_q, out_r, out_d, o0, o1, o2, act, q, kv, prior, mixed,
    sib_q, sib_r, pair_q, pair_r, side_q, side_r, blk_q, blk_r, blk_d, w_buf, ssem, rsem, lsem, esem, wsem,
):
    spot = place()
    hi, y, z, lo, c = spot
    sib = device(hi, y, z, lo, 1 - c)
    xn = device(hi, y, z, 1 - lo, c)
    hn = device(1 - hi, y, z, lo, c)
    greet([sib, xn, hn] + list(ring_neighbours(*spot).values()))
    wires = Sender(ssem, rsem, lsem)
    width = tok.shape[1]
    owner = c == hi

    @pl.when(hi == 0)
    def _():
        prior[...] = jnp.zeros_like(prior)

    j = lo * 2 + c
    windows = {"q": (win_q, sib_q, pair_q, side_q, blk_q), "r": (win_r, sib_r, pair_r, side_r, blk_r)}
    swaps = {}
    for name in "qr":
        win, from_sib = windows[name][:2]
        swaps[name] = wires.remote(win.at[:, core_lanes(name, 1 - c)], from_sib, sib)
    r16 = pl.ds(mul(j * 16, 16), 16)
    swap_d = wires.remote(win_d.at[:, core_lanes("d", 1 - c)], blk_d.at[r16], sib)
    blk_d[r16, :] = win_d[:, core_lanes("d", c)]
    across = {}
    for name in "qr":
        win, from_sib, pair, side, _blk = windows[name]
        own = win[:, core_lanes(name, c)]
        swaps[name].wait_recv()
        got = from_sib[...]
        pair[0:16], pair[16:32], pair[32:48] = window_block(
            jnp.where(c == 0, own, got), jnp.where(c == 0, got, own), 16
        )
        across[name] = wires.remote(pair, side, xn)
    swap_d.wait_recv()
    r32 = pl.ds(mul(lo * 32, 16), 32)
    across_d = wires.remote(blk_d.at[r32], blk_d.at[r32], xn)

    def pass_expert(k):
        return pltpu.make_async_remote_copy(
            src_ref=(e0, e1, e2)[k],
            dst_ref=(o0, o1, o2)[k],
            send_sem=esem.at[0, k],
            recv_sem=esem.at[1, k],
            device_id=sib,
            device_id_type=MESH,
        )

    blocks = {"q": blk_q, "r": blk_r, "d": blk_d}
    outs = {"q": out_q, "r": out_r, "d": out_d}
    group_q = Gather(wires, "q", blocks, outs, spot)
    group_r = Gather(wires, "rd", blocks, outs, spot)

    def whole_block(name):
        _win, _sib, pair, side, blk = windows[name]
        across[name].wait_recv()
        own, got = pair[...], side[...]
        blk[0:32], blk[32:48], blk[48:80] = window_block(
            jnp.where(lo == 0, own, got), jnp.where(lo == 0, got, own), 32
        )

    whole_block("q")
    for step in group_q.steps:
        step()
    whole_block("r")
    across_d.wait_recv()
    for step in group_q.near:
        step()
    group_r.steps[0]()
    for step in group_q.far:
        step()
    group_q.finish()

    @pl.when(owner)
    def _():
        for k in range(3):
            pass_expert(k).start()

    def load(i, slot):
        return pltpu.make_async_copy(out_q.at[:, :, :, pl.ds(i * 512, 512)], w_buf.at[slot], wsem.at[slot])

    later = wires.describe(kv, prior, hn)

    def work():
        order = (7, 2, 3, 4, 5, 6, 0, 1)
        here = seq_rows()
        cosine, sine = cos[here, :], sin[here, :]
        load(order[0], 0).start()
        for n, i in enumerate(order):
            slot = n % 2
            load(i, slot).wait()
            if n + 1 < len(order):
                load(order[n + 1], 1 - slot).start()
            w = w_buf[slot].reshape(width, 512)
            if n == 0:
                gains = gain_rows(w[:, (GAINS - 28) * 128 : (GAINS - 27) * 128])
                normed, _inv = rms_forward(tok[...].astype(F32), gains[0:1])
                act[...] = normed.astype(BF16)
                w = w[:, :256]
            x = dot(act[...], w)
            for t in range(w.shape[1] // 128):
                tile = 4 * i + t
                v = x[:, t * 128 : (t + 1) * 128]
                if tile < 20:
                    v = v * cosine + pltpu.roll(v, 64, 1) * sine
                if tile < 10:
                    q[:, tile * 128 : (tile + 1) * 128] = v.astype(BF16)
                else:
                    kv[:, (tile - 10) * 128 : (tile - 9) * 128] = v.astype(BF16)
            if i == 6:

                @pl.when(hi == 0)
                def _():
                    later.start()

            yield
        for _ in range(4):
            yield

        @pl.when(hi == 1)
        def _():
            later.wait_recv()

        own_ok, prior_ok = allowed_keys(seg_row, seg_col)
        for h in range(HEADS):
            _query, _keys, values, probs = head_probs(h, q, kv, prior, own_ok, prior_ok, width)
            mixed[:, h * 128 : (h + 1) * 128] = dot(probs.astype(BF16), values).astype(BF16)
            yield

    interleave(group_r.steps[1:] + group_r.near + group_r.far + [group_r.finish], work())

    @pl.when(hi == 0)
    def _():
        later.wait_send()

    @pl.when(owner)
    def _():
        for k in range(3):
            pass_expert(k).wait_send()

    @pl.when(jnp.logical_not(owner))
    def _():
        for k in range(3):
            pass_expert(k).wait_recv()

    wires.finish()


def forward(shard_q, shard_r, down, experts, tokens, cos, sin, seg_row, seg_col):
    rows, width = tokens.shape
    offset = 4 * lax.rem(lax.axis_index("exp"), 4)
    window = lambda s: lax.dynamic_update_slice(jnp.zeros((32, s.shape[1]), BF16), s, (offset, 0))
    down = jnp.pad(down, ((0, 2), (0, 0)))
    sems = 2 + 1 + 3 + 36 * 2 * 3 + 8
    vmem, anywhere = pl.BlockSpec(memory_space=pltpu.VMEM), pl.BlockSpec(memory_space=pl.ANY)
    half = {name: PIECES[name][1] * 128 for name in PIECES}
    out = pl.pallas_call(
        forward_kernel,
        out_shape=(
            shape(BF16, 4, 4, 80, Q_WIDE),
            shape(BF16, 4, 4, 80, R_WIDE),
            shape(BF16, 4, 4, 64, D_WIDE),
            *(shape(BF16, *w.shape) for w in experts),
            shape(BF16, rows, width),
            shape(BF16, rows, width),
            shape(BF16, rows, 2 * width),
            shape(BF16, rows, 2 * width),
            shape(BF16, rows, width),
        ),
        in_specs=[vmem] * 3 + [anywhere] * 3 + [vmem] * 5,
        out_specs=(anywhere,) * 6 + (vmem,) * 5,
        scratch_shapes=[pltpu.VMEM((n, half[name]), BF16) for n in (32, 48, 48, 80) for name in "qr"]
        + [
            pltpu.VMEM((64, half["d"]), BF16),
            pltpu.VMEM((2, 4, 4, 80, 512), BF16),
            pltpu.SemaphoreType.DMA((sems,)),
            pltpu.SemaphoreType.DMA((sems,)),
            pltpu.SemaphoreType.DMA((3,)),
            pltpu.SemaphoreType.DMA((2, 3)),
            pltpu.SemaphoreType.DMA((2,)),
        ],
        compiler_params=pltpu.CompilerParams(collective_id=1, has_side_effects=True, vmem_limit_bytes=56 << 20),
        name="gather_attend",
    )(window(shard_q), window(shard_r), down, *experts, tokens, cos, sin, seg_row, seg_col)
    w_q, w_r, w_d = (out[k].reshape(16 * out[k].shape[2], out[k].shape[3]) for k in range(3))
    return (w_q, w_r, w_d, out[3:6]) + tuple(out[6:])


class RingSum:
    def __init__(self, wires, names, hold, from_sib, bufs, to_sib, spot):
        hi, y, z, lo, c = spot
        self.wires, self.names, self.hold, self.from_sib, self.bufs, self.to_sib = (
            wires, names, hold, from_sib, bufs, to_sib,
        )
        self.sib = device(hi, y, z, lo, 1 - c)
        self.nb = ring_neighbours(hi, y, z, lo, c)
        self.first_axis, self.second_axis = ("y", "z"), ("z", "y")
        self.ring, self.coming = {}, {}
        orders = []
        for u in UNITS:
            p1, p2 = (y, z) if u == 0 else (z, y)
            ones = (opp(p1), up(p1), dn(p1), p1)
            orders.append([(q1, q2) if u == 0 else (q2, q1) for q2 in (opp(p2), up(p2), dn(p2), p2) for q1 in ones])
        self.orders = orders
        self.steps = []
        for i in range(4):
            for u in UNITS:
                self.steps.append(functools.partial(self.far_step, u, i))
        for i in range(4):
            for u in UNITS:
                self.steps.append(functools.partial(self.near_step, u, i, 1))
            for u in UNITS:
                self.steps.append(functools.partial(self.near_step, u, i, -1))
        for i in range(4):
            for u in UNITS:
                self.steps.append(functools.partial(self.own_step, u, i))
        for u in UNITS:
            self.steps.append(functools.partial(self.last_step, u))

    def blocks(self, refs, u, index):
        return {name: refs[name][u].at[index] for name in self.names}

    def start(self):
        for k in range(16):
            for u in UNITS:
                at = self.orders[u][k]
                src, dst = self.blocks(self.to_sib, u, at), self.blocks(self.from_sib, u, at)
                self.coming[u, k] = self.pair(src, dst, self.sib)

    def pair(self, src, dst, to):
        return [self.wires.remote(src[name], dst[name], to) for name in self.names]

    def add_in(self, dst, *more):
        @pl.loop(0, dst.shape[-2] // 16)
        def _(i):
            r = pl.ds(mul(i * 16, 16), 16)
            value = dst[r, :].astype(F32)
            for ref in more:
                value = value + ref[r, :].astype(F32)
            dst[r, :] = value.astype(BF16)

    def ready(self, u, k):
        arrived(self.coming[u, k])
        at = self.orders[u][k]
        blk, more = self.blocks(self.hold, u, at), self.blocks(self.from_sib, u, at)
        for name in self.names:
            self.add_in(blk[name], more[name])
        return blk

    def half(self, blk, u, h):
        cut = {}
        for name in self.names:
            s, w, w0 = PIECES[name][2][u]
            cut[name] = blk[name].at[:, pl.ds(0, w0 * 128) if h == 0 else pl.ds(w0 * 128, (w - w0) * 128)]
        return cut

    def buffer(self, u, i, slot):
        return {name: self.bufs[name][u][i].at[slot] for name in self.names}

    def far_block(self, u, slot, blk, axis):
        self.ring[u, slot, 0] = self.pair(self.half(blk, u, 0), self.buffer(u, 0, slot), self.nb[axis, 1])
        self.ring[u, slot, 1] = self.pair(self.half(blk, u, 1), self.buffer(u, 1, slot), self.nb[axis, -1])

    def near_block(self, u, slot, blk, axis, way):
        h = 0 if way == 1 else 1
        arrived(self.ring[u, slot, h])
        dst, more = self.half(blk, u, h), self.buffer(u, h, slot)
        for name in self.names:
            self.add_in(dst[name], more[name])
        self.ring[u, slot, 2 + h] = self.pair(blk, self.buffer(u, 2 + h, slot), self.nb[axis, way])

    def own_block(self, u, slot, blk):
        arrived(self.ring[u, slot, 2])
        arrived(self.ring[u, slot, 3])
        one, two = self.buffer(u, 2, slot), self.buffer(u, 3, slot)
        for name in self.names:
            self.add_in(blk[name], one[name], two[name])

    def far_step(self, u, i):
        self.far_block(u, i, self.ready(u, i), self.second_axis[u])

    def near_step(self, u, i, way):
        self.near_block(u, i, self.ready(u, (4 if way == 1 else 8) + i), self.second_axis[u], way)

    def own_step(self, u, i):
        blk = self.ready(u, 12 + i)
        self.own_block(u, i, blk)
        axis = self.first_axis[u]
        if i == 0:
            for h in (0, 1):
                self.ring[u, 4, h] = self.pair(self.half(blk, u, h), self.buffer(u, h, 4), self.nb[axis, 2])
        elif i < 3:
            self.ring[u, 4, 1 + i] = self.pair(blk, self.buffer(u, 1 + i, 4), self.nb[axis, 1 if i == 1 else -1])

    def last_step(self, u):
        blk = self.blocks(self.hold, u, self.orders[u][15])
        self.own_block(u, 4, blk)
        for h in (0, 1):
            arrived(self.ring[u, 4, h])
            dst, more = self.half(blk, u, h), self.buffer(u, h, 4)
            for name in self.names:
                self.add_in(dst[name], more[name])


def sum_scratch():
    scratch = []
    for rows, _tiles, units in PIECES.values():
        for s, w, w0 in units:
            scratch += [pltpu.VMEM((4, 4, rows, w * 128), BF16)] * 2
            scratch += [pltpu.VMEM((5, rows, t * 128), BF16) for t in (w0, w - w0, w, w)]
    return scratch


def backward_kernel(
    left_r, right_r, sdown, act, q, kv, prior, seg_row, seg_col, grad_mixed, cos, sin, tok, grad_hidden, gain_f, w_q,
    p0, p1, p2,
    fin_q, fin_r, fin_d, t0, t1, t2, grad_tokens,
    *scratch,
):
    names = list(PIECES)
    hold, from_sib, bufs = {}, {}, {}
    scratch = list(scratch)
    for name in names:
        hold[name], from_sib[name], bufs[name] = [], [], []
        for u in UNITS:
            hold[name].append(scratch.pop(0))
            from_sib[name].append(scratch.pop(0))
            bufs[name].append([scratch.pop(0) for _ in range(4)])
    sums, sides, mids, fars = ({name: scratch.pop(0) for name in names} for _ in range(4))
    accs = {name: scratch.pop(0) for name in names}
    sent = [scratch.pop(0) for _ in UNITS]
    grad_own, grad_prior, later, left_q, right_q, total, w_buf, gain_tile = scratch[:8]
    ssem, rsem, lsem, esend, erecv, wsem, piece_sem = scratch[8:]
    spot = place()
    hi, y, z, lo, c = spot
    sib = device(hi, y, z, lo, 1 - c)
    xn = device(hi, y, z, 1 - lo, c)
    hn = device(1 - hi, y, z, lo, c)
    greet([sib, xn, hn, device(1 - hi, y, z, lo, 1 - c)] + list(ring_neighbours(*spot).values()))
    wires = Sender(ssem, rsem, lsem)
    rows, width = tok.shape

    owner = c == hi
    parts, totals = (p0, p1, p2), (t0, t1, t2)
    across = device(1 - hi, y, z, lo, hi)

    def rows_of(ref, core):
        n = ref.shape[0] // 2
        return ref.at[pl.ds(mul(core * n, 16), n)]

    def expert_copy(src, dst, k, tag, to):
        return pltpu.make_async_remote_copy(
            src_ref=src, dst_ref=dst, send_sem=esend.at[k], recv_sem=erecv.at[tag], device_id=to, device_id_type=MESH
        )

    def across_piece(k, i):
        n = parts[k].shape[0]
        return pltpu.make_async_remote_copy(
            src_ref=parts[k].at[pl.ds(i * 64, 64)],
            dst_ref=totals[k].at[pl.ds(mul(c * n + i * 64, 16), 64)],
            send_sem=piece_sem.at[0, k, i],
            recv_sem=piece_sem.at[1, k, 10 * c + i],
            device_id=across,
            device_id_type=MESH,
        )

    def coming_piece(k, i, core):
        n = parts[k].shape[0]
        rows_ = totals[k].at[pl.ds(mul(core * n + i * 64, 16), 64)]
        return pltpu.make_async_remote_copy(
            src_ref=rows_,
            dst_ref=rows_,
            send_sem=piece_sem.at[0, k, i],
            recv_sem=piece_sem.at[1, k, 10 * core + i],
            device_id=across,
            device_id_type=MESH,
        )

    pieces = [(k, i) for k in range(3) for i in range(parts[k].shape[0] // 64)]

    def send_near(k):
        return expert_copy(parts[k], rows_of(totals[k], c), k, k, sib)

    def near_half(k):
        return expert_copy(rows_of(totals[k], 1 - c), rows_of(totals[k], 1 - c), k, k, sib)

    def expert_steps():
        for n, (k, i) in enumerate(pieces):
            across_piece(k, i).start()
            if n == len(pieces) // 2:

                @pl.when(jnp.logical_not(owner))
                def _():
                    for k in range(3):
                        send_near(k).start()

            yield

    own_d = []
    for u in UNITS:
        s, w = unit_tiles("d", u, None)
        own_d.append(wires.local(sdown.at[:, :, :, lanes("d", u, None, c)], hold["d"][u]))

    def products(left, right, name, core, refs):
        for u in UNITS:
            r = right[:, lanes(name, u, None, core)]
            for m in (0, 1):
                v = t_dot(left[:, m * 640 : (m + 1) * 640], r).astype(BF16)
                for b in range(8):
                    refs[u][2 * m + b // 4, b % 4] = v[b * 80 : (b + 1) * 80]

    def views(name, refs):
        return [ref.at[:, :, :, pl.ds(0, PIECES[name][2][u][1] * 128)] for u, ref in enumerate(refs)]

    to_sib_r = views("r", sent)
    products(left_r, right_r, "r", 1 - c, to_sib_r)
    to_sib_d = [sdown.at[:, :, :, lanes("d", u, None, 1 - c)] for u in UNITS]
    group_r = RingSum(wires, "rd", hold, from_sib, bufs, {"r": to_sib_r, "d": to_sib_d}, spot)
    group_r.start()
    products(left_r, right_r, "r", c, hold["r"])
    for copy in own_d:
        copy.wait()

    def load(i):
        return pltpu.make_async_copy(w_q.at[:, pl.ds(i * 512, 512)], w_buf.at[i % 2], wsem.at[i % 2])

    load_gains = pltpu.make_async_copy(w_q.at[:, pl.ds(GAINS * 128, 128)], gain_tile, wsem.at[2])
    exchange_kv = wires.describe(grad_prior, later, hn)
    to_sib_q = views("q", sent)
    group_q = RingSum(wires, "q", hold, from_sib, bufs, {"q": to_sib_q}, spot)

    def work():
        load(0).start()
        load_gains.start()
        here = seq_rows()
        cosine, sine = cos[here, :], sin[here, :]
        own_ok, prior_ok = allowed_keys(seg_row, seg_col)
        inv_root = 128.0**-0.5

        @pl.when(hi == 1)
        def _():
            later[...] = jnp.zeros_like(later)

        for h in range(HEADS):
            query, keys, values, probs = head_probs(h, q, kv, prior, own_ok, prior_ok, width)
            mine = slice(h * 128, (h + 1) * 128)
            behind = slice(width + h * 128, width + (h + 1) * 128)
            gm = grad_mixed[:, mine]
            grad_probs = dot_t(gm, values)
            inner = jnp.sum(probs * grad_probs, axis=-1, keepdims=True)
            grad_scores = (probs * (grad_probs - inner)).astype(BF16)
            grad_values = t_dot(probs.astype(BF16), gm)
            gq = dot(grad_scores, keys) * inv_root
            grad_keys = t_dot(grad_scores, query) * inv_root
            right_q[0:rows, mine] = (gq * cosine - pltpu.roll(gq, 64, 1) * sine).astype(BF16)
            grad_own[:, mine] = grad_keys[rows:]
            grad_own[:, behind] = grad_values[rows:]
            grad_prior[:, mine] = grad_keys[:rows].astype(BF16)
            grad_prior[:, behind] = grad_values[:rows].astype(BF16)
            yield

        @pl.when(hi == 1)
        def _():
            exchange_kv.start()

        right_q[0:rows, 3 * width :] = jnp.zeros((rows, Q_WIDE - 3 * width), BF16)
        right_q[rows:, :] = (iota((16, Q_WIDE), 1) == iota((16, Q_WIDE), 0) + GAINS * 128).astype(BF16)
        left_q[0:rows, :] = act[...]
        total[...] = jnp.zeros_like(total)

        def add_chunk(i):
            load(i).wait()
            if i < 7:
                load(i + 1).start()
            total[...] += dot_t(right_q[0:rows, i * 512 : (i + 1) * 512], w_buf[i % 2])

        for i in (0, 1):
            add_chunk(i)
            yield

        @pl.when(hi == 0)
        def _():
            exchange_kv.wait_recv()

        for h in range(HEADS):
            mine = slice(h * 128, (h + 1) * 128)
            gk = grad_own[:, mine] + later[:, mine].astype(F32)
            right_q[0:rows, width + h * 128 : width + (h + 1) * 128] = (
                gk * cosine - pltpu.roll(gk, 64, 1) * sine
            ).astype(BF16)
        right_q[0:rows, 2 * width : 3 * width] = (grad_own[:, width:] + later[:, width:].astype(F32)).astype(BF16)
        yield
        for i in range(2, 8):
            add_chunk(i)
            yield
        load_gains.wait()
        gain = gain_rows(gain_tile[...])[0:1]
        values = tok[...].astype(F32)
        _normed, inv = rms_forward(values, gain)
        grad_norm, gain_sum = rms_backward(values, inv, gain, total[...])
        grad_tokens[...] = grad_hidden[...] + grad_norm
        row = iota((16, width), 0)
        left_q[rows:, :] = jnp.where(row == 0, gain_sum, jnp.where(row == 1, gain_f[...], 0.0)).astype(BF16)
        yield
        for k in range(16):
            for u in UNITS:
                wires.settle(group_r.coming[u, k][0])
        products(left_q, right_q, "q", 1 - c, to_sib_q)
        group_q.start()
        yield
        products(left_q, right_q, "q", c, hold["q"])
        yield

    def window_sums(group):
        copies = {}
        for name in group:
            n = PIECES[name][0]
            for u in UNITS:
                s, w = unit_tiles(name, u, None)
                sums[name][:, s * 128 : (s + w) * 128] = hold[name][u][y, z]
            window = 48 if n == 80 else 32
            copies[name] = wires.remote(sums[name].at[pl.ds(mul((1 - lo) * 32, 16), window)], sides[name], xn)
        yield
        for name in group:
            copies[name].wait_recv()
            window = sides[name].shape[0]
            r = pl.ds(mul(lo * 32, 16), window)
            mids[name][...] = (sums[name][r, :].astype(F32) + sides[name][...].astype(F32)).astype(BF16)
            copies[name] = wires.remote(mids[name], fars[name], hn)
        yield
        fins = {"q": fin_q, "r": fin_r, "d": fin_d}
        for name in group:
            copies[name].wait_recv()
            accs[name][...] = mids[name][...].astype(F32) + fars[name][...].astype(F32)
            n = fins[name].shape[0]
            mine = core_lanes(name, c)
            copies[name] = wires.remote(
                accs[name].at[pl.ds(mul((1 - c) * 16, 16), n)], fins[name].at[:, mine], sib
            )
            fins[name][:, mine] = accs[name][pl.ds(mul(c * 16, 16), n), :]
        yield
        for name in group:
            copies[name].wait_recv()

    experts = expert_steps()
    busy = work()
    for step in group_r.steps[:24]:
        step()
        next(busy, None)
        next(experts, None)
    for _ in busy:
        next(experts, None)
    rest = list(group_r.steps[24:])
    for step in group_q.steps[:24]:
        step()
        next(experts, None)
        if rest:
            rest.pop(0)()
    for _ in experts:
        pass
    interleave(group_q.steps[24:], window_sums("rd"))
    for _ in window_sums("q"):
        pass
    for k, i in pieces:
        across_piece(k, i).wait_send()

    @pl.when(owner)
    def _():
        for k in range(3):
            near_half(k).wait_recv()

    @pl.when(jnp.logical_not(owner))
    def _():
        for k in range(3):
            send_near(k).wait_send()
        for k, i in pieces:
            for core in (0, 1):
                coming_piece(k, i, core).wait_recv()

    @pl.when(hi == 1)
    def _():
        exchange_kv.wait_send()

    wires.finish()


def backward(operands, parts):
    rows, width = operands[12].shape
    vmem, anywhere = pl.BlockSpec(memory_space=pltpu.VMEM), pl.BlockSpec(memory_space=pl.ANY)
    half = {name: PIECES[name][1] * 128 for name in PIECES}
    window = {"q": 48, "r": 48, "d": 32}
    fin = {"q": (32, Q_WIDE), "r": (32, R_WIDE), "d": (16, D_WIDE)}
    scratch = sum_scratch()
    scratch += [pltpu.VMEM((PIECES[name][0], half[name]), BF16) for name in PIECES]
    scratch += [pltpu.VMEM((window[name], half[name]), BF16) for _ in range(3) for name in PIECES]
    scratch += [pltpu.VMEM((window[name], half[name]), F32) for name in PIECES]
    scratch += [pltpu.VMEM((4, 4, 80, 1024), BF16)] * 2
    scratch += [
        pltpu.VMEM((rows, 2 * width), F32),
        pltpu.VMEM((rows, 2 * width), BF16),
        pltpu.VMEM((rows, 2 * width), BF16),
        pltpu.VMEM((rows + 16, width), BF16),
        pltpu.VMEM((rows + 16, Q_WIDE), BF16),
        pltpu.VMEM((rows, width), F32),
        pltpu.VMEM((2, width, 512), BF16),
        pltpu.VMEM((width, 128), BF16),
    ]
    sems = 1 + 3 * (32 + 2 * 4 * 5 + 3)
    scratch += [pltpu.SemaphoreType.DMA((n,)) for n in (sems, sems, 2, 3, 3, 3)]
    scratch += [pltpu.SemaphoreType.DMA((2, 3, 20))]
    spec = [vmem] * len(operands)
    spec[2] = spec[15] = anywhere
    return pl.pallas_call(
        backward_kernel,
        out_shape=tuple(shape(F32, *fin[name]) for name in PIECES)
        + tuple(shape(BF16, 2 * p.shape[0], p.shape[1]) for p in parts)
        + (shape(F32, rows, width),),
        in_specs=spec + [anywhere] * 3,
        out_specs=(vmem,) * 3 + (anywhere,) * 3 + (vmem,),
        scratch_shapes=scratch,
        compiler_params=pltpu.CompilerParams(collective_id=2, has_side_effects=True, vmem_limit_bytes=60 << 20),
        name="attend_back_sums",
    )(*operands, *parts)


PART_AXES = (("y", "z", "g"), ("z", "g", "y"), ("g", "y", "z")) * 2
PARTS = len(PART_AXES)


def lane_cuts(*sizes):
    return tuple((sum(sizes[:i]), n) for i, n in enumerate(sizes))


ROW_CUTS = lane_cuts(4, 4, 3, 3, 3, 3)
LAST_OUT_CUTS = lane_cuts(3, 3, 3, 3, 4, 5)
LAST_BACK_CUTS = lane_cuts(3, 3, 3, 3, 4, 4)


def exchange_kernel(cuts, outward, work, counts, *refs):
    n = len(cuts)
    n_in, n_out, n_scratch = counts
    work_in, refs = refs[n : n + n_in], refs[:n] + refs[n + n_in :]
    work_out, refs = refs[2 * n : 2 * n + n_out], refs[: 2 * n] + refs[2 * n + n_out :]
    work_scratch = refs[4 * n + 3 :]
    stages = [refs[0:n], refs[2 * n : 3 * n], refs[3 * n : 4 * n], refs[n : 2 * n]]
    ssem, rsem, lsem = refs[4 * n : 4 * n + 3]
    hi, y, z, lo, c = place()
    me = {"y": y, "z": z}

    def along(axis, k):
        q = dict(me)
        q[axis] = lax.rem(me[axis] + k, 4)
        return q[axis], device(hi, q["y"], q["z"], lo, c)

    hi_or, c_or, lo_or = (hi, 1 - hi), (c, 1 - c), (lo, 1 - lo)

    def target(d, b):
        if outward:
            return device(hi_or[b], y, z, lo_or[d], hi), lo_or[d] * 2 + hi_or[b], lo * 2 + c, 2 * d + c
        return device(c, y, z, lo_or[d], c_or[b]), lo_or[d] * 2 + c_or[b], lo * 2 + hi, 2 * d + hi

    def source(d, b):
        if outward:
            return device(c, y, z, lo_or[d], c_or[b]), lo_or[d] * 2 + c_or[b], 2 * d + c_or[b]
        return device(hi_or[b], y, z, lo_or[d], hi), lo_or[d] * 2 + hi_or[b], 2 * d + hi_or[b]

    corners = ((1, 1), (0, 1), (1, 0))
    stays = c == hi
    moves = jnp.logical_not(stays)
    bar = pltpu.get_barrier_semaphore()

    def greet_one(to):
        pl.semaphore_signal(bar, inc=1, device_id=to, device_id_type=MESH)

    for axis in "yz":
        for k in (1, 2, 3):
            greet_one(along(axis, k)[1])
    for corner in corners:
        greet_one(source(*corner)[0])

    @pl.when(moves)
    def _():
        greet_one(source(0, 0)[0])
        pl.semaphore_wait(bar, 10 if outward else 11)

    @pl.when(stays)
    def _():
        if not outward:
            greet_one(device(hi, y, z, lo, 1 - c))
        pl.semaphore_wait(bar, 9)

    every = slice(None)

    def view(ref, axis, v, lanes):
        index = {"y": (v, every, every), "z": (every, v, every), "g": (every, every, v)}[axis]
        return ref.at[index + (every, pl.ds(lanes[0] * 128, lanes[1] * 128))]

    def remote(src, dst, k, tag, to):
        return pltpu.make_async_remote_copy(
            src_ref=src, dst_ref=dst, send_sem=ssem.at[k], recv_sem=rsem.at[tag], device_id=to, device_id_type=MESH
        )

    pending = {}
    sent = []
    used = [0, 0]

    def go(part, phase):
        axis = PART_AXES[part][phase]
        waits = []
        for a in range(n):
            src, dst = stages[phase][a], stages[phase + 1][a]
            lanes = cuts[a][part]
            base, kept = used
            used[0] += 4
            used[1] += 1
            if axis != "g":
                own = view(dst, axis, me[axis], lanes)
                for k in (2, 1, 3):
                    v, to = along(axis, k)
                    copy = remote(view(src, axis, v, lanes), own, base + k, base + k, to)
                    copy.start()
                    waits.append(copy.wait_recv)
                    sent.append(copy.wait_send)
                keep = pltpu.make_async_copy(view(src, axis, me[axis], lanes), own, lsem.at[kept])
                keep.start()
                waits.append(keep.wait)
                continue
            for d, b in corners:
                to, there, here, tag = target(d, b)
                copy = remote(view(src, axis, there, lanes), view(dst, axis, here, lanes), base + 2 * d + b, base + tag, to)
                copy.start()
                sent.append(copy.wait_send)
                _from, place_, tag = source(d, b)
                block = view(dst, axis, place_, lanes)
                waits.append(remote(block, block, base + 2 * d + b, base + tag, _from).wait_recv)
            to, there, here, tag = target(0, 0)
            keep = pltpu.make_async_copy(view(src, axis, there, lanes), view(dst, axis, here, lanes), lsem.at[kept])
            copy = remote(view(src, axis, there, lanes), view(dst, axis, here, lanes), base, base + tag, to)
            _from, place_, tag = source(0, 0)
            block = view(dst, axis, place_, lanes)
            coming = remote(block, block, base, base + tag, _from)

            @pl.when(stays)
            def _(keep=keep):
                keep.start()

            @pl.when(moves)
            def _(copy=copy):
                copy.start()

            def wait_corner(keep=keep, coming=coming):
                @pl.when(stays)
                def _():
                    keep.wait()

                @pl.when(moves)
                def _():
                    coming.wait_recv()

            def wait_sent(copy=copy):
                @pl.when(moves)
                def _():
                    copy.wait_send()

            waits.append(wait_corner)
            sent.append(wait_sent)
        pending[part, phase] = waits

    work(-1, work_in, work_out, work_scratch)
    for phase in (0, 1, 2):
        for part in range(PARTS):
            if phase > 0:
                for wait in pending[part, phase - 1]:
                    wait()
            go(part, phase)
        work(phase, work_in, work_out, work_scratch)
    for part in range(PARTS):
        for wait in pending[part, 2]:
            wait()
    work(3, work_in, work_out, work_scratch)
    for wait in sent:
        wait()


def exchange(collective_id, outward, arrays, cuts, work, work_in, work_out, work_scratch=()):
    n = len(arrays)
    split = [a.reshape((4, 4, 4) + a.shape[1:]) for a in arrays]
    shapes = [jax.ShapeDtypeStruct(a.shape, a.dtype) for a in split]
    vmem = pl.BlockSpec(memory_space=pltpu.VMEM)
    out = pl.pallas_call(
        functools.partial(exchange_kernel, cuts, outward, work, (len(work_in), len(work_out), len(work_scratch))),
        out_shape=tuple(shapes) + tuple(work_out),
        in_specs=[pl.BlockSpec(memory_space=pl.ANY)] * (n + len(work_in)),
        out_specs=(pl.BlockSpec(memory_space=pl.ANY),) * n + (vmem,) * len(work_out),
        scratch_shapes=[pltpu.VMEM(s.shape, s.dtype) for s in shapes] * 2
        + [
            pltpu.SemaphoreType.DMA((12 * PARTS * n,)),
            pltpu.SemaphoreType.DMA((12 * PARTS * n,)),
            pltpu.SemaphoreType.DMA((3 * PARTS * n,)),
        ]
        + list(work_scratch),
        compiler_params=pltpu.CompilerParams(
            collective_id=collective_id, has_side_effects=True, vmem_limit_bytes=56 << 20
        ),
        name="exchange_rows",
    )(*split, *work_in)
    return [o.reshape(a.shape) for o, a in zip(out, arrays)] + list(out[n:])


def route_kernel(tok, mixed, routes, out_w, router_w, gains, hidden_one, act, gates_t, slot_t):
    rows, width = tok.shape
    hidden = tok[...].astype(F32) + dot(mixed[...], out_w[...])
    hidden_one[...] = hidden
    router = router_w[...]
    normed, _inv = rms_forward(hidden, gain_rows(gains[...])[1:2])
    low = normed.astype(BF16)
    act[...] = low
    expert = iota((rows, 128), 1)
    named = routes[...]
    member = named[:, 0:1] == expert
    for k in range(1, named.shape[1]):
        member = member | (named[:, k : k + 1] == expert)
    logits = jnp.where(member, dot(low, router), NEG_BIG)
    expo = jnp.where(member, jnp.exp(logits - jnp.max(logits, axis=-1, keepdims=True)), 0.0)
    gates_t[...] = (expo / jnp.sum(expo, axis=-1, keepdims=True)).T
    before = (iota((rows, rows), 1) < iota((rows, rows), 0)).astype(BF16)
    rank = dot(before, member.astype(BF16))
    slot_t[...] = jnp.where(member, rank, -1.0).T


def route(tokens, mixed, routes, w_r, w_q):
    rows, width = tokens.shape
    whole = lambda a: pl.BlockSpec(a.shape, lambda i: (0, 0))
    operands = (tokens, mixed, routes)
    outs = (
        shape(F32, rows, width),
        shape(BF16, rows, width),
        shape(F32, 128, rows),
        shape(F32, 128, rows),
    )
    return pl.pallas_call(
        route_kernel,
        grid=(1,),
        out_shape=outs,
        in_specs=[whole(a) for a in operands]
        + [
            pl.BlockSpec((width, 1280), lambda i: (0, 0)),
            pl.BlockSpec((width, 128), lambda i: (0, ROUTER)),
            pl.BlockSpec((width, 128), lambda i: (0, GAINS)),
        ],
        out_specs=tuple(whole(a) for a in outs),
        compiler_params=pltpu.CompilerParams(vmem_limit_bytes=56 << 20),
        name="route",
    )(*operands, w_r, w_r, w_q)


EVEN = 16


def even_places(slot_t):
    experts, rows = slot_t.shape
    wide = jnp.broadcast_to(slot_t[:, None, :], (experts, EVEN, rows))
    place_of = iota((experts, EVEN, rows), 1).astype(F32)
    return wide == place_of


def dispatch_kernel(act, grad, gates, slot_t, out_r, out_l):
    block, even, _lanes = out_r.shape
    rows, width = act.shape
    here = pl.ds(pl.multiple_of(pl.program_id(0) * block, block), block)
    slots = slot_t[here, :]
    places = even_places(slots)
    last = slots == float(EVEN)
    hot = places.astype(F32).reshape(block * even, rows).astype(BF16)
    last_hot = last.astype(BF16)
    x, g = act[...], grad[...]
    out_r[:, :, :width] = dot(hot, x).astype(BF16).reshape(block, even, width)
    out_r[:, :, width:] = dot(hot, g).astype(BF16).reshape(block, even, width)
    gt = gates[here, :]
    at_slot = jnp.sum(
        jnp.where(places, jnp.broadcast_to(gt[:, None, :], places.shape), 0.0).reshape(block * even, rows),
        axis=-1,
        keepdims=True,
    )
    spread = jnp.broadcast_to(at_slot, (block * even, 128)).reshape(block, even, 128)
    lane_of = iota((block, even, 128), 1) == iota((block, even, 128), 2)
    even_gates = jnp.sum(jnp.where(lane_of, spread, 0.0), axis=1)
    last_gates = jnp.sum(jnp.where(last, gt, 0.0), axis=-1, keepdims=True)
    slot_gates = jnp.where(iota((block, 128), 1) == EVEN, last_gates, even_gates)
    out_l[...] = jnp.concatenate([dot(last_hot, x), dot(last_hot, g), slot_gates], axis=1).reshape(
        block, 1, 2 * width + 128
    )


def dispatch(act, grad, gates_t, slot_t, experts):
    width = act.shape[1]
    block = 8
    whole = lambda a: pl.BlockSpec(a.shape, lambda i: (0, 0))
    cut = lambda n, lanes: pl.BlockSpec((block, n, lanes), lambda i: (i, 0, 0))
    return pl.pallas_call(
        dispatch_kernel,
        grid=(experts // block,),
        out_shape=(
            shape(BF16, experts, EVEN, 2 * width),
            shape(F32, experts, 1, 2 * width + 128),
        ),
        in_specs=[whole(act), whole(grad), whole(gates_t), whole(slot_t)],
        out_specs=(cut(EVEN, 2 * width), cut(1, 2 * width + 128)),
        compiler_params=pltpu.CompilerParams(vmem_limit_bytes=32 << 20),
        name="dispatch",
    )(act, grad, gates_t, slot_t)


def expert_kernel(rows_r, rows_l, o0, o1, o2, e0, e1, e2, out_r, out_l, all_x, all_g, hidden, d_gate, d_up, w_gate, w_up, w_down, sem):
    hi, _y, _z, _lo, c = place()

    def take(sources):
        copies = loads(sources, (w_gate, w_up, w_down), sem)
        for copy in copies:
            copy.start()
        for copy in copies:
            copy.wait()

    @pl.when((pl.program_id(0) == 0) & (c == hi))
    def _():
        take((e0, e1, e2))

    @pl.when((pl.program_id(0) == 0) & (c != hi))
    def _():
        take((o0, o1, o2))

    sources, _one, _lanes = rows_l.shape
    width = rows_r.shape[-1] // 2
    last = rows_l[...].reshape(sources, rows_l.shape[-1])
    even = sources * EVEN
    x = jnp.concatenate([rows_r[:, :, :width].reshape(even, width), last[:, :width].astype(BF16)], axis=0)
    g = jnp.concatenate(
        [rows_r[:, :, width:].reshape(even, width).astype(F32), last[:, width : 2 * width]], axis=0
    )
    sent = last[:, 2 * width :]
    spread = jnp.broadcast_to(sent[:, None, :], (sources, EVEN, 128))
    own = iota((sources, EVEN, 128), 1) == iota((sources, EVEN, 128), 2)
    even_gates = jnp.sum(jnp.where(own, spread, 0.0).reshape(even, 128), axis=-1, keepdims=True)
    last_gates = jnp.sum(jnp.where(iota((sources, 128), 1) == EVEN, sent, 0.0), axis=-1, keepdims=True)
    grad_result = (jnp.concatenate([even_gates, last_gates], axis=0) * g).astype(BF16)
    all_x[...] = x
    all_g[...] = grad_result
    gate = dot(x, w_gate[...])
    up_ = dot(x, w_up[...])
    silu, slope = silu_parts(gate)
    low = (silu * up_).astype(BF16)
    hidden[...] = low
    grad_hidden = dot_t(grad_result, w_down[...])
    grad_gate = (grad_hidden * up_ * slope).astype(BF16)
    grad_up = (grad_hidden * silu).astype(BF16)
    d_gate[...] = grad_gate
    d_up[...] = grad_up
    result = dot(low, w_down[...]).astype(BF16)
    grad_in = (dot_t(grad_gate, w_gate[...]) + dot_t(grad_up, w_up[...])).astype(BF16)
    out_r[:, :, :width] = result[:even].reshape(sources, EVEN, width)
    out_r[:, :, width:] = grad_in[:even].reshape(sources, EVEN, width)
    out_l[...] = jnp.concatenate([result[even:], grad_in[even:]], axis=1).astype(F32).reshape(sources, 1, 2 * width)


def expert(rows_r, rows_l, passed, own):
    devices, _even, width = rows_r.shape
    width = width // 2
    inner = own[0].shape[1]
    steps = 4
    src = devices // steps
    rows = src * (EVEN + 1)
    total = rows * steps
    cut = lambda n, lanes: pl.BlockSpec((src, n, lanes), lambda i: (i, 0, 0))
    flat = lambda lanes: pl.BlockSpec((rows, lanes), lambda i: (i, 0))
    return pl.pallas_call(
        expert_kernel,
        grid=(steps,),
        out_shape=(
            shape(BF16, devices, EVEN, 2 * width),
            shape(F32, devices, 1, 2 * width),
            shape(BF16, total, width),
            shape(BF16, total, width),
            shape(BF16, total, inner),
            shape(BF16, total, inner),
            shape(BF16, total, inner),
        ),
        in_specs=[cut(EVEN, 2 * width), cut(1, rows_l.shape[-1])] + [pl.BlockSpec(memory_space=pl.ANY)] * 6,
        scratch_shapes=[pltpu.VMEM(w.shape, BF16) for w in own] + [pltpu.SemaphoreType.DMA((3,))],
        out_specs=(
            cut(EVEN, 2 * width),
            cut(1, 2 * width),
            flat(width),
            flat(width),
            flat(inner),
            flat(inner),
            flat(inner),
        ),
        compiler_params=pltpu.CompilerParams(vmem_limit_bytes=60 << 20),
        name="expert",
    )(rows_r, rows_l, *passed, *own)


def loads(ins, bufs, sem):
    return [pltpu.make_async_copy(src, dst, sem.at[k]) for k, (src, dst) in enumerate(zip(ins, bufs))]


def shared_work(phase, ins, outs, scratch):
    w_r, *others = ins
    out_s, grad_in, grad_gu, grad_down = outs
    sgu, sdown, act, grad, hidden, sem = scratch
    inner = sdown.shape[0]
    copies = loads([w_r.at[:, pl.ds(1280, 2 * inner)]] + others, (sgu, sdown, act, grad), sem) if phase < 1 else []
    if phase == -1:
        for copy in copies:
            copy.start()
    elif phase == 0:
        for copy in copies:
            copy.wait()
        gate = dot(act[...], sgu[:, :inner])
        up_ = dot(act[...], sgu[:, inner:])
        silu, slope = silu_parts(gate)
        hidden[...] = (silu * up_).astype(BF16)
        grad_hidden = dot_t(grad[...], sdown[...])
        grad_gu[:, :inner] = (grad_hidden * up_ * slope).astype(BF16)
        grad_gu[:, inner:] = (grad_hidden * silu).astype(BF16)
    elif phase == 1:
        out_s[...] = dot(hidden[...], sdown[...])
        grad_in[...] = dot_t(grad_gu[...], sgu[...])
    elif phase == 2:

        @pl.loop(0, inner // 256)
        def _(i):
            r = pl.ds(mul(i * 256, 256), 256)
            grad_down[r, :] = t_dot(hidden[:, r], grad[...]).astype(BF16)


def expert_work(phase, ins, outs, scratch):
    bufs, products, from_sib = scratch[0:5], scratch[5:8], scratch[8:11]
    load_sem, send_sem, recv_sem = scratch[11:]
    all_x, all_g, hidden, d_gate, d_up = bufs
    hi, y, z, lo, c = place()
    copies = loads(ins, bufs, load_sem) if phase < 1 else []

    def swap(k):
        n = products[k].shape[0] // 2
        return pltpu.make_async_remote_copy(
            src_ref=products[k].at[pl.ds(mul((1 - c) * n, 16), n)],
            dst_ref=from_sib[k],
            send_sem=send_sem.at[k],
            recv_sem=recv_sem.at[k],
            device_id=device(hi, y, z, lo, 1 - c),
            device_id_type=MESH,
        )

    def add(k):
        swap(k).wait_recv()
        n = products[k].shape[0] // 2

        @pl.loop(0, n // 64)
        def _(i):
            r = pl.ds(mul(i * 64, 64), 64)
            own = products[k][pl.ds(mul(c * n + i * 64, 64), 64), :]
            outs[k][r, :] = (own.astype(F32) + from_sib[k][r, :].astype(F32)).astype(BF16)

    if phase == -1:
        for copy in copies:
            copy.start()
    elif phase < 2:
        if phase == 0:
            for copy in copies:
                copy.wait()
        grad, out = (d_gate, products[0]) if phase == 0 else (d_up, products[1])

        @pl.loop(0, out.shape[0] // 256)
        def _(i):
            r = pl.ds(mul(i * 256, 256), 256)
            out[r, :] = t_dot(all_x[:, r], grad[...]).astype(BF16)

        swap(phase).start()
    elif phase == 2:

        @pl.loop(0, products[2].shape[0] // 128)
        def _(i):
            r = pl.ds(mul(i * 128, 128), 128)
            products[2][r, :] = t_dot(hidden[:, r], all_g[...]).astype(BF16)

        swap(2).start()
        add(0)
        add(1)
    else:
        add(2)
        for k in range(3):
            swap(k).wait_send()


def split_terms(w):
    top = w.astype(BF16)
    rest = w - top.astype(F32)
    mid = rest.astype(BF16)
    return top, mid, (rest - mid.astype(F32)).astype(BF16)


def combine_kernel(
    back_r, back_l, slot_t, gates_t, grad, hidden_one, out_s, grad_in_s, mixed, act, grad_gu, router_w, out_w, gains,
    layer_out, grad_hidden, grad_mixed, left, right, grad_gain,
):
    experts = back_r.shape[0]
    rows, width = hidden_one.shape
    slots = slot_t[0:experts, :]
    places = even_places(slots)
    last = slots == float(EVEN)
    out_rows = back_r[:, :, :width].reshape(experts * EVEN, width)
    last_l = back_l[...].reshape(experts, 2 * width).astype(BF16)
    gt = gates_t[0:experts, :]
    even_w = jnp.where(places, jnp.broadcast_to(gt[:, None, :], places.shape), 0.0).reshape(experts * EVEN, rows)
    last_w = jnp.where(last, gt, 0.0)
    routed = jnp.zeros((rows, width), F32)
    for e_term, l_term in zip(split_terms(even_w), split_terms(last_w)):
        routed = routed + t_dot(e_term, out_rows) + t_dot(l_term, last_l[:, :width])
    hidden = hidden_one[...]
    layer_out[...] = (hidden + out_s[...] + routed).astype(BF16)
    g = grad[...]
    dots = dot_t(out_rows, g).reshape(experts, EVEN, rows)
    dots_last = dot_t(last_l[:, :width], g)
    grad_gates = jnp.sum(jnp.where(places, dots, 0.0), axis=1) + jnp.where(last, dots_last, 0.0)
    logits_t = gt * (grad_gates - jnp.sum(gt * grad_gates, axis=0, keepdims=True))
    low_logits = jnp.concatenate([logits_t, jnp.zeros((128 - experts, rows), F32)], axis=0).T.astype(BF16)
    hot = places.astype(F32).reshape(experts * EVEN, rows).astype(BF16)
    grad_routed = t_dot(hot, back_r[:, :, width:].reshape(experts * EVEN, width)) + t_dot(last.astype(BF16), last_l[:, width:])
    router = router_w[...]
    grad_act = grad_routed + dot_t(low_logits, router) + grad_in_s[...]
    gain = gain_rows(gains[...])[1:2]
    _normed, inv = rms_forward(hidden, gain)
    grad_norm, gain_sum = rms_backward(hidden, inv, gain, grad_act)
    grad_gain[...] = gain_sum
    total = g.astype(F32) + grad_norm
    grad_hidden[...] = total
    low = total.astype(BF16)
    left[0:rows, :] = mixed[...]
    left[rows:, :] = act[...]
    right[0:rows, :width] = low
    right[0:rows, width:] = jnp.zeros((rows, R_WIDE - width), BF16)
    right[rows:, :width] = jnp.zeros((rows, width), BF16)
    right[rows:, width : ROUTER * 128] = grad_gu[...]
    right[rows:, ROUTER * 128 : (ROUTER + 1) * 128] = low_logits
    right[rows:, (ROUTER + 1) * 128 :] = jnp.zeros((rows, R_WIDE - (ROUTER + 1) * 128), BF16)
    grad_mixed[...] = dot_t(low, out_w[...]).astype(BF16)


def combine(operands, w_r, w_q):
    rows, width = operands[5].shape
    whole = lambda a: pl.BlockSpec(a.shape, lambda i: (0,) * len(a.shape))
    outs = (
        shape(BF16, rows, width),
        shape(F32, rows, width),
        shape(BF16, rows, width),
        shape(BF16, 2 * rows, width),
        shape(BF16, 2 * rows, R_WIDE),
        shape(F32, 1, width),
    )
    return pl.pallas_call(
        combine_kernel,
        grid=(1,),
        out_shape=outs,
        in_specs=[whole(a) for a in operands]
        + [
            pl.BlockSpec((width, 128), lambda i: (0, ROUTER)),
            pl.BlockSpec((width, 1280), lambda i: (0, 0)),
            pl.BlockSpec((width, 128), lambda i: (0, GAINS)),
        ],
        out_specs=tuple(whole(a) for a in outs),
        compiler_params=pltpu.CompilerParams(vmem_limit_bytes=56 << 20),
        name="combine",
    )(*operands, w_r, w_r, w_q)


def per_device(
    tokens,
    cotangent,
    segments,
    routes,
    norm_gain_attn,
    w_query,
    w_key,
    w_value,
    w_out,
    norm_gain_ffn,
    w_router,
    shared_gate,
    shared_up,
    shared_down,
    expert_gate,
    expert_up,
    expert_down,
):
    rows = tokens.shape[1]
    width = tokens.shape[2]
    experts = w_router.shape[1]
    tokens, grad, routes = tokens[0], cotangent[0], routes[0]
    seg_row = segments
    seg_col = segments.reshape(-1, 1)
    own_experts = (expert_gate[0], expert_up[0], expert_down[0])

    def spread(w):
        w = w.reshape(w.shape[0], experts, w.shape[1] // experts)
        return jnp.pad(w, ((0, 0), (0, 0), (0, 2))).reshape(w.shape[0], experts * 16)

    own_rows = w_query.shape[0]
    zeros = lambda n: jnp.zeros((own_rows, n), BF16)
    shard_q = jnp.concatenate(
        [w_query, w_key, w_value, norm_gain_attn[:, None], norm_gain_ffn[:, None], zeros(254)], axis=1
    )
    shard_r = jnp.concatenate([w_out, spread(shared_gate), spread(shared_up), w_router, zeros(256 - experts)], axis=1)
    cos, sin = rotary_tables(2 * rows)
    w_q, w_r, w_d, expert_w, act_attn, q, kv, prior, mixed = forward(
        shard_q, shard_r, shared_down, own_experts, tokens, cos, sin, seg_row, seg_col
    )
    hidden_one, act_ffn, gates_t, slot_t = route(tokens, mixed, routes, w_r, w_q)
    rows_r, rows_l = dispatch(act_ffn, grad, gates_t, slot_t, experts)
    rows_r, rows_l, out_s, grad_in_s, grad_gu, grad_sdown = exchange(
        3,
        True,
        (rows_r, rows_l),
        (ROW_CUTS, LAST_OUT_CUTS),
        shared_work,
        (w_r, w_d, act_ffn, grad),
        (shape(F32, rows, width), shape(F32, rows, width), shape(BF16, rows, 2048), shape(BF16, 1024, width)),
        (
            pltpu.VMEM((width, 2048), BF16),
            pltpu.VMEM((1024, width), BF16),
            pltpu.VMEM((rows, width), BF16),
            pltpu.VMEM((rows, width), BF16),
            pltpu.VMEM((rows, 1024), BF16),
            pltpu.SemaphoreType.DMA((4,)),
        ),
    )
    out_r, out_l, *kept = expert(rows_r, rows_l, expert_w, own_experts)
    back_r, back_l, *parts = exchange(
        4,
        False,
        (out_r, out_l),
        (ROW_CUTS, LAST_BACK_CUTS),
        expert_work,
        tuple(kept),
        tuple(shape(BF16, w.shape[0] // 2, w.shape[1]) for w in own_experts),
        [pltpu.VMEM(a.shape, BF16) for a in kept]
        + [pltpu.VMEM(w.shape, BF16) for w in own_experts]
        + [pltpu.VMEM((w.shape[0] // 2, w.shape[1]), BF16) for w in own_experts]
        + [pltpu.SemaphoreType.DMA((n,)) for n in (5, 3, 3)],
    )
    layer_out, grad_hidden, grad_mixed, left_r, right_r, gain_ffn = combine(
        (back_r, back_l, slot_t, gates_t, grad, hidden_one, out_s, grad_in_s, mixed, act_ffn, grad_gu), w_r, w_q
    )
    fin_q, fin_r, fin_d, *sums, grad_tokens = backward(
        (left_r, right_r, grad_sdown.reshape(4, 4, 64, width), act_attn, q, kv, prior, seg_row, seg_col)
        + (grad_mixed, cos, sin, tokens, grad_hidden, gain_ffn, w_q),
        parts,
    )
    offset = 4 * lax.rem(lax.axis_index("exp"), 4)
    own_q = lax.dynamic_slice(fin_q, (offset, 0), (own_rows, Q_WIDE))
    own_r = lax.dynamic_slice(fin_r, (offset, 0), (own_rows, R_WIDE))

    def gathered_hidden(w):
        return w.reshape(w.shape[0], experts, 16)[:, :, :14].reshape(w.shape[0], experts * 14)

    core = lax.rem(lax.axis_index("exp"), 2)
    kept_here = (core == lax.axis_index("seq")) & (jnp.arange(2) == core)
    expert_grads = [
        jnp.where(kept_here[:, None, None], own[None], total.reshape((2,) + own.shape)).astype(F32).reshape(1, *total.shape)
        for own, total in zip(parts, sums)
    ]
    router = ROUTER * 128
    return (
        layer_out[None],
        grad_tokens[None],
        own_q[:, GAINS * 128],
        own_q[:, :1280],
        own_q[:, 1280:2560],
        own_q[:, 2560:3840],
        own_r[:, :1280],
        own_q[:, GAINS * 128 + 1],
        own_r[:, router : router + experts],
        gathered_hidden(own_r[:, 1280:2304]),
        gathered_hidden(own_r[:, 2304:3328]),
        fin_d[:14],
        *expert_grads,
    )


def solution(mesh):
    rows = P("exp", None)
    deep = P("exp", None, None)
    split = P("exp", "seq", None)
    gain = P("exp")
    in_specs = (split, split, rows, split, gain, rows, rows, rows, rows, gain) + (rows,) * 4 + (deep,) * 3
    out_specs = (split, split, gain, rows, rows, rows, rows, gain) + (rows,) * 4 + (deep,) * 3
    return jax.shard_map(per_device, mesh=mesh, in_specs=in_specs, out_specs=out_specs, check_vma=False)
```

```python
import functools
import jax
import jax.numpy as jnp
import numpy as np
from jax import lax
from jax.experimental import pallas as pl
from jax.experimental.pallas import tpu as pltpu
from jax.sharding import PartitionSpec as P

HEADS = 10
EPSILON = 1e-06
NEG_BIG = -1e30
F32 = jnp.float32
BF16 = jnp.bfloat16
MESH = pl.DeviceIdType.MESH

PIECES = {
    "q": (80, 16, ((0, 8, 4), (8, 8, 4))),
    "r": (80, 14, ((0, 7, 4), (7, 7, 4))),
    "d": (64, 5, ((0, 3, 2), (3, 2, 1))),
}
Q_WIDE, R_WIDE, D_WIDE = 4096, 3584, 1280
GAINS = 30
ROUTER = 26
UNITS = (0, 1)


def place():
    hi = lax.axis_index("seq")
    e = lax.axis_index("exp")
    return hi, e // 16, lax.rem(e // 4, 4), lax.rem(e // 2, 2), lax.rem(e, 2)


def device(hi, y, z, lo, c):
    return (hi, ((y * 4 + z) * 2 + lo) * 2 + c)


def up(v):
    return lax.rem(v + 1, 4)


def dn(v):
    return lax.rem(v + 3, 4)


def opp(v):
    return lax.rem(v + 2, 4)


def mul(v, m=128):
    return pl.multiple_of(v, m)


def greet(devices):
    bar = pltpu.get_barrier_semaphore()
    for to in devices:
        pl.semaphore_signal(bar, inc=1, device_id=to, device_id_type=MESH)
    pl.semaphore_wait(bar, len(devices))


class Sender:
    def __init__(self, send_sem, recv_sem, local_sem):
        self.sems = (send_sem, recv_sem, local_sem)
        self.sent = []
        self.kept = 0

    def describe(self, src, dst, to):
        k = len(self.sent)
        self.sent.append(None)
        return pltpu.make_async_remote_copy(
            src_ref=src,
            dst_ref=dst,
            send_sem=self.sems[0].at[k],
            recv_sem=self.sems[1].at[k],
            device_id=to,
            device_id_type=MESH,
        )

    def remote(self, src, dst, to):
        copy = self.describe(src, dst, to)
        copy.start()
        self.sent[-1] = copy
        return copy

    def local(self, src, dst):
        copy = pltpu.make_async_copy(src, dst, self.sems[2].at[self.kept])
        self.kept += 1
        copy.start()
        return copy

    def settle(self, copy):
        copy.wait_send()
        self.sent = [None if one is copy else one for one in self.sent]

    def finish(self):
        for copy in self.sent:
            if copy is not None:
                copy.wait_send()


def arrived(copies):
    for copy in copies:
        copy.wait_recv()


def ring_neighbours(hi, y, z, lo, c):
    return {
        ("y", 1): device(hi, up(y), z, lo, c),
        ("y", -1): device(hi, dn(y), z, lo, c),
        ("z", 1): device(hi, y, up(z), lo, c),
        ("z", -1): device(hi, y, dn(z), lo, c),
        ("y", 2): device(hi, opp(y), z, lo, c),
        ("z", 2): device(hi, y, opp(z), lo, c),
    }


def unit_tiles(piece, u, half):
    s, w, w0 = PIECES[piece][2][u]
    return ((s, w0), (s + w0, w - w0))[half] if half is not None else (s, w)


def lanes(piece, u, half, core):
    s, w = unit_tiles(piece, u, half)
    return pl.ds(mul(core * (PIECES[piece][1] * 128) + s * 128), w * 128)


def core_lanes(piece, core):
    n = PIECES[piece][1] * 128
    return pl.ds(mul(core * n), n)


def interleave(steps, work):
    for step in steps:
        step()
        next(work, None)
    for _ in work:
        pass


def dot(a, b):
    return jnp.dot(a, b, preferred_element_type=F32)


def dot_t(a, b):
    return lax.dot_general(a, b, (((1,), (1,)), ((), ())), preferred_element_type=F32)


def t_dot(a, b):
    return lax.dot_general(a, b, (((0,), (0,)), ((), ())), preferred_element_type=F32)


def iota(shape, dim):
    return lax.broadcasted_iota(jnp.int32, shape, dim)


def shape(dtype, *dims):
    return jax.ShapeDtypeStruct(dims, dtype)


def gain_rows(tile):
    pick = (iota((8, 128), 1) == iota((8, 128), 0)).astype(BF16)
    return dot_t(pick, tile)


def rms_forward(values, gain):
    inv_rms = lax.rsqrt(jnp.mean(values * values, axis=-1, keepdims=True) + EPSILON)
    return values * inv_rms * gain, inv_rms


def rms_backward(values, inv_rms, gain, upstream):
    weighted = upstream * gain
    inner = jnp.mean(weighted * values, axis=-1, keepdims=True)
    grad_in = inv_rms * weighted - values * (inv_rms * inv_rms * inv_rms) * inner
    grad_gain = jnp.sum(upstream * values * inv_rms, axis=0, keepdims=True)
    return grad_in, grad_gain


def rotary_tables(rows):
    freq = np.power(10000.0, -2.0 * np.arange(64) / 128)
    angles = np.arange(rows)[:, None] * freq[None, :]
    cos, sin = np.cos(angles), np.sin(angles)
    return (
        jnp.asarray(np.concatenate([cos, cos], axis=1), F32),
        jnp.asarray(np.concatenate([-sin, sin], axis=1), F32),
    )


def silu_parts(pre_act):
    sigma = jax.nn.sigmoid(pre_act)
    return (pre_act * sigma, sigma * (1.0 + pre_act * (1.0 - sigma)))


def seq_rows():
    return pl.ds(mul(lax.axis_index("seq") * 128), 128)


def allowed_keys(seg_row, seg_col):
    hi = lax.axis_index("seq")
    here = seq_rows()
    mine = seg_col[here, :]
    rows = mine.shape[0]
    own = (seg_row[:, here] == mine) & (iota((rows, rows), 1) <= iota((rows, rows), 0))
    prior = (seg_row[:, 0:rows] == mine) & (hi == 1)
    return own, prior


def head_probs(h, q, kv, prior, own_ok, prior_ok, width):
    here = slice(h * 128, (h + 1) * 128)
    behind = slice(width + h * 128, width + (h + 1) * 128)
    query = q[:, here]
    keys = jnp.concatenate([prior[:, here], kv[:, here]], axis=0)
    values = jnp.concatenate([prior[:, behind], kv[:, behind]], axis=0)
    scores = dot_t(query, keys) * (128.0**-0.5)
    rows = query.shape[0]
    scores = jnp.concatenate(
        [jnp.where(prior_ok, scores[:, :rows], NEG_BIG), jnp.where(own_ok, scores[:, rows:], NEG_BIG)], axis=1
    )
    expo = jnp.exp(scores - jnp.max(scores, axis=-1, keepdims=True))
    return query, keys, values, expo / jnp.sum(expo, axis=-1, keepdims=True)


class Gather:
    def __init__(self, wires, names, blocks, outs, spot):
        hi, y, z, lo, c = spot
        self.wires, self.names, self.outs, self.core = wires, names, outs, c
        self.sib = device(hi, y, z, lo, 1 - c)
        nb = ring_neighbours(hi, y, z, lo, c)
        self.keep = []
        units = []
        for u in UNITS:
            a1, a2 = ("y", "z") if u == 0 else ("z", "y")
            p1, p2 = (y, z) if u == 0 else (z, y)
            units.append(
                dict(p1=p1, p2=p2, up1=nb[a1, 1], dn1=nb[a1, -1], up2=nb[a2, 1], dn2=nb[a2, -1], got={}, second=[], sib=[])
            )
        self.units = units
        self.steps = [functools.partial(self.own_block, blocks, y, z)]
        for u in UNITS:
            self.steps.append(functools.partial(self.first_axis, u, "up1", 0))
        for u in UNITS:
            self.steps.append(functools.partial(self.first_axis, u, "dn1", 1))
        for u in UNITS:
            self.steps.append(functools.partial(self.first_far, u))
        turn = (lambda p: p, dn, up, opp)
        self.near, self.far = [], []
        for k in range(4):
            for u in UNITS:
                q1 = turn[k](units[u]["p1"])
                self.near.append(functools.partial(self.second_axis, u, k, q1))
                self.far.append(functools.partial(self.second_far, u, k, q1))

    def region(self, name, u, half, q1, q2):
        by, bz = (q1, q2) if u == 0 else (q2, q1)
        return self.outs[name].at[by, bz, :, lanes(name, u, half, self.core)]

    def send(self, u, half, q1, q2, to, src=None):
        copies = []
        for name in self.names:
            dst = self.region(name, u, half, q1, q2)
            copies.append(self.wires.remote(src[name] if src else dst, dst, to))
        return copies

    def spread(self, u, q1, src=None):
        unit = self.units[u]
        at = (q1, unit["p2"])
        unit["second"].append((self.send(u, None, *at, unit["up2"], src), self.send(u, None, *at, unit["dn2"], src)))
        unit["sib"].append(self.send(u, None, *at, self.sib, src))

    def own_block(self, blocks, y, z):
        for name in self.names:
            self.keep.append(self.wires.local(blocks[name], self.outs[name].at[y, z, :, core_lanes(name, self.core)]))
        for u, unit in enumerate(self.units):
            src = {}
            for name in self.names:
                s, w = unit_tiles(name, u, None)
                src[name] = blocks[name].at[:, pl.ds(s * 128, w * 128)]
            at = (unit["p1"], unit["p2"])
            unit["got"]["up1"] = self.send(u, None, *at, unit["up1"], src)
            unit["got"]["dn1"] = self.send(u, None, *at, unit["dn1"], src)
            self.spread(u, unit["p1"], src)

    def first_axis(self, u, way, half):
        unit = self.units[u]
        arrived(unit["got"][way])
        q1 = dn(unit["p1"]) if way == "up1" else up(unit["p1"])
        unit["got"]["far", half] = self.send(u, half, q1, unit["p2"], unit[way])
        self.spread(u, q1)

    def first_far(self, u):
        unit = self.units[u]
        arrived(unit["got"]["far", 0])
        arrived(unit["got"]["far", 1])
        self.spread(u, opp(unit["p1"]))

    def second_axis(self, u, k, q1):
        unit = self.units[u]
        for half, way, turn in ((0, "up2", dn), (1, "dn2", up)):
            arrived(unit["second"][k][half])
            at = (q1, turn(unit["p2"]))
            unit["got"][k, half] = self.send(u, half, *at, unit[way])
            unit["sib"].append(self.send(u, None, *at, self.sib))

    def second_far(self, u, k, q1):
        unit = self.units[u]
        arrived(unit["got"][k, 0])
        arrived(unit["got"][k, 1])
        unit["sib"].append(self.send(u, None, q1, opp(unit["p2"]), self.sib))

    def finish(self):
        for unit in self.units:
            for copies in unit["sib"]:
                arrived(copies)
        for copy in self.keep:
            copy.wait()


def window_block(first, second, shift):
    n = first.shape[0]
    return first[0:shift], first[shift:n] + second[0 : n - shift], second[n - shift : n]


def forward_kernel(
    win_q, win_r, win_d, e0, e1, e2, tok, cos, sin, seg_row, seg_col,
    out_q, out_r, out_d, o0, o1, o2, act, q, kv, prior, mixed,
    sib_q, sib_r, pair_q, pair_r, side_q, side_r, blk_q, blk_r, blk_d, w_buf, ssem, rsem, lsem, esem, wsem,
):
    spot = place()
    hi, y, z, lo, c = spot
    sib = device(hi, y, z, lo, 1 - c)
    xn = device(hi, y, z, 1 - lo, c)
    hn = device(1 - hi, y, z, lo, c)
    greet([sib, xn, hn] + list(ring_neighbours(*spot).values()))
    wires = Sender(ssem, rsem, lsem)
    width = tok.shape[1]
    owner = c == hi

    @pl.when(hi == 0)
    def _():
        prior[...] = jnp.zeros_like(prior)

    j = lo * 2 + c
    windows = {"q": (win_q, sib_q, pair_q, side_q, blk_q), "r": (win_r, sib_r, pair_r, side_r, blk_r)}
    swaps = {}
    for name in "qr":
        win, from_sib = windows[name][:2]
        swaps[name] = wires.remote(win.at[:, core_lanes(name, 1 - c)], from_sib, sib)
    r16 = pl.ds(mul(j * 16, 16), 16)
    swap_d = wires.remote(win_d.at[:, core_lanes("d", 1 - c)], blk_d.at[r16], sib)
    blk_d[r16, :] = win_d[:, core_lanes("d", c)]
    across = {}
    for name in "qr":
        win, from_sib, pair, side, _blk = windows[name]
        own = win[:, core_lanes(name, c)]
        swaps[name].wait_recv()
        got = from_sib[...]
        pair[0:16], pair[16:32], pair[32:48] = window_block(
            jnp.where(c == 0, own, got), jnp.where(c == 0, got, own), 16
        )
        across[name] = wires.remote(pair, side, xn)
    swap_d.wait_recv()
    r32 = pl.ds(mul(lo * 32, 16), 32)
    across_d = wires.remote(blk_d.at[r32], blk_d.at[r32], xn)

    def pass_expert(k):
        return pltpu.make_async_remote_copy(
            src_ref=(e0, e1, e2)[k],
            dst_ref=(o0, o1, o2)[k],
            send_sem=esem.at[0, k],
            recv_sem=esem.at[1, k],
            device_id=sib,
            device_id_type=MESH,
        )

    blocks = {"q": blk_q, "r": blk_r, "d": blk_d}
    outs = {"q": out_q, "r": out_r, "d": out_d}
    group_q = Gather(wires, "q", blocks, outs, spot)
    group_r = Gather(wires, "rd", blocks, outs, spot)

    def whole_block(name):
        _win, _sib, pair, side, blk = windows[name]
        across[name].wait_recv()
        own, got = pair[...], side[...]
        blk[0:32], blk[32:48], blk[48:80] = window_block(
            jnp.where(lo == 0, own, got), jnp.where(lo == 0, got, own), 32
        )

    whole_block("q")
    for step in group_q.steps:
        step()
    whole_block("r")
    across_d.wait_recv()
    for step in group_q.near:
        step()
    group_r.steps[0]()
    for step in group_q.far:
        step()
    group_q.finish()

    @pl.when(owner)
    def _():
        for k in range(3):
            pass_expert(k).start()

    def load(i, slot):
        return pltpu.make_async_copy(out_q.at[:, :, :, pl.ds(i * 512, 512)], w_buf.at[slot], wsem.at[slot])

    later = wires.describe(kv, prior, hn)

    def work():
        order = (7, 2, 3, 4, 5, 6, 0, 1)
        here = seq_rows()
        cosine, sine = cos[here, :], sin[here, :]
        load(order[0], 0).start()
        for n, i in enumerate(order):
            slot = n % 2
            load(i, slot).wait()
            if n + 1 < len(order):
                load(order[n + 1], 1 - slot).start()
            w = w_buf[slot].reshape(width, 512)
            if n == 0:
                gains = gain_rows(w[:, (GAINS - 28) * 128 : (GAINS - 27) * 128])
                normed, _inv = rms_forward(tok[...].astype(F32), gains[0:1])
                act[...] = normed.astype(BF16)
                w = w[:, :256]
            x = dot(act[...], w)
            for t in range(w.shape[1] // 128):
                tile = 4 * i + t
                v = x[:, t * 128 : (t + 1) * 128]
                if tile < 20:
                    v = v * cosine + pltpu.roll(v, 64, 1) * sine
                if tile < 10:
                    q[:, tile * 128 : (tile + 1) * 128] = v.astype(BF16)
                else:
                    kv[:, (tile - 10) * 128 : (tile - 9) * 128] = v.astype(BF16)
            if i == 6:

                @pl.when(hi == 0)
                def _():
                    later.start()

            yield
        for _ in range(4):
            yield

        @pl.when(hi == 1)
        def _():
            later.wait_recv()

        own_ok, prior_ok = allowed_keys(seg_row, seg_col)
        for h in range(HEADS):
            _query, _keys, values, probs = head_probs(h, q, kv, prior, own_ok, prior_ok, width)
            mixed[:, h * 128 : (h + 1) * 128] = dot(probs.astype(BF16), values).astype(BF16)
            yield

    interleave(group_r.steps[1:] + group_r.near + group_r.far + [group_r.finish], work())

    @pl.when(hi == 0)
    def _():
        later.wait_send()

    @pl.when(owner)
    def _():
        for k in range(3):
            pass_expert(k).wait_send()

    @pl.when(jnp.logical_not(owner))
    def _():
        for k in range(3):
            pass_expert(k).wait_recv()

    wires.finish()


def forward(shard_q, shard_r, down, experts, tokens, cos, sin, seg_row, seg_col):
    rows, width = tokens.shape
    offset = 4 * lax.rem(lax.axis_index("exp"), 4)
    window = lambda s: lax.dynamic_update_slice(jnp.zeros((32, s.shape[1]), BF16), s, (offset, 0))
    down = jnp.pad(down, ((0, 2), (0, 0)))
    sems = 2 + 1 + 3 + 36 * 2 * 3 + 8
    vmem, anywhere = pl.BlockSpec(memory_space=pltpu.VMEM), pl.BlockSpec(memory_space=pl.ANY)
    half = {name: PIECES[name][1] * 128 for name in PIECES}
    out = pl.pallas_call(
        forward_kernel,
        out_shape=(
            shape(BF16, 4, 4, 80, Q_WIDE),
            shape(BF16, 4, 4, 80, R_WIDE),
            shape(BF16, 4, 4, 64, D_WIDE),
            *(shape(BF16, *w.shape) for w in experts),
            shape(BF16, rows, width),
            shape(BF16, rows, width),
            shape(BF16, rows, 2 * width),
            shape(BF16, rows, 2 * width),
            shape(BF16, rows, width),
        ),
        in_specs=[vmem] * 3 + [anywhere] * 3 + [vmem] * 5,
        out_specs=(anywhere,) * 6 + (vmem,) * 5,
        scratch_shapes=[pltpu.VMEM((n, half[name]), BF16) for n in (32, 48, 48, 80) for name in "qr"]
        + [
            pltpu.VMEM((64, half["d"]), BF16),
            pltpu.VMEM((2, 4, 4, 80, 512), BF16),
            pltpu.SemaphoreType.DMA((sems,)),
            pltpu.SemaphoreType.DMA((sems,)),
            pltpu.SemaphoreType.DMA((3,)),
            pltpu.SemaphoreType.DMA((2, 3)),
            pltpu.SemaphoreType.DMA((2,)),
        ],
        compiler_params=pltpu.CompilerParams(collective_id=1, has_side_effects=True, vmem_limit_bytes=56 << 20),
        name="gather_attend",
    )(window(shard_q), window(shard_r), down, *experts, tokens, cos, sin, seg_row, seg_col)
    w_q, w_r, w_d = (out[k].reshape(16 * out[k].shape[2], out[k].shape[3]) for k in range(3))
    return (w_q, w_r, w_d, out[3:6]) + tuple(out[6:])


class RingSum:
    def __init__(self, wires, names, hold, from_sib, bufs, to_sib, spot):
        hi, y, z, lo, c = spot
        self.wires, self.names, self.hold, self.from_sib, self.bufs, self.to_sib = (
            wires, names, hold, from_sib, bufs, to_sib,
        )
        self.sib = device(hi, y, z, lo, 1 - c)
        self.nb = ring_neighbours(hi, y, z, lo, c)
        self.first_axis, self.second_axis = ("y", "z"), ("z", "y")
        self.ring, self.coming = {}, {}
        orders = []
        for u in UNITS:
            p1, p2 = (y, z) if u == 0 else (z, y)
            ones = (opp(p1), up(p1), dn(p1), p1)
            orders.append([(q1, q2) if u == 0 else (q2, q1) for q2 in (opp(p2), up(p2), dn(p2), p2) for q1 in ones])
        self.orders = orders
        self.steps = []
        for i in range(4):
            for u in UNITS:
                self.steps.append(functools.partial(self.far_step, u, i))
        for i in range(4):
            for u in UNITS:
                self.steps.append(functools.partial(self.near_step, u, i, 1))
            for u in UNITS:
                self.steps.append(functools.partial(self.near_step, u, i, -1))
        for i in range(4):
            for u in UNITS:
                self.steps.append(functools.partial(self.own_step, u, i))
        for u in UNITS:
            self.steps.append(functools.partial(self.last_step, u))

    def blocks(self, refs, u, index):
        return {name: refs[name][u].at[index] for name in self.names}

    def start(self):
        for k in range(16):
            for u in UNITS:
                at = self.orders[u][k]
                src, dst = self.blocks(self.to_sib, u, at), self.blocks(self.from_sib, u, at)
                self.coming[u, k] = self.pair(src, dst, self.sib)

    def pair(self, src, dst, to):
        return [self.wires.remote(src[name], dst[name], to) for name in self.names]

    def add_in(self, dst, *more):
        @pl.loop(0, dst.shape[-2] // 16)
        def _(i):
            r = pl.ds(mul(i * 16, 16), 16)
            value = dst[r, :].astype(F32)
            for ref in more:
                value = value + ref[r, :].astype(F32)
            dst[r, :] = value.astype(BF16)

    def ready(self, u, k):
        arrived(self.coming[u, k])
        at = self.orders[u][k]
        blk, more = self.blocks(self.hold, u, at), self.blocks(self.from_sib, u, at)
        for name in self.names:
            self.add_in(blk[name], more[name])
        return blk

    def half(self, blk, u, h):
        cut = {}
        for name in self.names:
            s, w, w0 = PIECES[name][2][u]
            cut[name] = blk[name].at[:, pl.ds(0, w0 * 128) if h == 0 else pl.ds(w0 * 128, (w - w0) * 128)]
        return cut

    def buffer(self, u, i, slot):
        return {name: self.bufs[name][u][i].at[slot] for name in self.names}

    def far_block(self, u, slot, blk, axis):
        self.ring[u, slot, 0] = self.pair(self.half(blk, u, 0), self.buffer(u, 0, slot), self.nb[axis, 1])
        self.ring[u, slot, 1] = self.pair(self.half(blk, u, 1), self.buffer(u, 1, slot), self.nb[axis, -1])

    def near_block(self, u, slot, blk, axis, way):
        h = 0 if way == 1 else 1
        arrived(self.ring[u, slot, h])
        dst, more = self.half(blk, u, h), self.buffer(u, h, slot)
        for name in self.names:
            self.add_in(dst[name], more[name])
        self.ring[u, slot, 2 + h] = self.pair(blk, self.buffer(u, 2 + h, slot), self.nb[axis, way])

    def own_block(self, u, slot, blk):
        arrived(self.ring[u, slot, 2])
        arrived(self.ring[u, slot, 3])
        one, two = self.buffer(u, 2, slot), self.buffer(u, 3, slot)
        for name in self.names:
            self.add_in(blk[name], one[name], two[name])

    def far_step(self, u, i):
        self.far_block(u, i, self.ready(u, i), self.second_axis[u])

    def near_step(self, u, i, way):
        self.near_block(u, i, self.ready(u, (4 if way == 1 else 8) + i), self.second_axis[u], way)

    def own_step(self, u, i):
        blk = self.ready(u, 12 + i)
        self.own_block(u, i, blk)
        axis = self.first_axis[u]
        if i == 0:
            for h in (0, 1):
                self.ring[u, 4, h] = self.pair(self.half(blk, u, h), self.buffer(u, h, 4), self.nb[axis, 2])
        elif i < 3:
            self.ring[u, 4, 1 + i] = self.pair(blk, self.buffer(u, 1 + i, 4), self.nb[axis, 1 if i == 1 else -1])

    def last_step(self, u):
        blk = self.blocks(self.hold, u, self.orders[u][15])
        self.own_block(u, 4, blk)
        for h in (0, 1):
            arrived(self.ring[u, 4, h])
            dst, more = self.half(blk, u, h), self.buffer(u, h, 4)
            for name in self.names:
                self.add_in(dst[name], more[name])


def sum_scratch():
    scratch = []
    for rows, _tiles, units in PIECES.values():
        for s, w, w0 in units:
            scratch += [pltpu.VMEM((4, 4, rows, w * 128), BF16)] * 2
            scratch += [pltpu.VMEM((5, rows, t * 128), BF16) for t in (w0, w - w0, w, w)]
    return scratch


def backward_kernel(
    left_r, right_r, sdown, act, q, kv, prior, seg_row, seg_col, grad_mixed, cos, sin, tok, grad_hidden, gain_f, w_q,
    p0, p1, p2,
    fin_q, fin_r, fin_d, t0, t1, t2, grad_tokens,
    *scratch,
):
    names = list(PIECES)
    hold, from_sib, bufs = {}, {}, {}
    scratch = list(scratch)
    for name in names:
        hold[name], from_sib[name], bufs[name] = [], [], []
        for u in UNITS:
            hold[name].append(scratch.pop(0))
            from_sib[name].append(scratch.pop(0))
            bufs[name].append([scratch.pop(0) for _ in range(4)])
    sums, sides, mids, fars = ({name: scratch.pop(0) for name in names} for _ in range(4))
    accs = {name: scratch.pop(0) for name in names}
    sent = [scratch.pop(0) for _ in UNITS]
    grad_own, grad_prior, later, left_q, right_q, total, w_buf, gain_tile = scratch[:8]
    ssem, rsem, lsem, esend, erecv, wsem, piece_sem = scratch[8:]
    spot = place()
    hi, y, z, lo, c = spot
    sib = device(hi, y, z, lo, 1 - c)
    xn = device(hi, y, z, 1 - lo, c)
    hn = device(1 - hi, y, z, lo, c)
    greet([sib, xn, hn, device(1 - hi, y, z, lo, 1 - c)] + list(ring_neighbours(*spot).values()))
    wires = Sender(ssem, rsem, lsem)
    rows, width = tok.shape

    owner = c == hi
    parts, totals = (p0, p1, p2), (t0, t1, t2)
    across = device(1 - hi, y, z, lo, hi)

    def rows_of(ref, core):
        n = ref.shape[0] // 2
        return ref.at[pl.ds(mul(core * n, 16), n)]

    def expert_copy(src, dst, k, tag, to):
        return pltpu.make_async_remote_copy(
            src_ref=src, dst_ref=dst, send_sem=esend.at[k], recv_sem=erecv.at[tag], device_id=to, device_id_type=MESH
        )

    def across_piece(k, i):
        n = parts[k].shape[0]
        return pltpu.make_async_remote_copy(
            src_ref=parts[k].at[pl.ds(i * 64, 64)],
            dst_ref=totals[k].at[pl.ds(mul(c * n + i * 64, 16), 64)],
            send_sem=piece_sem.at[0, k, i],
            recv_sem=piece_sem.at[1, k, 10 * c + i],
            device_id=across,
            device_id_type=MESH,
        )

    def coming_piece(k, i, core):
        n = parts[k].shape[0]
        rows_ = totals[k].at[pl.ds(mul(core * n + i * 64, 16), 64)]
        return pltpu.make_async_remote_copy(
            src_ref=rows_,
            dst_ref=rows_,
            send_sem=piece_sem.at[0, k, i],
            recv_sem=piece_sem.at[1, k, 10 * core + i],
            device_id=across,
            device_id_type=MESH,
        )

    pieces = [(k, i) for k in range(3) for i in range(parts[k].shape[0] // 64)]

    def send_near(k):
        return expert_copy(parts[k], rows_of(totals[k], c), k, k, sib)

    def near_half(k):
        return expert_copy(rows_of(totals[k], 1 - c), rows_of(totals[k], 1 - c), k, k, sib)

    def expert_steps():
        for n, (k, i) in enumerate(pieces):
            across_piece(k, i).start()
            if n == len(pieces) // 2:

                @pl.when(jnp.logical_not(owner))
                def _():
                    for k in range(3):
                        send_near(k).start()

            yield

    own_d = []
    for u in UNITS:
        s, w = unit_tiles("d", u, None)
        own_d.append(wires.local(sdown.at[:, :, :, lanes("d", u, None, c)], hold["d"][u]))

    def products(left, right, name, core, refs):
        for u in UNITS:
            r = right[:, lanes(name, u, None, core)]
            for m in (0, 1):
                v = t_dot(left[:, m * 640 : (m + 1) * 640], r).astype(BF16)
                for b in range(8):
                    refs[u][2 * m + b // 4, b % 4] = v[b * 80 : (b + 1) * 80]

    def views(name, refs):
        return [ref.at[:, :, :, pl.ds(0, PIECES[name][2][u][1] * 128)] for u, ref in enumerate(refs)]

    to_sib_r = views("r", sent)
    products(left_r, right_r, "r", 1 - c, to_sib_r)
    to_sib_d = [sdown.at[:, :, :, lanes("d", u, None, 1 - c)] for u in UNITS]
    group_r = RingSum(wires, "rd", hold, from_sib, bufs, {"r": to_sib_r, "d": to_sib_d}, spot)
    group_r.start()
    products(left_r, right_r, "r", c, hold["r"])
    for copy in own_d:
        copy.wait()

    def load(i):
        return pltpu.make_async_copy(w_q.at[:, pl.ds(i * 512, 512)], w_buf.at[i % 2], wsem.at[i % 2])

    load_gains = pltpu.make_async_copy(w_q.at[:, pl.ds(GAINS * 128, 128)], gain_tile, wsem.at[2])
    exchange_kv = wires.describe(grad_prior, later, hn)
    to_sib_q = views("q", sent)
    group_q = RingSum(wires, "q", hold, from_sib, bufs, {"q": to_sib_q}, spot)

    def work():
        load(0).start()
        load_gains.start()
        here = seq_rows()
        cosine, sine = cos[here, :], sin[here, :]
        own_ok, prior_ok = allowed_keys(seg_row, seg_col)
        inv_root = 128.0**-0.5

        @pl.when(hi == 1)
        def _():
            later[...] = jnp.zeros_like(later)

        for h in range(HEADS):
            query, keys, values, probs = head_probs(h, q, kv, prior, own_ok, prior_ok, width)
            mine = slice(h * 128, (h + 1) * 128)
            behind = slice(width + h * 128, width + (h + 1) * 128)
            gm = grad_mixed[:, mine]
            grad_probs = dot_t(gm, values)
            inner = jnp.sum(probs * grad_probs, axis=-1, keepdims=True)
            grad_scores = (probs * (grad_probs - inner)).astype(BF16)
            grad_values = t_dot(probs.astype(BF16), gm)
            gq = dot(grad_scores, keys) * inv_root
            grad_keys = t_dot(grad_scores, query) * inv_root
            right_q[0:rows, mine] = (gq * cosine - pltpu.roll(gq, 64, 1) * sine).astype(BF16)
            grad_own[:, mine] = grad_keys[rows:]
            grad_own[:, behind] = grad_values[rows:]
            grad_prior[:, mine] = grad_keys[:rows].astype(BF16)
            grad_prior[:, behind] = grad_values[:rows].astype(BF16)
            yield

        @pl.when(hi == 1)
        def _():
            exchange_kv.start()

        right_q[0:rows, 3 * width :] = jnp.zeros((rows, Q_WIDE - 3 * width), BF16)
        right_q[rows:, :] = (iota((16, Q_WIDE), 1) == iota((16, Q_WIDE), 0) + GAINS * 128).astype(BF16)
        left_q[0:rows, :] = act[...]
        total[...] = jnp.zeros_like(total)

        def add_chunk(i):
            load(i).wait()
            if i < 7:
                load(i + 1).start()
            total[...] += dot_t(right_q[0:rows, i * 512 : (i + 1) * 512], w_buf[i % 2])

        for i in (0, 1):
            add_chunk(i)
            yield

        @pl.when(hi == 0)
        def _():
            exchange_kv.wait_recv()

        for h in range(HEADS):
            mine = slice(h * 128, (h + 1) * 128)
            gk = grad_own[:, mine] + later[:, mine].astype(F32)
            right_q[0:rows, width + h * 128 : width + (h + 1) * 128] = (
                gk * cosine - pltpu.roll(gk, 64, 1) * sine
            ).astype(BF16)
        right_q[0:rows, 2 * width : 3 * width] = (grad_own[:, width:] + later[:, width:].astype(F32)).astype(BF16)
        yield
        for i in range(2, 8):
            add_chunk(i)
            yield
        load_gains.wait()
        gain = gain_rows(gain_tile[...])[0:1]
        values = tok[...].astype(F32)
        _normed, inv = rms_forward(values, gain)
        grad_norm, gain_sum = rms_backward(values, inv, gain, total[...])
        grad_tokens[...] = grad_hidden[...] + grad_norm
        row = iota((16, width), 0)
        left_q[rows:, :] = jnp.where(row == 0, gain_sum, jnp.where(row == 1, gain_f[...], 0.0)).astype(BF16)
        yield
        for k in range(16):
            for u in UNITS:
                wires.settle(group_r.coming[u, k][0])
        products(left_q, right_q, "q", 1 - c, to_sib_q)
        group_q.start()
        yield
        products(left_q, right_q, "q", c, hold["q"])
        yield

    def window_sums(group):
        copies = {}
        for name in group:
            n = PIECES[name][0]
            for u in UNITS:
                s, w = unit_tiles(name, u, None)
                sums[name][:, s * 128 : (s + w) * 128] = hold[name][u][y, z]
            window = 48 if n == 80 else 32
            copies[name] = wires.remote(sums[name].at[pl.ds(mul((1 - lo) * 32, 16), window)], sides[name], xn)
        yield
        for name in group:
            copies[name].wait_recv()
            window = sides[name].shape[0]
            r = pl.ds(mul(lo * 32, 16), window)
            mids[name][...] = (sums[name][r, :].astype(F32) + sides[name][...].astype(F32)).astype(BF16)
            copies[name] = wires.remote(mids[name], fars[name], hn)
        yield
        fins = {"q": fin_q, "r": fin_r, "d": fin_d}
        for name in group:
            copies[name].wait_recv()
            accs[name][...] = mids[name][...].astype(F32) + fars[name][...].astype(F32)
            n = fins[name].shape[0]
            mine = core_lanes(name, c)
            copies[name] = wires.remote(
                accs[name].at[pl.ds(mul((1 - c) * 16, 16), n)], fins[name].at[:, mine], sib
            )
            fins[name][:, mine] = accs[name][pl.ds(mul(c * 16, 16), n), :]
        yield
        for name in group:
            copies[name].wait_recv()

    experts = expert_steps()
    busy = work()
    for step in group_r.steps[:24]:
        step()
        next(busy, None)
        next(experts, None)
    for _ in busy:
        next(experts, None)
    rest = list(group_r.steps[24:])
    for step in group_q.steps[:24]:
        step()
        next(experts, None)
        if rest:
            rest.pop(0)()
    for _ in experts:
        pass
    interleave(group_q.steps[24:], window_sums("rd"))
    for _ in window_sums("q"):
        pass
    for k, i in pieces:
        across_piece(k, i).wait_send()

    @pl.when(owner)
    def _():
        for k in range(3):
            near_half(k).wait_recv()

    @pl.when(jnp.logical_not(owner))
    def _():
        for k in range(3):
            send_near(k).wait_send()
        for k, i in pieces:
            for core in (0, 1):
                coming_piece(k, i, core).wait_recv()

    @pl.when(hi == 1)
    def _():
        exchange_kv.wait_send()

    wires.finish()


def backward(operands, parts):
    rows, width = operands[12].shape
    vmem, anywhere = pl.BlockSpec(memory_space=pltpu.VMEM), pl.BlockSpec(memory_space=pl.ANY)
    half = {name: PIECES[name][1] * 128 for name in PIECES}
    window = {"q": 48, "r": 48, "d": 32}
    fin = {"q": (32, Q_WIDE), "r": (32, R_WIDE), "d": (16, D_WIDE)}
    scratch = sum_scratch()
    scratch += [pltpu.VMEM((PIECES[name][0], half[name]), BF16) for name in PIECES]
    scratch += [pltpu.VMEM((window[name], half[name]), BF16) for _ in range(3) for name in PIECES]
    scratch += [pltpu.VMEM((window[name], half[name]), F32) for name in PIECES]
    scratch += [pltpu.VMEM((4, 4, 80, 1024), BF16)] * 2
    scratch += [
        pltpu.VMEM((rows, 2 * width), F32),
        pltpu.VMEM((rows, 2 * width), BF16),
        pltpu.VMEM((rows, 2 * width), BF16),
        pltpu.VMEM((rows + 16, width), BF16),
        pltpu.VMEM((rows + 16, Q_WIDE), BF16),
        pltpu.VMEM((rows, width), F32),
        pltpu.VMEM((2, width, 512), BF16),
        pltpu.VMEM((width, 128), BF16),
    ]
    sems = 1 + 3 * (32 + 2 * 4 * 5 + 3)
    scratch += [pltpu.SemaphoreType.DMA((n,)) for n in (sems, sems, 2, 3, 3, 3)]
    scratch += [pltpu.SemaphoreType.DMA((2, 3, 20))]
    spec = [vmem] * len(operands)
    spec[2] = spec[15] = anywhere
    return pl.pallas_call(
        backward_kernel,
        out_shape=tuple(shape(F32, *fin[name]) for name in PIECES)
        + tuple(shape(BF16, 2 * p.shape[0], p.shape[1]) for p in parts)
        + (shape(F32, rows, width),),
        in_specs=spec + [anywhere] * 3,
        out_specs=(vmem,) * 3 + (anywhere,) * 3 + (vmem,),
        scratch_shapes=scratch,
        compiler_params=pltpu.CompilerParams(collective_id=2, has_side_effects=True, vmem_limit_bytes=60 << 20),
        name="attend_back_sums",
    )(*operands, *parts)


PART_AXES = (("y", "z", "g"), ("z", "g", "y"), ("g", "y", "z")) * 2
PARTS = len(PART_AXES)
TURNS = (2, 1, 3, 0)


def lane_cuts(*sizes):
    return tuple((sum(sizes[:i]), n) for i, n in enumerate(sizes))


ROW_CUTS = lane_cuts(4, 4, 3, 3, 3, 3)
LAST_OUT_CUTS = lane_cuts(3, 3, 3, 3, 4, 5)
LAST_BACK_CUTS = lane_cuts(3, 3, 3, 3, 4, 4)


class Exchange:
    def __init__(self, outward, cuts, stages, sems, spot):
        self.outward, self.cuts, self.stages, self.spot = outward, cuts, stages, spot
        self.ssem, self.rsem, self.lsem = sems
        hi, y, z, lo, c = spot
        self.stays = c == hi
        self.moves = jnp.logical_not(self.stays)
        self.pending, self.sent, self.used = {}, [], [0, 0]

    def along(self, axis, k):
        hi, y, z, lo, c = self.spot
        q = {"y": y, "z": z}
        q[axis] = lax.rem(q[axis] + k, 4)
        return q[axis], device(hi, q["y"], q["z"], lo, c)

    def target(self, d, b):
        hi, y, z, lo, c = self.spot
        lo_, hi_, c_ = (lo, 1 - lo)[d], (hi, 1 - hi)[b], (c, 1 - c)[b]
        if self.outward:
            return device(hi_, y, z, lo_, hi), lo_ * 2 + hi_, lo * 2 + c, 2 * d + c
        return device(c, y, z, lo_, c_), lo_ * 2 + c_, lo * 2 + hi, 2 * d + hi

    def source(self, d, b):
        hi, y, z, lo, c = self.spot
        lo_, hi_, c_ = (lo, 1 - lo)[d], (hi, 1 - hi)[b], (c, 1 - c)[b]
        if self.outward:
            return device(c, y, z, lo_, c_), lo_ * 2 + c_, 2 * d + c_
        return device(hi_, y, z, lo_, hi), lo_ * 2 + hi_, 2 * d + hi_

    corners = ((1, 1), (0, 1), (1, 0))

    def greet(self):
        hi, y, z, lo, c = self.spot
        bar = pltpu.get_barrier_semaphore()

        def greet_one(to):
            pl.semaphore_signal(bar, inc=1, device_id=to, device_id_type=MESH)

        for axis in "yz":
            for k in (1, 2, 3):
                greet_one(self.along(axis, k)[1])
        for corner in self.corners:
            greet_one(self.source(*corner)[0])

        @pl.when(self.moves)
        def _():
            greet_one(self.source(0, 0)[0])
            pl.semaphore_wait(bar, 10 if self.outward else 11)

        @pl.when(self.stays)
        def _():
            if not self.outward:
                greet_one(device(hi, y, z, lo, 1 - c))
            pl.semaphore_wait(bar, 9)

    def view(self, ref, axis, v, cut, at):
        every = slice(None)
        first = every if at is None else at
        index = {"y": (v, every, every), "z": (first, v, every), "g": (first, every, v)}[axis]
        return ref.at[index + (every, pl.ds(cut[0] * 128, cut[1] * 128))]

    def remote(self, src, dst, k, tag, to):
        return pltpu.make_async_remote_copy(
            src_ref=src,
            dst_ref=dst,
            send_sem=self.ssem.at[k],
            recv_sem=self.rsem.at[tag],
            device_id=to,
            device_id_type=MESH,
        )

    def go(self, part, phase, turn=None, at=None):
        axis = PART_AXES[part][phase]
        hi, y, z, lo, c = self.spot
        waits = self.pending.setdefault((part, phase), [])
        for a, cuts in enumerate(self.cuts):
            src, dst = self.stages[phase][a], self.stages[phase + 1][a]
            cut = cuts[part]
            base, kept = self.used
            self.used[0] += 4
            self.used[1] += 1
            if axis != "g":
                here = y if axis == "y" else z
                rows = at if axis == "z" else None
                own = self.view(dst, axis, here, cut, rows)
                for k in (turn,) if axis == "y" and turn is not None else TURNS:
                    v, to = self.along(axis, k)
                    if k == 0:
                        keep = pltpu.make_async_copy(self.view(src, axis, here, cut, rows), own, self.lsem.at[kept])
                        keep.start()
                        waits.append(keep.wait)
                        continue
                    copy = self.remote(self.view(src, axis, v, cut, rows), own, base + k, base + k, to)
                    copy.start()
                    waits.append(copy.wait_recv)
                    self.sent.append(copy.wait_send)
                continue
            for d, b in self.corners:
                to, there, here, tag = self.target(d, b)
                copy = self.remote(
                    self.view(src, axis, there, cut, at), self.view(dst, axis, here, cut, at), base + 2 * d + b, base + tag, to
                )
                copy.start()
                self.sent.append(copy.wait_send)
                sender, place_, tag = self.source(d, b)
                block = self.view(dst, axis, place_, cut, at)
                waits.append(self.remote(block, block, base + 2 * d + b, base + tag, sender).wait_recv)
            self.go_corner(src, dst, cut, at, base, kept, waits)

    def go_corner(self, src, dst, cut, at, base, kept, waits):
        to, there, here, tag = self.target(0, 0)
        mine, landing = self.view(src, "g", there, cut, at), self.view(dst, "g", here, cut, at)
        keep = pltpu.make_async_copy(mine, landing, self.lsem.at[kept])
        copy = self.remote(mine, landing, base, base + tag, to)
        sender, place_, tag = self.source(0, 0)
        block = self.view(dst, "g", place_, cut, at)
        coming = self.remote(block, block, base, base + tag, sender)

        @pl.when(self.stays)
        def _():
            keep.start()

        @pl.when(self.moves)
        def _():
            copy.start()

        def wait_corner():
            @pl.when(self.stays)
            def _():
                keep.wait()

            @pl.when(self.moves)
            def _():
                coming.wait_recv()

        def wait_sent():
            @pl.when(self.moves)
            def _():
                copy.wait_send()

        waits.append(wait_corner)
        self.sent.append(wait_sent)

    def first(self, turn, at):
        for part in range(PARTS):
            self.go(part, 0, turn, at)

    def next(self, phase):
        for part in range(PARTS):
            self.wait(part, phase - 1)
            self.go(part, phase)

    def wait(self, part, phase):
        for wait in self.pending[part, phase]:
            wait()

    def finish(self):
        for part in range(PARTS):
            self.wait(part, 2)
        for wait in self.sent:
            wait()


def exchange_sems(arrays):
    return [pltpu.SemaphoreType.DMA((n * arrays,)) for n in (160, 160, 40)]


EVEN = 16


def even_places(slot_t):
    experts, rows = slot_t.shape
    wide = jnp.broadcast_to(slot_t[:, None, :], (experts, EVEN, rows))
    return wide == iota((experts, EVEN, rows), 1).astype(F32)


def loads(ins, bufs, sem, start=0):
    return [pltpu.make_async_copy(src, dst, sem.at[start + k]) for k, (src, dst) in enumerate(zip(ins, bufs))]


def route_kernel(
    tok, mixed, routes, grad, w_q, w_r, w_d,
    out_r, out_l, hidden_one, act, gates_t, slot_t, out_s, grad_in, grad_gu, grad_down,
    src_r, src_l, b1_r, b1_l, b2_r, b2_l, out_w, router_w, gains, sgu, sdown, hidden_s, ssem, rsem, lsem, wsem,
):
    spot = place()
    y = spot[1]
    rows, width = tok.shape
    inner = sdown.shape[0]
    first_loads = loads(
        (w_r.at[:, pl.ds(0, width)], w_r.at[:, pl.ds(ROUTER * 128, 128)], w_q.at[:, pl.ds(GAINS * 128, 128)]),
        (out_w, router_w, gains),
        wsem,
    )
    later_loads = loads((w_r.at[:, pl.ds(width, 2 * inner)], w_d), (sgu, sdown), wsem, 3)
    for copy in first_loads + later_loads:
        copy.start()
    swap = Exchange(
        True, (ROW_CUTS, LAST_OUT_CUTS), ((src_r, src_l), (b1_r, b1_l), (b2_r, b2_l), (out_r, out_l)), (ssem, rsem, lsem), spot
    )
    swap.greet()
    for copy in first_loads:
        copy.wait()
    hidden = tok[...].astype(F32) + dot(mixed[...], out_w[...])
    hidden_one[...] = hidden
    router = router_w[...]
    normed, _inv = rms_forward(hidden, gain_rows(gains[...])[1:2])
    low = normed.astype(BF16)
    act[...] = low
    expert = iota((rows, 128), 1)
    named = routes[...]
    member = named[:, 0:1] == expert
    for k in range(1, named.shape[1]):
        member = member | (named[:, k : k + 1] == expert)
    logits = jnp.where(member, dot(low, router), NEG_BIG)
    expo = jnp.where(member, jnp.exp(logits - jnp.max(logits, axis=-1, keepdims=True)), 0.0)
    gates_t[...] = (expo / jnp.sum(expo, axis=-1, keepdims=True)).T
    before = (iota((rows, rows), 1) < iota((rows, rows), 0)).astype(BF16)
    rank = dot(before, member.astype(BF16))
    slot_t[...] = jnp.where(member, rank, -1.0).T

    block = 16
    g = grad[...]
    for turn in TURNS:
        v = lax.rem(y + turn, 4)
        here = pl.ds(mul(v * block, block), block)
        slots = slot_t[here, :]
        places = even_places(slots)
        last = slots == float(EVEN)
        hot = places.astype(F32).reshape(block * EVEN, rows).astype(BF16)
        last_hot = last.astype(BF16)
        src_r[v, :, :, :, 0:width] = dot(hot, low).astype(BF16).reshape(4, 4, EVEN, width)
        src_r[v, :, :, :, width:] = dot(hot, g).astype(BF16).reshape(4, 4, EVEN, width)
        gt = gates_t[here, :]
        at_slot = jnp.sum(
            jnp.where(places, jnp.broadcast_to(gt[:, None, :], places.shape), 0.0).reshape(block * EVEN, rows),
            axis=-1,
            keepdims=True,
        )
        spread = jnp.broadcast_to(at_slot, (block * EVEN, 128)).reshape(block, EVEN, 128)
        lane_of = iota((block, EVEN, 128), 1) == iota((block, EVEN, 128), 2)
        even_gates = jnp.sum(jnp.where(lane_of, spread, 0.0), axis=1)
        last_gates = jnp.sum(jnp.where(last, gt, 0.0), axis=-1, keepdims=True)
        slot_gates = jnp.where(iota((block, 128), 1) == EVEN, last_gates, even_gates)
        src_l[v] = jnp.concatenate([dot(last_hot, low), dot(last_hot, g), slot_gates], axis=1).reshape(
            4, 4, 1, 2 * width + 128
        )
        swap.first(turn, v)

    for copy in later_loads:
        copy.wait()
    gate = dot(low, sgu[:, :inner])
    up_ = dot(low, sgu[:, inner:])
    silu, slope = silu_parts(gate)
    hidden_s[...] = (silu * up_).astype(BF16)
    grad_hidden = dot_t(g, sdown[...])
    grad_gu[:, :inner] = (grad_hidden * up_ * slope).astype(BF16)
    grad_gu[:, inner:] = (grad_hidden * silu).astype(BF16)
    swap.next(1)
    out_s[...] = dot(hidden_s[...], sdown[...])
    grad_in[...] = dot_t(grad_gu[...], sgu[...])
    swap.next(2)

    @pl.loop(0, inner // 256)
    def _(i):
        r = pl.ds(mul(i * 256, 256), 256)
        grad_down[r, :] = t_dot(hidden_s[:, r], grad[...]).astype(BF16)

    swap.finish()


def route(tokens, mixed, routes, grad, w_q, w_r, w_d):
    rows, width = tokens.shape
    vmem, anywhere = pl.BlockSpec(memory_space=pltpu.VMEM), pl.BlockSpec(memory_space=pl.ANY)
    r, last = (4, 4, 4, EVEN, 2 * width), (4, 4, 4, 1, 2 * width + 128)
    return pl.pallas_call(
        route_kernel,
        out_shape=(
            shape(BF16, *r),
            shape(F32, *last),
            shape(F32, rows, width),
            shape(BF16, rows, width),
            shape(F32, 128, rows),
            shape(F32, 128, rows),
            shape(F32, rows, width),
            shape(F32, rows, width),
            shape(BF16, rows, 2048),
            shape(BF16, 1024, width),
        ),
        in_specs=[vmem] * 4 + [anywhere] * 3,
        out_specs=(anywhere,) * 2 + (vmem,) * 8,
        scratch_shapes=[pltpu.VMEM(r, BF16), pltpu.VMEM(last, F32)] * 3
        + [
            pltpu.VMEM((width, width), BF16),
            pltpu.VMEM((width, 128), BF16),
            pltpu.VMEM((width, 128), BF16),
            pltpu.VMEM((width, 2048), BF16),
            pltpu.VMEM((1024, width), BF16),
            pltpu.VMEM((rows, 1024), BF16),
        ]
        + exchange_sems(2)
        + [pltpu.SemaphoreType.DMA((5,))],
        compiler_params=pltpu.CompilerParams(collective_id=3, has_side_effects=True, vmem_limit_bytes=56 << 20),
        name="route_shared",
    )(tokens, mixed, routes, grad, w_q, w_r, w_d)


def expert_rows(rows_r, rows_l, width):
    sources = 16
    last = rows_l.reshape(sources, rows_l.shape[-1])
    even = sources * EVEN
    both = rows_r.reshape(even, 2 * width)
    x = jnp.concatenate([both[:, :width], last[:, :width].astype(BF16)], axis=0)
    g = jnp.concatenate([both[:, width:].astype(F32), last[:, width : 2 * width]], axis=0)
    sent = last[:, 2 * width :]
    spread = jnp.broadcast_to(sent[:, None, :], (sources, EVEN, 128))
    own = iota((sources, EVEN, 128), 1) == iota((sources, EVEN, 128), 2)
    even_gates = jnp.sum(jnp.where(own, spread, 0.0).reshape(even, 128), axis=-1, keepdims=True)
    last_gates = jnp.sum(jnp.where(iota((sources, 128), 1) == EVEN, sent, 0.0), axis=-1, keepdims=True)
    return x, (jnp.concatenate([even_gates, last_gates], axis=0) * g).astype(BF16)


def expert_kernel(
    rows_r, rows_l, o0, o1, o2, e0, e1, e2,
    back_r, back_l, p0, p1, p2,
    src_r, src_l, b1_r, b1_l, b2_r, b2_l, in_r, in_l, w_gate, w_up, w_down, all_x, all_g, hidden, d_gate, d_up,
    g_gate, g_up, g_down, s_gate, s_up, s_down, ssem, rsem, lsem, wsem, isem, osem, xsem,
):
    spot = place()
    hi, y, z, lo, c = spot
    width = all_x.shape[1]
    outs, products, from_sib = (p0, p1, p2), (g_gate, g_up, g_down), (s_gate, s_up, s_down)
    weights = (w_gate, w_up, w_down)
    owner = c == hi
    swap = Exchange(
        False, (ROW_CUTS, LAST_BACK_CUTS), ((src_r, src_l), (b1_r, b1_l), (b2_r, b2_l), (back_r, back_l)), (ssem, rsem, lsem), spot
    )

    @pl.when(owner)
    def _():
        for copy in loads((e0, e1, e2), weights, wsem):
            copy.start()

    @pl.when(jnp.logical_not(owner))
    def _():
        for copy in loads((o0, o1, o2), weights, wsem):
            copy.start()

    def block(n):
        v = lax.rem(y + TURNS[n], 4)
        return v, loads((rows_r.at[v], rows_l.at[v]), (in_r.at[n % 2], in_l.at[n % 2]), isem.at[n % 2])

    coming = {0: block(0)[1]}
    for copy in coming[0]:
        copy.start()
    swap.greet()
    for copy in loads((e0, e1, e2), weights, wsem):
        copy.wait()
    step = all_x.shape[0] // 4
    even = 16 * EVEN
    for n, turn in enumerate(TURNS):
        v = lax.rem(y + turn, 4)
        if n + 1 < 4:
            coming[n + 1] = block(n + 1)[1]
            for copy in coming[n + 1]:
                copy.start()
        for copy in coming[n]:
            copy.wait()
        here = slice(n * step, (n + 1) * step)
        x, grad_result = expert_rows(in_r[n % 2], in_l[n % 2], width)
        all_x[here, :] = x
        all_g[here, :] = grad_result
        gate = dot(x, w_gate[...])
        up_ = dot(x, w_up[...])
        silu, slope = silu_parts(gate)
        low = (silu * up_).astype(BF16)
        hidden[here, :] = low
        grad_hidden = dot_t(grad_result, w_down[...])
        grad_gate = (grad_hidden * up_ * slope).astype(BF16)
        grad_up = (grad_hidden * silu).astype(BF16)
        d_gate[here, :] = grad_gate
        d_up[here, :] = grad_up
        result = dot(low, w_down[...]).astype(BF16)
        grad_in = (dot_t(grad_gate, w_gate[...]) + dot_t(grad_up, w_up[...])).astype(BF16)
        src_r[v, :, :, :, 0:width] = result[:even].reshape(4, 4, EVEN, width)
        src_r[v, :, :, :, width:] = grad_in[:even].reshape(4, 4, EVEN, width)
        src_l[v] = jnp.concatenate([result[even:], grad_in[even:]], axis=1).astype(F32).reshape(4, 4, 1, 2 * width)
        swap.first(turn, v)

    def half(k, core):
        n = products[k].shape[0] // 2
        return products[k].at[pl.ds(mul(core * n, 16), n)]

    def trade(k):
        return pltpu.make_async_remote_copy(
            src_ref=half(k, 1 - c),
            dst_ref=from_sib[k],
            send_sem=xsem.at[0, k],
            recv_sem=xsem.at[1, k],
            device_id=device(hi, y, z, lo, 1 - c),
            device_id_type=MESH,
        )

    def product(k, left, right, wide):
        out = products[k]

        @pl.loop(0, out.shape[0] // wide)
        def _(i):
            r = pl.ds(mul(i * wide, wide), wide)
            out[r, :] = t_dot(left[:, r], right[...]).astype(BF16)

        trade(k).start()

    def add(k):
        trade(k).wait_recv()
        n = products[k].shape[0] // 2

        @pl.loop(0, n // 64)
        def _(i):
            own = pl.ds(mul(c * n + i * 64, 64), 64)
            more = from_sib[k][pl.ds(mul(i * 64, 64), 64), :].astype(F32)
            products[k][own, :] = (products[k][own, :].astype(F32) + more).astype(BF16)

        copy = pltpu.make_async_copy(half(k, c), outs[k], osem.at[k])
        copy.start()
        return copy

    product(0, all_x, d_gate, 256)
    swap.next(1)
    product(1, all_x, d_up, 256)
    product(2, hidden, all_g, 128)
    kept = [add(0)]
    swap.next(2)
    kept += [add(1), add(2)]
    swap.finish()
    for k in range(3):
        trade(k).wait_send()
        kept[k].wait()


def expert(rows_r, rows_l, passed, own):
    width = rows_r.shape[-1] // 2
    inner = own[0].shape[1]
    total = 64 * (EVEN + 1)
    anywhere = pl.BlockSpec(memory_space=pl.ANY)
    r, last = (4, 4, 4, EVEN, 2 * width), (4, 4, 4, 1, 2 * width)
    return pl.pallas_call(
        expert_kernel,
        out_shape=(shape(BF16, *r), shape(F32, *last)) + tuple(shape(BF16, w.shape[0] // 2, w.shape[1]) for w in own),
        in_specs=[anywhere] * 8,
        out_specs=(anywhere,) * 5,
        scratch_shapes=[pltpu.VMEM(r, BF16), pltpu.VMEM(last, F32)] * 3
        + [pltpu.VMEM((2,) + rows_r.shape[1:], BF16), pltpu.VMEM((2,) + rows_l.shape[1:], F32)]
        + [pltpu.VMEM(w.shape, BF16) for w in own]
        + [pltpu.VMEM((total, n), BF16) for n in (width, width, inner, inner, inner)]
        + [pltpu.VMEM(w.shape, BF16) for w in own]
        + [pltpu.VMEM((w.shape[0] // 2, w.shape[1]), BF16) for w in own]
        + exchange_sems(2)
        + [pltpu.SemaphoreType.DMA(n) for n in ((3,), (2, 2), (3,), (2, 3))],
        compiler_params=pltpu.CompilerParams(collective_id=4, has_side_effects=True, vmem_limit_bytes=62 << 20),
        name="expert_back",
    )(rows_r, rows_l, *passed, *own)


def split_terms(w):
    top = w.astype(BF16)
    rest = w - top.astype(F32)
    mid = rest.astype(BF16)
    return top, mid, (rest - mid.astype(F32)).astype(BF16)


def combine_kernel(
    back_r, back_l, slot_t, gates_t, grad, hidden_one, out_s, grad_in_s, mixed, act, grad_gu, router_w, out_w, gains,
    layer_out, grad_hidden, grad_mixed, left, right, grad_gain,
):
    experts = back_r.shape[0]
    rows, width = hidden_one.shape
    slots = slot_t[0:experts, :]
    places = even_places(slots)
    last = slots == float(EVEN)
    out_rows = back_r[:, :, :width].reshape(experts * EVEN, width)
    last_l = back_l[...].reshape(experts, 2 * width).astype(BF16)
    gt = gates_t[0:experts, :]
    even_w = jnp.where(places, jnp.broadcast_to(gt[:, None, :], places.shape), 0.0).reshape(experts * EVEN, rows)
    last_w = jnp.where(last, gt, 0.0)
    routed = jnp.zeros((rows, width), F32)
    for e_term, l_term in zip(split_terms(even_w), split_terms(last_w)):
        routed = routed + t_dot(e_term, out_rows) + t_dot(l_term, last_l[:, :width])
    hidden = hidden_one[...]
    layer_out[...] = (hidden + out_s[...] + routed).astype(BF16)
    g = grad[...]
    dots = dot_t(out_rows, g).reshape(experts, EVEN, rows)
    dots_last = dot_t(last_l[:, :width], g)
    grad_gates = jnp.sum(jnp.where(places, dots, 0.0), axis=1) + jnp.where(last, dots_last, 0.0)
    logits_t = gt * (grad_gates - jnp.sum(gt * grad_gates, axis=0, keepdims=True))
    low_logits = jnp.concatenate([logits_t, jnp.zeros((128 - experts, rows), F32)], axis=0).T.astype(BF16)
    hot = places.astype(F32).reshape(experts * EVEN, rows).astype(BF16)
    grad_routed = t_dot(hot, back_r[:, :, width:].reshape(experts * EVEN, width)) + t_dot(last.astype(BF16), last_l[:, width:])
    router = router_w[...]
    grad_act = grad_routed + dot_t(low_logits, router) + grad_in_s[...]
    gain = gain_rows(gains[...])[1:2]
    _normed, inv = rms_forward(hidden, gain)
    grad_norm, gain_sum = rms_backward(hidden, inv, gain, grad_act)
    grad_gain[...] = gain_sum
    total = g.astype(F32) + grad_norm
    grad_hidden[...] = total
    low = total.astype(BF16)
    left[0:rows, :] = mixed[...]
    left[rows:, :] = act[...]
    right[0:rows, :width] = low
    right[0:rows, width:] = jnp.zeros((rows, R_WIDE - width), BF16)
    right[rows:, :width] = jnp.zeros((rows, width), BF16)
    right[rows:, width : ROUTER * 128] = grad_gu[...]
    right[rows:, ROUTER * 128 : (ROUTER + 1) * 128] = low_logits
    right[rows:, (ROUTER + 1) * 128 :] = jnp.zeros((rows, R_WIDE - (ROUTER + 1) * 128), BF16)
    grad_mixed[...] = dot_t(low, out_w[...]).astype(BF16)


def combine(operands, w_r, w_q):
    rows, width = operands[5].shape
    whole = lambda a: pl.BlockSpec(a.shape, lambda i: (0,) * len(a.shape))
    outs = (
        shape(BF16, rows, width),
        shape(F32, rows, width),
        shape(BF16, rows, width),
        shape(BF16, 2 * rows, width),
        shape(BF16, 2 * rows, R_WIDE),
        shape(F32, 1, width),
    )
    return pl.pallas_call(
        combine_kernel,
        grid=(1,),
        out_shape=outs,
        in_specs=[whole(a) for a in operands]
        + [
            pl.BlockSpec((width, 128), lambda i: (0, ROUTER)),
            pl.BlockSpec((width, 1280), lambda i: (0, 0)),
            pl.BlockSpec((width, 128), lambda i: (0, GAINS)),
        ],
        out_specs=tuple(whole(a) for a in outs),
        compiler_params=pltpu.CompilerParams(vmem_limit_bytes=56 << 20),
        name="combine",
    )(*operands, w_r, w_r, w_q)


def per_device(
    tokens,
    cotangent,
    segments,
    routes,
    norm_gain_attn,
    w_query,
    w_key,
    w_value,
    w_out,
    norm_gain_ffn,
    w_router,
    shared_gate,
    shared_up,
    shared_down,
    expert_gate,
    expert_up,
    expert_down,
):
    rows = tokens.shape[1]
    width = tokens.shape[2]
    experts = w_router.shape[1]
    tokens, grad, routes = tokens[0], cotangent[0], routes[0]
    seg_row = segments
    seg_col = segments.reshape(-1, 1)
    own_experts = (expert_gate[0], expert_up[0], expert_down[0])

    def spread(w):
        w = w.reshape(w.shape[0], experts, w.shape[1] // experts)
        return jnp.pad(w, ((0, 0), (0, 0), (0, 2))).reshape(w.shape[0], experts * 16)

    own_rows = w_query.shape[0]
    zeros = lambda n: jnp.zeros((own_rows, n), BF16)
    shard_q = jnp.concatenate(
        [w_query, w_key, w_value, norm_gain_attn[:, None], norm_gain_ffn[:, None], zeros(254)], axis=1
    )
    shard_r = jnp.concatenate([w_out, spread(shared_gate), spread(shared_up), w_router, zeros(256 - experts)], axis=1)
    cos, sin = rotary_tables(2 * rows)
    w_q, w_r, w_d, expert_w, act_attn, q, kv, prior, mixed = forward(
        shard_q, shard_r, shared_down, own_experts, tokens, cos, sin, seg_row, seg_col
    )
    rows_r, rows_l, hidden_one, act_ffn, gates_t, slot_t, out_s, grad_in_s, grad_gu, grad_sdown = route(
        tokens, mixed, routes, grad, w_q, w_r, w_d
    )
    back_r, back_l, *parts = expert(rows_r, rows_l, expert_w, own_experts)
    back_r, back_l = (a.reshape((experts,) + a.shape[3:]) for a in (back_r, back_l))
    layer_out, grad_hidden, grad_mixed, left_r, right_r, gain_ffn = combine(
        (back_r, back_l, slot_t, gates_t, grad, hidden_one, out_s, grad_in_s, mixed, act_ffn, grad_gu), w_r, w_q
    )
    fin_q, fin_r, fin_d, *sums, grad_tokens = backward(
        (left_r, right_r, grad_sdown.reshape(4, 4, 64, width), act_attn, q, kv, prior, seg_row, seg_col)
        + (grad_mixed, cos, sin, tokens, grad_hidden, gain_ffn, w_q),
        parts,
    )
    offset = 4 * lax.rem(lax.axis_index("exp"), 4)
    own_q = lax.dynamic_slice(fin_q, (offset, 0), (own_rows, Q_WIDE))
    own_r = lax.dynamic_slice(fin_r, (offset, 0), (own_rows, R_WIDE))

    def gathered_hidden(w):
        return w.reshape(w.shape[0], experts, 16)[:, :, :14].reshape(w.shape[0], experts * 14)

    core = lax.rem(lax.axis_index("exp"), 2)
    kept_here = (core == lax.axis_index("seq")) & (jnp.arange(2) == core)
    expert_grads = [
        jnp.where(kept_here[:, None, None], own[None], total.reshape((2,) + own.shape)).astype(F32).reshape(1, *total.shape)
        for own, total in zip(parts, sums)
    ]
    router = ROUTER * 128
    return (
        layer_out[None],
        grad_tokens[None],
        own_q[:, GAINS * 128],
        own_q[:, :1280],
        own_q[:, 1280:2560],
        own_q[:, 2560:3840],
        own_r[:, :1280],
        own_q[:, GAINS * 128 + 1],
        own_r[:, router : router + experts],
        gathered_hidden(own_r[:, 1280:2304]),
        gathered_hidden(own_r[:, 2304:3328]),
        fin_d[:14],
        *expert_grads,
    )


def solution(mesh):
    rows = P("exp", None)
    deep = P("exp", None, None)
    split = P("exp", "seq", None)
    gain = P("exp")
    in_specs = (split, split, rows, split, gain, rows, rows, rows, rows, gain) + (rows,) * 4 + (deep,) * 3
    out_specs = (split, split, gain, rows, rows, rows, rows, gain) + (rows,) * 4 + (deep,) * 3
    return jax.shard_map(per_device, mesh=mesh, in_specs=in_specs, out_specs=out_specs, check_vma=False)
```

```python
import functools
import jax
import jax.numpy as jnp
import numpy as np
from jax import lax
from jax.experimental import pallas as pl
from jax.experimental.pallas import tpu as pltpu
from jax.sharding import PartitionSpec as P

HEADS = 10
EPSILON = 1e-06
NEG_BIG = -1e30
F32 = jnp.float32
BF16 = jnp.bfloat16
MESH = pl.DeviceIdType.MESH

PIECES = {
    "q": (80, 16, ((0, 8, 4), (8, 8, 4))),
    "r": (80, 14, ((0, 7, 4), (7, 7, 4))),
    "d": (64, 5, ((0, 3, 2), (3, 2, 1))),
}
Q_WIDE, R_WIDE, D_WIDE = 4096, 3584, 1280
GAINS = 30
ROUTER = 26
UNITS = (0, 1)


def place():
    hi = lax.axis_index("seq")
    e = lax.axis_index("exp")
    return hi, e // 16, lax.rem(e // 4, 4), lax.rem(e // 2, 2), lax.rem(e, 2)


def device(hi, y, z, lo, c):
    return (hi, ((y * 4 + z) * 2 + lo) * 2 + c)


def up(v):
    return lax.rem(v + 1, 4)


def dn(v):
    return lax.rem(v + 3, 4)


def opp(v):
    return lax.rem(v + 2, 4)


def mul(v, m=128):
    return pl.multiple_of(v, m)


def greet(devices):
    bar = pltpu.get_barrier_semaphore()
    for to in devices:
        pl.semaphore_signal(bar, inc=1, device_id=to, device_id_type=MESH)
    pl.semaphore_wait(bar, len(devices))


class Sender:
    def __init__(self, send_sem, recv_sem, local_sem):
        self.sems = (send_sem, recv_sem, local_sem)
        self.sent = []
        self.kept = 0

    def describe(self, src, dst, to):
        k = len(self.sent)
        self.sent.append(None)
        return pltpu.make_async_remote_copy(
            src_ref=src,
            dst_ref=dst,
            send_sem=self.sems[0].at[k],
            recv_sem=self.sems[1].at[k],
            device_id=to,
            device_id_type=MESH,
        )

    def remote(self, src, dst, to):
        copy = self.describe(src, dst, to)
        copy.start()
        self.sent[-1] = copy
        return copy

    def local(self, src, dst):
        copy = pltpu.make_async_copy(src, dst, self.sems[2].at[self.kept])
        self.kept += 1
        copy.start()
        return copy

    def settle(self, copy):
        copy.wait_send()
        self.sent = [None if one is copy else one for one in self.sent]

    def finish(self):
        for copy in self.sent:
            if copy is not None:
                copy.wait_send()


def arrived(copies):
    for copy in copies:
        copy.wait_recv()


def ring_neighbours(hi, y, z, lo, c):
    return {
        ("y", 1): device(hi, up(y), z, lo, c),
        ("y", -1): device(hi, dn(y), z, lo, c),
        ("z", 1): device(hi, y, up(z), lo, c),
        ("z", -1): device(hi, y, dn(z), lo, c),
        ("y", 2): device(hi, opp(y), z, lo, c),
        ("z", 2): device(hi, y, opp(z), lo, c),
    }


def unit_tiles(piece, u, half):
    s, w, w0 = PIECES[piece][2][u]
    return ((s, w0), (s + w0, w - w0))[half] if half is not None else (s, w)


def lanes(piece, u, half, core):
    s, w = unit_tiles(piece, u, half)
    return pl.ds(mul(core * (PIECES[piece][1] * 128) + s * 128), w * 128)


def core_lanes(piece, core):
    n = PIECES[piece][1] * 128
    return pl.ds(mul(core * n), n)


def interleave(steps, work):
    for step in steps:
        step()
        next(work, None)
    for _ in work:
        pass


def dot(a, b):
    return jnp.dot(a, b, preferred_element_type=F32)


def dot_t(a, b):
    return lax.dot_general(a, b, (((1,), (1,)), ((), ())), preferred_element_type=F32)


def t_dot(a, b):
    return lax.dot_general(a, b, (((0,), (0,)), ((), ())), preferred_element_type=F32)


def iota(shape, dim):
    return lax.broadcasted_iota(jnp.int32, shape, dim)


def shape(dtype, *dims):
    return jax.ShapeDtypeStruct(dims, dtype)


def gain_rows(tile):
    pick = (iota((8, 128), 1) == iota((8, 128), 0)).astype(BF16)
    return dot_t(pick, tile)


def rms_forward(values, gain):
    inv_rms = lax.rsqrt(jnp.mean(values * values, axis=-1, keepdims=True) + EPSILON)
    return values * inv_rms * gain, inv_rms


def rms_backward(values, inv_rms, gain, upstream):
    weighted = upstream * gain
    inner = jnp.mean(weighted * values, axis=-1, keepdims=True)
    grad_in = inv_rms * weighted - values * (inv_rms * inv_rms * inv_rms) * inner
    grad_gain = jnp.sum(upstream * values * inv_rms, axis=0, keepdims=True)
    return grad_in, grad_gain


def rotary_tables(rows):
    freq = np.power(10000.0, -2.0 * np.arange(64) / 128)
    angles = np.arange(rows)[:, None] * freq[None, :]
    cos, sin = np.cos(angles), np.sin(angles)
    return (
        jnp.asarray(np.concatenate([cos, cos], axis=1), F32),
        jnp.asarray(np.concatenate([-sin, sin], axis=1), F32),
    )


def silu_parts(pre_act):
    sigma = jax.nn.sigmoid(pre_act)
    return (pre_act * sigma, sigma * (1.0 + pre_act * (1.0 - sigma)))


def seq_rows():
    return pl.ds(mul(lax.axis_index("seq") * 128), 128)


def allowed_keys(seg_row):
    hi = lax.axis_index("seq")
    rows = seg_row.shape[1] // 2
    across = lambda at: jnp.broadcast_to(seg_row[:, at].astype(F32), (rows, rows))
    here = across(seq_rows())
    mine = here.T
    own = (here == mine) & (iota((rows, rows), 1) <= iota((rows, rows), 0))
    prior = (across(slice(0, rows)) == mine) & (hi == 1)
    return own, prior


def head_probs(h, q, kv, prior, own_ok, prior_ok, width):
    here = slice(h * 128, (h + 1) * 128)
    behind = slice(width + h * 128, width + (h + 1) * 128)
    query = q[:, here]
    keys = jnp.concatenate([prior[:, here], kv[:, here]], axis=0)
    values = jnp.concatenate([prior[:, behind], kv[:, behind]], axis=0)
    scores = dot_t(query, keys) * (128.0**-0.5)
    rows = query.shape[0]
    scores = jnp.concatenate(
        [jnp.where(prior_ok, scores[:, :rows], NEG_BIG), jnp.where(own_ok, scores[:, rows:], NEG_BIG)], axis=1
    )
    expo = jnp.exp(scores - jnp.max(scores, axis=-1, keepdims=True))
    return query, keys, values, expo / jnp.sum(expo, axis=-1, keepdims=True)


class Gather:
    def __init__(self, wires, names, blocks, outs, spot):
        hi, y, z, lo, c = spot
        self.wires, self.names, self.outs, self.core = wires, names, outs, c
        self.sib = device(hi, y, z, lo, 1 - c)
        nb = ring_neighbours(hi, y, z, lo, c)
        self.keep = []
        units = []
        for u in UNITS:
            a1, a2 = ("y", "z") if u == 0 else ("z", "y")
            p1, p2 = (y, z) if u == 0 else (z, y)
            units.append(
                dict(p1=p1, p2=p2, up1=nb[a1, 1], dn1=nb[a1, -1], up2=nb[a2, 1], dn2=nb[a2, -1], got={}, second=[], sib=[])
            )
        self.units = units
        self.steps = [functools.partial(self.own_block, blocks, y, z)]
        for u in UNITS:
            self.steps.append(functools.partial(self.first_axis, u, "up1", 0))
        for u in UNITS:
            self.steps.append(functools.partial(self.first_axis, u, "dn1", 1))
        for u in UNITS:
            self.steps.append(functools.partial(self.first_far, u))
        turn = (lambda p: p, dn, up, opp)
        self.near, self.far = [], []
        for k in range(4):
            for u in UNITS:
                q1 = turn[k](units[u]["p1"])
                self.near.append(functools.partial(self.second_axis, u, k, q1))
                self.far.append(functools.partial(self.second_far, u, k, q1))

    def region(self, name, u, half, q1, q2):
        by, bz = (q1, q2) if u == 0 else (q2, q1)
        return self.outs[name].at[by, bz, :, lanes(name, u, half, self.core)]

    def send(self, u, half, q1, q2, to, src=None):
        copies = []
        for name in self.names:
            dst = self.region(name, u, half, q1, q2)
            copies.append(self.wires.remote(src[name] if src else dst, dst, to))
        return copies

    def spread(self, u, q1, src=None):
        unit = self.units[u]
        at = (q1, unit["p2"])
        unit["second"].append((self.send(u, None, *at, unit["up2"], src), self.send(u, None, *at, unit["dn2"], src)))
        unit["sib"].append(self.send(u, None, *at, self.sib, src))

    def own_block(self, blocks, y, z):
        for name in self.names:
            self.keep.append(self.wires.local(blocks[name], self.outs[name].at[y, z, :, core_lanes(name, self.core)]))
        for u, unit in enumerate(self.units):
            src = {}
            for name in self.names:
                s, w = unit_tiles(name, u, None)
                src[name] = blocks[name].at[:, pl.ds(s * 128, w * 128)]
            at = (unit["p1"], unit["p2"])
            unit["got"]["up1"] = self.send(u, None, *at, unit["up1"], src)
            unit["got"]["dn1"] = self.send(u, None, *at, unit["dn1"], src)
            self.spread(u, unit["p1"], src)

    def first_axis(self, u, way, half):
        unit = self.units[u]
        arrived(unit["got"][way])
        q1 = dn(unit["p1"]) if way == "up1" else up(unit["p1"])
        unit["got"]["far", half] = self.send(u, half, q1, unit["p2"], unit[way])
        self.spread(u, q1)

    def first_far(self, u):
        unit = self.units[u]
        arrived(unit["got"]["far", 0])
        arrived(unit["got"]["far", 1])
        self.spread(u, opp(unit["p1"]))

    def second_axis(self, u, k, q1):
        unit = self.units[u]
        for half, way, turn in ((0, "up2", dn), (1, "dn2", up)):
            arrived(unit["second"][k][half])
            at = (q1, turn(unit["p2"]))
            unit["got"][k, half] = self.send(u, half, *at, unit[way])
            unit["sib"].append(self.send(u, None, *at, self.sib))

    def second_far(self, u, k, q1):
        unit = self.units[u]
        arrived(unit["got"][k, 0])
        arrived(unit["got"][k, 1])
        unit["sib"].append(self.send(u, None, q1, opp(unit["p2"]), self.sib))

    def finish(self):
        for unit in self.units:
            for copies in unit["sib"]:
                arrived(copies)
        for copy in self.keep:
            copy.wait()


def window_block(first, second, shift):
    n = first.shape[0]
    return first[0:shift], first[shift:n] + second[0 : n - shift], second[n - shift : n]


def make_windows(j, shards, win_q, win_r, win_d):
    query_w, key_w, value_w, out_w, gate_w, up_w, router_w, gain_a, gain_f, down_w = shards
    own_rows, width = query_w.shape
    place_rows = (iota((32, own_rows), 0) == iota((32, own_rows), 1) + 4 * j).astype(BF16)
    put = lambda w: dot(place_rows, w).astype(BF16)
    for k, w in enumerate((query_w, key_w, value_w)):
        win_q[:, k * width : (k + 1) * width] = put(w[...])
    row = iota((8, own_rows), 0)
    gains = jnp.where(row == 0, gain_a[...].astype(F32), jnp.where(row == 1, gain_f[...].astype(F32), 0.0)).astype(BF16)
    column = (iota((8, 128), 1) == iota((8, 128), 0)).astype(BF16)
    win_q[:, GAINS * 128 : (GAINS + 1) * 128] = put(t_dot(gains, column).astype(BF16))
    win_q[:, (GAINS + 1) * 128 :] = jnp.zeros((32, 128), BF16)
    win_r[:, 0:width] = put(out_w[...])
    narrow, wide = gate_w.shape[1], 1024
    row, col = iota((narrow, wide), 0), iota((narrow, wide), 1)
    spread = ((row == col - 2 * (col // 16)) & (lax.rem(col, 16) < 14)).astype(BF16)
    for k, w in enumerate((gate_w, up_w)):
        win_r[:, width + k * wide : width + (k + 1) * wide] = dot(put(w[...]), spread).astype(BF16)
    start, n = ROUTER * 128, router_w.shape[1]
    win_r[:, start:] = jnp.concatenate([put(router_w[...]), jnp.zeros((32, 256 - n), BF16)], axis=1)
    n = down_w.shape[0]
    place_rows = (iota((16, n), 0) == iota((16, n), 1)).astype(BF16)
    win_d[...] = dot(place_rows, down_w[...]).astype(BF16)


def forward_kernel(
    query_w, key_w, value_w, out_w, gate_w, up_w, router_w, gain_a, gain_f, down_w, e0, e1, e2, tok, cos, sin, seg_row,
    out_q, out_r, out_d, o0, o1, o2, act, q, kv, prior, mixed,
    win_q, win_r, win_d, sib_q, sib_r, pair_q, pair_r, side_q, side_r, blk_q, blk_r, blk_d, w_buf, ssem, rsem, lsem, esem, wsem,
):
    spot = place()
    hi, y, z, lo, c = spot
    sib = device(hi, y, z, lo, 1 - c)
    xn = device(hi, y, z, 1 - lo, c)
    hn = device(1 - hi, y, z, lo, c)
    width = tok.shape[1]
    make_windows(
        lo * 2 + c, (query_w, key_w, value_w, out_w, gate_w, up_w, router_w, gain_a, gain_f, down_w), win_q, win_r, win_d
    )
    greet([sib, xn, hn] + list(ring_neighbours(*spot).values()))
    wires = Sender(ssem, rsem, lsem)
    owner = c == hi

    @pl.when(hi == 0)
    def _():
        prior[...] = jnp.zeros_like(prior)

    j = lo * 2 + c
    windows = {"q": (win_q, sib_q, pair_q, side_q, blk_q), "r": (win_r, sib_r, pair_r, side_r, blk_r)}
    swaps = {}
    for name in "qr":
        win, from_sib = windows[name][:2]
        swaps[name] = wires.remote(win.at[:, core_lanes(name, 1 - c)], from_sib, sib)
    r16 = pl.ds(mul(j * 16, 16), 16)
    swap_d = wires.remote(win_d.at[:, core_lanes("d", 1 - c)], blk_d.at[r16], sib)
    blk_d[r16, :] = win_d[:, core_lanes("d", c)]
    across = {}
    for name in "qr":
        win, from_sib, pair, side, _blk = windows[name]
        own = win[:, core_lanes(name, c)]
        swaps[name].wait_recv()
        got = from_sib[...]
        pair[0:16], pair[16:32], pair[32:48] = window_block(
            jnp.where(c == 0, own, got), jnp.where(c == 0, got, own), 16
        )
        across[name] = wires.remote(pair, side, xn)
    swap_d.wait_recv()
    r32 = pl.ds(mul(lo * 32, 16), 32)
    across_d = wires.remote(blk_d.at[r32], blk_d.at[r32], xn)

    def pass_expert(k):
        return pltpu.make_async_remote_copy(
            src_ref=(e0, e1, e2)[k],
            dst_ref=(o0, o1, o2)[k],
            send_sem=esem.at[0, k],
            recv_sem=esem.at[1, k],
            device_id=sib,
            device_id_type=MESH,
        )

    blocks = {"q": blk_q, "r": blk_r, "d": blk_d}
    outs = {"q": out_q, "r": out_r, "d": out_d}
    group_q = Gather(wires, "q", blocks, outs, spot)
    group_r = Gather(wires, "rd", blocks, outs, spot)

    def whole_block(name):
        _win, _sib, pair, side, blk = windows[name]
        across[name].wait_recv()
        own, got = pair[...], side[...]
        blk[0:32], blk[32:48], blk[48:80] = window_block(
            jnp.where(lo == 0, own, got), jnp.where(lo == 0, got, own), 32
        )

    whole_block("q")
    for step in group_q.steps:
        step()
    whole_block("r")
    across_d.wait_recv()
    for step in group_q.near:
        step()
    group_r.steps[0]()
    for step in group_q.far:
        step()
    group_q.finish()

    @pl.when(owner)
    def _():
        for k in range(3):
            pass_expert(k).start()

    def load(i, slot):
        return pltpu.make_async_copy(out_q.at[:, :, :, pl.ds(i * 512, 512)], w_buf.at[slot], wsem.at[slot])

    later = wires.describe(kv, prior, hn)

    def work():
        order = (7, 2, 3, 4, 5, 6, 0, 1)
        here = seq_rows()
        cosine, sine = cos[here, :], sin[here, :]
        load(order[0], 0).start()
        for n, i in enumerate(order):
            slot = n % 2
            load(i, slot).wait()
            if n + 1 < len(order):
                load(order[n + 1], 1 - slot).start()
            w = w_buf[slot].reshape(width, 512)
            if n == 0:
                gains = gain_rows(w[:, (GAINS - 28) * 128 : (GAINS - 27) * 128])
                normed, _inv = rms_forward(tok[...].astype(F32), gains[0:1])
                act[...] = normed.astype(BF16)
                w = w[:, :256]
            x = dot(act[...], w)
            for t in range(w.shape[1] // 128):
                tile = 4 * i + t
                v = x[:, t * 128 : (t + 1) * 128]
                if tile < 20:
                    v = v * cosine + pltpu.roll(v, 64, 1) * sine
                if tile < 10:
                    q[:, tile * 128 : (tile + 1) * 128] = v.astype(BF16)
                else:
                    kv[:, (tile - 10) * 128 : (tile - 9) * 128] = v.astype(BF16)
            if i == 6:

                @pl.when(hi == 0)
                def _():
                    later.start()

            yield
        for _ in range(4):
            yield

        @pl.when(hi == 1)
        def _():
            later.wait_recv()

        own_ok, prior_ok = allowed_keys(seg_row)
        for h in range(HEADS):
            _query, _keys, values, probs = head_probs(h, q, kv, prior, own_ok, prior_ok, width)
            mixed[:, h * 128 : (h + 1) * 128] = dot(probs.astype(BF16), values).astype(BF16)
            yield

    interleave(group_r.steps[1:] + group_r.near + group_r.far + [group_r.finish], work())

    @pl.when(hi == 0)
    def _():
        later.wait_send()

    @pl.when(owner)
    def _():
        for k in range(3):
            pass_expert(k).wait_send()

    @pl.when(jnp.logical_not(owner))
    def _():
        for k in range(3):
            pass_expert(k).wait_recv()

    wires.finish()


def forward(shards, experts, tokens, cos, sin, seg_row):
    rows, width = tokens.shape
    sems = 2 + 1 + 3 + 36 * 2 * 3 + 8
    vmem, anywhere = pl.BlockSpec(memory_space=pltpu.VMEM), pl.BlockSpec(memory_space=pl.ANY)
    half = {name: PIECES[name][1] * 128 for name in PIECES}
    out = pl.pallas_call(
        forward_kernel,
        out_shape=(
            shape(BF16, 4, 4, 80, Q_WIDE),
            shape(BF16, 4, 4, 80, R_WIDE),
            shape(BF16, 4, 4, 64, D_WIDE),
            *(shape(BF16, *w.shape) for w in experts),
            shape(BF16, rows, width),
            shape(BF16, rows, width),
            shape(BF16, rows, 2 * width),
            shape(BF16, rows, 2 * width),
            shape(BF16, rows, width),
        ),
        in_specs=[vmem] * len(shards) + [anywhere] * 3 + [vmem] * 4,
        out_specs=(anywhere,) * 6 + (vmem,) * 5,
        scratch_shapes=[pltpu.VMEM(dims, BF16) for dims in ((32, Q_WIDE), (32, R_WIDE), (16, D_WIDE))]
        + [pltpu.VMEM((n, half[name]), BF16) for n in (32, 48, 48, 80) for name in "qr"]
        + [
            pltpu.VMEM((64, half["d"]), BF16),
            pltpu.VMEM((2, 4, 4, 80, 512), BF16),
            pltpu.SemaphoreType.DMA((sems,)),
            pltpu.SemaphoreType.DMA((sems,)),
            pltpu.SemaphoreType.DMA((3,)),
            pltpu.SemaphoreType.DMA((2, 3)),
            pltpu.SemaphoreType.DMA((2,)),
        ],
        compiler_params=pltpu.CompilerParams(collective_id=1, has_side_effects=True, vmem_limit_bytes=56 << 20),
        name="gather_attend",
    )(*shards, *experts, tokens, cos, sin, seg_row)
    w_q, w_r, w_d = (out[k].reshape(16 * out[k].shape[2], out[k].shape[3]) for k in range(3))
    return (w_q, w_r, w_d, out[3:6]) + tuple(out[6:])


START = (3, 1, 1)
R_PIECES = range(11, 24)
Q_PIECES = range(0, 18, 2)
KV_GAP = 4


class RingSum:
    def __init__(self, wires, names, hold, from_sib, bufs, to_sib, spot):
        hi, y, z, lo, c = spot
        self.wires, self.names, self.hold, self.from_sib, self.bufs, self.to_sib = (
            wires, names, hold, from_sib, bufs, to_sib,
        )
        self.sib = device(hi, y, z, lo, 1 - c)
        self.nb = ring_neighbours(hi, y, z, lo, c)
        self.first_axis, self.second_axis = ("y", "z"), ("z", "y")
        self.ring, self.coming = {}, {}
        orders = []
        for u in UNITS:
            p1, p2 = (y, z) if u == 0 else (z, y)
            ones = (opp(p1), up(p1), dn(p1), p1)
            orders.append([(q1, q2) if u == 0 else (q2, q1) for q2 in (opp(p2), up(p2), dn(p2), p2) for q1 in ones])
        self.orders = orders
        self.steps = []
        for i in range(4):
            for u in UNITS:
                self.steps.append(functools.partial(self.far_step, u, i))
        for i in range(4):
            for u in UNITS:
                self.steps.append(functools.partial(self.near_step, u, i, 1))
            for u in UNITS:
                self.steps.append(functools.partial(self.near_step, u, i, -1))
        for i in range(4):
            for u in UNITS:
                self.steps.append(functools.partial(self.own_step, u, i))
        for u in UNITS:
            self.steps.append(functools.partial(self.last_step, u))

    def blocks(self, refs, u, index):
        return {name: refs[name][u].at[index] for name in self.names}

    def start(self):
        for k in range(16):
            for u in UNITS:
                at = self.orders[u][k]
                src, dst = self.blocks(self.to_sib, u, at), self.blocks(self.from_sib, u, at)
                self.coming[u, k] = self.pair(src, dst, self.sib)

    def pair(self, src, dst, to):
        return [self.wires.remote(src[name], dst[name], to) for name in self.names]

    def add_in(self, dst, *more):
        @pl.loop(0, dst.shape[-2] // 16)
        def _(i):
            r = pl.ds(mul(i * 16, 16), 16)
            value = dst[r, :].astype(F32)
            for ref in more:
                value = value + ref[r, :].astype(F32)
            dst[r, :] = value.astype(BF16)

    def ready(self, u, k):
        arrived(self.coming[u, k])
        at = self.orders[u][k]
        blk, more = self.blocks(self.hold, u, at), self.blocks(self.from_sib, u, at)
        for name in self.names:
            self.add_in(blk[name], more[name])
        return blk

    def half(self, blk, u, h):
        cut = {}
        for name in self.names:
            s, w, w0 = PIECES[name][2][u]
            cut[name] = blk[name].at[:, pl.ds(0, w0 * 128) if h == 0 else pl.ds(w0 * 128, (w - w0) * 128)]
        return cut

    def buffer(self, u, i, slot):
        return {name: self.bufs[name][u][i].at[slot] for name in self.names}

    def far_block(self, u, slot, blk, axis):
        self.ring[u, slot, 0] = self.pair(self.half(blk, u, 0), self.buffer(u, 0, slot), self.nb[axis, 1])
        self.ring[u, slot, 1] = self.pair(self.half(blk, u, 1), self.buffer(u, 1, slot), self.nb[axis, -1])

    def near_block(self, u, slot, blk, axis, way):
        h = 0 if way == 1 else 1
        arrived(self.ring[u, slot, h])
        dst, more = self.half(blk, u, h), self.buffer(u, h, slot)
        for name in self.names:
            self.add_in(dst[name], more[name])
        self.ring[u, slot, 2 + h] = self.pair(blk, self.buffer(u, 2 + h, slot), self.nb[axis, way])

    def own_block(self, u, slot, blk):
        arrived(self.ring[u, slot, 2])
        arrived(self.ring[u, slot, 3])
        one, two = self.buffer(u, 2, slot), self.buffer(u, 3, slot)
        for name in self.names:
            self.add_in(blk[name], one[name], two[name])

    def far_step(self, u, i):
        self.far_block(u, i, self.ready(u, i), self.second_axis[u])

    def near_step(self, u, i, way):
        self.near_block(u, i, self.ready(u, (4 if way == 1 else 8) + i), self.second_axis[u], way)

    def own_step(self, u, i):
        blk = self.ready(u, 12 + i)
        self.own_block(u, i, blk)
        axis = self.first_axis[u]
        if i == 0:
            for h in (0, 1):
                self.ring[u, 4, h] = self.pair(self.half(blk, u, h), self.buffer(u, h, 4), self.nb[axis, 2])
        elif i < 3:
            self.ring[u, 4, 1 + i] = self.pair(blk, self.buffer(u, 1 + i, 4), self.nb[axis, 1 if i == 1 else -1])

    def last_step(self, u):
        blk = self.blocks(self.hold, u, self.orders[u][15])
        self.own_block(u, 4, blk)
        for h in (0, 1):
            arrived(self.ring[u, 4, h])
            dst, more = self.half(blk, u, h), self.buffer(u, h, 4)
            for name in self.names:
                self.add_in(dst[name], more[name])


def sum_scratch():
    scratch = []
    for rows, _tiles, units in PIECES.values():
        for s, w, w0 in units:
            scratch += [pltpu.VMEM((4, 4, rows, w * 128), BF16)] * 2
            scratch += [pltpu.VMEM((5, rows, t * 128), BF16) for t in (w0, w - w0, w, w)]
    return scratch


def backward_kernel(
    left_r, right_r, sdown, act, q, kv, prior, seg_row, grad_mixed, cos, sin, tok, grad_hidden, gain_f, w_q,
    p0, p1, p2,
    fin_q, fin_r, fin_d, t0, t1, t2, grad_tokens,
    *scratch,
):
    names = list(PIECES)
    hold, from_sib, bufs = {}, {}, {}
    scratch = list(scratch)
    for name in names:
        hold[name], from_sib[name], bufs[name] = [], [], []
        for u in UNITS:
            hold[name].append(scratch.pop(0))
            from_sib[name].append(scratch.pop(0))
            bufs[name].append([scratch.pop(0) for _ in range(4)])
    sums, sides, mids, fars = ({name: scratch.pop(0) for name in names} for _ in range(4))
    accs = {name: scratch.pop(0) for name in names}
    sent = [scratch.pop(0) for _ in UNITS]
    grad_own, grad_prior, later, left_q, right_q, total, w_buf, gain_tile = scratch[:8]
    ssem, rsem, lsem, esend, erecv, wsem, piece_sem = scratch[8:]
    spot = place()
    hi, y, z, lo, c = spot
    sib = device(hi, y, z, lo, 1 - c)
    xn = device(hi, y, z, 1 - lo, c)
    hn = device(1 - hi, y, z, lo, c)
    greet([sib, xn, hn, device(1 - hi, y, z, lo, 1 - c)] + list(ring_neighbours(*spot).values()))
    wires = Sender(ssem, rsem, lsem)
    rows, width = tok.shape

    owner = c == hi
    parts, totals = (p0, p1, p2), (t0, t1, t2)
    across = device(1 - hi, y, z, lo, hi)

    def rows_of(ref, core):
        n = ref.shape[0] // 2
        return ref.at[pl.ds(mul(core * n, 16), n)]

    def expert_copy(src, dst, k, tag, to):
        return pltpu.make_async_remote_copy(
            src_ref=src, dst_ref=dst, send_sem=esend.at[k], recv_sem=erecv.at[tag], device_id=to, device_id_type=MESH
        )

    def across_piece(k, i):
        n = parts[k].shape[0]
        return pltpu.make_async_remote_copy(
            src_ref=parts[k].at[pl.ds(i * 64, 64)],
            dst_ref=totals[k].at[pl.ds(mul(c * n + i * 64, 16), 64)],
            send_sem=piece_sem.at[0, k, i],
            recv_sem=piece_sem.at[1, k, 10 * c + i],
            device_id=across,
            device_id_type=MESH,
        )

    def coming_piece(k, i, core):
        n = parts[k].shape[0]
        rows_ = totals[k].at[pl.ds(mul(core * n + i * 64, 16), 64)]
        return pltpu.make_async_remote_copy(
            src_ref=rows_,
            dst_ref=rows_,
            send_sem=piece_sem.at[0, k, i],
            recv_sem=piece_sem.at[1, k, 10 * core + i],
            device_id=across,
            device_id_type=MESH,
        )

    pieces = [(k, i) for k in range(3) for i in range(parts[k].shape[0] // 64)]

    def send_near(k):
        return expert_copy(parts[k], rows_of(totals[k], c), k, k, sib)

    def near_half(k):
        return expert_copy(rows_of(totals[k], 1 - c), rows_of(totals[k], 1 - c), k, k, sib)

    def expert_steps():
        for n, (k, i) in enumerate(pieces):
            across_piece(k, i).start()
            if n == len(pieces) // 2:

                @pl.when(jnp.logical_not(owner))
                def _():
                    for k in range(3):
                        send_near(k).start()

            yield

    experts = expert_steps()
    for _ in range(START[0]):
        next(experts, None)

    own_d = []
    for u in UNITS:
        s, w = unit_tiles("d", u, None)
        own_d.append(wires.local(sdown.at[:, :, :, lanes("d", u, None, c)], hold["d"][u]))

    def products(left, right, name, core, refs):
        for u in UNITS:
            r = right[:, lanes(name, u, None, core)]
            for m in (0, 1):
                v = t_dot(left[:, m * 640 : (m + 1) * 640], r).astype(BF16)
                for b in range(8):
                    refs[u][2 * m + b // 4, b % 4] = v[b * 80 : (b + 1) * 80]

    def views(name, refs):
        return [ref.at[:, :, :, pl.ds(0, PIECES[name][2][u][1] * 128)] for u, ref in enumerate(refs)]

    to_sib_r = views("r", sent)
    products(left_r, right_r, "r", 1 - c, to_sib_r)
    to_sib_d = [sdown.at[:, :, :, lanes("d", u, None, 1 - c)] for u in UNITS]
    group_r = RingSum(wires, "rd", hold, from_sib, bufs, {"r": to_sib_r, "d": to_sib_d}, spot)
    group_r.start()
    for _ in range(START[1]):
        next(experts, None)
    products(left_r, right_r, "r", c, hold["r"])
    for copy in own_d:
        copy.wait()
    for _ in range(START[2]):
        next(experts, None)

    def load(i):
        return pltpu.make_async_copy(w_q.at[:, pl.ds(i * 512, 512)], w_buf.at[i % 2], wsem.at[i % 2])

    load_gains = pltpu.make_async_copy(w_q.at[:, pl.ds(GAINS * 128, 128)], gain_tile, wsem.at[2])
    halves = [pl.ds(start, 640) for start in (0, width, 640, width + 640)]
    exchange_kv = [wires.describe(grad_prior.at[:, cut], later.at[:, cut], hn) for cut in halves]
    to_sib_q = views("q", sent)
    group_q = RingSum(wires, "q", hold, from_sib, bufs, {"q": to_sib_q}, spot)

    def work():
        load(0).start()
        load_gains.start()
        here = seq_rows()
        cosine, sine = cos[here, :], sin[here, :]
        own_ok, prior_ok = allowed_keys(seg_row)
        inv_root = 128.0**-0.5

        @pl.when(hi == 1)
        def _():
            later[...] = jnp.zeros_like(later)

        for h in range(HEADS):
            query, keys, values, probs = head_probs(h, q, kv, prior, own_ok, prior_ok, width)
            mine = slice(h * 128, (h + 1) * 128)
            behind = slice(width + h * 128, width + (h + 1) * 128)
            gm = grad_mixed[:, mine]
            grad_probs = dot_t(gm, values)
            inner = jnp.sum(probs * grad_probs, axis=-1, keepdims=True)
            grad_scores = (probs * (grad_probs - inner)).astype(BF16)
            grad_values = t_dot(probs.astype(BF16), gm)
            gq = dot(grad_scores, keys) * inv_root
            grad_keys = t_dot(grad_scores, query) * inv_root
            right_q[0:rows, mine] = (gq * cosine - pltpu.roll(gq, 64, 1) * sine).astype(BF16)
            grad_own[:, mine] = grad_keys[rows:]
            grad_own[:, behind] = grad_values[rows:]
            grad_prior[:, mine] = grad_keys[:rows].astype(BF16)
            grad_prior[:, behind] = grad_values[:rows].astype(BF16)
            if h % 5 == 4:

                @pl.when(hi == 1)
                def _():
                    for copy in exchange_kv[:2] if h == 4 else exchange_kv[2:]:
                        copy.start()

            yield

        right_q[0:rows, 3 * width :] = jnp.zeros((rows, Q_WIDE - 3 * width), BF16)
        right_q[rows:, :] = (iota((16, Q_WIDE), 1) == iota((16, Q_WIDE), 0) + GAINS * 128).astype(BF16)
        left_q[0:rows, :] = act[...]
        total[...] = jnp.zeros_like(total)

        def add_chunk(i):
            load(i).wait()
            if i < 7:
                load(i + 1).start()
            total[...] += dot_t(right_q[0:rows, i * 512 : (i + 1) * 512], w_buf[i % 2])

        for i in (0, 1):
            add_chunk(i)
            yield

        for _ in range(KV_GAP):
            yield

        @pl.when(hi == 0)
        def _():
            for copy in exchange_kv:
                copy.wait_recv()

        for h in range(HEADS):
            mine = slice(h * 128, (h + 1) * 128)
            gk = grad_own[:, mine] + later[:, mine].astype(F32)
            right_q[0:rows, width + h * 128 : width + (h + 1) * 128] = (
                gk * cosine - pltpu.roll(gk, 64, 1) * sine
            ).astype(BF16)
        right_q[0:rows, 2 * width : 3 * width] = (grad_own[:, width:] + later[:, width:].astype(F32)).astype(BF16)
        yield
        for i in range(2, 8):
            add_chunk(i)
            yield
        load_gains.wait()
        gain = gain_rows(gain_tile[...])[0:1]
        values = tok[...].astype(F32)
        _normed, inv = rms_forward(values, gain)
        grad_norm, gain_sum = rms_backward(values, inv, gain, total[...])
        grad_tokens[...] = grad_hidden[...] + grad_norm
        row = iota((16, width), 0)
        left_q[rows:, :] = jnp.where(row == 0, gain_sum, jnp.where(row == 1, gain_f[...], 0.0)).astype(BF16)
        yield
        for k in range(16):
            for u in UNITS:
                wires.settle(group_r.coming[u, k][0])
        products(left_q, right_q, "q", 1 - c, to_sib_q)
        group_q.start()
        yield
        products(left_q, right_q, "q", c, hold["q"])
        yield

    def window_sums(group):
        copies = {}
        for name in group:
            n = PIECES[name][0]
            for u in UNITS:
                s, w = unit_tiles(name, u, None)
                sums[name][:, s * 128 : (s + w) * 128] = hold[name][u][y, z]
            window = 48 if n == 80 else 32
            copies[name] = wires.remote(sums[name].at[pl.ds(mul((1 - lo) * 32, 16), window)], sides[name], xn)
        yield
        for name in group:
            copies[name].wait_recv()
            window = sides[name].shape[0]
            r = pl.ds(mul(lo * 32, 16), window)
            mids[name][...] = (sums[name][r, :].astype(F32) + sides[name][...].astype(F32)).astype(BF16)
            copies[name] = wires.remote(mids[name], fars[name], hn)
        yield
        fins = {"q": fin_q, "r": fin_r, "d": fin_d}
        for name in group:
            copies[name].wait_recv()
            accs[name][...] = mids[name][...].astype(F32) + fars[name][...].astype(F32)
            n = fins[name].shape[0]
            mine = core_lanes(name, c)
            copies[name] = wires.remote(
                accs[name].at[pl.ds(mul((1 - c) * 16, 16), n)], fins[name].at[:, mine], sib
            )
            fins[name][:, mine] = accs[name][pl.ds(mul(c * 16, 16), n), :]
        yield
        for name in group:
            copies[name].wait_recv()

    busy = work()
    for n, step in enumerate(group_r.steps[:24]):
        step()
        next(busy, None)
        if n in R_PIECES:
            next(experts, None)
    for _ in busy:
        pass
    rest = list(group_r.steps[24:])
    for n, step in enumerate(group_q.steps[:24]):
        step()
        if n in Q_PIECES:
            next(experts, None)
        if rest:
            rest.pop(0)()
    for _ in experts:
        pass
    interleave(group_q.steps[24:], window_sums("rd"))
    for _ in window_sums("q"):
        pass
    for k, i in pieces:
        across_piece(k, i).wait_send()

    @pl.when(owner)
    def _():
        for k in range(3):
            near_half(k).wait_recv()

    @pl.when(jnp.logical_not(owner))
    def _():
        for k in range(3):
            send_near(k).wait_send()
        for k, i in pieces:
            for core in (0, 1):
                coming_piece(k, i, core).wait_recv()

    @pl.when(hi == 1)
    def _():
        for copy in exchange_kv:
            copy.wait_send()

    wires.finish()


def backward(operands, parts):
    rows, width = operands[11].shape
    vmem, anywhere = pl.BlockSpec(memory_space=pltpu.VMEM), pl.BlockSpec(memory_space=pl.ANY)
    half = {name: PIECES[name][1] * 128 for name in PIECES}
    window = {"q": 48, "r": 48, "d": 32}
    fin = {"q": (32, Q_WIDE), "r": (32, R_WIDE), "d": (16, D_WIDE)}
    scratch = sum_scratch()
    scratch += [pltpu.VMEM((PIECES[name][0], half[name]), BF16) for name in PIECES]
    scratch += [pltpu.VMEM((window[name], half[name]), BF16) for _ in range(3) for name in PIECES]
    scratch += [pltpu.VMEM((window[name], half[name]), F32) for name in PIECES]
    scratch += [pltpu.VMEM((4, 4, 80, 1024), BF16)] * 2
    scratch += [
        pltpu.VMEM((rows, 2 * width), F32),
        pltpu.VMEM((rows, 2 * width), BF16),
        pltpu.VMEM((rows, 2 * width), BF16),
        pltpu.VMEM((rows + 16, width), BF16),
        pltpu.VMEM((rows + 16, Q_WIDE), BF16),
        pltpu.VMEM((rows, width), F32),
        pltpu.VMEM((2, width, 512), BF16),
        pltpu.VMEM((width, 128), BF16),
    ]
    sems = 4 + 3 * (32 + 2 * 4 * 5 + 3)
    scratch += [pltpu.SemaphoreType.DMA((n,)) for n in (sems, sems, 2, 3, 3, 3)]
    scratch += [pltpu.SemaphoreType.DMA((2, 3, 20))]
    spec = [vmem] * len(operands)
    spec[2] = spec[14] = anywhere
    return pl.pallas_call(
        backward_kernel,
        out_shape=tuple(shape(F32, *fin[name]) for name in PIECES)
        + tuple(shape(BF16, 2 * p.shape[0], p.shape[1]) for p in parts)
        + (shape(F32, rows, width),),
        in_specs=spec + [anywhere] * 3,
        out_specs=(vmem,) * 3 + (anywhere,) * 3 + (vmem,),
        scratch_shapes=scratch,
        compiler_params=pltpu.CompilerParams(collective_id=2, has_side_effects=True, vmem_limit_bytes=60 << 20),
        name="attend_back_sums",
    )(*operands, *parts)


PART_AXES = (("y", "z", "g"), ("z", "g", "y"), ("g", "y", "z")) * 2
PARTS = len(PART_AXES)
TURNS = (2, 1, 3, 0)


def lane_cuts(*sizes):
    return tuple((sum(sizes[:i]), n) for i, n in enumerate(sizes))


ROW_CUTS = lane_cuts(4, 4, 3, 3, 3, 3)
LAST_OUT_CUTS = lane_cuts(3, 3, 3, 3, 4, 5)
LAST_BACK_CUTS = lane_cuts(3, 3, 3, 3, 4, 4)


class Exchange:
    def __init__(self, outward, cuts, stages, sems, spot):
        self.outward, self.cuts, self.stages, self.spot = outward, cuts, stages, spot
        self.ssem, self.rsem, self.lsem = sems
        hi, y, z, lo, c = spot
        self.stays = c == hi
        self.moves = jnp.logical_not(self.stays)
        self.pending, self.sent, self.used = {}, [], [0, 0]

    def along(self, axis, k):
        hi, y, z, lo, c = self.spot
        q = {"y": y, "z": z}
        q[axis] = lax.rem(q[axis] + k, 4)
        return q[axis], device(hi, q["y"], q["z"], lo, c)

    def target(self, d, b):
        hi, y, z, lo, c = self.spot
        lo_, hi_, c_ = (lo, 1 - lo)[d], (hi, 1 - hi)[b], (c, 1 - c)[b]
        if self.outward:
            return device(hi_, y, z, lo_, hi), lo_ * 2 + hi_, lo * 2 + c, 2 * d + c
        return device(c, y, z, lo_, c_), lo_ * 2 + c_, lo * 2 + hi, 2 * d + hi

    def source(self, d, b):
        hi, y, z, lo, c = self.spot
        lo_, hi_, c_ = (lo, 1 - lo)[d], (hi, 1 - hi)[b], (c, 1 - c)[b]
        if self.outward:
            return device(c, y, z, lo_, c_), lo_ * 2 + c_, 2 * d + c_
        return device(hi_, y, z, lo_, hi), lo_ * 2 + hi_, 2 * d + hi_

    corners = ((1, 1), (0, 1), (1, 0))

    def greet(self):
        hi, y, z, lo, c = self.spot
        bar = pltpu.get_barrier_semaphore()

        def greet_one(to):
            pl.semaphore_signal(bar, inc=1, device_id=to, device_id_type=MESH)

        for axis in "yz":
            for k in (1, 2, 3):
                greet_one(self.along(axis, k)[1])
        for corner in self.corners:
            greet_one(self.source(*corner)[0])

        @pl.when(self.moves)
        def _():
            greet_one(self.source(0, 0)[0])
            pl.semaphore_wait(bar, 10 if self.outward else 11)

        @pl.when(self.stays)
        def _():
            if not self.outward:
                greet_one(device(hi, y, z, lo, 1 - c))
            pl.semaphore_wait(bar, 9)

    def view(self, ref, axis, v, cut, at):
        every = slice(None)
        first = every if at is None else at
        index = {"y": (v, every, every), "z": (first, v, every), "g": (first, every, v)}[axis]
        return ref.at[index + (every, pl.ds(cut[0] * 128, cut[1] * 128))]

    def remote(self, src, dst, k, tag, to):
        return pltpu.make_async_remote_copy(
            src_ref=src,
            dst_ref=dst,
            send_sem=self.ssem.at[k],
            recv_sem=self.rsem.at[tag],
            device_id=to,
            device_id_type=MESH,
        )

    def go(self, part, phase, turn=None, at=None):
        axis = PART_AXES[part][phase]
        hi, y, z, lo, c = self.spot
        waits = self.pending.setdefault((part, phase), [])
        for a, cuts in enumerate(self.cuts):
            src, dst = self.stages[phase][a], self.stages[phase + 1][a]
            cut = cuts[part]
            base, kept = self.used
            self.used[0] += 4
            self.used[1] += 1
            if axis != "g":
                here = y if axis == "y" else z
                rows = at if axis == "z" else None
                own = self.view(dst, axis, here, cut, rows)
                for k in (turn,) if axis == "y" and turn is not None else TURNS:
                    v, to = self.along(axis, k)
                    if k == 0:
                        keep = pltpu.make_async_copy(self.view(src, axis, here, cut, rows), own, self.lsem.at[kept])
                        keep.start()
                        waits.append(keep.wait)
                        continue
                    copy = self.remote(self.view(src, axis, v, cut, rows), own, base + k, base + k, to)
                    copy.start()
                    waits.append(copy.wait_recv)
                    self.sent.append(copy.wait_send)
                continue
            for d, b in self.corners:
                to, there, here, tag = self.target(d, b)
                copy = self.remote(
                    self.view(src, axis, there, cut, at), self.view(dst, axis, here, cut, at), base + 2 * d + b, base + tag, to
                )
                copy.start()
                self.sent.append(copy.wait_send)
                sender, place_, tag = self.source(d, b)
                block = self.view(dst, axis, place_, cut, at)
                waits.append(self.remote(block, block, base + 2 * d + b, base + tag, sender).wait_recv)
            self.go_corner(src, dst, cut, at, base, kept, waits)

    def go_corner(self, src, dst, cut, at, base, kept, waits):
        to, there, here, tag = self.target(0, 0)
        mine, landing = self.view(src, "g", there, cut, at), self.view(dst, "g", here, cut, at)
        keep = pltpu.make_async_copy(mine, landing, self.lsem.at[kept])
        copy = self.remote(mine, landing, base, base + tag, to)
        sender, place_, tag = self.source(0, 0)
        block = self.view(dst, "g", place_, cut, at)
        coming = self.remote(block, block, base, base + tag, sender)

        @pl.when(self.stays)
        def _():
            keep.start()

        @pl.when(self.moves)
        def _():
            copy.start()

        def wait_corner():
            @pl.when(self.stays)
            def _():
                keep.wait()

            @pl.when(self.moves)
            def _():
                coming.wait_recv()

        def wait_sent():
            @pl.when(self.moves)
            def _():
                copy.wait_send()

        waits.append(wait_corner)
        self.sent.append(wait_sent)

    def first(self, turn, at):
        for part in range(PARTS):
            self.go(part, 0, turn, at)

    def next(self, phase):
        for part in range(PARTS):
            self.wait(part, phase - 1)
            self.go(part, phase)

    def wait(self, part, phase):
        for wait in self.pending[part, phase]:
            wait()

    def finish(self):
        for part in range(PARTS):
            self.wait(part, 2)
        for wait in self.sent:
            wait()


def exchange_sems(arrays):
    return [pltpu.SemaphoreType.DMA((n * arrays,)) for n in (160, 160, 40)]


EVEN = 16


def even_places(slot_t):
    experts, rows = slot_t.shape
    wide = jnp.broadcast_to(slot_t[:, None, :], (experts, EVEN, rows))
    return wide == iota((experts, EVEN, rows), 1).astype(F32)


def loads(ins, bufs, sem, start=0):
    return [pltpu.make_async_copy(src, dst, sem.at[start + k]) for k, (src, dst) in enumerate(zip(ins, bufs))]


def route_kernel(
    tok, mixed, routes, grad, w_q, w_r, w_d,
    out_r, out_l, hidden_one, act, gates_t, slot_t, out_s, grad_in, grad_gu, grad_down,
    src_r, src_l, b1_r, b1_l, b2_r, b2_l, out_w, router_w, gains, sgu, sdown, hidden_s, ssem, rsem, lsem, wsem,
):
    spot = place()
    y = spot[1]
    rows, width = tok.shape
    inner = sdown.shape[0]
    first_loads = loads(
        (w_r.at[:, pl.ds(0, width)], w_r.at[:, pl.ds(ROUTER * 128, 128)], w_q.at[:, pl.ds(GAINS * 128, 128)]),
        (out_w, router_w, gains),
        wsem,
    )
    later_loads = loads((w_r.at[:, pl.ds(width, 2 * inner)], w_d), (sgu, sdown), wsem, 3)
    for copy in first_loads + later_loads:
        copy.start()
    swap = Exchange(
        True, (ROW_CUTS, LAST_OUT_CUTS), ((src_r, src_l), (b1_r, b1_l), (b2_r, b2_l), (out_r, out_l)), (ssem, rsem, lsem), spot
    )
    swap.greet()
    for copy in first_loads:
        copy.wait()
    hidden = tok[...].astype(F32) + dot(mixed[...], out_w[...])
    hidden_one[...] = hidden
    router = router_w[...]
    normed, _inv = rms_forward(hidden, gain_rows(gains[...])[1:2])
    low = normed.astype(BF16)
    act[...] = low
    expert = iota((rows, 128), 1)
    named = routes[...]
    member = named[:, 0:1] == expert
    for k in range(1, named.shape[1]):
        member = member | (named[:, k : k + 1] == expert)
    logits = jnp.where(member, dot(low, router), NEG_BIG)
    expo = jnp.where(member, jnp.exp(logits - jnp.max(logits, axis=-1, keepdims=True)), 0.0)
    gates_t[...] = (expo / jnp.sum(expo, axis=-1, keepdims=True)).T
    before = (iota((rows, rows), 1) < iota((rows, rows), 0)).astype(BF16)
    rank = dot(before, member.astype(BF16))
    slot_t[...] = jnp.where(member, rank, -1.0).T

    block = 16
    g = grad[...]
    for turn in TURNS:
        v = lax.rem(y + turn, 4)
        here = pl.ds(mul(v * block, block), block)
        slots = slot_t[here, :]
        places = even_places(slots)
        last = slots == float(EVEN)
        hot = places.astype(F32).reshape(block * EVEN, rows).astype(BF16)
        last_hot = last.astype(BF16)
        src_r[v, :, :, :, 0:width] = dot(hot, low).astype(BF16).reshape(4, 4, EVEN, width)
        src_r[v, :, :, :, width:] = dot(hot, g).astype(BF16).reshape(4, 4, EVEN, width)
        gt = gates_t[here, :]
        at_slot = jnp.sum(
            jnp.where(places, jnp.broadcast_to(gt[:, None, :], places.shape), 0.0).reshape(block * EVEN, rows),
            axis=-1,
            keepdims=True,
        )
        spread = jnp.broadcast_to(at_slot, (block * EVEN, 128)).reshape(block, EVEN, 128)
        lane_of = iota((block, EVEN, 128), 1) == iota((block, EVEN, 128), 2)
        even_gates = jnp.sum(jnp.where(lane_of, spread, 0.0), axis=1)
        last_gates = jnp.sum(jnp.where(last, gt, 0.0), axis=-1, keepdims=True)
        slot_gates = jnp.where(iota((block, 128), 1) == EVEN, last_gates, even_gates)
        src_l[v] = jnp.concatenate([dot(last_hot, low), dot(last_hot, g), slot_gates], axis=1).reshape(
            4, 4, 1, 2 * width + 128
        )
        swap.first(turn, v)

    for copy in later_loads:
        copy.wait()
    gate = dot(low, sgu[:, :inner])
    up_ = dot(low, sgu[:, inner:])
    silu, slope = silu_parts(gate)
    hidden_s[...] = (silu * up_).astype(BF16)
    grad_hidden = dot_t(g, sdown[...])
    grad_gu[:, :inner] = (grad_hidden * up_ * slope).astype(BF16)
    grad_gu[:, inner:] = (grad_hidden * silu).astype(BF16)
    swap.next(1)
    out_s[...] = dot(hidden_s[...], sdown[...])
    grad_in[...] = dot_t(grad_gu[...], sgu[...])
    swap.next(2)

    @pl.loop(0, inner // 256)
    def _(i):
        r = pl.ds(mul(i * 256, 256), 256)
        grad_down[r, :] = t_dot(hidden_s[:, r], grad[...]).astype(BF16)

    swap.finish()


def route(tokens, mixed, routes, grad, w_q, w_r, w_d):
    rows, width = tokens.shape
    vmem, anywhere = pl.BlockSpec(memory_space=pltpu.VMEM), pl.BlockSpec(memory_space=pl.ANY)
    r, last = (4, 4, 4, EVEN, 2 * width), (4, 4, 4, 1, 2 * width + 128)
    return pl.pallas_call(
        route_kernel,
        out_shape=(
            shape(BF16, *r),
            shape(F32, *last),
            shape(F32, rows, width),
            shape(BF16, rows, width),
            shape(F32, 128, rows),
            shape(F32, 128, rows),
            shape(F32, rows, width),
            shape(F32, rows, width),
            shape(BF16, rows, 2048),
            shape(BF16, 1024, width),
        ),
        in_specs=[vmem] * 4 + [anywhere] * 3,
        out_specs=(anywhere,) * 2 + (vmem,) * 8,
        scratch_shapes=[pltpu.VMEM(r, BF16), pltpu.VMEM(last, F32)] * 3
        + [
            pltpu.VMEM((width, width), BF16),
            pltpu.VMEM((width, 128), BF16),
            pltpu.VMEM((width, 128), BF16),
            pltpu.VMEM((width, 2048), BF16),
            pltpu.VMEM((1024, width), BF16),
            pltpu.VMEM((rows, 1024), BF16),
        ]
        + exchange_sems(2)
        + [pltpu.SemaphoreType.DMA((5,))],
        compiler_params=pltpu.CompilerParams(collective_id=3, has_side_effects=True, vmem_limit_bytes=56 << 20),
        name="route_shared",
    )(tokens, mixed, routes, grad, w_q, w_r, w_d)


def expert_rows(rows_r, rows_l, width):
    sources = 16
    last = rows_l.reshape(sources, rows_l.shape[-1])
    even = sources * EVEN
    both = rows_r.reshape(even, 2 * width)
    x = jnp.concatenate([both[:, :width], last[:, :width].astype(BF16)], axis=0)
    g = jnp.concatenate([both[:, width:].astype(F32), last[:, width : 2 * width]], axis=0)
    sent = last[:, 2 * width :]
    spread = jnp.broadcast_to(sent[:, None, :], (sources, EVEN, 128))
    own = iota((sources, EVEN, 128), 1) == iota((sources, EVEN, 128), 2)
    even_gates = jnp.sum(jnp.where(own, spread, 0.0).reshape(even, 128), axis=-1, keepdims=True)
    last_gates = jnp.sum(jnp.where(iota((sources, 128), 1) == EVEN, sent, 0.0), axis=-1, keepdims=True)
    return x, (jnp.concatenate([even_gates, last_gates], axis=0) * g).astype(BF16)


def expert_kernel(
    rows_r, rows_l, o0, o1, o2, e0, e1, e2,
    back_r, back_l, p0, p1, p2,
    src_r, src_l, b1_r, b1_l, b2_r, b2_l, in_r, in_l, w_gate, w_up, w_down, all_x, all_g, hidden, d_gate, d_up,
    g_gate, g_up, g_down, s_gate, s_up, s_down, ssem, rsem, lsem, wsem, isem, osem, xsem,
):
    spot = place()
    hi, y, z, lo, c = spot
    width = all_x.shape[1]
    outs, products, from_sib = (p0, p1, p2), (g_gate, g_up, g_down), (s_gate, s_up, s_down)
    weights = (w_gate, w_up, w_down)
    owner = c == hi
    swap = Exchange(
        False, (ROW_CUTS, LAST_BACK_CUTS), ((src_r, src_l), (b1_r, b1_l), (b2_r, b2_l), (back_r, back_l)), (ssem, rsem, lsem), spot
    )

    @pl.when(owner)
    def _():
        for copy in loads((e0, e1, e2), weights, wsem):
            copy.start()

    @pl.when(jnp.logical_not(owner))
    def _():
        for copy in loads((o0, o1, o2), weights, wsem):
            copy.start()

    def block(n):
        v = lax.rem(y + TURNS[n], 4)
        return v, loads((rows_r.at[v], rows_l.at[v]), (in_r.at[n % 2], in_l.at[n % 2]), isem.at[n % 2])

    coming = {0: block(0)[1]}
    for copy in coming[0]:
        copy.start()
    swap.greet()
    for copy in loads((e0, e1, e2), weights, wsem):
        copy.wait()
    step = all_x.shape[0] // 4
    even = 16 * EVEN
    for n, turn in enumerate(TURNS):
        v = lax.rem(y + turn, 4)
        if n + 1 < 4:
            coming[n + 1] = block(n + 1)[1]
            for copy in coming[n + 1]:
                copy.start()
        for copy in coming[n]:
            copy.wait()
        here = slice(n * step, (n + 1) * step)
        x, grad_result = expert_rows(in_r[n % 2], in_l[n % 2], width)
        all_x[here, :] = x
        all_g[here, :] = grad_result
        gate = dot(x, w_gate[...])
        up_ = dot(x, w_up[...])
        silu, slope = silu_parts(gate)
        low = (silu * up_).astype(BF16)
        hidden[here, :] = low
        grad_hidden = dot_t(grad_result, w_down[...])
        grad_gate = (grad_hidden * up_ * slope).astype(BF16)
        grad_up = (grad_hidden * silu).astype(BF16)
        d_gate[here, :] = grad_gate
        d_up[here, :] = grad_up
        result = dot(low, w_down[...]).astype(BF16)
        grad_in = (dot_t(grad_gate, w_gate[...]) + dot_t(grad_up, w_up[...])).astype(BF16)
        src_r[v, :, :, :, 0:width] = result[:even].reshape(4, 4, EVEN, width)
        src_r[v, :, :, :, width:] = grad_in[:even].reshape(4, 4, EVEN, width)
        src_l[v] = jnp.concatenate([result[even:], grad_in[even:]], axis=1).astype(F32).reshape(4, 4, 1, 2 * width)
        swap.first(turn, v)

    def half(k, core):
        n = products[k].shape[0] // 2
        return products[k].at[pl.ds(mul(core * n, 16), n)]

    def trade(k):
        return pltpu.make_async_remote_copy(
            src_ref=half(k, 1 - c),
            dst_ref=from_sib[k],
            send_sem=xsem.at[0, k],
            recv_sem=xsem.at[1, k],
            device_id=device(hi, y, z, lo, 1 - c),
            device_id_type=MESH,
        )

    def product(k, left, right, wide):
        out = products[k]

        @pl.loop(0, out.shape[0] // wide)
        def _(i):
            r = pl.ds(mul(i * wide, wide), wide)
            out[r, :] = t_dot(left[:, r], right[...]).astype(BF16)

        trade(k).start()

    def add(k):
        trade(k).wait_recv()
        n = products[k].shape[0] // 2

        @pl.loop(0, n // 64)
        def _(i):
            own = pl.ds(mul(c * n + i * 64, 64), 64)
            more = from_sib[k][pl.ds(mul(i * 64, 64), 64), :].astype(F32)
            products[k][own, :] = (products[k][own, :].astype(F32) + more).astype(BF16)

        copy = pltpu.make_async_copy(half(k, c), outs[k], osem.at[k])
        copy.start()
        return copy

    product(0, all_x, d_gate, 256)
    swap.next(1)
    product(1, all_x, d_up, 256)
    product(2, hidden, all_g, 128)
    kept = [add(0)]
    swap.next(2)
    kept += [add(1), add(2)]
    swap.finish()
    for k in range(3):
        trade(k).wait_send()
        kept[k].wait()


def expert(rows_r, rows_l, passed, own):
    width = rows_r.shape[-1] // 2
    inner = own[0].shape[1]
    total = 64 * (EVEN + 1)
    anywhere = pl.BlockSpec(memory_space=pl.ANY)
    r, last = (4, 4, 4, EVEN, 2 * width), (4, 4, 4, 1, 2 * width)
    return pl.pallas_call(
        expert_kernel,
        out_shape=(shape(BF16, *r), shape(F32, *last)) + tuple(shape(BF16, w.shape[0] // 2, w.shape[1]) for w in own),
        in_specs=[anywhere] * 8,
        out_specs=(anywhere,) * 5,
        scratch_shapes=[pltpu.VMEM(r, BF16), pltpu.VMEM(last, F32)] * 3
        + [pltpu.VMEM((2,) + rows_r.shape[1:], BF16), pltpu.VMEM((2,) + rows_l.shape[1:], F32)]
        + [pltpu.VMEM(w.shape, BF16) for w in own]
        + [pltpu.VMEM((total, n), BF16) for n in (width, width, inner, inner, inner)]
        + [pltpu.VMEM(w.shape, BF16) for w in own]
        + [pltpu.VMEM((w.shape[0] // 2, w.shape[1]), BF16) for w in own]
        + exchange_sems(2)
        + [pltpu.SemaphoreType.DMA(n) for n in ((3,), (2, 2), (3,), (2, 3))],
        compiler_params=pltpu.CompilerParams(collective_id=4, has_side_effects=True, vmem_limit_bytes=62 << 20),
        name="expert_back",
    )(rows_r, rows_l, *passed, *own)


def split_terms(w):
    top = w.astype(BF16)
    rest = w - top.astype(F32)
    mid = rest.astype(BF16)
    return top, mid, (rest - mid.astype(F32)).astype(BF16)


def combine_kernel(
    back_r, back_l, slot_t, gates_t, grad, hidden_one, out_s, grad_in_s, mixed, act, grad_gu, router_w, out_w, gains,
    layer_out, grad_hidden, grad_mixed, left, right, grad_gain,
):
    experts = back_r.shape[0]
    rows, width = hidden_one.shape
    slots = slot_t[0:experts, :]
    places = even_places(slots)
    last = slots == float(EVEN)
    out_rows = back_r[:, :, :width].reshape(experts * EVEN, width)
    last_l = back_l[...].reshape(experts, 2 * width).astype(BF16)
    gt = gates_t[0:experts, :]
    even_w = jnp.where(places, jnp.broadcast_to(gt[:, None, :], places.shape), 0.0).reshape(experts * EVEN, rows)
    last_w = jnp.where(last, gt, 0.0)
    routed = jnp.zeros((rows, width), F32)
    for e_term, l_term in zip(split_terms(even_w), split_terms(last_w)):
        routed = routed + t_dot(e_term, out_rows) + t_dot(l_term, last_l[:, :width])
    hidden = hidden_one[...]
    layer_out[...] = (hidden + out_s[...] + routed).astype(BF16)
    g = grad[...]
    dots = dot_t(out_rows, g).reshape(experts, EVEN, rows)
    dots_last = dot_t(last_l[:, :width], g)
    grad_gates = jnp.sum(jnp.where(places, dots, 0.0), axis=1) + jnp.where(last, dots_last, 0.0)
    logits_t = gt * (grad_gates - jnp.sum(gt * grad_gates, axis=0, keepdims=True))
    low_logits = jnp.concatenate([logits_t, jnp.zeros((128 - experts, rows), F32)], axis=0).T.astype(BF16)
    hot = places.astype(F32).reshape(experts * EVEN, rows).astype(BF16)
    grad_routed = t_dot(hot, back_r[:, :, width:].reshape(experts * EVEN, width)) + t_dot(last.astype(BF16), last_l[:, width:])
    router = router_w[...]
    grad_act = grad_routed + dot_t(low_logits, router) + grad_in_s[...]
    gain = gain_rows(gains[...])[1:2]
    _normed, inv = rms_forward(hidden, gain)
    grad_norm, gain_sum = rms_backward(hidden, inv, gain, grad_act)
    grad_gain[...] = gain_sum
    total = g.astype(F32) + grad_norm
    grad_hidden[...] = total
    low = total.astype(BF16)
    left[0:rows, :] = mixed[...]
    left[rows:, :] = act[...]
    right[0:rows, :width] = low
    right[0:rows, width:] = jnp.zeros((rows, R_WIDE - width), BF16)
    right[rows:, :width] = jnp.zeros((rows, width), BF16)
    right[rows:, width : ROUTER * 128] = grad_gu[...]
    right[rows:, ROUTER * 128 : (ROUTER + 1) * 128] = low_logits
    right[rows:, (ROUTER + 1) * 128 :] = jnp.zeros((rows, R_WIDE - (ROUTER + 1) * 128), BF16)
    grad_mixed[...] = dot_t(low, out_w[...]).astype(BF16)


def combine(operands, w_r, w_q):
    rows, width = operands[5].shape
    whole = lambda a: pl.BlockSpec(a.shape, lambda i: (0,) * len(a.shape))
    outs = (
        shape(BF16, rows, width),
        shape(F32, rows, width),
        shape(BF16, rows, width),
        shape(BF16, 2 * rows, width),
        shape(BF16, 2 * rows, R_WIDE),
        shape(F32, 1, width),
    )
    return pl.pallas_call(
        combine_kernel,
        grid=(1,),
        out_shape=outs,
        in_specs=[whole(a) for a in operands]
        + [
            pl.BlockSpec((width, 128), lambda i: (0, ROUTER)),
            pl.BlockSpec((width, 1280), lambda i: (0, 0)),
            pl.BlockSpec((width, 128), lambda i: (0, GAINS)),
        ],
        out_specs=tuple(whole(a) for a in outs),
        compiler_params=pltpu.CompilerParams(vmem_limit_bytes=56 << 20),
        name="combine",
    )(*operands, w_r, w_r, w_q)


def finish_kernel(
    p0, p1, p2, t0, t1, t2, fin_q, fin_r, fin_d,
    g0, g1, g2, query, key, value, out, router, gate, up_, down, gains,
):
    i = pl.program_id(0)
    hi, _y, _z, lo, c = place()
    half = i // (pl.num_programs(0) // 2)
    here = jnp.logical_and(c == hi, half == c)
    for part, total, whole in ((p0, t0, g0), (p1, t1, g1), (p2, t2, g2)):

        @pl.when(here)
        def _(part=part, whole=whole):
            whole[...] = part[...].astype(F32)

        @pl.when(jnp.logical_not(here))
        def _(total=total, whole=whole):
            whole[...] = total[...].astype(F32)

    own_rows, width = query.shape
    tile = ROUTER * 128
    for place_ in range(4):

        @pl.when((i == 0) & (lo * 2 + c == place_))
        def _(rows=slice(4 * place_, 4 * place_ + own_rows)):
            query[...] = fin_q[rows, 0:width]
            key[...] = fin_q[rows, width : 2 * width]
            value[...] = fin_q[rows, 2 * width : 3 * width]
            out[...] = fin_r[rows, 0:width]
            router[...] = fin_r[rows, tile : tile + router.shape[1]]
            wide, narrow = 1024, gate.shape[1]
            row, col = iota((wide, narrow), 0), iota((wide, narrow), 1)
            pick = ((col == row - 2 * (row // 16)) & (lax.rem(row, 16) < 14)).astype(BF16)
            for dst, start in ((gate, width), (up_, width + wide)):
                dst[...] = sum(dot(t, pick) for t in split_terms(fin_r[rows, start : start + wide]))
            column = (iota((8, 128), 1) == iota((8, 128), 0)).astype(BF16)
            both = sum(dot_t(column, t) for t in split_terms(fin_q[:, GAINS * 128 : (GAINS + 1) * 128]))
            gains[...] = both[:, rows]

    @pl.when(i == 0)
    def _():
        down[...] = fin_d[0 : down.shape[0], :]


def finish(parts, sums, fin_q, fin_r, fin_d, own_rows, experts, inner):
    steps = 4
    width = fin_d.shape[1]
    whole = lambda a: pl.BlockSpec(a.shape, lambda i: (0, 0))
    block = lambda a: pl.BlockSpec((a.shape[0] // steps, a.shape[1]), lambda i: (i, 0))
    first = steps // 2

    def own_step(i):
        hi, core = lax.axis_index("seq"), lax.rem(lax.axis_index("exp"), 2)
        j = jnp.clip(i - core * first, 0, first - 1)
        return jnp.where(hi == core, j, 0)

    def total_step(i):
        hi, core = lax.axis_index("seq"), lax.rem(lax.axis_index("exp"), 2)
        inside = jnp.logical_and(hi == core, i // first == core)
        return jnp.where(inside, jnp.where(core == 0, first, first - 1), i)

    half_block = lambda a: pl.BlockSpec((2 * a.shape[0] // steps, a.shape[1]), lambda i: (own_step(i), 0))
    total_block = lambda a: pl.BlockSpec((a.shape[0] // steps, a.shape[1]), lambda i: (total_step(i), 0))
    small = (
        [shape(F32, own_rows, width)] * 4
        + [shape(F32, own_rows, experts)]
        + [shape(F32, own_rows, inner)] * 2
        + [shape(F32, inner // experts, width), shape(F32, 8, own_rows)]
    )
    return pl.pallas_call(
        finish_kernel,
        grid=(steps,),
        out_shape=[shape(F32, *t.shape) for t in sums] + small,
        in_specs=[half_block(p) for p in parts] + [total_block(t) for t in sums] + [whole(a) for a in (fin_q, fin_r, fin_d)],
        out_specs=[block(t) for t in sums] + [whole(a) for a in small],
        compiler_params=pltpu.CompilerParams(vmem_limit_bytes=60 << 20),
        name="finish",
    )(*parts, *sums, fin_q, fin_r, fin_d)


def per_device(
    tokens,
    cotangent,
    segments,
    routes,
    norm_gain_attn,
    w_query,
    w_key,
    w_value,
    w_out,
    norm_gain_ffn,
    w_router,
    shared_gate,
    shared_up,
    shared_down,
    expert_gate,
    expert_up,
    expert_down,
):
    rows = tokens.shape[1]
    width = tokens.shape[2]
    experts = w_router.shape[1]
    tokens, grad, routes = tokens[0], cotangent[0], routes[0]
    own_experts = (expert_gate[0], expert_up[0], expert_down[0])

    own_rows = w_query.shape[0]
    shards = (w_query, w_key, w_value, w_out, shared_gate, shared_up, w_router)
    shards += (norm_gain_attn.reshape(1, -1), norm_gain_ffn.reshape(1, -1), shared_down)
    cos, sin = rotary_tables(2 * rows)
    w_q, w_r, w_d, expert_w, act_attn, q, kv, prior, mixed = forward(
        shards, own_experts, tokens, cos, sin, segments
    )
    rows_r, rows_l, hidden_one, act_ffn, gates_t, slot_t, out_s, grad_in_s, grad_gu, grad_sdown = route(
        tokens, mixed, routes, grad, w_q, w_r, w_d
    )
    back_r, back_l, *parts = expert(rows_r, rows_l, expert_w, own_experts)
    back_r, back_l = (a.reshape((experts,) + a.shape[3:]) for a in (back_r, back_l))
    layer_out, grad_hidden, grad_mixed, left_r, right_r, gain_ffn = combine(
        (back_r, back_l, slot_t, gates_t, grad, hidden_one, out_s, grad_in_s, mixed, act_ffn, grad_gu), w_r, w_q
    )
    fin_q, fin_r, fin_d, *sums, grad_tokens = backward(
        (left_r, right_r, grad_sdown.reshape(4, 4, 64, width), act_attn, q, kv, prior, segments)
        + (grad_mixed, cos, sin, tokens, grad_hidden, gain_ffn, w_q),
        parts,
    )
    *expert_grads, query, key, value, out, router, gate, up_grad, down, gains = finish(
        parts, sums, fin_q, fin_r, fin_d, own_rows, experts, shared_gate.shape[1]
    )
    return (
        layer_out[None],
        grad_tokens[None],
        gains[0],
        query,
        key,
        value,
        out,
        gains[1],
        router,
        gate,
        up_grad,
        down,
        *(g[None] for g in expert_grads),
    )


def solution(mesh):
    rows = P("exp", None)
    deep = P("exp", None, None)
    split = P("exp", "seq", None)
    gain = P("exp")
    in_specs = (split, split, rows, split, gain, rows, rows, rows, rows, gain) + (rows,) * 4 + (deep,) * 3
    out_specs = (split, split, gain, rows, rows, rows, rows, gain) + (rows,) * 4 + (deep,) * 3
    return jax.shard_map(per_device, mesh=mesh, in_specs=in_specs, out_specs=out_specs, check_vma=False)
```

```python
import functools
import jax
import jax.numpy as jnp
import numpy as np
from jax import lax
from jax.experimental import pallas as pl
from jax.experimental.pallas import tpu as pltpu
from jax.sharding import PartitionSpec as P

HEADS = 10
EPSILON = 1e-06
NEG_BIG = -1e30
F32 = jnp.float32
BF16 = jnp.bfloat16
MESH = pl.DeviceIdType.MESH

PIECES = {
    "q": (80, 16, ((0, 8, 4), (8, 8, 4))),
    "r": (80, 14, ((0, 7, 4), (7, 7, 4))),
    "d": (64, 5, ((0, 3, 2), (3, 2, 1))),
}
Q_WIDE, R_WIDE, D_WIDE = 4096, 3584, 1280
GAINS = 30
ROUTER = 26
UNITS = (0, 1)


def place():
    hi = lax.axis_index("seq")
    e = lax.axis_index("exp")
    return hi, e // 16, lax.rem(e // 4, 4), lax.rem(e // 2, 2), lax.rem(e, 2)


def device(hi, y, z, lo, c):
    return (hi, ((y * 4 + z) * 2 + lo) * 2 + c)


def up(v):
    return lax.rem(v + 1, 4)


def dn(v):
    return lax.rem(v + 3, 4)


def opp(v):
    return lax.rem(v + 2, 4)


def mul(v, m=128):
    return pl.multiple_of(v, m)


def greet(devices):
    bar = pltpu.get_barrier_semaphore()
    for to in devices:
        pl.semaphore_signal(bar, inc=1, device_id=to, device_id_type=MESH)
    pl.semaphore_wait(bar, len(devices))


class Sender:
    def __init__(self, send_sem, recv_sem, local_sem):
        self.sems = (send_sem, recv_sem, local_sem)
        self.sent = []
        self.kept = 0

    def describe(self, src, dst, to):
        k = len(self.sent)
        self.sent.append(None)
        return pltpu.make_async_remote_copy(
            src_ref=src,
            dst_ref=dst,
            send_sem=self.sems[0].at[k],
            recv_sem=self.sems[1].at[k],
            device_id=to,
            device_id_type=MESH,
        )

    def remote(self, src, dst, to):
        copy = self.describe(src, dst, to)
        copy.start()
        self.sent[-1] = copy
        return copy

    def local(self, src, dst):
        copy = pltpu.make_async_copy(src, dst, self.sems[2].at[self.kept])
        self.kept += 1
        copy.start()
        return copy

    def settle(self, copy):
        copy.wait_send()
        self.sent = [None if one is copy else one for one in self.sent]

    def finish(self):
        for copy in self.sent:
            if copy is not None:
                copy.wait_send()


def arrived(copies):
    for copy in copies:
        copy.wait_recv()


def ring_neighbours(hi, y, z, lo, c):
    return {
        ("y", 1): device(hi, up(y), z, lo, c),
        ("y", -1): device(hi, dn(y), z, lo, c),
        ("z", 1): device(hi, y, up(z), lo, c),
        ("z", -1): device(hi, y, dn(z), lo, c),
        ("y", 2): device(hi, opp(y), z, lo, c),
        ("z", 2): device(hi, y, opp(z), lo, c),
    }


def unit_tiles(piece, u, half):
    s, w, w0 = PIECES[piece][2][u]
    return ((s, w0), (s + w0, w - w0))[half] if half is not None else (s, w)


def lanes(piece, u, half, core):
    s, w = unit_tiles(piece, u, half)
    return pl.ds(mul(core * (PIECES[piece][1] * 128) + s * 128), w * 128)


def core_lanes(piece, core):
    n = PIECES[piece][1] * 128
    return pl.ds(mul(core * n), n)


def interleave(steps, work):
    for step in steps:
        step()
        next(work, None)
    for _ in work:
        pass


def dot(a, b):
    return jnp.dot(a, b, preferred_element_type=F32)


def dot_t(a, b):
    return lax.dot_general(a, b, (((1,), (1,)), ((), ())), preferred_element_type=F32)


def t_dot(a, b):
    return lax.dot_general(a, b, (((0,), (0,)), ((), ())), preferred_element_type=F32)


def iota(shape, dim):
    return lax.broadcasted_iota(jnp.int32, shape, dim)


def shape(dtype, *dims):
    return jax.ShapeDtypeStruct(dims, dtype)


def gain_rows(tile):
    pick = (iota((8, 128), 1) == iota((8, 128), 0)).astype(BF16)
    return dot_t(pick, tile)


def rms_forward(values, gain):
    inv_rms = lax.rsqrt(jnp.mean(values * values, axis=-1, keepdims=True) + EPSILON)
    return values * inv_rms * gain, inv_rms


def rms_backward(values, inv_rms, gain, upstream):
    weighted = upstream * gain
    inner = jnp.mean(weighted * values, axis=-1, keepdims=True)
    grad_in = inv_rms * weighted - values * (inv_rms * inv_rms * inv_rms) * inner
    grad_gain = jnp.sum(upstream * values * inv_rms, axis=0, keepdims=True)
    return grad_in, grad_gain


def rotary_tables(rows):
    freq = np.power(10000.0, -2.0 * np.arange(64) / 128)
    angles = np.arange(rows)[:, None] * freq[None, :]
    cos, sin = np.cos(angles), np.sin(angles)
    return (
        jnp.asarray(np.concatenate([cos, cos], axis=1), F32),
        jnp.asarray(np.concatenate([-sin, sin], axis=1), F32),
    )


def silu_parts(pre_act):
    sigma = jax.nn.sigmoid(pre_act)
    return (pre_act * sigma, sigma * (1.0 + pre_act * (1.0 - sigma)))


def seq_rows():
    return pl.ds(mul(lax.axis_index("seq") * 128), 128)


def allowed_keys(seg_row):
    hi = lax.axis_index("seq")
    rows = seg_row.shape[1] // 2
    across = lambda at: jnp.broadcast_to(seg_row[:, at].astype(F32), (rows, rows))
    here = across(seq_rows())
    mine = here.T
    own = (here == mine) & (iota((rows, rows), 1) <= iota((rows, rows), 0))
    prior = (across(slice(0, rows)) == mine) & (hi == 1)
    return own, prior


def head_probs(h, q, kv, prior, own_ok, prior_ok, width):
    here = slice(h * 128, (h + 1) * 128)
    behind = slice(width + h * 128, width + (h + 1) * 128)
    query = q[:, here]
    keys = jnp.concatenate([prior[:, here], kv[:, here]], axis=0)
    values = jnp.concatenate([prior[:, behind], kv[:, behind]], axis=0)
    scores = dot_t(query, keys) * (128.0**-0.5)
    rows = query.shape[0]
    scores = jnp.concatenate(
        [jnp.where(prior_ok, scores[:, :rows], NEG_BIG), jnp.where(own_ok, scores[:, rows:], NEG_BIG)], axis=1
    )
    expo = jnp.exp(scores - jnp.max(scores, axis=-1, keepdims=True))
    return query, keys, values, expo / jnp.sum(expo, axis=-1, keepdims=True)


class Gather:
    def __init__(self, wires, names, blocks, outs, spot):
        hi, y, z, lo, c = spot
        self.wires, self.names, self.outs, self.core = wires, names, outs, c
        self.sib = device(hi, y, z, lo, 1 - c)
        nb = ring_neighbours(hi, y, z, lo, c)
        self.keep = []
        units = []
        for u in UNITS:
            a1, a2 = ("y", "z") if u == 0 else ("z", "y")
            p1, p2 = (y, z) if u == 0 else (z, y)
            units.append(
                dict(p1=p1, p2=p2, up1=nb[a1, 1], dn1=nb[a1, -1], up2=nb[a2, 1], dn2=nb[a2, -1], got={}, second=[], sib=[])
            )
        self.units = units
        self.steps = [functools.partial(self.own_block, blocks, y, z)]
        for u in UNITS:
            self.steps.append(functools.partial(self.first_axis, u, "up1", 0))
        for u in UNITS:
            self.steps.append(functools.partial(self.first_axis, u, "dn1", 1))
        for u in UNITS:
            self.steps.append(functools.partial(self.first_far, u))
        turn = (lambda p: p, dn, up, opp)
        self.near, self.far = [], []
        for k in range(4):
            for u in UNITS:
                q1 = turn[k](units[u]["p1"])
                self.near.append(functools.partial(self.second_axis, u, k, q1))
                self.far.append(functools.partial(self.second_far, u, k, q1))

    def region(self, name, u, half, q1, q2):
        by, bz = (q1, q2) if u == 0 else (q2, q1)
        return self.outs[name].at[by, bz, :, lanes(name, u, half, self.core)]

    def send(self, u, half, q1, q2, to, src=None):
        copies = []
        for name in self.names:
            dst = self.region(name, u, half, q1, q2)
            copies.append(self.wires.remote(src[name] if src else dst, dst, to))
        return copies

    def spread(self, u, q1, src=None):
        unit = self.units[u]
        at = (q1, unit["p2"])
        unit["second"].append((self.send(u, None, *at, unit["up2"], src), self.send(u, None, *at, unit["dn2"], src)))
        unit["sib"].append(self.send(u, None, *at, self.sib, src))

    def own_block(self, blocks, y, z):
        for name in self.names:
            self.keep.append(self.wires.local(blocks[name], self.outs[name].at[y, z, :, core_lanes(name, self.core)]))
        for u, unit in enumerate(self.units):
            src = {}
            for name in self.names:
                s, w = unit_tiles(name, u, None)
                src[name] = blocks[name].at[:, pl.ds(s * 128, w * 128)]
            at = (unit["p1"], unit["p2"])
            unit["got"]["up1"] = self.send(u, None, *at, unit["up1"], src)
            unit["got"]["dn1"] = self.send(u, None, *at, unit["dn1"], src)
            self.spread(u, unit["p1"], src)

    def first_axis(self, u, way, half):
        unit = self.units[u]
        arrived(unit["got"][way])
        q1 = dn(unit["p1"]) if way == "up1" else up(unit["p1"])
        unit["got"]["far", half] = self.send(u, half, q1, unit["p2"], unit[way])
        self.spread(u, q1)

    def first_far(self, u):
        unit = self.units[u]
        arrived(unit["got"]["far", 0])
        arrived(unit["got"]["far", 1])
        self.spread(u, opp(unit["p1"]))

    def second_axis(self, u, k, q1):
        unit = self.units[u]
        for half, way, turn in ((0, "up2", dn), (1, "dn2", up)):
            arrived(unit["second"][k][half])
            at = (q1, turn(unit["p2"]))
            unit["got"][k, half] = self.send(u, half, *at, unit[way])
            unit["sib"].append(self.send(u, None, *at, self.sib))

    def second_far(self, u, k, q1):
        unit = self.units[u]
        arrived(unit["got"][k, 0])
        arrived(unit["got"][k, 1])
        unit["sib"].append(self.send(u, None, q1, opp(unit["p2"]), self.sib))

    def finish(self):
        for unit in self.units:
            for copies in unit["sib"]:
                arrived(copies)
        for copy in self.keep:
            copy.wait()


def window_block(first, second, shift):
    n = first.shape[0]
    return first[0:shift], first[shift:n] + second[0 : n - shift], second[n - shift : n]


def make_windows(j, shards, win_q, win_r, win_d):
    query_w, key_w, value_w, out_w, gate_w, up_w, router_w, gain_a, gain_f, down_w = shards
    own_rows, width = query_w.shape
    place_rows = (iota((32, own_rows), 0) == iota((32, own_rows), 1) + 4 * j).astype(BF16)
    put = lambda w: dot(place_rows, w).astype(BF16)
    for k, w in enumerate((query_w, key_w, value_w)):
        win_q[:, k * width : (k + 1) * width] = put(w[...])
    row = iota((8, own_rows), 0)
    gains = jnp.where(row == 0, gain_a[...].astype(F32), jnp.where(row == 1, gain_f[...].astype(F32), 0.0)).astype(BF16)
    column = (iota((8, 128), 1) == iota((8, 128), 0)).astype(BF16)
    win_q[:, GAINS * 128 : (GAINS + 1) * 128] = put(t_dot(gains, column).astype(BF16))
    win_q[:, (GAINS + 1) * 128 :] = jnp.zeros((32, 128), BF16)
    win_r[:, 0:width] = put(out_w[...])
    narrow, wide = gate_w.shape[1], 1024
    row, col = iota((narrow, wide), 0), iota((narrow, wide), 1)
    spread = ((row == col - 2 * (col // 16)) & (lax.rem(col, 16) < 14)).astype(BF16)
    for k, w in enumerate((gate_w, up_w)):
        win_r[:, width + k * wide : width + (k + 1) * wide] = dot(put(w[...]), spread).astype(BF16)
    start, n = ROUTER * 128, router_w.shape[1]
    win_r[:, start:] = jnp.concatenate([put(router_w[...]), jnp.zeros((32, 256 - n), BF16)], axis=1)
    n = down_w.shape[0]
    place_rows = (iota((16, n), 0) == iota((16, n), 1)).astype(BF16)
    win_d[...] = dot(place_rows, down_w[...]).astype(BF16)


def forward_kernel(
    query_w, key_w, value_w, out_w, gate_w, up_w, router_w, gain_a, gain_f, down_w, e0, e1, e2, tok, cos, sin, seg_row,
    out_q, out_r, out_d, o0, o1, o2, act, q, kv, prior, mixed,
    win_q, win_r, win_d, sib_q, sib_r, pair_q, pair_r, side_q, side_r, blk_q, blk_r, blk_d, w_buf, ssem, rsem, lsem, esem, wsem,
):
    spot = place()
    hi, y, z, lo, c = spot
    sib = device(hi, y, z, lo, 1 - c)
    xn = device(hi, y, z, 1 - lo, c)
    hn = device(1 - hi, y, z, lo, c)
    width = tok.shape[1]
    make_windows(
        lo * 2 + c, (query_w, key_w, value_w, out_w, gate_w, up_w, router_w, gain_a, gain_f, down_w), win_q, win_r, win_d
    )
    greet([sib, xn, hn] + list(ring_neighbours(*spot).values()))
    wires = Sender(ssem, rsem, lsem)
    owner = c == hi

    @pl.when(hi == 0)
    def _():
        prior[...] = jnp.zeros_like(prior)

    j = lo * 2 + c
    windows = {"q": (win_q, sib_q, pair_q, side_q, blk_q), "r": (win_r, sib_r, pair_r, side_r, blk_r)}
    swaps = {}
    for name in "qr":
        win, from_sib = windows[name][:2]
        swaps[name] = wires.remote(win.at[:, core_lanes(name, 1 - c)], from_sib, sib)
    r16 = pl.ds(mul(j * 16, 16), 16)
    swap_d = wires.remote(win_d.at[:, core_lanes("d", 1 - c)], blk_d.at[r16], sib)
    blk_d[r16, :] = win_d[:, core_lanes("d", c)]
    across = {}
    for name in "qr":
        win, from_sib, pair, side, _blk = windows[name]
        own = win[:, core_lanes(name, c)]
        swaps[name].wait_recv()
        got = from_sib[...]
        pair[0:16], pair[16:32], pair[32:48] = window_block(
            jnp.where(c == 0, own, got), jnp.where(c == 0, got, own), 16
        )
        across[name] = wires.remote(pair, side, xn)
    swap_d.wait_recv()
    r32 = pl.ds(mul(lo * 32, 16), 32)
    across_d = wires.remote(blk_d.at[r32], blk_d.at[r32], xn)

    def pass_expert(k):
        return pltpu.make_async_remote_copy(
            src_ref=(e0, e1, e2)[k],
            dst_ref=(o0, o1, o2)[k],
            send_sem=esem.at[0, k],
            recv_sem=esem.at[1, k],
            device_id=sib,
            device_id_type=MESH,
        )

    blocks = {"q": blk_q, "r": blk_r, "d": blk_d}
    outs = {"q": out_q, "r": out_r, "d": out_d}
    group_q = Gather(wires, "q", blocks, outs, spot)
    group_r = Gather(wires, "rd", blocks, outs, spot)

    def whole_block(name):
        _win, _sib, pair, side, blk = windows[name]
        across[name].wait_recv()
        own, got = pair[...], side[...]
        blk[0:32], blk[32:48], blk[48:80] = window_block(
            jnp.where(lo == 0, own, got), jnp.where(lo == 0, got, own), 32
        )

    whole_block("q")
    for step in group_q.steps:
        step()
    whole_block("r")
    across_d.wait_recv()
    for step in group_q.near:
        step()
    group_r.steps[0]()
    for step in group_q.far:
        step()
    group_q.finish()

    @pl.when(owner)
    def _():
        for k in range(3):
            pass_expert(k).start()

    def load(i, slot):
        return pltpu.make_async_copy(out_q.at[:, :, :, pl.ds(i * 512, 512)], w_buf.at[slot], wsem.at[slot])

    later = wires.describe(kv, prior, hn)

    def work():
        order = (7, 2, 3, 4, 5, 6, 0, 1)
        here = seq_rows()
        cosine, sine = cos[here, :], sin[here, :]
        load(order[0], 0).start()
        for n, i in enumerate(order):
            slot = n % 2
            load(i, slot).wait()
            if n + 1 < len(order):
                load(order[n + 1], 1 - slot).start()
            w = w_buf[slot].reshape(width, 512)
            if n == 0:
                gains = gain_rows(w[:, (GAINS - 28) * 128 : (GAINS - 27) * 128])
                normed, _inv = rms_forward(tok[...].astype(F32), gains[0:1])
                act[...] = normed.astype(BF16)
                w = w[:, :256]
            x = dot(act[...], w)
            for t in range(w.shape[1] // 128):
                tile = 4 * i + t
                v = x[:, t * 128 : (t + 1) * 128]
                if tile < 20:
                    v = v * cosine + pltpu.roll(v, 64, 1) * sine
                if tile < 10:
                    q[:, tile * 128 : (tile + 1) * 128] = v.astype(BF16)
                else:
                    kv[:, (tile - 10) * 128 : (tile - 9) * 128] = v.astype(BF16)
            if i == 6:

                @pl.when(hi == 0)
                def _():
                    later.start()

            yield
        for _ in range(4):
            yield

        @pl.when(hi == 1)
        def _():
            later.wait_recv()

        own_ok, prior_ok = allowed_keys(seg_row)
        for h in range(HEADS):
            _query, _keys, values, probs = head_probs(h, q, kv, prior, own_ok, prior_ok, width)
            mixed[:, h * 128 : (h + 1) * 128] = dot(probs.astype(BF16), values).astype(BF16)
            yield

    interleave(group_r.steps[1:] + group_r.near + group_r.far + [group_r.finish], work())

    @pl.when(hi == 0)
    def _():
        later.wait_send()

    @pl.when(owner)
    def _():
        for k in range(3):
            pass_expert(k).wait_send()

    @pl.when(jnp.logical_not(owner))
    def _():
        for k in range(3):
            pass_expert(k).wait_recv()

    wires.finish()


def forward(shards, experts, tokens, cos, sin, seg_row):
    rows, width = tokens.shape
    sems = 2 + 1 + 3 + 36 * 2 * 3 + 8
    vmem, anywhere = pl.BlockSpec(memory_space=pltpu.VMEM), pl.BlockSpec(memory_space=pl.ANY)
    half = {name: PIECES[name][1] * 128 for name in PIECES}
    out = pl.pallas_call(
        forward_kernel,
        out_shape=(
            shape(BF16, 4, 4, 80, Q_WIDE),
            shape(BF16, 4, 4, 80, R_WIDE),
            shape(BF16, 4, 4, 64, D_WIDE),
            *(shape(BF16, *w.shape) for w in experts),
            shape(BF16, rows, width),
            shape(BF16, rows, width),
            shape(BF16, rows, 2 * width),
            shape(BF16, rows, 2 * width),
            shape(BF16, rows, width),
        ),
        in_specs=[vmem] * len(shards) + [anywhere] * 3 + [vmem] * 4,
        out_specs=(anywhere,) * 6 + (vmem,) * 5,
        scratch_shapes=[pltpu.VMEM(dims, BF16) for dims in ((32, Q_WIDE), (32, R_WIDE), (16, D_WIDE))]
        + [pltpu.VMEM((n, half[name]), BF16) for n in (32, 48, 48, 80) for name in "qr"]
        + [
            pltpu.VMEM((64, half["d"]), BF16),
            pltpu.VMEM((2, 4, 4, 80, 512), BF16),
            pltpu.SemaphoreType.DMA((sems,)),
            pltpu.SemaphoreType.DMA((sems,)),
            pltpu.SemaphoreType.DMA((3,)),
            pltpu.SemaphoreType.DMA((2, 3)),
            pltpu.SemaphoreType.DMA((2,)),
        ],
        compiler_params=pltpu.CompilerParams(collective_id=1, has_side_effects=True, vmem_limit_bytes=56 << 20),
        name="gather_attend",
    )(*shards, *experts, tokens, cos, sin, seg_row)
    w_q, w_r, w_d = (out[k].reshape(16 * out[k].shape[2], out[k].shape[3]) for k in range(3))
    return (w_q, w_r, w_d, out[3:6]) + tuple(out[6:])


START = (3, 1, 1)
R_PIECES = range(11, 24)
Q_PIECES = range(0, 18, 2)
KV_GAP = 4


class RingSum:
    def __init__(self, wires, names, hold, from_sib, bufs, to_sib, spot):
        hi, y, z, lo, c = spot
        self.wires, self.names, self.hold, self.from_sib, self.bufs, self.to_sib = (
            wires, names, hold, from_sib, bufs, to_sib,
        )
        self.sib = device(hi, y, z, lo, 1 - c)
        self.nb = ring_neighbours(hi, y, z, lo, c)
        self.first_axis, self.second_axis = ("y", "z"), ("z", "y")
        self.ring, self.coming = {}, {}
        orders = []
        for u in UNITS:
            p1, p2 = (y, z) if u == 0 else (z, y)
            ones = (opp(p1), up(p1), dn(p1), p1)
            orders.append([(q1, q2) if u == 0 else (q2, q1) for q2 in (opp(p2), up(p2), dn(p2), p2) for q1 in ones])
        self.orders = orders
        self.steps = []
        for i in range(4):
            for u in UNITS:
                self.steps.append(functools.partial(self.far_step, u, i))
        for i in range(4):
            for u in UNITS:
                self.steps.append(functools.partial(self.near_step, u, i, 1))
            for u in UNITS:
                self.steps.append(functools.partial(self.near_step, u, i, -1))
        for i in range(4):
            for u in UNITS:
                self.steps.append(functools.partial(self.own_step, u, i))
        for u in UNITS:
            self.steps.append(functools.partial(self.last_step, u))

    def blocks(self, refs, u, index):
        return {name: refs[name][u].at[index] for name in self.names}

    def start(self):
        for k in range(16):
            for u in UNITS:
                at = self.orders[u][k]
                src, dst = self.blocks(self.to_sib, u, at), self.blocks(self.from_sib, u, at)
                self.coming[u, k] = self.pair(src, dst, self.sib)

    def pair(self, src, dst, to):
        return [self.wires.remote(src[name], dst[name], to) for name in self.names]

    def add_in(self, dst, *more):
        @pl.loop(0, dst.shape[-2] // 16)
        def _(i):
            r = pl.ds(mul(i * 16, 16), 16)
            value = dst[r, :].astype(F32)
            for ref in more:
                value = value + ref[r, :].astype(F32)
            dst[r, :] = value.astype(BF16)

    def ready(self, u, k):
        arrived(self.coming[u, k])
        at = self.orders[u][k]
        blk, more = self.blocks(self.hold, u, at), self.blocks(self.from_sib, u, at)
        for name in self.names:
            self.add_in(blk[name], more[name])
        return blk

    def half(self, blk, u, h):
        cut = {}
        for name in self.names:
            s, w, w0 = PIECES[name][2][u]
            cut[name] = blk[name].at[:, pl.ds(0, w0 * 128) if h == 0 else pl.ds(w0 * 128, (w - w0) * 128)]
        return cut

    def buffer(self, u, i, slot):
        return {name: self.bufs[name][u][i].at[slot] for name in self.names}

    def far_block(self, u, slot, blk, axis):
        self.ring[u, slot, 0] = self.pair(self.half(blk, u, 0), self.buffer(u, 0, slot), self.nb[axis, 1])
        self.ring[u, slot, 1] = self.pair(self.half(blk, u, 1), self.buffer(u, 1, slot), self.nb[axis, -1])

    def near_block(self, u, slot, blk, axis, way):
        h = 0 if way == 1 else 1
        arrived(self.ring[u, slot, h])
        dst, more = self.half(blk, u, h), self.buffer(u, h, slot)
        for name in self.names:
            self.add_in(dst[name], more[name])
        self.ring[u, slot, 2 + h] = self.pair(blk, self.buffer(u, 2 + h, slot), self.nb[axis, way])

    def own_block(self, u, slot, blk):
        arrived(self.ring[u, slot, 2])
        arrived(self.ring[u, slot, 3])
        one, two = self.buffer(u, 2, slot), self.buffer(u, 3, slot)
        for name in self.names:
            self.add_in(blk[name], one[name], two[name])

    def far_step(self, u, i):
        self.far_block(u, i, self.ready(u, i), self.second_axis[u])

    def near_step(self, u, i, way):
        self.near_block(u, i, self.ready(u, (4 if way == 1 else 8) + i), self.second_axis[u], way)

    def own_step(self, u, i):
        blk = self.ready(u, 12 + i)
        self.own_block(u, i, blk)
        axis = self.first_axis[u]
        if i == 0:
            for h in (0, 1):
                self.ring[u, 4, h] = self.pair(self.half(blk, u, h), self.buffer(u, h, 4), self.nb[axis, 2])
        elif i < 3:
            self.ring[u, 4, 1 + i] = self.pair(blk, self.buffer(u, 1 + i, 4), self.nb[axis, 1 if i == 1 else -1])

    def last_step(self, u):
        blk = self.blocks(self.hold, u, self.orders[u][15])
        self.own_block(u, 4, blk)
        for h in (0, 1):
            arrived(self.ring[u, 4, h])
            dst, more = self.half(blk, u, h), self.buffer(u, h, 4)
            for name in self.names:
                self.add_in(dst[name], more[name])


def sum_scratch():
    scratch = []
    for rows, _tiles, units in PIECES.values():
        for s, w, w0 in units:
            scratch += [pltpu.VMEM((4, 4, rows, w * 128), BF16)] * 2
            scratch += [pltpu.VMEM((5, rows, t * 128), BF16) for t in (w0, w - w0, w, w)]
    return scratch


def backward_kernel(
    left_r, right_r, sdown, act, q, kv, prior, seg_row, grad_mixed, cos, sin, tok, grad_hidden, gain_f, w_q,
    p0, p1, p2,
    fin_q, fin_r, fin_d, t0, t1, t2, grad_tokens,
    *scratch,
):
    names = list(PIECES)
    hold, from_sib, bufs = {}, {}, {}
    scratch = list(scratch)
    for name in names:
        hold[name], from_sib[name], bufs[name] = [], [], []
        for u in UNITS:
            hold[name].append(scratch.pop(0))
            from_sib[name].append(scratch.pop(0))
            bufs[name].append([scratch.pop(0) for _ in range(4)])
    sums, sides, mids, fars = ({name: scratch.pop(0) for name in names} for _ in range(4))
    accs = {name: scratch.pop(0) for name in names}
    sent = [scratch.pop(0) for _ in UNITS]
    grad_own, grad_prior, later, left_q, right_q, total, w_buf, gain_tile = scratch[:8]
    ssem, rsem, lsem, esend, erecv, wsem, piece_sem = scratch[8:]
    spot = place()
    hi, y, z, lo, c = spot
    sib = device(hi, y, z, lo, 1 - c)
    xn = device(hi, y, z, 1 - lo, c)
    hn = device(1 - hi, y, z, lo, c)
    greet([sib, xn, hn, device(1 - hi, y, z, lo, 1 - c)] + list(ring_neighbours(*spot).values()))
    wires = Sender(ssem, rsem, lsem)
    rows, width = tok.shape

    owner = c == hi
    parts, totals = (p0, p1, p2), (t0, t1, t2)
    across = device(1 - hi, y, z, lo, hi)

    def rows_of(ref, core):
        n = ref.shape[0] // 2
        return ref.at[pl.ds(mul(core * n, 16), n)]

    def expert_copy(src, dst, k, tag, to):
        return pltpu.make_async_remote_copy(
            src_ref=src, dst_ref=dst, send_sem=esend.at[k], recv_sem=erecv.at[tag], device_id=to, device_id_type=MESH
        )

    def across_piece(k, i):
        n = parts[k].shape[0]
        return pltpu.make_async_remote_copy(
            src_ref=parts[k].at[pl.ds(i * 64, 64)],
            dst_ref=totals[k].at[pl.ds(mul(c * n + i * 64, 16), 64)],
            send_sem=piece_sem.at[0, k, i],
            recv_sem=piece_sem.at[1, k, 10 * c + i],
            device_id=across,
            device_id_type=MESH,
        )

    def coming_piece(k, i, core):
        n = parts[k].shape[0]
        rows_ = totals[k].at[pl.ds(mul(core * n + i * 64, 16), 64)]
        return pltpu.make_async_remote_copy(
            src_ref=rows_,
            dst_ref=rows_,
            send_sem=piece_sem.at[0, k, i],
            recv_sem=piece_sem.at[1, k, 10 * core + i],
            device_id=across,
            device_id_type=MESH,
        )

    pieces = [(k, i) for k in range(3) for i in range(parts[k].shape[0] // 64)]

    def send_near(k):
        return expert_copy(parts[k], rows_of(totals[k], c), k, k, sib)

    def near_half(k):
        return expert_copy(rows_of(totals[k], 1 - c), rows_of(totals[k], 1 - c), k, k, sib)

    def expert_steps():
        for n, (k, i) in enumerate(pieces):
            across_piece(k, i).start()
            if n == len(pieces) // 2:

                @pl.when(jnp.logical_not(owner))
                def _():
                    for k in range(3):
                        send_near(k).start()

            yield

    experts = expert_steps()
    for _ in range(START[0]):
        next(experts, None)

    own_d = []
    for u in UNITS:
        s, w = unit_tiles("d", u, None)
        own_d.append(wires.local(sdown.at[:, :, :, lanes("d", u, None, c)], hold["d"][u]))

    def products(left, right, name, core, refs):
        for u in UNITS:
            r = right[:, lanes(name, u, None, core)]
            for m in (0, 1):
                v = t_dot(left[:, m * 640 : (m + 1) * 640], r).astype(BF16)
                for b in range(8):
                    refs[u][2 * m + b // 4, b % 4] = v[b * 80 : (b + 1) * 80]

    def views(name, refs):
        return [ref.at[:, :, :, pl.ds(0, PIECES[name][2][u][1] * 128)] for u, ref in enumerate(refs)]

    to_sib_r = views("r", sent)
    products(left_r, right_r, "r", 1 - c, to_sib_r)
    to_sib_d = [sdown.at[:, :, :, lanes("d", u, None, 1 - c)] for u in UNITS]
    group_r = RingSum(wires, "rd", hold, from_sib, bufs, {"r": to_sib_r, "d": to_sib_d}, spot)
    group_r.start()
    for _ in range(START[1]):
        next(experts, None)
    products(left_r, right_r, "r", c, hold["r"])
    for copy in own_d:
        copy.wait()
    for _ in range(START[2]):
        next(experts, None)

    def load(i):
        return pltpu.make_async_copy(w_q.at[:, pl.ds(i * 512, 512)], w_buf.at[i % 2], wsem.at[i % 2])

    load_gains = pltpu.make_async_copy(w_q.at[:, pl.ds(GAINS * 128, 128)], gain_tile, wsem.at[2])
    halves = [pl.ds(start, 640) for start in (0, width, 640, width + 640)]
    exchange_kv = [wires.describe(grad_prior.at[:, cut], later.at[:, cut], hn) for cut in halves]
    to_sib_q = views("q", sent)
    group_q = RingSum(wires, "q", hold, from_sib, bufs, {"q": to_sib_q}, spot)

    def work():
        load(0).start()
        load_gains.start()
        here = seq_rows()
        cosine, sine = cos[here, :], sin[here, :]
        own_ok, prior_ok = allowed_keys(seg_row)
        inv_root = 128.0**-0.5

        @pl.when(hi == 1)
        def _():
            later[...] = jnp.zeros_like(later)

        for h in range(HEADS):
            query, keys, values, probs = head_probs(h, q, kv, prior, own_ok, prior_ok, width)
            mine = slice(h * 128, (h + 1) * 128)
            behind = slice(width + h * 128, width + (h + 1) * 128)
            gm = grad_mixed[:, mine]
            grad_probs = dot_t(gm, values)
            inner = jnp.sum(probs * grad_probs, axis=-1, keepdims=True)
            grad_scores = (probs * (grad_probs - inner)).astype(BF16)
            grad_values = t_dot(probs.astype(BF16), gm)
            gq = dot(grad_scores, keys) * inv_root
            grad_keys = t_dot(grad_scores, query) * inv_root
            right_q[0:rows, mine] = (gq * cosine - pltpu.roll(gq, 64, 1) * sine).astype(BF16)
            grad_own[:, mine] = grad_keys[rows:]
            grad_own[:, behind] = grad_values[rows:]
            grad_prior[:, mine] = grad_keys[:rows].astype(BF16)
            grad_prior[:, behind] = grad_values[:rows].astype(BF16)
            if h % 5 == 4:

                @pl.when(hi == 1)
                def _():
                    for copy in exchange_kv[:2] if h == 4 else exchange_kv[2:]:
                        copy.start()

            yield

        right_q[0:rows, 3 * width :] = jnp.zeros((rows, Q_WIDE - 3 * width), BF16)
        right_q[rows:, :] = (iota((16, Q_WIDE), 1) == iota((16, Q_WIDE), 0) + GAINS * 128).astype(BF16)
        left_q[0:rows, :] = act[...]
        total[...] = jnp.zeros_like(total)

        def add_chunk(i):
            load(i).wait()
            if i < 7:
                load(i + 1).start()
            total[...] += dot_t(right_q[0:rows, i * 512 : (i + 1) * 512], w_buf[i % 2])

        for i in (0, 1):
            add_chunk(i)
            yield

        for _ in range(KV_GAP):
            yield

        @pl.when(hi == 0)
        def _():
            for copy in exchange_kv:
                copy.wait_recv()

        for h in range(HEADS):
            mine = slice(h * 128, (h + 1) * 128)
            gk = grad_own[:, mine] + later[:, mine].astype(F32)
            right_q[0:rows, width + h * 128 : width + (h + 1) * 128] = (
                gk * cosine - pltpu.roll(gk, 64, 1) * sine
            ).astype(BF16)
        right_q[0:rows, 2 * width : 3 * width] = (grad_own[:, width:] + later[:, width:].astype(F32)).astype(BF16)
        yield
        for i in range(2, 8):
            add_chunk(i)
            yield
        load_gains.wait()
        gain = gain_rows(gain_tile[...])[0:1]
        values = tok[...].astype(F32)
        _normed, inv = rms_forward(values, gain)
        grad_norm, gain_sum = rms_backward(values, inv, gain, total[...])
        grad_tokens[...] = grad_hidden[...] + grad_norm
        row = iota((16, width), 0)
        left_q[rows:, :] = jnp.where(row == 0, gain_sum, jnp.where(row == 1, gain_f[...], 0.0)).astype(BF16)
        yield
        for k in range(16):
            for u in UNITS:
                wires.settle(group_r.coming[u, k][0])
        products(left_q, right_q, "q", 1 - c, to_sib_q)
        group_q.start()
        yield
        products(left_q, right_q, "q", c, hold["q"])
        yield

    def window_sums(group):
        copies = {}
        for name in group:
            n = PIECES[name][0]
            for u in UNITS:
                s, w = unit_tiles(name, u, None)
                sums[name][:, s * 128 : (s + w) * 128] = hold[name][u][y, z]
            window = 48 if n == 80 else 32
            copies[name] = wires.remote(sums[name].at[pl.ds(mul((1 - lo) * 32, 16), window)], sides[name], xn)
        yield
        for name in group:
            copies[name].wait_recv()
            window = sides[name].shape[0]
            r = pl.ds(mul(lo * 32, 16), window)
            mids[name][...] = (sums[name][r, :].astype(F32) + sides[name][...].astype(F32)).astype(BF16)
            copies[name] = wires.remote(mids[name], fars[name], hn)
        yield
        fins = {"q": fin_q, "r": fin_r, "d": fin_d}
        for name in group:
            copies[name].wait_recv()
            accs[name][...] = mids[name][...].astype(F32) + fars[name][...].astype(F32)
            n = fins[name].shape[0]
            mine = core_lanes(name, c)
            copies[name] = wires.remote(
                accs[name].at[pl.ds(mul((1 - c) * 16, 16), n)], fins[name].at[:, mine], sib
            )
            fins[name][:, mine] = accs[name][pl.ds(mul(c * 16, 16), n), :]
        yield
        for name in group:
            copies[name].wait_recv()

    busy = work()
    for n, step in enumerate(group_r.steps[:24]):
        step()
        next(busy, None)
        if n in R_PIECES:
            next(experts, None)
    for _ in busy:
        pass
    rest = list(group_r.steps[24:])
    for n, step in enumerate(group_q.steps[:24]):
        step()
        if n in Q_PIECES:
            next(experts, None)
        if rest:
            rest.pop(0)()
    for _ in experts:
        pass
    first, second = window_sums("rd"), window_sums("q")
    next(first)
    for step in group_q.steps[24:]:
        step()
    next(second)
    for _ in first:
        next(second, None)
    for _ in second:
        pass
    for k, i in pieces:
        across_piece(k, i).wait_send()

    @pl.when(owner)
    def _():
        for k in range(3):
            near_half(k).wait_recv()

    @pl.when(jnp.logical_not(owner))
    def _():
        for k in range(3):
            send_near(k).wait_send()
        for k, i in pieces:
            for core in (0, 1):
                coming_piece(k, i, core).wait_recv()

    @pl.when(hi == 1)
    def _():
        for copy in exchange_kv:
            copy.wait_send()

    wires.finish()


def backward(operands, parts):
    rows, width = operands[11].shape
    vmem, anywhere = pl.BlockSpec(memory_space=pltpu.VMEM), pl.BlockSpec(memory_space=pl.ANY)
    half = {name: PIECES[name][1] * 128 for name in PIECES}
    window = {"q": 48, "r": 48, "d": 32}
    fin = {"q": (32, Q_WIDE), "r": (32, R_WIDE), "d": (16, D_WIDE)}
    scratch = sum_scratch()
    scratch += [pltpu.VMEM((PIECES[name][0], half[name]), BF16) for name in PIECES]
    scratch += [pltpu.VMEM((window[name], half[name]), BF16) for _ in range(3) for name in PIECES]
    scratch += [pltpu.VMEM((window[name], half[name]), F32) for name in PIECES]
    scratch += [pltpu.VMEM((4, 4, 80, 1024), BF16)] * 2
    scratch += [
        pltpu.VMEM((rows, 2 * width), F32),
        pltpu.VMEM((rows, 2 * width), BF16),
        pltpu.VMEM((rows, 2 * width), BF16),
        pltpu.VMEM((rows + 16, width), BF16),
        pltpu.VMEM((rows + 16, Q_WIDE), BF16),
        pltpu.VMEM((rows, width), F32),
        pltpu.VMEM((2, width, 512), BF16),
        pltpu.VMEM((width, 128), BF16),
    ]
    sems = 4 + 3 * (32 + 2 * 4 * 5 + 3)
    scratch += [pltpu.SemaphoreType.DMA((n,)) for n in (sems, sems, 2, 3, 3, 3)]
    scratch += [pltpu.SemaphoreType.DMA((2, 3, 20))]
    spec = [vmem] * len(operands)
    spec[2] = spec[14] = anywhere
    return pl.pallas_call(
        backward_kernel,
        out_shape=tuple(shape(F32, *fin[name]) for name in PIECES)
        + tuple(shape(BF16, 2 * p.shape[0], p.shape[1]) for p in parts)
        + (shape(F32, rows, width),),
        in_specs=spec + [anywhere] * 3,
        out_specs=(vmem,) * 3 + (anywhere,) * 3 + (vmem,),
        scratch_shapes=scratch,
        compiler_params=pltpu.CompilerParams(collective_id=2, has_side_effects=True, vmem_limit_bytes=60 << 20),
        name="attend_back_sums",
    )(*operands, *parts)


PART_AXES = (("y", "z", "g"), ("z", "g", "y"), ("g", "y", "z")) * 2
PARTS = len(PART_AXES)
TURNS = (2, 1, 3, 0)


def lane_cuts(*sizes):
    return tuple((sum(sizes[:i]), n) for i, n in enumerate(sizes))


ROW_CUTS = lane_cuts(4, 4, 3, 3, 3, 3)
LAST_OUT_CUTS = lane_cuts(3, 3, 3, 3, 4, 5)
LAST_BACK_CUTS = lane_cuts(3, 3, 3, 3, 4, 4)


class Exchange:
    def __init__(self, outward, cuts, stages, sems, spot):
        self.outward, self.cuts, self.stages, self.spot = outward, cuts, stages, spot
        self.ssem, self.rsem, self.lsem = sems
        hi, y, z, lo, c = spot
        self.stays = c == hi
        self.moves = jnp.logical_not(self.stays)
        self.pending, self.sent, self.used, self.made = {}, [], [0, 0], []

    def along(self, axis, k):
        hi, y, z, lo, c = self.spot
        q = {"y": y, "z": z}
        q[axis] = lax.rem(q[axis] + k, 4)
        return q[axis], device(hi, q["y"], q["z"], lo, c)

    def target(self, d, b):
        hi, y, z, lo, c = self.spot
        lo_, hi_, c_ = (lo, 1 - lo)[d], (hi, 1 - hi)[b], (c, 1 - c)[b]
        if self.outward:
            return device(hi_, y, z, lo_, hi), lo_ * 2 + hi_, lo * 2 + c, 2 * d + c
        return device(c, y, z, lo_, c_), lo_ * 2 + c_, lo * 2 + hi, 2 * d + hi

    def source(self, d, b):
        hi, y, z, lo, c = self.spot
        lo_, hi_, c_ = (lo, 1 - lo)[d], (hi, 1 - hi)[b], (c, 1 - c)[b]
        if self.outward:
            return device(c, y, z, lo_, c_), lo_ * 2 + c_, 2 * d + c_
        return device(hi_, y, z, lo_, hi), lo_ * 2 + hi_, 2 * d + hi_

    corners = ((1, 1), (0, 1), (1, 0))

    def greet(self):
        hi, y, z, lo, c = self.spot
        bar = pltpu.get_barrier_semaphore()

        def greet_one(to):
            pl.semaphore_signal(bar, inc=1, device_id=to, device_id_type=MESH)

        for axis in "yz":
            for k in (1, 2, 3):
                greet_one(self.along(axis, k)[1])
        for corner in self.corners:
            greet_one(self.source(*corner)[0])

        @pl.when(self.moves)
        def _():
            greet_one(self.source(0, 0)[0])
            pl.semaphore_wait(bar, 10 if self.outward else 11)

        @pl.when(self.stays)
        def _():
            if not self.outward:
                greet_one(device(hi, y, z, lo, 1 - c))
            pl.semaphore_wait(bar, 9)

    def view(self, ref, axis, v, cut, at):
        every = slice(None)
        first = every if at is None else at
        index = {"y": (v, every, every), "z": (first, v, every), "g": (first, every, v)}[axis]
        return ref.at[index + (every, pl.ds(cut[0] * 128, cut[1] * 128))]

    def remote(self, src, dst, k, tag, to):
        return pltpu.make_async_remote_copy(
            src_ref=src,
            dst_ref=dst,
            send_sem=self.ssem.at[k],
            recv_sem=self.rsem.at[tag],
            device_id=to,
            device_id_type=MESH,
        )

    def go(self, part, phase, turn=None, at=None):
        axis = PART_AXES[part][phase]
        hi, y, z, lo, c = self.spot
        waits = self.pending.setdefault((part, phase), [])
        for a, cuts in enumerate(self.cuts):
            src, dst = self.stages[phase][a], self.stages[phase + 1][a]
            cut = cuts[part]
            base, kept = self.used
            self.used[0] += 4
            self.used[1] += 1
            if axis != "g":
                here = y if axis == "y" else z
                rows = at if axis == "z" else None
                own = self.view(dst, axis, here, cut, rows)
                for k in (turn,) if axis == "y" and turn is not None else TURNS:
                    v, to = self.along(axis, k)
                    if k == 0:
                        keep = pltpu.make_async_copy(self.view(src, axis, here, cut, rows), own, self.lsem.at[kept])
                        keep.start()
                        waits.append(keep.wait)
                        continue
                    copy = self.remote(self.view(src, axis, v, cut, rows), own, base + k, base + k, to)
                    copy.start()
                    waits.append(copy.wait_recv)
                    self.sent.append(copy.wait_send)
                continue
            for d, b in self.corners:
                to, there, here, tag = self.target(d, b)
                copy = self.remote(
                    self.view(src, axis, there, cut, at), self.view(dst, axis, here, cut, at), base + 2 * d + b, base + tag, to
                )
                copy.start()
                self.sent.append(copy.wait_send)
                sender, place_, tag = self.source(d, b)
                block = self.view(dst, axis, place_, cut, at)
                waits.append(self.remote(block, block, base + 2 * d + b, base + tag, sender).wait_recv)
            self.go_corner(src, dst, cut, at, base, kept, waits)

    def go_corner(self, src, dst, cut, at, base, kept, waits):
        to, there, here, tag = self.target(0, 0)
        mine, landing = self.view(src, "g", there, cut, at), self.view(dst, "g", here, cut, at)
        keep = pltpu.make_async_copy(mine, landing, self.lsem.at[kept])
        copy = self.remote(mine, landing, base, base + tag, to)
        sender, place_, tag = self.source(0, 0)
        block = self.view(dst, "g", place_, cut, at)
        coming = self.remote(block, block, base, base + tag, sender)

        @pl.when(self.stays)
        def _():
            keep.start()

        @pl.when(self.moves)
        def _():
            copy.start()

        def wait_corner():
            @pl.when(self.stays)
            def _():
                keep.wait()

            @pl.when(self.moves)
            def _():
                coming.wait_recv()

        def wait_sent():
            @pl.when(self.moves)
            def _():
                copy.wait_send()

        waits.append(wait_corner)
        self.sent.append(wait_sent)

    def first(self, turn, at):
        now = PARTS // 2 if self.outward else PARTS
        for part in range(now):
            self.go(part, 0, turn, at)
        self.made.append((turn, at))
        if len(self.made) == 4:
            for part in range(now, PARTS):
                for turn, at in self.made:
                    self.go(part, 0, turn, at)

    def next(self, phase):
        for part in range(PARTS):
            self.wait(part, phase - 1)
            self.go(part, phase)

    def wait(self, part, phase):
        for wait in self.pending[part, phase]:
            wait()

    def finish(self):
        for part in range(PARTS):
            self.wait(part, 2)
        for wait in self.sent:
            wait()


def exchange_sems(arrays):
    return [pltpu.SemaphoreType.DMA((n * arrays,)) for n in (160, 160, 40)]


EVEN = 16


def even_places(slot_t):
    experts, rows = slot_t.shape
    wide = jnp.broadcast_to(slot_t[:, None, :], (experts, EVEN, rows))
    return wide == iota((experts, EVEN, rows), 1).astype(F32)


def loads(ins, bufs, sem, start=0):
    return [pltpu.make_async_copy(src, dst, sem.at[start + k]) for k, (src, dst) in enumerate(zip(ins, bufs))]


def route_kernel(
    tok, mixed, routes, grad, w_q, w_r, w_d,
    out_r, out_l, hidden_one, act, gates_t, slot_t, out_s, grad_in, grad_gu, grad_down,
    src_r, src_l, b1_r, b1_l, b2_r, b2_l, out_w, router_w, gains, sgu, sdown, hidden_s, ssem, rsem, lsem, wsem,
):
    spot = place()
    y = spot[1]
    rows, width = tok.shape
    inner = sdown.shape[0]
    first_loads = loads(
        (w_r.at[:, pl.ds(0, width)], w_r.at[:, pl.ds(ROUTER * 128, 128)], w_q.at[:, pl.ds(GAINS * 128, 128)]),
        (out_w, router_w, gains),
        wsem,
    )
    later_loads = loads((w_r.at[:, pl.ds(width, 2 * inner)], w_d), (sgu, sdown), wsem, 3)
    for copy in first_loads + later_loads:
        copy.start()
    swap = Exchange(
        True, (ROW_CUTS, LAST_OUT_CUTS), ((src_r, src_l), (b1_r, b1_l), (b2_r, b2_l), (out_r, out_l)), (ssem, rsem, lsem), spot
    )
    swap.greet()
    for copy in first_loads:
        copy.wait()
    hidden = tok[...].astype(F32) + dot(mixed[...], out_w[...])
    hidden_one[...] = hidden
    router = router_w[...]
    normed, _inv = rms_forward(hidden, gain_rows(gains[...])[1:2])
    low = normed.astype(BF16)
    act[...] = low
    expert = iota((rows, 128), 1)
    named = routes[...]
    member = named[:, 0:1] == expert
    for k in range(1, named.shape[1]):
        member = member | (named[:, k : k + 1] == expert)
    logits = jnp.where(member, dot(low, router), NEG_BIG)
    expo = jnp.where(member, jnp.exp(logits - jnp.max(logits, axis=-1, keepdims=True)), 0.0)
    gates_t[...] = (expo / jnp.sum(expo, axis=-1, keepdims=True)).T
    before = (iota((rows, rows), 1) < iota((rows, rows), 0)).astype(BF16)
    rank = dot(before, member.astype(BF16))
    slot_t[...] = jnp.where(member, rank, -1.0).T

    block = 16
    g = grad[...]
    for turn in TURNS:
        v = lax.rem(y + turn, 4)
        here = pl.ds(mul(v * block, block), block)
        slots = slot_t[here, :]
        places = even_places(slots)
        last = slots == float(EVEN)
        hot = places.astype(F32).reshape(block * EVEN, rows).astype(BF16)
        last_hot = last.astype(BF16)
        src_r[v, :, :, :, 0:width] = dot(hot, low).astype(BF16).reshape(4, 4, EVEN, width)
        src_r[v, :, :, :, width:] = dot(hot, g).astype(BF16).reshape(4, 4, EVEN, width)
        gt = gates_t[here, :]
        at_slot = jnp.sum(
            jnp.where(places, jnp.broadcast_to(gt[:, None, :], places.shape), 0.0).reshape(block * EVEN, rows),
            axis=-1,
            keepdims=True,
        )
        spread = jnp.broadcast_to(at_slot, (block * EVEN, 128)).reshape(block, EVEN, 128)
        lane_of = iota((block, EVEN, 128), 1) == iota((block, EVEN, 128), 2)
        even_gates = jnp.sum(jnp.where(lane_of, spread, 0.0), axis=1)
        last_gates = jnp.sum(jnp.where(last, gt, 0.0), axis=-1, keepdims=True)
        slot_gates = jnp.where(iota((block, 128), 1) == EVEN, last_gates, even_gates)
        src_l[v] = jnp.concatenate([dot(last_hot, low), dot(last_hot, g), slot_gates], axis=1).reshape(
            4, 4, 1, 2 * width + 128
        )
        swap.first(turn, v)

    for copy in later_loads:
        copy.wait()
    gate = dot(low, sgu[:, :inner])
    up_ = dot(low, sgu[:, inner:])
    silu, slope = silu_parts(gate)
    hidden_s[...] = (silu * up_).astype(BF16)
    grad_hidden = dot_t(g, sdown[...])
    grad_gu[:, :inner] = (grad_hidden * up_ * slope).astype(BF16)
    grad_gu[:, inner:] = (grad_hidden * silu).astype(BF16)
    swap.next(1)
    out_s[...] = dot(hidden_s[...], sdown[...])
    grad_in[...] = dot_t(grad_gu[...], sgu[...])
    swap.next(2)

    @pl.loop(0, inner // 256)
    def _(i):
        r = pl.ds(mul(i * 256, 256), 256)
        grad_down[r, :] = t_dot(hidden_s[:, r], grad[...]).astype(BF16)

    swap.finish()


def route(tokens, mixed, routes, grad, w_q, w_r, w_d):
    rows, width = tokens.shape
    vmem, anywhere = pl.BlockSpec(memory_space=pltpu.VMEM), pl.BlockSpec(memory_space=pl.ANY)
    r, last = (4, 4, 4, EVEN, 2 * width), (4, 4, 4, 1, 2 * width + 128)
    return pl.pallas_call(
        route_kernel,
        out_shape=(
            shape(BF16, *r),
            shape(F32, *last),
            shape(F32, rows, width),
            shape(BF16, rows, width),
            shape(F32, 128, rows),
            shape(F32, 128, rows),
            shape(F32, rows, width),
            shape(F32, rows, width),
            shape(BF16, rows, 2048),
            shape(BF16, 1024, width),
        ),
        in_specs=[vmem] * 4 + [anywhere] * 3,
        out_specs=(anywhere,) * 2 + (vmem,) * 8,
        scratch_shapes=[pltpu.VMEM(r, BF16), pltpu.VMEM(last, F32)] * 3
        + [
            pltpu.VMEM((width, width), BF16),
            pltpu.VMEM((width, 128), BF16),
            pltpu.VMEM((width, 128), BF16),
            pltpu.VMEM((width, 2048), BF16),
            pltpu.VMEM((1024, width), BF16),
            pltpu.VMEM((rows, 1024), BF16),
        ]
        + exchange_sems(2)
        + [pltpu.SemaphoreType.DMA((5,))],
        compiler_params=pltpu.CompilerParams(collective_id=3, has_side_effects=True, vmem_limit_bytes=56 << 20),
        name="route_shared",
    )(tokens, mixed, routes, grad, w_q, w_r, w_d)


def expert_rows(rows_r, rows_l, width):
    sources = 16
    last = rows_l.reshape(sources, rows_l.shape[-1])
    even = sources * EVEN
    both = rows_r.reshape(even, 2 * width)
    x = jnp.concatenate([both[:, :width], last[:, :width].astype(BF16)], axis=0)
    g = jnp.concatenate([both[:, width:].astype(F32), last[:, width : 2 * width]], axis=0)
    sent = last[:, 2 * width :]
    spread = jnp.broadcast_to(sent[:, None, :], (sources, EVEN, 128))
    own = iota((sources, EVEN, 128), 1) == iota((sources, EVEN, 128), 2)
    even_gates = jnp.sum(jnp.where(own, spread, 0.0).reshape(even, 128), axis=-1, keepdims=True)
    last_gates = jnp.sum(jnp.where(iota((sources, 128), 1) == EVEN, sent, 0.0), axis=-1, keepdims=True)
    return x, (jnp.concatenate([even_gates, last_gates], axis=0) * g).astype(BF16)


def expert_kernel(
    rows_r, rows_l, o0, o1, o2, e0, e1, e2,
    back_r, back_l, p0, p1, p2,
    src_r, src_l, b1_r, b1_l, b2_r, b2_l, in_r, in_l, w_gate, w_up, w_down, all_x, all_g, hidden, d_gate, d_up,
    g_gate, g_up, g_down, s_gate, s_up, s_down, ssem, rsem, lsem, wsem, isem, osem, xsem,
):
    spot = place()
    hi, y, z, lo, c = spot
    width = all_x.shape[1]
    outs, products, from_sib = (p0, p1, p2), (g_gate, g_up, g_down), (s_gate, s_up, s_down)
    weights = (w_gate, w_up, w_down)
    owner = c == hi
    swap = Exchange(
        False, (ROW_CUTS, LAST_BACK_CUTS), ((src_r, src_l), (b1_r, b1_l), (b2_r, b2_l), (back_r, back_l)), (ssem, rsem, lsem), spot
    )

    @pl.when(owner)
    def _():
        for copy in loads((e0, e1, e2), weights, wsem):
            copy.start()

    @pl.when(jnp.logical_not(owner))
    def _():
        for copy in loads((o0, o1, o2), weights, wsem):
            copy.start()

    def block(n):
        v = lax.rem(y + TURNS[n], 4)
        return v, loads((rows_r.at[v], rows_l.at[v]), (in_r.at[n % 2], in_l.at[n % 2]), isem.at[n % 2])

    coming = {0: block(0)[1]}
    for copy in coming[0]:
        copy.start()
    swap.greet()
    for copy in loads((e0, e1, e2), weights, wsem):
        copy.wait()
    step = all_x.shape[0] // 4
    even = 16 * EVEN
    for n, turn in enumerate(TURNS):
        v = lax.rem(y + turn, 4)
        if n + 1 < 4:
            coming[n + 1] = block(n + 1)[1]
            for copy in coming[n + 1]:
                copy.start()
        for copy in coming[n]:
            copy.wait()
        here = slice(n * step, (n + 1) * step)
        x, grad_result = expert_rows(in_r[n % 2], in_l[n % 2], width)
        all_x[here, :] = x
        all_g[here, :] = grad_result
        gate = dot(x, w_gate[...])
        up_ = dot(x, w_up[...])
        silu, slope = silu_parts(gate)
        low = (silu * up_).astype(BF16)
        hidden[here, :] = low
        grad_hidden = dot_t(grad_result, w_down[...])
        grad_gate = (grad_hidden * up_ * slope).astype(BF16)
        grad_up = (grad_hidden * silu).astype(BF16)
        d_gate[here, :] = grad_gate
        d_up[here, :] = grad_up
        result = dot(low, w_down[...]).astype(BF16)
        grad_in = (dot_t(grad_gate, w_gate[...]) + dot_t(grad_up, w_up[...])).astype(BF16)
        src_r[v, :, :, :, 0:width] = result[:even].reshape(4, 4, EVEN, width)
        src_r[v, :, :, :, width:] = grad_in[:even].reshape(4, 4, EVEN, width)
        src_l[v] = jnp.concatenate([result[even:], grad_in[even:]], axis=1).astype(F32).reshape(4, 4, 1, 2 * width)
        swap.first(turn, v)

    def half(k, core):
        n = products[k].shape[0] // 2
        return products[k].at[pl.ds(mul(core * n, 16), n)]

    def trade(k):
        return pltpu.make_async_remote_copy(
            src_ref=half(k, 1 - c),
            dst_ref=from_sib[k],
            send_sem=xsem.at[0, k],
            recv_sem=xsem.at[1, k],
            device_id=device(hi, y, z, lo, 1 - c),
            device_id_type=MESH,
        )

    def product(k, left, right, wide):
        out = products[k]

        @pl.loop(0, out.shape[0] // wide)
        def _(i):
            r = pl.ds(mul(i * wide, wide), wide)
            out[r, :] = t_dot(left[:, r], right[...]).astype(BF16)

        trade(k).start()

    def add(k):
        trade(k).wait_recv()
        n = products[k].shape[0] // 2

        @pl.loop(0, n // 64)
        def _(i):
            own = pl.ds(mul(c * n + i * 64, 64), 64)
            more = from_sib[k][pl.ds(mul(i * 64, 64), 64), :].astype(F32)
            products[k][own, :] = (products[k][own, :].astype(F32) + more).astype(BF16)

        copy = pltpu.make_async_copy(half(k, c), outs[k], osem.at[k])
        copy.start()
        return copy

    product(0, all_x, d_gate, 256)
    swap.next(1)
    product(1, all_x, d_up, 256)
    product(2, hidden, all_g, 128)
    kept = [add(0)]
    swap.next(2)
    kept += [add(1), add(2)]
    swap.finish()
    for k in range(3):
        trade(k).wait_send()
        kept[k].wait()


def expert(rows_r, rows_l, passed, own):
    width = rows_r.shape[-1] // 2
    inner = own[0].shape[1]
    total = 64 * (EVEN + 1)
    anywhere = pl.BlockSpec(memory_space=pl.ANY)
    r, last = (4, 4, 4, EVEN, 2 * width), (4, 4, 4, 1, 2 * width)
    return pl.pallas_call(
        expert_kernel,
        out_shape=(shape(BF16, *r), shape(F32, *last)) + tuple(shape(BF16, w.shape[0] // 2, w.shape[1]) for w in own),
        in_specs=[anywhere] * 8,
        out_specs=(anywhere,) * 5,
        scratch_shapes=[pltpu.VMEM(r, BF16), pltpu.VMEM(last, F32)] * 3
        + [pltpu.VMEM((2,) + rows_r.shape[1:], BF16), pltpu.VMEM((2,) + rows_l.shape[1:], F32)]
        + [pltpu.VMEM(w.shape, BF16) for w in own]
        + [pltpu.VMEM((total, n), BF16) for n in (width, width, inner, inner, inner)]
        + [pltpu.VMEM(w.shape, BF16) for w in own]
        + [pltpu.VMEM((w.shape[0] // 2, w.shape[1]), BF16) for w in own]
        + exchange_sems(2)
        + [pltpu.SemaphoreType.DMA(n) for n in ((3,), (2, 2), (3,), (2, 3))],
        compiler_params=pltpu.CompilerParams(collective_id=4, has_side_effects=True, vmem_limit_bytes=62 << 20),
        name="expert_back",
    )(rows_r, rows_l, *passed, *own)


def split_terms(w):
    top = w.astype(BF16)
    rest = w - top.astype(F32)
    mid = rest.astype(BF16)
    return top, mid, (rest - mid.astype(F32)).astype(BF16)


def combine_kernel(
    back_r, back_l, slot_t, gates_t, grad, hidden_one, out_s, grad_in_s, mixed, act, grad_gu, router_w, out_w, gains,
    layer_out, grad_hidden, grad_mixed, left, right, grad_gain,
):
    experts = back_r.shape[0]
    rows, width = hidden_one.shape
    slots = slot_t[0:experts, :]
    places = even_places(slots)
    last = slots == float(EVEN)
    out_rows = back_r[:, :, :width].reshape(experts * EVEN, width)
    last_l = back_l[...].reshape(experts, 2 * width).astype(BF16)
    gt = gates_t[0:experts, :]
    even_w = jnp.where(places, jnp.broadcast_to(gt[:, None, :], places.shape), 0.0).reshape(experts * EVEN, rows)
    last_w = jnp.where(last, gt, 0.0)
    routed = jnp.zeros((rows, width), F32)
    for e_term, l_term in zip(split_terms(even_w), split_terms(last_w)):
        routed = routed + t_dot(e_term, out_rows) + t_dot(l_term, last_l[:, :width])
    hidden = hidden_one[...]
    layer_out[...] = (hidden + out_s[...] + routed).astype(BF16)
    g = grad[...]
    dots = dot_t(out_rows, g).reshape(experts, EVEN, rows)
    dots_last = dot_t(last_l[:, :width], g)
    grad_gates = jnp.sum(jnp.where(places, dots, 0.0), axis=1) + jnp.where(last, dots_last, 0.0)
    logits_t = gt * (grad_gates - jnp.sum(gt * grad_gates, axis=0, keepdims=True))
    low_logits = jnp.concatenate([logits_t, jnp.zeros((128 - experts, rows), F32)], axis=0).T.astype(BF16)
    hot = places.astype(F32).reshape(experts * EVEN, rows).astype(BF16)
    grad_routed = t_dot(hot, back_r[:, :, width:].reshape(experts * EVEN, width)) + t_dot(last.astype(BF16), last_l[:, width:])
    router = router_w[...]
    grad_act = grad_routed + dot_t(low_logits, router) + grad_in_s[...]
    gain = gain_rows(gains[...])[1:2]
    _normed, inv = rms_forward(hidden, gain)
    grad_norm, gain_sum = rms_backward(hidden, inv, gain, grad_act)
    grad_gain[...] = gain_sum
    total = g.astype(F32) + grad_norm
    grad_hidden[...] = total
    low = total.astype(BF16)
    left[0:rows, :] = mixed[...]
    left[rows:, :] = act[...]
    right[0:rows, :width] = low
    right[0:rows, width:] = jnp.zeros((rows, R_WIDE - width), BF16)
    right[rows:, :width] = jnp.zeros((rows, width), BF16)
    right[rows:, width : ROUTER * 128] = grad_gu[...]
    right[rows:, ROUTER * 128 : (ROUTER + 1) * 128] = low_logits
    right[rows:, (ROUTER + 1) * 128 :] = jnp.zeros((rows, R_WIDE - (ROUTER + 1) * 128), BF16)
    grad_mixed[...] = dot_t(low, out_w[...]).astype(BF16)


def combine(operands, w_r, w_q):
    rows, width = operands[5].shape
    whole = lambda a: pl.BlockSpec(a.shape, lambda i: (0,) * len(a.shape))
    outs = (
        shape(BF16, rows, width),
        shape(F32, rows, width),
        shape(BF16, rows, width),
        shape(BF16, 2 * rows, width),
        shape(BF16, 2 * rows, R_WIDE),
        shape(F32, 1, width),
    )
    return pl.pallas_call(
        combine_kernel,
        grid=(1,),
        out_shape=outs,
        in_specs=[whole(a) for a in operands]
        + [
            pl.BlockSpec((width, 128), lambda i: (0, ROUTER)),
            pl.BlockSpec((width, 1280), lambda i: (0, 0)),
            pl.BlockSpec((width, 128), lambda i: (0, GAINS)),
        ],
        out_specs=tuple(whole(a) for a in outs),
        compiler_params=pltpu.CompilerParams(vmem_limit_bytes=56 << 20),
        name="combine",
    )(*operands, w_r, w_r, w_q)


def finish_kernel(
    p0, p1, p2, t0, t1, t2, fin_q, fin_r, fin_d,
    g0, g1, g2, query, key, value, out, router, gate, up_, down, gains,
):
    i = pl.program_id(0)
    hi, _y, _z, lo, c = place()
    half = i // (pl.num_programs(0) // 2)
    here = jnp.logical_and(c == hi, half == c)
    for part, total, whole in ((p0, t0, g0), (p1, t1, g1), (p2, t2, g2)):

        @pl.when(here)
        def _(part=part, whole=whole):
            whole[...] = part[...].astype(F32)

        @pl.when(jnp.logical_not(here))
        def _(total=total, whole=whole):
            whole[...] = total[...].astype(F32)

    own_rows, width = query.shape
    tile = ROUTER * 128
    for place_ in range(4):

        @pl.when((i == 0) & (lo * 2 + c == place_))
        def _(rows=slice(4 * place_, 4 * place_ + own_rows)):
            query[...] = fin_q[rows, 0:width]
            key[...] = fin_q[rows, width : 2 * width]
            value[...] = fin_q[rows, 2 * width : 3 * width]
            out[...] = fin_r[rows, 0:width]
            router[...] = fin_r[rows, tile : tile + router.shape[1]]
            wide, narrow = 1024, gate.shape[1]
            row, col = iota((wide, narrow), 0), iota((wide, narrow), 1)
            pick = ((col == row - 2 * (row // 16)) & (lax.rem(row, 16) < 14)).astype(BF16)
            for dst, start in ((gate, width), (up_, width + wide)):
                dst[...] = sum(dot(t, pick) for t in split_terms(fin_r[rows, start : start + wide]))
            column = (iota((8, 128), 1) == iota((8, 128), 0)).astype(BF16)
            both = sum(dot_t(column, t) for t in split_terms(fin_q[:, GAINS * 128 : (GAINS + 1) * 128]))
            gains[...] = both[:, rows]

    @pl.when(i == 0)
    def _():
        down[...] = fin_d[0 : down.shape[0], :]


def finish(parts, sums, fin_q, fin_r, fin_d, own_rows, experts, inner):
    steps = 4
    width = fin_d.shape[1]
    whole = lambda a: pl.BlockSpec(a.shape, lambda i: (0, 0))
    block = lambda a: pl.BlockSpec((a.shape[0] // steps, a.shape[1]), lambda i: (i, 0))
    first = steps // 2

    def own_step(i):
        hi, core = lax.axis_index("seq"), lax.rem(lax.axis_index("exp"), 2)
        j = jnp.clip(i - core * first, 0, first - 1)
        return jnp.where(hi == core, j, 0)

    def total_step(i):
        hi, core = lax.axis_index("seq"), lax.rem(lax.axis_index("exp"), 2)
        inside = jnp.logical_and(hi == core, i // first == core)
        return jnp.where(inside, jnp.where(core == 0, first, first - 1), i)

    half_block = lambda a: pl.BlockSpec((2 * a.shape[0] // steps, a.shape[1]), lambda i: (own_step(i), 0))
    total_block = lambda a: pl.BlockSpec((a.shape[0] // steps, a.shape[1]), lambda i: (total_step(i), 0))
    small = (
        [shape(F32, own_rows, width)] * 4
        + [shape(F32, own_rows, experts)]
        + [shape(F32, own_rows, inner)] * 2
        + [shape(F32, inner // experts, width), shape(F32, 8, own_rows)]
    )
    return pl.pallas_call(
        finish_kernel,
        grid=(steps,),
        out_shape=[shape(F32, *t.shape) for t in sums] + small,
        in_specs=[half_block(p) for p in parts] + [total_block(t) for t in sums] + [whole(a) for a in (fin_q, fin_r, fin_d)],
        out_specs=[block(t) for t in sums] + [whole(a) for a in small],
        compiler_params=pltpu.CompilerParams(vmem_limit_bytes=60 << 20),
        name="finish",
    )(*parts, *sums, fin_q, fin_r, fin_d)


def per_device(
    tokens,
    cotangent,
    segments,
    routes,
    norm_gain_attn,
    w_query,
    w_key,
    w_value,
    w_out,
    norm_gain_ffn,
    w_router,
    shared_gate,
    shared_up,
    shared_down,
    expert_gate,
    expert_up,
    expert_down,
):
    rows = tokens.shape[1]
    width = tokens.shape[2]
    experts = w_router.shape[1]
    tokens, grad, routes = tokens[0], cotangent[0], routes[0]
    own_experts = (expert_gate[0], expert_up[0], expert_down[0])

    own_rows = w_query.shape[0]
    shards = (w_query, w_key, w_value, w_out, shared_gate, shared_up, w_router)
    shards += (norm_gain_attn.reshape(1, -1), norm_gain_ffn.reshape(1, -1), shared_down)
    cos, sin = rotary_tables(2 * rows)
    w_q, w_r, w_d, expert_w, act_attn, q, kv, prior, mixed = forward(
        shards, own_experts, tokens, cos, sin, segments
    )
    rows_r, rows_l, hidden_one, act_ffn, gates_t, slot_t, out_s, grad_in_s, grad_gu, grad_sdown = route(
        tokens, mixed, routes, grad, w_q, w_r, w_d
    )
    back_r, back_l, *parts = expert(rows_r, rows_l, expert_w, own_experts)
    back_r, back_l = (a.reshape((experts,) + a.shape[3:]) for a in (back_r, back_l))
    layer_out, grad_hidden, grad_mixed, left_r, right_r, gain_ffn = combine(
        (back_r, back_l, slot_t, gates_t, grad, hidden_one, out_s, grad_in_s, mixed, act_ffn, grad_gu), w_r, w_q
    )
    fin_q, fin_r, fin_d, *sums, grad_tokens = backward(
        (left_r, right_r, grad_sdown.reshape(4, 4, 64, width), act_attn, q, kv, prior, segments)
        + (grad_mixed, cos, sin, tokens, grad_hidden, gain_ffn, w_q),
        parts,
    )
    *expert_grads, query, key, value, out, router, gate, up_grad, down, gains = finish(
        parts, sums, fin_q, fin_r, fin_d, own_rows, experts, shared_gate.shape[1]
    )
    return (
        layer_out[None],
        grad_tokens[None],
        gains[0],
        query,
        key,
        value,
        out,
        gains[1],
        router,
        gate,
        up_grad,
        down,
        *(g[None] for g in expert_grads),
    )


def solution(mesh):
    rows = P("exp", None)
    deep = P("exp", None, None)
    split = P("exp", "seq", None)
    gain = P("exp")
    in_specs = (split, split, rows, split, gain, rows, rows, rows, rows, gain) + (rows,) * 4 + (deep,) * 3
    out_specs = (split, split, gain, rows, rows, rows, rows, gain) + (rows,) * 4 + (deep,) * 3
    return jax.shard_map(per_device, mesh=mesh, in_specs=in_specs, out_specs=out_specs, check_vma=False)
```
